32 devices in a mesh: band: 32 (over z, y, x, core).
Axes of the slice: x: 2, y: 2, z: 4, core: 2. Of those that a mesh axis runs over, the one named last changes fastest.
Arguments:
- orbitals: bfloat16 [64, 884736], P('band'), may hold values from -24 to 24
Outputs:
- exchange: float32 [64, 884736], P('band')
- gram: float32 [64, 2], P('band')
- energy: float32 [], replicated
The draws below stay inside these ranges and needn't reach their ends.
All inputs are finite; a program needn't handle non-finite values.
Results may differ from the reference program's by a relative error of at most 0.0055.
The reference program's roundings to bfloat16 on the way count: a program that leaves them out, or rounds other values in their place, can miss the bound.
Values may be sent and summed in bfloat16 or wider, within the bound.
No kernel may reach another device: no remote copies, remote signals or barrier semaphores. Data moves between devices by JAX's collectives and lax.ppermute only.
A program may use at most 256 MiB of HBM per device.

```python
import math
import jax
import jax.numpy as jnp
from jax import lax

G = 96
B_DEV = 2
NGRID = 884736
NB = 64
N_BAND = 32


def draw_orbitals(key, part):
    key = jax.random.fold_in(key, 11)
    key_scale, key_values = jax.random.split(key, 2)
    band_index = jnp.arange(NB, dtype=jnp.float32)
    band_ramp = 3.0 ** (band_index / max(NB - 1, 1))
    factor = jnp.exp(jax.random.uniform(key_scale, (NB,), jnp.float32, math.log(0.5), 0.0))
    last_band = jnp.arange(NB) == NB - 1
    factor = jnp.where(last_band, jnp.float32(1.0), factor)
    values = jnp.clip(jax.random.normal(key_values, (NB, NGRID), jnp.float32), -4.0, 4.0)
    return (values * (band_ramp * factor)[:, None]).astype(jnp.bfloat16)


def setup_inputs(seed: int = 0) -> dict:
    keys = jax.random.split(jax.random.key(seed), 2)
    orbitals = draw_orbitals(jax.random.fold_in(keys[1], 71), 0)
    return {"orbitals": orbitals}


WAVE_UNIT = 0.05
SCREEN_SQ = 0.0121


def dft_tables(size):
    grid_positions = jnp.arange(size, dtype=jnp.int32)
    phases = (grid_positions[:, None] * grid_positions[None, :]) % size
    angles = phases.astype(jnp.float32) * (2.0 * math.pi / size)
    return jnp.cos(angles).astype(jnp.bfloat16), jnp.sin(angles).astype(jnp.bfloat16)


def coulomb(size):
    grid_positions = jnp.arange(size, dtype=jnp.int32)
    frequency = jnp.where(grid_positions <= size // 2, grid_positions, grid_positions - size).astype(jnp.float32)
    squared = frequency * frequency
    total_sq = WAVE_UNIT * (squared[:, None, None] + squared[None, :, None] + squared[None, None, :])
    safe_sq = jnp.where(total_sq > 0, total_sq, jnp.float32(1.0))
    screened = 4.0 * math.pi * (1.0 - jnp.exp(-total_sq / (4.0 * SCREEN_SQ))) / safe_sq
    return jnp.where(total_sq > 0, screened, jnp.float32(math.pi / SCREEN_SQ))


def along(matrix, field):
    return jnp.einsum('ka,pabc->pbck', matrix.astype(jnp.float32), field.astype(jnp.float32))


def solve_pairs(density, cosine_table, sine_table, kernel):
    real_part = along(cosine_table, density).astype(jnp.bfloat16)
    imag_part = (-along(sine_table, density)).astype(jnp.bfloat16)
    for section in range(2):
        updated_real = (along(cosine_table, real_part) + along(sine_table, imag_part)).astype(jnp.bfloat16)
        new_imag = (along(cosine_table, imag_part) - along(sine_table, real_part)).astype(jnp.bfloat16)
        real_part, imag_part = updated_real, new_imag
    real_part = (real_part * kernel).astype(jnp.bfloat16)
    imag_part = (imag_part * kernel).astype(jnp.bfloat16)
    for section in range(2):
        updated_real = (along(cosine_table, real_part) - along(sine_table, imag_part)).astype(jnp.bfloat16)
        new_imag = (along(cosine_table, imag_part) + along(sine_table, real_part)).astype(jnp.bfloat16)
        real_part, imag_part = updated_real, new_imag
    return (along(cosine_table, real_part) - along(sine_table, imag_part)) / jnp.float32(NGRID)


def reference(orbitals):
    cosine_table, sine_table = dft_tables(G)
    kernel = coulomb(G)
    band_block_list = orbitals.reshape(N_BAND, B_DEV, NGRID)
    previous = jnp.roll(band_block_list, 1, axis=0)

    def pair_block(items):
        own_block, partner = items
        own_wide = own_block.astype(jnp.float32)
        partner_full_row = partner.astype(jnp.float32)
        density = (own_wide[:, None, :] * partner_full_row[None, :, :]).astype(jnp.bfloat16)
        density = density.reshape(B_DEV * B_DEV, G, G, G)
        potential = solve_pairs(density, cosine_table, sine_table, kernel).reshape(B_DEV, B_DEV, NGRID)
        own_terms = jnp.sum(potential * partner_full_row[None, :, :], axis=1)
        partner_terms = jnp.sum(potential * own_wide[:, None, :], axis=0)
        return own_terms, partner_terms

    own_terms, partner_terms = lax.map(pair_block, (band_block_list, previous))
    exchange = own_terms + jnp.roll(partner_terms, -1, axis=0)
    gram = jnp.einsum('egw,ejw->egj', band_block_list.astype(jnp.float32), exchange,
                      precision=lax.Precision.HIGHEST) / jnp.float32(NGRID)
    diagonal = jnp.sum(jnp.diagonal(gram, axis1=1, axis2=2))
    energy = -diagonal / jnp.float32(2 * NB)
    return exchange.reshape(NB, NGRID), gram.reshape(NB, B_DEV), energy
```

```python
import jax
import jax.numpy as jnp
import ml_dtypes
import numpy as np
from jax import lax
from jax.experimental import pallas as pl
from jax.experimental.pallas import tpu as pltpu
from jax.sharding import PartitionSpec as P

G = 96
HALF = G // 2 + 1
NGRID = G * G * G
LANES = 128
ROWS = NGRID // LANES
PLANE = G * G // LANES
QUADS = G // 4
Y_PITCH = 104
WAVE_UNIT = 0.05
SCREEN_SQ = 0.0121
BF16 = jnp.bfloat16
F32 = jnp.float32


def dft_tables():
    n = np.arange(G)
    phases = (n[:, None] * n[None, :]) % G
    angles = phases.astype(np.float32) * np.float32(2.0 * np.pi / G)
    rounded = [f(angles).astype(ml_dtypes.bfloat16).astype(np.float32) for f in (np.cos, np.sin)]
    return rounded[0], rounded[1]


def section_tables():
    c, s = dft_tables()
    h = HALF
    t1 = np.zeros((Y_PITCH, G), np.float32)
    t1[:h] = c[:h]
    t1[h : 2 * h] = -s[:h]
    t2 = np.block([[c, s], [-s, c]])
    t3 = np.zeros((2, 2, LANES, 4, 2, 64), np.float32)
    back = (G - np.arange(h)) % G
    for p in range(2):
        t3[0, p, :G, 0, p, :h] = c[:h].T
        t3[1, p, :G, 0, p, :h] = s[:h].T
        t3[0, p, :G, 1, p, :h] = -s[:h].T
        t3[1, p, :G, 1, p, :h] = c[:h].T
        t3[0, p, :G, 2, p, :h] = c[back].T
        t3[1, p, :G, 2, p, :h] = s[back].T
        t3[0, p, :G, 3, p, :h] = s[back].T
        t3[1, p, :G, 3, p, :h] = -c[back].T
    t3 = t3.reshape(4 * LANES, 4 * LANES)
    order = np.concatenate([np.arange(G // 2), G - 1 - np.arange(G // 2)])
    a1 = np.block([[c[:, order], -s[:, order]], [s[:, order], c[:, order]]])
    rows = np.arange(G).reshape(QUADS, 4).T.reshape(-1)
    a2 = np.block([[c[rows], -s[rows]], [s[rows], c[rows]]])
    weight = np.full((h, 1), 2.0, np.float32)
    weight[0] = weight[h - 1] = 1.0
    a3 = np.zeros((3, 2, 2, 2, 64, 2, LANES), np.float32)
    for third in range(3):
        for lane in range(LANES):
            r, x3 = divmod(third * LANES + lane, G)
            for p in range(2):
                a3[third, r - third, 0, p, :h, p, lane] = weight[:, 0] * c[x3, :h]
                a3[third, r - third, 1, p, :h, p, lane] = -weight[:, 0] * s[x3, :h]
    a3 = a3.reshape(3, 4 * LANES, 2 * LANES)
    sel = np.zeros((2, 2 * LANES, 2 * LANES), np.float32)
    for r in range(4):
        for x in range(G):
            sel[r // 2, r * G + x - (r // 2) * LANES, (r % 2) * LANES + x] = 1.0
    return [t.astype(ml_dtypes.bfloat16) for t in (t1, t2, t3, a1, a2, a3, sel)]


def screening():
    n = np.arange(G)
    m = np.where(n <= G // 2, n, n - G).astype(np.float64)
    sq = m * m
    q2 = WAVE_UNIT * (sq[:HALF, None, None] + sq[None, :, None] + sq[None, None, :HALF])
    safe = np.where(q2 > 0, q2, 1.0)
    kern = 4.0 * np.pi * (1.0 - np.exp(-q2 / (4.0 * SCREEN_SQ))) / safe
    kern = np.where(q2 > 0, kern, np.pi / SCREEN_SQ)
    out = np.zeros((HALF, G, 2, 64), np.float32)
    out[:, :, :, :HALF] = kern[:, :, None, :]
    return out.reshape(HALF * G, LANES)


def dot(a, b):
    return jnp.dot(a, b, preferred_element_type=F32)


def lanes(*parts):
    return jnp.concatenate(parts, axis=1)


def stack(*parts):
    return jnp.concatenate(parts, axis=0)


def widen(src, dst, chunk):
    @pl.loop(0, src.shape[0] // chunk)
    def _(i):
        at = pl.ds(i * chunk, chunk)
        dst[at, :] = src[at, :].astype(F32)


def split_rows(rows, sel_ref):
    first = dot(lanes(rows[0], rows[1]), sel_ref[0])
    second = dot(lanes(rows[1], rows[2]), sel_ref[1])
    return [first[:, :LANES], first[:, LANES:], second[:, :LANES], second[:, LANES:]]


def pairs_kernel(
    own_ref, par_ref, t1, t2, t3, a1, a2, a3, sel, kern,
    own_out, par_out, energy_out,
    own_f, par_f, own_u, yw, z, x34, staged,
):
    widen(own_ref, own_f, 576)
    widen(par_ref, par_f, 576)

    @pl.loop(0, QUADS)
    def _(q):
        for p in range(2):
            rows = [
                own_f[pl.ds(2 * (3 * q + s) + p, G, stride=2 * PLANE), :].astype(BF16)
                for s in range(3)
            ]
            for r, part in enumerate(split_rows(rows, sel)):
                own_u[p, 4 * q + r] = part.astype(BF16)

    half_y = G * Y_PITCH

    @pl.loop(0, QUADS)
    def _(q):
        rows = [par_f[pl.ds(3 * q + s, G, stride=PLANE), :].astype(BF16) for s in range(3)]
        for r, part in enumerate(split_rows(rows, sel)):
            b = 4 * q + r
            density = [(own_u[p, b].astype(F32) * part).astype(BF16) for p in range(2)]
            y = dot(t1[...], lanes(*density))
            for p in range(2):
                at = pl.multiple_of(p * half_y + b * Y_PITCH, 8)
                yw[pl.ds(at, Y_PITCH), :] = y[:, p * LANES : (p + 1) * LANES]

    @pl.loop(0, HALF)
    def _(k1):
        def line(p, part):
            return yw[pl.ds(p * half_y + part * HALF + k1, G, stride=Y_PITCH), :].astype(BF16)

        out = dot(t2[...], stack(lanes(line(0, 0), line(1, 0)), lanes(line(0, 1), line(1, 1))))
        at = pl.ds(pl.multiple_of(k1 * G, 16), G)
        x34[at, : 2 * LANES] = out[:G].astype(BF16)
        x34[at, 2 * LANES :] = out[G:].astype(BF16)

    chunk = 336

    @pl.loop(0, HALF * G // chunk)
    def _(m):
        at = pl.ds(pl.multiple_of(m * chunk, 16), chunk)
        field = x34[at, :]
        factor = kern[at, :]
        for h in range(2):
            out = dot(field, t3[:, 2 * h * LANES : 2 * (h + 1) * LANES])
            for e in range(2):
                spectrum = out[:, e * LANES : (e + 1) * LANES].astype(BF16).astype(F32)
                z[2 * h + e, at, :] = spectrum * factor

    @pl.loop(0, G // 2)
    def _(pair):
        parts = []
        for e in range(2):
            k2 = 2 * pair + e
            mirror = G + jnp.where(k2 == 0, 0, G - k2)
            parts.append(
                stack(
                    z[0, pl.ds(k2, G // 2, stride=G), :].astype(BF16),
                    z[2, pl.ds(mirror, G // 2, stride=G), :].astype(BF16),
                    z[1, pl.ds(k2, G // 2, stride=G), :].astype(BF16),
                    z[3, pl.ds(mirror, G // 2, stride=G), :].astype(BF16),
                )
            )
        out = dot(a1[...], lanes(*parts))
        for e in range(2):
            at = pl.multiple_of((2 * pair + e) * 2 * G, 8)
            yw[pl.ds(at, 2 * G), :] = out[:, e * LANES : (e + 1) * LANES]

    @pl.loop(0, G // 2)
    def _(pair):
        parts = []
        for e in range(2):
            x1 = 2 * pair + e
            parts.append(
                stack(
                    yw[pl.ds(x1, G, stride=2 * G), :].astype(BF16),
                    yw[pl.ds(G + x1, G, stride=2 * G), :].astype(BF16),
                )
            )
        out = dot(a2[...], lanes(*parts))
        for r in range(4):
            block = [
                lanes(
                    out[r * QUADS : (r + 1) * QUADS, e * LANES : (e + 1) * LANES],
                    out[G + r * QUADS : G + (r + 1) * QUADS, e * LANES : (e + 1) * LANES],
                )
                for e in range(2)
            ]
            at = pl.multiple_of((r // 2) * G * QUADS + pair * 2 * QUADS, 16)
            left = (r % 2) * 2 * LANES
            x34[pl.ds(at, 2 * QUADS), left : left + 2 * LANES] = stack(*block).astype(BF16)

    energy_out[...] = jnp.zeros_like(energy_out)
    planes = 8
    block_rows = planes * QUADS
    scale = F32(1.0 / NGRID)

    @pl.loop(0, G // planes)
    def _(ch):
        at = pl.multiple_of(ch * block_rows, 16)
        low = x34[pl.ds(at, block_rows), :]
        high = x34[pl.ds(G * QUADS + at, block_rows), :]
        fields = [low, lanes(low[:, 2 * LANES :], high[:, : 2 * LANES]), high]
        total = jnp.zeros((QUADS, LANES), F32)
        for third in range(3):
            out = dot(fields[third], a3[third]) * scale
            for i in range(planes):
                row = (ch * planes + i) * PLANE + third
                partner = par_f[pl.ds(row, QUADS, stride=3), :]
                sent = jnp.zeros((QUADS, LANES), F32)
                for p in range(2):
                    potential = out[i * QUADS : (i + 1) * QUADS, p * LANES : (p + 1) * LANES]
                    own_at = pl.ds(2 * row + p, QUADS, stride=6)
                    own_out[own_at, :] = potential * partner
                    sent = sent + potential * own_f[own_at, :]
                total = total + sent * partner
                staged[pl.ds(i * PLANE + third, QUADS, stride=3), :] = sent
        energy_out[...] += total
        at = pl.multiple_of(ch * planes * PLANE, 16)
        par_out[pl.ds(at, planes * PLANE), :] = staged[...].astype(BF16)


def pair_terms(own, partner, tables, kern, interpret=False):
    vmem = pl.BlockSpec(memory_space=pltpu.VMEM)
    return pl.pallas_call(
        pairs_kernel,
        out_shape=(
            jax.ShapeDtypeStruct((2 * ROWS, LANES), F32),
            jax.ShapeDtypeStruct((ROWS, LANES), BF16),
            jax.ShapeDtypeStruct((QUADS, LANES), F32),
        ),
        in_specs=[vmem] * 10,
        out_specs=(vmem, vmem, vmem),
        scratch_shapes=[
            pltpu.VMEM((2 * ROWS, LANES), F32),
            pltpu.VMEM((ROWS, LANES), F32),
            pltpu.VMEM((2, G, G, LANES), BF16),
            pltpu.VMEM((2 * G * Y_PITCH, LANES), F32),
            pltpu.VMEM((4, HALF * G, LANES), F32),
            pltpu.VMEM((HALF * G, 4 * LANES), BF16),
            pltpu.VMEM((8 * PLANE, LANES), F32),
        ],
        compiler_params=pltpu.CompilerParams(vmem_limit_bytes=62 * 1024 * 1024),
        cost_estimate=pl.CostEstimate(
            flops=20_000_000_000, bytes_accessed=20_000_000, transcendentals=0
        ),
        interpret=interpret,
        name="pair_terms",
    )(own, partner, *tables, kern)


BLOCK = 576


def sum_kernel(own_ref, first_ref, second_ref, back0_ref, back1_ref, out_ref, gram_ref, orb, exch):
    orb[...] = own_ref[...].astype(F32)
    exch[...] = first_ref[...] + second_ref[...]
    total = []
    for p, back in enumerate((back0_ref, back1_ref)):
        at = pl.ds(p, BLOCK, stride=2)
        value = exch[at, :] + back[...].astype(F32)
        exch[at, :] = value
        total.append(value)
    out_ref[...] = exch[...]

    @pl.when(pl.program_id(0) == 0)
    def _():
        gram_ref[...] = jnp.zeros_like(gram_ref)

    for i in range(2):
        bands = orb[pl.ds(i, BLOCK, stride=2), :]
        for p in range(2):
            gram_ref[2 * i + p] += jnp.sum((bands * total[p]).reshape(-1, 8, LANES), axis=0)


def add_returned(own, first, second, back0, back1, interpret=False):
    wide = pl.BlockSpec((2 * BLOCK, LANES), lambda i: (i, 0))
    flat = pl.BlockSpec((BLOCK, LANES), lambda i: (i, 0))
    return pl.pallas_call(
        sum_kernel,
        grid=(ROWS // BLOCK,),
        out_shape=(
            jax.ShapeDtypeStruct((2 * ROWS, LANES), F32),
            jax.ShapeDtypeStruct((4, 8, LANES), F32),
        ),
        in_specs=[wide, wide, wide, flat, flat],
        out_specs=(wide, pl.BlockSpec((4, 8, LANES), lambda i: (0, 0, 0))),
        scratch_shapes=[pltpu.VMEM((2 * BLOCK, LANES), F32)] * 2,
        interpret=interpret,
        name="add_returned",
    )(own, first, second, back0, back1)


def from_behind(block, axis, distance):
    size = lax.axis_size(axis)
    return lax.ppermute(block, axis, [((i - distance) % size, i) for i in range(size)])


def sum_over(value, axis):
    size = lax.axis_size(axis)
    if size & (size - 1):
        return lax.psum(value, axis)
    step = 1
    while step < size:
        value = value + lax.ppermute(value, axis, [(i ^ step, i) for i in range(size)])
        step *= 2
    return value


def per_device(orbitals):
    tables = section_tables()
    kern = screening()
    bands = orbitals.reshape(2, ROWS, LANES)
    own = bands.transpose(1, 0, 2).reshape(2 * ROWS, LANES)
    previous = [from_behind(bands[j], "band", 1) for j in range(2)]
    first, sent0, energy0 = pair_terms(own, previous[0], tables, kern)
    back0 = from_behind(sent0, "band", -1)
    second, sent1, energy1 = pair_terms(own, previous[1], tables, kern)
    back1 = from_behind(sent1, "band", -1)
    pair_energy = jnp.sum(energy0 + energy1).reshape(1, 1)
    total = sum_over(jnp.broadcast_to(pair_energy, (8, LANES)), "band")[0, 0]
    energy = -2.0 * total / F32(NGRID) / F32(2 * lax.axis_size("band") * orbitals.shape[0])
    exchange, gram = add_returned(own, first, second, back0, back1)
    gram = jnp.sum(gram, axis=(1, 2)).reshape(2, 2) / F32(NGRID)
    exchange = exchange.reshape(ROWS, 2, LANES).transpose(1, 0, 2).reshape(2, NGRID)
    return exchange, gram, energy


def solution(mesh):
    return jax.shard_map(
        per_device,
        mesh=mesh,
        in_specs=(P("band", None),),
        out_specs=(P("band", None), P("band", None), P()),
        check_vma=False,
    )
```

```python
import jax
import jax.numpy as jnp
import ml_dtypes
import numpy as np
from jax import lax
from jax.experimental import pallas as pl
from jax.experimental.pallas import tpu as pltpu
from jax.sharding import PartitionSpec as P

G = 96
HALF = G // 2 + 1
NGRID = G * G * G
LANES = 128
ROWS = NGRID // LANES
PLANE = G * G // LANES
QUADS = G // 4
KPAD = HALF + 1
Y_ROWS = 104
Y_PITCH = Y_ROWS + 1
Z_PITCH = G + 1
W_PITCH = 2 * G + 1
F_PITCH = PLANE + 1
WAVE_UNIT = 0.05
SCREEN_SQ = 0.0121
BF16 = jnp.bfloat16
F32 = jnp.float32


def dft_tables():
    n = np.arange(G)
    phases = (n[:, None] * n[None, :]) % G
    angles = phases.astype(np.float32) * np.float32(2.0 * np.pi / G)
    rounded = [f(angles).astype(ml_dtypes.bfloat16).astype(np.float32) for f in (np.cos, np.sin)]
    return rounded[0], rounded[1]


def section_tables():
    c, s = dft_tables()
    h = HALF
    t1 = np.zeros((Y_ROWS, G), np.float32)
    t1[:h] = c[:h]
    t1[h : 2 * h] = -s[:h]
    t2 = np.block([[c, s], [-s, c]])
    t3 = np.zeros((2, 2, LANES, 4, 2, 64), np.float32)
    back = (G - np.arange(h)) % G
    for p in range(2):
        t3[0, p, :G, 0, p, :h] = c[:h].T
        t3[1, p, :G, 0, p, :h] = s[:h].T
        t3[0, p, :G, 1, p, :h] = -s[:h].T
        t3[1, p, :G, 1, p, :h] = c[:h].T
        t3[0, p, :G, 2, p, :h] = c[back].T
        t3[1, p, :G, 2, p, :h] = s[back].T
        t3[0, p, :G, 3, p, :h] = s[back].T
        t3[1, p, :G, 3, p, :h] = -c[back].T
    t3 = t3.reshape(4 * LANES, 4 * LANES)
    order = np.concatenate([np.arange(G // 2), G - 1 - np.arange(G // 2)])
    a1 = np.block([[c[:, order], -s[:, order]], [s[:, order], c[:, order]]])
    rows = np.arange(G).reshape(QUADS, 4).T.reshape(-1)
    a2 = np.block([[c[rows], -s[rows]], [s[rows], c[rows]]])
    weight = np.full((h, 1), 2.0, np.float32)
    weight[0] = weight[h - 1] = 1.0
    a3 = np.zeros((3, 2, 2, 2, 64, 2, LANES), np.float32)
    for third in range(3):
        for lane in range(LANES):
            r, x3 = divmod(third * LANES + lane, G)
            for p in range(2):
                a3[third, r - third, 0, p, :h, p, lane] = weight[:, 0] * c[x3, :h]
                a3[third, r - third, 1, p, :h, p, lane] = -weight[:, 0] * s[x3, :h]
    a3 = a3.reshape(3, 4 * LANES, 2 * LANES)
    sel = np.zeros((2, 2 * LANES, 2 * LANES), np.float32)
    for r in range(4):
        for x in range(G):
            sel[r // 2, r * G + x - (r // 2) * LANES, (r % 2) * LANES + x] = 1.0
    return [t.astype(ml_dtypes.bfloat16) for t in (t1, t2, t3, a1, a2, a3, sel)]


def screening():
    n = np.arange(G)
    m = np.where(n <= G // 2, n, n - G).astype(np.float64)
    sq = m * m
    q2 = WAVE_UNIT * (sq[:HALF, None, None] + sq[None, :, None] + sq[None, None, :HALF])
    safe = np.where(q2 > 0, q2, 1.0)
    kern = 4.0 * np.pi * (1.0 - np.exp(-q2 / (4.0 * SCREEN_SQ))) / safe
    kern = np.where(q2 > 0, kern, np.pi / SCREEN_SQ)
    out = np.zeros((KPAD, G, 2, 64), np.float32)
    out[:HALF, :, :, :HALF] = kern[:, :, None, :]
    return out.reshape(KPAD * G, LANES)


def dot(a, b):
    return jnp.dot(a, b, preferred_element_type=F32)


def lanes(*parts):
    return jnp.concatenate(parts, axis=1)


def stack(*parts):
    return jnp.concatenate(parts, axis=0)


def split_rows(rows, sel_ref):
    first = dot(lanes(rows[0], rows[1]), sel_ref[0])
    second = dot(lanes(rows[1], rows[2]), sel_ref[1])
    return [first[:, :LANES], first[:, LANES:], second[:, :LANES], second[:, LANES:]]


def widen_planes(src, dst):
    @pl.loop(0, G // 2)
    def _(i):
        value = src[pl.ds(pl.multiple_of(i * 2 * PLANE, 16), 2 * PLANE), :].astype(F32)
        dst[pl.ds(2 * i * F_PITCH, PLANE), :] = value[:PLANE]
        dst[pl.ds((2 * i + 1) * F_PITCH, PLANE), :] = value[PLANE:]


def split_kernel(raw_ref, out0, out1, wide):
    wide[...] = raw_ref[...].astype(F32)
    for p, out in enumerate((out0, out1)):
        out[...] = wide[pl.ds(p, out.shape[0], stride=2), :].astype(BF16)


def split_bands(raw, interpret=False):
    rows = 1152
    flat = pl.BlockSpec((rows, LANES), lambda i: (i, 0))
    return pl.pallas_call(
        split_kernel,
        grid=(ROWS // rows,),
        out_shape=(jax.ShapeDtypeStruct((ROWS, LANES), BF16),) * 2,
        in_specs=[pl.BlockSpec((2 * rows, LANES), lambda i: (i, 0))],
        out_specs=(flat, flat),
        scratch_shapes=[pltpu.VMEM((2 * rows, LANES), F32)],
        interpret=interpret,
        name="split_bands",
    )(raw)


def rows_kernel(own0, own1, sel, out, wide):
    for p, own in enumerate((own0, own1)):
        widen_planes(own, wide)

        @pl.loop(0, QUADS)
        def _(q):
            rows = [wide[pl.ds(3 * q + s, G, stride=F_PITCH), :].astype(BF16) for s in range(3)]
            for r, part in enumerate(split_rows(rows, sel)):
                out[p, 4 * q + r] = part.astype(BF16)


def padded_rows(own0, own1, sel, interpret=False):
    vmem = pl.BlockSpec(memory_space=pltpu.VMEM)
    return pl.pallas_call(
        rows_kernel,
        out_shape=jax.ShapeDtypeStruct((2, G, G, LANES), BF16),
        in_specs=[vmem] * 3,
        out_specs=vmem,
        scratch_shapes=[pltpu.VMEM((G * F_PITCH, LANES), F32)],
        compiler_params=pltpu.CompilerParams(vmem_limit_bytes=32 * 1024 * 1024),
        interpret=interpret,
        name="padded_rows",
    )(own0, own1, sel)


def pairs_kernel(
    own0, own1, own_u, par_ref, t1, t2, t3, a1, a2, a3, sel, kern,
    own_out, par_out, energy_out,
    par_f, yw, z, x34, own_f, staged,
):
    widen_planes(par_ref, par_f)
    half_y = G * Y_PITCH

    @pl.loop(0, QUADS)
    def _(q):
        rows = [par_f[pl.ds(3 * q + s, G, stride=F_PITCH), :].astype(BF16) for s in range(3)]
        for r, part in enumerate(split_rows(rows, sel)):
            b = 4 * q + r
            density = [(own_u[p, b].astype(F32) * part).astype(BF16) for p in range(2)]
            y = dot(t1[...], lanes(*density))
            for p in range(2):
                yw[pl.ds(p * half_y + b * Y_PITCH, Y_ROWS), :] = y[:, p * LANES : (p + 1) * LANES]

    @pl.loop(0, HALF, unroll=7)
    def _(k1):
        def line(p, part):
            return yw[pl.ds(p * half_y + part * HALF + k1, G, stride=Y_PITCH), :].astype(BF16)

        out = dot(t2[...], stack(lanes(line(0, 0), line(1, 0)), lanes(line(0, 1), line(1, 1))))
        at = pl.ds(pl.multiple_of(k1 * G, 16), G)
        x34[at, : 2 * LANES] = out[:G].astype(BF16)
        x34[at, 2 * LANES :] = out[G:].astype(BF16)

    @pl.loop(0, KPAD // 2)
    def _(m):
        at = pl.ds(pl.multiple_of(m * 2 * G, 16), 2 * G)
        field = x34[at, :]
        factor = kern[at, :]
        for h in range(2):
            out = dot(field, t3[:, 2 * h * LANES : 2 * (h + 1) * LANES])
            for e in range(2):
                spectrum = out[:, e * LANES : (e + 1) * LANES].astype(BF16).astype(F32)
                value = spectrum * factor
                for i in range(2):
                    row = (2 * m + i) * Z_PITCH
                    z[2 * h + e, pl.ds(row, G), :] = value[i * G : (i + 1) * G]

    @pl.loop(0, G // 2, unroll=2)
    def _(pair):
        parts = []
        for e in range(2):
            k2 = 2 * pair + e
            mirror = Z_PITCH + jnp.where(k2 == 0, 0, G - k2)
            parts.append(
                stack(
                    z[0, pl.ds(k2, G // 2, stride=Z_PITCH), :].astype(BF16),
                    z[2, pl.ds(mirror, G // 2, stride=Z_PITCH), :].astype(BF16),
                    z[1, pl.ds(k2, G // 2, stride=Z_PITCH), :].astype(BF16),
                    z[3, pl.ds(mirror, G // 2, stride=Z_PITCH), :].astype(BF16),
                )
            )
        out = dot(a1[...], lanes(*parts))
        for e in range(2):
            at = (2 * pair + e) * W_PITCH
            yw[pl.ds(at, 2 * G), :] = out[:, e * LANES : (e + 1) * LANES]

    @pl.loop(0, G // 2, unroll=2)
    def _(pair):
        parts = []
        for e in range(2):
            x1 = 2 * pair + e
            parts.append(
                stack(
                    yw[pl.ds(x1, G, stride=W_PITCH), :].astype(BF16),
                    yw[pl.ds(G + x1, G, stride=W_PITCH), :].astype(BF16),
                )
            )
        out = dot(a2[...], lanes(*parts))
        for r in range(4):
            block = [
                lanes(
                    out[r * QUADS : (r + 1) * QUADS, e * LANES : (e + 1) * LANES],
                    out[G + r * QUADS : G + (r + 1) * QUADS, e * LANES : (e + 1) * LANES],
                )
                for e in range(2)
            ]
            at = pl.multiple_of((r // 2) * G * QUADS + pair * 2 * QUADS, 16)
            left = (r % 2) * 2 * LANES
            x34[pl.ds(at, 2 * QUADS), left : left + 2 * LANES] = stack(*block).astype(BF16)

    energy_out[...] = jnp.zeros_like(energy_out)
    planes = 8
    block_rows = planes * QUADS
    scale = F32(1.0 / NGRID)

    @pl.loop(0, G // planes)
    def _(ch):
        at = pl.multiple_of(ch * block_rows, 16)
        low = x34[pl.ds(at, block_rows), :]
        high = x34[pl.ds(G * QUADS + at, block_rows), :]
        fields = [low, lanes(low[:, 2 * LANES :], high[:, : 2 * LANES]), high]
        flat = pl.ds(pl.multiple_of(ch * planes * PLANE, 16), planes * PLANE)
        own_f[0] = own0[flat, :].astype(F32)
        own_f[1] = own1[flat, :].astype(F32)
        total = jnp.zeros((QUADS, LANES), F32)
        for third in range(3):
            out = dot(fields[third], a3[third]) * scale
            for i in range(planes):
                plane = ch * planes + i
                partner = par_f[pl.ds(plane * F_PITCH + third, QUADS, stride=3), :]
                here = pl.ds(i * PLANE + third, QUADS, stride=3)
                there = pl.ds(plane * PLANE + third, QUADS, stride=3)
                sent = jnp.zeros((QUADS, LANES), F32)
                for p in range(2):
                    potential = out[i * QUADS : (i + 1) * QUADS, p * LANES : (p + 1) * LANES]
                    own_out[p, there, :] = potential * partner
                    sent = sent + potential * own_f[p, here, :]
                total = total + sent * partner
                staged[here, :] = sent
        energy_out[...] += total
        par_out[flat, :] = staged[...].astype(BF16)


def pair_terms(own0, own1, own_u, partner, tables, kern, interpret=False):
    vmem = pl.BlockSpec(memory_space=pltpu.VMEM)
    return pl.pallas_call(
        pairs_kernel,
        out_shape=(
            jax.ShapeDtypeStruct((2, ROWS, LANES), F32),
            jax.ShapeDtypeStruct((ROWS, LANES), BF16),
            jax.ShapeDtypeStruct((QUADS, LANES), F32),
        ),
        in_specs=[vmem] * 12,
        out_specs=(vmem, vmem, vmem),
        scratch_shapes=[
            pltpu.VMEM((G * F_PITCH, LANES), F32),
            pltpu.VMEM((2 * G * Y_PITCH, LANES), F32),
            pltpu.VMEM((4, KPAD * Z_PITCH, LANES), F32),
            pltpu.VMEM((KPAD * G, 4 * LANES), BF16),
            pltpu.VMEM((2, 8 * PLANE, LANES), F32),
            pltpu.VMEM((8 * PLANE, LANES), F32),
        ],
        compiler_params=pltpu.CompilerParams(vmem_limit_bytes=62 * 1024 * 1024),
        cost_estimate=pl.CostEstimate(
            flops=20_000_000_000, bytes_accessed=20_000_000, transcendentals=0
        ),
        interpret=interpret,
        name="pair_terms",
    )(own0, own1, own_u, partner, *tables, kern)


BLOCK = 1152


def first_sum_kernel(own0, own1, first, second, back0, exch0, part1, gram_ref):
    @pl.when(pl.program_id(0) == 0)
    def _():
        gram_ref[...] = jnp.zeros_like(gram_ref)

    exchange = first[0] + second[0] + back0[...].astype(F32)
    exch0[...] = exchange
    part1[...] = first[1] + second[1]
    for i, own in enumerate((own0, own1)):
        gram_ref[i] += jnp.sum((own[...].astype(F32) * exchange).reshape(-1, 8, LANES), axis=0)


def first_sum(own, first, second, back0, interpret=False):
    flat = pl.BlockSpec((BLOCK, LANES), lambda i: (i, 0))
    both = pl.BlockSpec((2, BLOCK, LANES), lambda i: (0, i, 0))
    return pl.pallas_call(
        first_sum_kernel,
        grid=(ROWS // BLOCK,),
        out_shape=(
            jax.ShapeDtypeStruct((ROWS, LANES), F32),
            jax.ShapeDtypeStruct((ROWS, LANES), F32),
            jax.ShapeDtypeStruct((2, 8, LANES), F32),
        ),
        in_specs=[flat, flat, both, both, flat],
        out_specs=(flat, flat, pl.BlockSpec((2, 8, LANES), lambda i: (0, 0, 0))),
        compiler_params=pltpu.CompilerParams(vmem_limit_bytes=32 * 1024 * 1024),
        interpret=interpret,
        name="first_sum",
    )(*own, first, second, back0)


def last_sum_kernel(own0, own1, exch0, part1, back1, out_ref, gram_ref):
    @pl.when(pl.program_id(0) == 0)
    def _():
        gram_ref[...] = jnp.zeros_like(gram_ref)

    exchange = part1[...] + back1[...].astype(F32)
    out_ref[pl.ds(0, BLOCK, stride=2), :] = exch0[...]
    out_ref[pl.ds(1, BLOCK, stride=2), :] = exchange
    for i, own in enumerate((own0, own1)):
        gram_ref[i] += jnp.sum((own[...].astype(F32) * exchange).reshape(-1, 8, LANES), axis=0)


def last_sum(own, exch0, part1, back1, interpret=False):
    flat = pl.BlockSpec((BLOCK, LANES), lambda i: (i, 0))
    return pl.pallas_call(
        last_sum_kernel,
        grid=(ROWS // BLOCK,),
        out_shape=(
            jax.ShapeDtypeStruct((2 * ROWS, LANES), F32),
            jax.ShapeDtypeStruct((2, 8, LANES), F32),
        ),
        in_specs=[flat] * 5,
        out_specs=(
            pl.BlockSpec((2 * BLOCK, LANES), lambda i: (i, 0)),
            pl.BlockSpec((2, 8, LANES), lambda i: (0, 0, 0)),
        ),
        compiler_params=pltpu.CompilerParams(vmem_limit_bytes=32 * 1024 * 1024),
        interpret=interpret,
        name="last_sum",
    )(*own, exch0, part1, back1)


def from_behind(block, axis, distance):
    size = lax.axis_size(axis)
    return lax.ppermute(block, axis, [((i - distance) % size, i) for i in range(size)])


def sum_over(value, axis):
    size = lax.axis_size(axis)
    if size & (size - 1):
        return lax.psum(value, axis)
    steps = [1 << bit for bit in range(size.bit_length() - 1)]
    for step in [s for s in steps if s != 2] + [s for s in steps if s == 2]:
        value = value + lax.ppermute(value, axis, [(i ^ step, i) for i in range(size)])
    return value


def per_device(orbitals):
    tables = section_tables()
    kern = screening()
    raw = orbitals.reshape(2, ROWS, LANES).transpose(1, 0, 2).reshape(2 * ROWS, LANES)
    own = split_bands(raw)
    previous = [from_behind(own[j], "band", 1) for j in range(2)]
    own_u = padded_rows(*own, tables[-1])
    first, sent0, energy0 = pair_terms(*own, own_u, previous[0], tables, kern)
    back0 = from_behind(sent0, "band", -1)
    second, sent1, energy1 = pair_terms(*own, own_u, previous[1], tables, kern)
    back1 = from_behind(sent1, "band", -1)
    pair_energy = jnp.sum(energy0 + energy1).reshape(1, 1)
    total = sum_over(jnp.broadcast_to(pair_energy, (8, LANES)), "band")[0, 0]
    energy = -2.0 * total / F32(NGRID) / F32(2 * lax.axis_size("band") * orbitals.shape[0])
    exch0, part1, gram0 = first_sum(own, first, second, back0)
    exchange, gram1 = last_sum(own, exch0, part1, back1)
    gram = jnp.stack([jnp.sum(g, axis=(1, 2)) for g in (gram0, gram1)], axis=1) / F32(NGRID)
    exchange = exchange.reshape(ROWS, 2, LANES).transpose(1, 0, 2).reshape(2, NGRID)
    return exchange, gram, energy


def solution(mesh):
    return jax.shard_map(
        per_device,
        mesh=mesh,
        in_specs=(P("band", None),),
        out_specs=(P("band", None), P("band", None), P()),
        check_vma=False,
    )
```

```python
import functools

import jax
import jax.numpy as jnp
import ml_dtypes
import numpy as np
from jax import lax
from jax.experimental import pallas as pl
from jax.experimental.pallas import tpu as pltpu
from jax.sharding import PartitionSpec as P

G = 96
HALF = G // 2 + 1
NGRID = G * G * G
LANES = 128
ROWS = NGRID // LANES
PLANE = G * G // LANES
QUADS = G // 4
KPAD = HALF + 1
Y_ROWS = 104
Y_PITCH = Y_ROWS + 1
Z_PITCH = G + 1
W_PITCH = 2 * G + 1
F_PITCH = PLANE + 1
WAVE_UNIT = 0.05
SCREEN_SQ = 0.0121
BF16 = jnp.bfloat16
F32 = jnp.float32


def dft_tables():
    n = np.arange(G)
    phases = (n[:, None] * n[None, :]) % G
    angles = phases.astype(np.float32) * np.float32(2.0 * np.pi / G)
    rounded = [f(angles).astype(ml_dtypes.bfloat16).astype(np.float32) for f in (np.cos, np.sin)]
    return rounded[0], rounded[1]


def section_tables():
    c, s = dft_tables()
    h = HALF
    t1 = np.zeros((Y_ROWS, G), np.float32)
    t1[:h] = c[:h]
    t1[h : 2 * h] = -s[:h]
    t2 = np.block([[c, s], [-s, c]])
    t3 = np.zeros((2, LANES, 4, 64), np.float32)
    back = (G - np.arange(h)) % G
    t3[0, :G, 0, :h] = c[:h].T
    t3[1, :G, 0, :h] = s[:h].T
    t3[0, :G, 1, :h] = -s[:h].T
    t3[1, :G, 1, :h] = c[:h].T
    t3[0, :G, 2, :h] = c[back].T
    t3[1, :G, 2, :h] = s[back].T
    t3[0, :G, 3, :h] = s[back].T
    t3[1, :G, 3, :h] = -c[back].T
    t3 = t3.reshape(2 * LANES, 4 * 64)
    order = np.concatenate([np.arange(G // 2), G - 1 - np.arange(G // 2)])
    a1 = np.block([[c[:, order], -s[:, order]], [s[:, order], c[:, order]]])
    rows = np.arange(G).reshape(QUADS, 4).T.reshape(-1)
    a2 = np.block([[c[rows], -s[rows]], [s[rows], c[rows]]])
    weight = np.full((h, 1), 2.0, np.float32)
    weight[0] = weight[h - 1] = 1.0
    a3 = np.zeros((3, 2, 2, 2, 64, 2, LANES), np.float32)
    for third in range(3):
        for lane in range(LANES):
            r, x3 = divmod(third * LANES + lane, G)
            for p in range(2):
                a3[third, r - third, 0, p, :h, p, lane] = weight[:, 0] * c[x3, :h]
                a3[third, r - third, 1, p, :h, p, lane] = -weight[:, 0] * s[x3, :h]
    a3 = a3.reshape(3, 4 * LANES, 2 * LANES)
    sel = np.zeros((2, 2 * LANES, 2 * LANES), np.float32)
    for r in range(4):
        for x in range(G):
            sel[r // 2, r * G + x - (r // 2) * LANES, (r % 2) * LANES + x] = 1.0
    return [t.astype(ml_dtypes.bfloat16) for t in (t1, t2, t3, a1, a2, a3, sel)]


def screening():
    n = np.arange(G)
    m = np.where(n <= G // 2, n, n - G).astype(np.float64)
    sq = m * m
    q2 = WAVE_UNIT * (sq[:HALF, None, None] + sq[None, :, None] + sq[None, None, :HALF])
    safe = np.where(q2 > 0, q2, 1.0)
    kern = 4.0 * np.pi * (1.0 - np.exp(-q2 / (4.0 * SCREEN_SQ))) / safe
    kern = np.where(q2 > 0, kern, np.pi / SCREEN_SQ)
    out = np.zeros((KPAD, G, 2, 64), np.float32)
    out[:HALF, :, :, :HALF] = kern[:, :, None, :]
    return out.reshape(KPAD * G, LANES)


def dot(a, b):
    return jnp.dot(a, b, preferred_element_type=F32)


def lanes(*parts):
    return jnp.concatenate(parts, axis=1)


def stack(*parts):
    return jnp.concatenate(parts, axis=0)


def split_rows(rows, sel_ref):
    first = dot(lanes(rows[0], rows[1]), sel_ref[0])
    second = dot(lanes(rows[1], rows[2]), sel_ref[1])
    return [first[:, :LANES], first[:, LANES:], second[:, :LANES], second[:, LANES:]]


def widen_planes(src, dst):
    @pl.loop(0, G // 2)
    def _(i):
        value = src[pl.ds(pl.multiple_of(i * 2 * PLANE, 16), 2 * PLANE), :].astype(F32)
        dst[pl.ds(2 * i * F_PITCH, PLANE), :] = value[:PLANE]
        dst[pl.ds((2 * i + 1) * F_PITCH, PLANE), :] = value[PLANE:]


def band_kernel(p, raw_ref, out, wide):
    wide[...] = raw_ref[...].astype(F32)
    out[...] = wide[pl.ds(p, out.shape[0], stride=2), :].astype(BF16)


def take_band(raw, p, interpret=False):
    rows = 1152
    return pl.pallas_call(
        functools.partial(band_kernel, p),
        grid=(ROWS // rows,),
        out_shape=jax.ShapeDtypeStruct((ROWS, LANES), BF16),
        in_specs=[pl.BlockSpec((2 * rows, LANES), lambda i: (i, 0))],
        out_specs=pl.BlockSpec((rows, LANES), lambda i: (i, 0)),
        scratch_shapes=[pltpu.VMEM((2 * rows, LANES), F32)],
        compiler_params=pltpu.CompilerParams(vmem_limit_bytes=62 * 1024 * 1024),
        interpret=interpret,
        name="take_band",
    )(raw)


def rows_kernel(own0, own1, sel, out, wide):
    for p, own in enumerate((own0, own1)):
        widen_planes(own, wide)

        @pl.loop(0, QUADS)
        def _(q):
            rows = [wide[pl.ds(3 * q + s, G, stride=F_PITCH), :].astype(BF16) for s in range(3)]
            for r, part in enumerate(split_rows(rows, sel)):
                out[p, 4 * q + r] = part.astype(BF16)


def padded_rows(own0, own1, sel, interpret=False):
    vmem = pl.BlockSpec(memory_space=pltpu.VMEM)
    return pl.pallas_call(
        rows_kernel,
        out_shape=jax.ShapeDtypeStruct((2, G, G, LANES), BF16),
        in_specs=[vmem] * 3,
        out_specs=vmem,
        scratch_shapes=[pltpu.VMEM((G * F_PITCH, LANES), F32)],
        compiler_params=pltpu.CompilerParams(vmem_limit_bytes=62 * 1024 * 1024),
        interpret=interpret,
        name="padded_rows",
    )(own0, own1, sel)


def pairs_kernel(
    own0, own1, own_u, kern, par_ref, t1, t2, t3, a1, a2, a3, sel,
    own_out, par_out, energy_out,
    own_v, own_uv, kern_v, own_ov, par_ov, par_f, par_u, yw, z, x34, own_f, staged, sems,
):
    loads = [
        pltpu.make_async_copy(own_u, own_uv, sems.at[0]),
        pltpu.make_async_copy(kern, kern_v, sems.at[1]),
        pltpu.make_async_copy(own0, own_v.at[0], sems.at[2]),
        pltpu.make_async_copy(own1, own_v.at[1], sems.at[3]),
    ]
    for load in loads:
        load.start()

    widen_planes(par_ref, par_f)

    @pl.loop(0, QUADS, unroll=4)
    def _(q):
        rows = [par_f[pl.ds(3 * q + s, G, stride=F_PITCH), :].astype(BF16) for s in range(3)]
        for r, part in enumerate(split_rows(rows, sel)):
            par_u[4 * q + r] = part.astype(BF16)

    half_y = G * Y_PITCH
    loads[0].wait()

    @pl.loop(0, G // 2, unroll=4)
    def _(i):
        density = []
        for e in range(2):
            partner = par_u[2 * i + e].astype(F32)
            for p in range(2):
                density.append((own_uv[p, 2 * i + e].astype(F32) * partner).astype(BF16))
        out = dot(t1[...], lanes(*density))
        for e in range(2):
            for p in range(2):
                at = pl.ds(p * half_y + (2 * i + e) * Y_PITCH, Y_ROWS)
                yw[at, :] = out[:, (2 * e + p) * LANES : (2 * e + p + 1) * LANES]

    @pl.loop(0, HALF, unroll=7)
    def _(k1):
        def line(p, part):
            return yw[pl.ds(p * half_y + part * HALF + k1, G, stride=Y_PITCH), :].astype(BF16)

        out = dot(t2[...], stack(lanes(line(0, 0), line(1, 0)), lanes(line(0, 1), line(1, 1))))
        at = pl.ds(pl.multiple_of(k1 * G, 16), G)
        for p in range(2):
            for part in range(2):
                left = (2 * p + part) * LANES
                value = out[part * G : (part + 1) * G, p * LANES : (p + 1) * LANES]
                x34[at, left : left + LANES] = value.astype(BF16)

    loads[1].wait()

    @pl.loop(0, KPAD // 2, unroll=5)
    def _(m):
        at = pl.ds(pl.multiple_of(m * 2 * G, 16), 2 * G)
        factor = kern_v[at, :]
        out = [
            dot(x34[at, 2 * p * LANES : 2 * (p + 1) * LANES], t3[...]).astype(BF16)
            for p in range(2)
        ]
        for part in range(4):
            spectrum = lanes(*[o[:, part * 64 : (part + 1) * 64] for o in out]).astype(F32)
            value = spectrum * factor
            for i in range(2):
                row = (2 * m + i) * Z_PITCH
                z[part, pl.ds(row, G), :] = value[i * G : (i + 1) * G]

    @pl.loop(0, G // 4, unroll=3)
    def _(four):
        parts = []
        for e in range(4):
            k2 = 4 * four + e
            mirror = Z_PITCH + jnp.where(k2 == 0, 0, G - k2)
            parts.append(
                stack(
                    z[0, pl.ds(k2, G // 2, stride=Z_PITCH), :].astype(BF16),
                    z[2, pl.ds(mirror, G // 2, stride=Z_PITCH), :].astype(BF16),
                    z[1, pl.ds(k2, G // 2, stride=Z_PITCH), :].astype(BF16),
                    z[3, pl.ds(mirror, G // 2, stride=Z_PITCH), :].astype(BF16),
                )
            )
        out = dot(a1[...], lanes(*parts))
        for e in range(4):
            at = (4 * four + e) * W_PITCH
            yw[pl.ds(at, 2 * G), :] = out[:, e * LANES : (e + 1) * LANES]

    @pl.loop(0, G // 4, unroll=3)
    def _(four):
        parts = []
        for e in range(4):
            x1 = 4 * four + e
            parts.append(
                stack(
                    yw[pl.ds(x1, G, stride=W_PITCH), :].astype(BF16),
                    yw[pl.ds(G + x1, G, stride=W_PITCH), :].astype(BF16),
                )
            )
        out = dot(a2[...], lanes(*parts))
        for r in range(4):
            block = [
                lanes(
                    out[r * QUADS : (r + 1) * QUADS, e * LANES : (e + 1) * LANES],
                    out[G + r * QUADS : G + (r + 1) * QUADS, e * LANES : (e + 1) * LANES],
                )
                for e in range(4)
            ]
            at = pl.multiple_of((r // 2) * G * QUADS + four * 4 * QUADS, 16)
            left = (r % 2) * 2 * LANES
            x34[pl.ds(at, 4 * QUADS), left : left + 2 * LANES] = stack(*block).astype(BF16)

    loads[2].wait()
    loads[3].wait()
    energy_out[...] = jnp.zeros_like(energy_out)
    planes = 8
    block_rows = planes * QUADS
    scale = F32(1.0 / NGRID)

    @pl.loop(0, G // planes)
    def _(ch):
        at = pl.multiple_of(ch * block_rows, 16)
        low = x34[pl.ds(at, block_rows), :]
        high = x34[pl.ds(G * QUADS + at, block_rows), :]
        fields = [low, lanes(low[:, 2 * LANES :], high[:, : 2 * LANES]), high]
        flat = pl.ds(pl.multiple_of(ch * planes * PLANE, 16), planes * PLANE)
        own_f[...] = own_v[:, flat, :].astype(F32)
        total = jnp.zeros((QUADS, LANES), F32)
        for third in range(3):
            out = dot(fields[third], a3[third]) * scale
            for i in range(planes):
                plane = ch * planes + i
                partner = par_f[pl.ds(plane * F_PITCH + third, QUADS, stride=3), :]
                here = pl.ds(i * PLANE + third, QUADS, stride=3)
                there = pl.ds(plane * PLANE + third, QUADS, stride=3)
                sent = jnp.zeros((QUADS, LANES), F32)
                for p in range(2):
                    potential = out[i * QUADS : (i + 1) * QUADS, p * LANES : (p + 1) * LANES]
                    own_ov[p, there, :] = potential * partner
                    sent = sent + potential * own_f[p, here, :]
                total = total + sent * partner
                staged[here, :] = sent
        energy_out[...] += total
        par_ov[flat, :] = staged[...].astype(BF16)
        pltpu.make_async_copy(own_ov.at[:, flat, :], own_out.at[:, flat, :], sems.at[4]).start()
        pltpu.make_async_copy(par_ov.at[flat, :], par_out.at[flat, :], sems.at[5]).start()

    pltpu.make_async_copy(own_ov, own_out, sems.at[4]).wait()
    pltpu.make_async_copy(par_ov, par_out, sems.at[5]).wait()


def pair_terms(own0, own1, own_u, partner, tables, kern, interpret=False):
    vmem = pl.BlockSpec(memory_space=pltpu.VMEM)
    hbm = pl.BlockSpec(memory_space=pl.ANY)
    return pl.pallas_call(
        pairs_kernel,
        out_shape=(
            jax.ShapeDtypeStruct((2, ROWS, LANES), F32),
            jax.ShapeDtypeStruct((ROWS, LANES), BF16),
            jax.ShapeDtypeStruct((QUADS, LANES), F32),
        ),
        in_specs=[hbm] * 4 + [vmem] * 8,
        out_specs=(hbm, hbm, vmem),
        scratch_shapes=[
            pltpu.VMEM((2, ROWS, LANES), BF16),
            pltpu.VMEM((2, G, G, LANES), BF16),
            pltpu.VMEM((KPAD * G, LANES), F32),
            pltpu.VMEM((2, ROWS, LANES), F32),
            pltpu.VMEM((ROWS, LANES), BF16),
            pltpu.VMEM((G * F_PITCH, LANES), F32),
            pltpu.VMEM((G, G, LANES), BF16),
            pltpu.VMEM((2 * G * Y_PITCH, LANES), F32),
            pltpu.VMEM((4, KPAD * Z_PITCH, LANES), F32),
            pltpu.VMEM((KPAD * G, 4 * LANES), BF16),
            pltpu.VMEM((2, 8 * PLANE, LANES), F32),
            pltpu.VMEM((8 * PLANE, LANES), F32),
            pltpu.SemaphoreType.DMA((6,)),
        ],
        compiler_params=pltpu.CompilerParams(vmem_limit_bytes=62 * 1024 * 1024),
        cost_estimate=pl.CostEstimate(
            flops=20_000_000_000, bytes_accessed=20_000_000, transcendentals=0
        ),
        interpret=interpret,
        name="pair_terms",
    )(own0, own1, own_u, kern, partner, *tables)


BLOCK = 1152


def first_sum_kernel(own0, own1, first, second, back0, exch0, part1, gram_ref):
    @pl.when(pl.program_id(0) == 0)
    def _():
        gram_ref[...] = jnp.zeros_like(gram_ref)

    exchange = first[0] + second[0] + back0[...].astype(F32)
    exch0[...] = exchange
    part1[...] = first[1] + second[1]
    for i, own in enumerate((own0, own1)):
        gram_ref[i] += jnp.sum((own[...].astype(F32) * exchange).reshape(-1, 8, LANES), axis=0)


def first_sum(own, first, second, back0, interpret=False):
    flat = pl.BlockSpec((BLOCK, LANES), lambda i: (i, 0))
    both = pl.BlockSpec((2, BLOCK, LANES), lambda i: (0, i, 0))
    return pl.pallas_call(
        first_sum_kernel,
        grid=(ROWS // BLOCK,),
        out_shape=(
            jax.ShapeDtypeStruct((ROWS, LANES), F32),
            jax.ShapeDtypeStruct((ROWS, LANES), F32),
            jax.ShapeDtypeStruct((2, 8, LANES), F32),
        ),
        in_specs=[flat, flat, both, both, flat],
        out_specs=(flat, flat, pl.BlockSpec((2, 8, LANES), lambda i: (0, 0, 0))),
        compiler_params=pltpu.CompilerParams(vmem_limit_bytes=62 * 1024 * 1024),
        interpret=interpret,
        name="first_sum",
    )(*own, first, second, back0)


def last_sum_kernel(own0, own1, exch0, part1, back1, out_ref, gram_ref):
    @pl.when(pl.program_id(0) == 0)
    def _():
        gram_ref[...] = jnp.zeros_like(gram_ref)

    exchange = part1[...] + back1[...].astype(F32)
    out_ref[pl.ds(0, BLOCK, stride=2), :] = exch0[...]
    out_ref[pl.ds(1, BLOCK, stride=2), :] = exchange
    for i, own in enumerate((own0, own1)):
        gram_ref[i] += jnp.sum((own[...].astype(F32) * exchange).reshape(-1, 8, LANES), axis=0)


def last_sum(own, exch0, part1, back1, interpret=False):
    flat = pl.BlockSpec((BLOCK, LANES), lambda i: (i, 0))
    return pl.pallas_call(
        last_sum_kernel,
        grid=(ROWS // BLOCK,),
        out_shape=(
            jax.ShapeDtypeStruct((2 * ROWS, LANES), F32),
            jax.ShapeDtypeStruct((2, 8, LANES), F32),
        ),
        in_specs=[flat] * 5,
        out_specs=(
            pl.BlockSpec((2 * BLOCK, LANES), lambda i: (i, 0)),
            pl.BlockSpec((2, 8, LANES), lambda i: (0, 0, 0)),
        ),
        compiler_params=pltpu.CompilerParams(vmem_limit_bytes=62 * 1024 * 1024),
        interpret=interpret,
        name="last_sum",
    )(*own, exch0, part1, back1)


def from_behind(block, axis, distance):
    size = lax.axis_size(axis)
    return lax.ppermute(block, axis, [((i - distance) % size, i) for i in range(size)])


def sum_over(value, axis):
    size = lax.axis_size(axis)
    if size & (size - 1):
        return lax.psum(value, axis)
    steps = [1 << bit for bit in range(size.bit_length() - 1)]
    for step in [s for s in steps if s != 2] + [s for s in steps if s == 2]:
        value = value + lax.ppermute(value, axis, [(i ^ step, i) for i in range(size)])
    return value


def per_device(orbitals):
    tables = section_tables()
    kern = screening()
    raw = orbitals.reshape(2, ROWS, LANES).transpose(1, 0, 2).reshape(2 * ROWS, LANES)
    own = [take_band(raw, j) for j in range(2)]
    previous = [from_behind(own[j], "band", 1) for j in range(2)]
    own_u = padded_rows(*own, tables[-1])
    first, sent0, energy0 = pair_terms(*own, own_u, previous[0], tables, kern)
    back0 = from_behind(sent0, "band", -1)
    second, sent1, energy1 = pair_terms(*own, own_u, previous[1], tables, kern)
    back1 = from_behind(sent1, "band", -1)
    pair_energy = jnp.sum(energy0 + energy1).reshape(1, 1)
    total = sum_over(jnp.broadcast_to(pair_energy, (8, LANES)), "band")[0, 0]
    energy = -2.0 * total / F32(NGRID) / F32(2 * lax.axis_size("band") * orbitals.shape[0])
    exch0, part1, gram0 = first_sum(own, first, second, back0)
    exchange, gram1 = last_sum(own, exch0, part1, back1)
    gram = jnp.stack([jnp.sum(g, axis=(1, 2)) for g in (gram0, gram1)], axis=1) / F32(NGRID)
    exchange = exchange.reshape(ROWS, 2, LANES).transpose(1, 0, 2).reshape(2, NGRID)
    return exchange, gram, energy


def solution(mesh):
    return jax.shard_map(
        per_device,
        mesh=mesh,
        in_specs=(P("band", None),),
        out_specs=(P("band", None), P("band", None), P()),
        check_vma=False,
    )
```

```python
import functools

import jax
import jax.numpy as jnp
import ml_dtypes
import numpy as np
from jax import lax
from jax.experimental import pallas as pl
from jax.experimental.pallas import tpu as pltpu
from jax.sharding import PartitionSpec as P

G = 96
HALF = G // 2 + 1
NGRID = G * G * G
LANES = 128
ROWS = NGRID // LANES
PLANE = G * G // LANES
QUADS = G // 4
KPAD = HALF + 1
Y_ROWS = 104
Y_PITCH = Y_ROWS + 1
Z_PITCH = G + 1
W_PITCH = 2 * G + 1
F_PITCH = PLANE + 1
PLANES = 16
PIECES = 3
WAVE_UNIT = 0.05
SCREEN_SQ = 0.0121
VMEM_ALL = pltpu.CompilerParams(vmem_limit_bytes=62 * 1024 * 1024)
BF16 = jnp.bfloat16
F32 = jnp.float32


def dft_tables():
    n = np.arange(G)
    phases = (n[:, None] * n[None, :]) % G
    angles = phases.astype(np.float32) * np.float32(2.0 * np.pi / G)
    rounded = [f(angles).astype(ml_dtypes.bfloat16).astype(np.float32) for f in (np.cos, np.sin)]
    return rounded[0], rounded[1]


def section_tables():
    c, s = dft_tables()
    h = HALF
    t1 = np.zeros((Y_ROWS, G), np.float32)
    t1[:h] = c[:h]
    t1[h : 2 * h] = -s[:h]
    t2 = np.block([[c, s], [-s, c]])
    t3 = np.zeros((2, LANES, 4, 64), np.float32)
    back = (G - np.arange(h)) % G
    t3[0, :G, 0, :h] = c[:h].T
    t3[1, :G, 0, :h] = s[:h].T
    t3[0, :G, 1, :h] = -s[:h].T
    t3[1, :G, 1, :h] = c[:h].T
    t3[0, :G, 2, :h] = c[back].T
    t3[1, :G, 2, :h] = s[back].T
    t3[0, :G, 3, :h] = s[back].T
    t3[1, :G, 3, :h] = -c[back].T
    t3 = t3.reshape(2 * LANES, 4 * 64)
    order = np.concatenate([np.arange(G // 2), G - 1 - np.arange(G // 2)])
    a1 = np.block([[c[:, order], -s[:, order]], [s[:, order], c[:, order]]])
    rows = np.arange(G).reshape(QUADS, 4).T.reshape(-1)
    a2 = np.block([[c[rows], -s[rows]], [s[rows], c[rows]]])
    weight = np.full((h, 1), 2.0, np.float32)
    weight[0] = weight[h - 1] = 1.0
    a3 = np.zeros((3, 2, 2, 2, 64, 2, LANES), np.float32)
    for third in range(3):
        for lane in range(LANES):
            r, x3 = divmod(third * LANES + lane, G)
            for p in range(2):
                a3[third, r - third, 0, p, :h, p, lane] = weight[:, 0] * c[x3, :h]
                a3[third, r - third, 1, p, :h, p, lane] = -weight[:, 0] * s[x3, :h]
    a3 = a3.reshape(3, 4 * LANES, 2 * LANES)
    sel = np.zeros((2, 2 * LANES, 2 * LANES), np.float32)
    for r in range(4):
        for x in range(G):
            sel[r // 2, r * G + x - (r // 2) * LANES, (r % 2) * LANES + x] = 1.0
    return [t.astype(ml_dtypes.bfloat16) for t in (t1, t2, t3, a1, a2, a3, sel)]


def screening():
    n = np.arange(G)
    m = np.where(n <= G // 2, n, n - G).astype(np.float64)
    sq = m * m
    q2 = WAVE_UNIT * (sq[:HALF, None, None] + sq[None, :, None] + sq[None, None, :HALF])
    safe = np.where(q2 > 0, q2, 1.0)
    kern = 4.0 * np.pi * (1.0 - np.exp(-q2 / (4.0 * SCREEN_SQ))) / safe
    kern = np.where(q2 > 0, kern, np.pi / SCREEN_SQ)
    out = np.zeros((KPAD, G, 2, 64), np.float32)
    out[:HALF, :, :, :HALF] = kern[:, :, None, :]
    return out.reshape(KPAD * G, LANES)


def dot(a, b):
    return jnp.dot(a, b, preferred_element_type=F32)


def lanes(*parts):
    return jnp.concatenate(parts, axis=1)


def stack(*parts):
    return jnp.concatenate(parts, axis=0)


def split_rows(src, sel_ref, out, first, count):
    rows = [
        [src[pl.ds(3 * (first + i) + s, G, stride=F_PITCH), :].astype(BF16) for s in range(3)]
        for i in range(count)
    ]
    for half in range(2):
        part = dot(stack(*[lanes(r[half], r[half + 1]) for r in rows]), sel_ref[half])
        for i in range(count):
            for e in range(2):
                value = part[i * G : (i + 1) * G, e * LANES : (e + 1) * LANES]
                out[4 * (first + i) + 2 * half + e] = value.astype(BF16)


def widen_planes(src, dst):
    @pl.loop(0, G // 2, unroll=4)
    def _(i):
        value = src[pl.ds(pl.multiple_of(i * 2 * PLANE, 16), 2 * PLANE), :].astype(F32)
        dst[pl.ds(2 * i * F_PITCH, PLANE), :] = value[:PLANE]
        dst[pl.ds((2 * i + 1) * F_PITCH, PLANE), :] = value[PLANE:]


def band_kernel(raw_ref, pick, out):
    half = LANES
    for i in range(raw_ref.shape[0] // (4 * LANES)):
        top = raw_ref[4 * i * half : (4 * i + 2) * half, :]
        low = raw_ref[(4 * i + 2) * half : (4 * i + 4) * half, :]
        rows = dot(pick[...], lanes(top, low)).astype(BF16)
        out[2 * i * half : (2 * i + 1) * half, :] = rows[:, :half]
        out[(2 * i + 1) * half : (2 * i + 2) * half, :] = rows[:, half:]


def take_band(raw, p, interpret=False):
    pick = np.zeros((LANES, 2 * LANES), np.float32)
    pick[np.arange(LANES), 2 * np.arange(LANES) + p] = 1.0
    rows = 768
    return pl.pallas_call(
        band_kernel,
        grid=(ROWS // rows,),
        out_shape=jax.ShapeDtypeStruct((ROWS, LANES), BF16),
        in_specs=[
            pl.BlockSpec((2 * rows, LANES), lambda i: (i, 0)),
            pl.BlockSpec((LANES, 2 * LANES), lambda i: (0, 0)),
        ],
        out_specs=pl.BlockSpec((rows, LANES), lambda i: (i, 0)),
        compiler_params=VMEM_ALL,
        interpret=interpret,
        name="take_band",
    )(raw, pick.astype(ml_dtypes.bfloat16))


def rows_kernel(own0, own1, sel, out, wide):
    for p, own in enumerate((own0, own1)):
        widen_planes(own, wide)

        @pl.loop(0, QUADS // 4)
        def _(q):
            split_rows(wide, sel, out.at[p], 4 * q, 4)


def padded_rows(own0, own1, sel, interpret=False):
    vmem = pl.BlockSpec(memory_space=pltpu.VMEM)
    return pl.pallas_call(
        rows_kernel,
        out_shape=jax.ShapeDtypeStruct((2, G, G, LANES), BF16),
        in_specs=[vmem] * 3,
        out_specs=vmem,
        scratch_shapes=[pltpu.VMEM((G * F_PITCH, LANES), F32)],
        compiler_params=VMEM_ALL,
        interpret=interpret,
        name="padded_rows",
    )(own0, own1, sel)


def pairs_kernel(
    pieces, own0, own1, own_u, kern, par_ref, energy_in, t1, t2, t3, a1, a2, a3, sel, own_out, *rest
):
    par_out, energy_out = rest[:pieces], rest[pieces]
    own_v, own_uv, kern_v, own_ov, par_ov, par_f, par_u, yw, z, x34 = rest[pieces + 1 : pieces + 11]
    own_f, staged, total_ref, sems = rest[pieces + 11 :]
    loads = [
        pltpu.make_async_copy(own_u, own_uv, sems.at[0]),
        pltpu.make_async_copy(kern, kern_v, sems.at[1]),
        pltpu.make_async_copy(own0, own_v.at[0], sems.at[2]),
        pltpu.make_async_copy(own1, own_v.at[1], sems.at[3]),
    ]
    for load in loads:
        load.start()

    widen_planes(par_ref, par_f)

    @pl.loop(0, QUADS // 4)
    def _(q):
        split_rows(par_f, sel, par_u, 4 * q, 4)

    half_y = G * Y_PITCH
    loads[0].wait()

    @pl.loop(0, G // 2, unroll=4)
    def _(i):
        density = []
        for e in range(2):
            partner = par_u[2 * i + e].astype(F32)
            for p in range(2):
                density.append((own_uv[p, 2 * i + e].astype(F32) * partner).astype(BF16))
        out = dot(t1[...], lanes(*density))
        for e in range(2):
            for p in range(2):
                at = pl.ds(p * half_y + (2 * i + e) * Y_PITCH, Y_ROWS)
                yw[at, :] = out[:, (2 * e + p) * LANES : (2 * e + p + 1) * LANES]

    @pl.loop(0, HALF, unroll=7)
    def _(k1):
        def line(p, part):
            return yw[pl.ds(p * half_y + part * HALF + k1, G, stride=Y_PITCH), :].astype(BF16)

        out = dot(t2[...], stack(lanes(line(0, 0), line(1, 0)), lanes(line(0, 1), line(1, 1))))
        at = pl.ds(pl.multiple_of(k1 * G, 16), G)
        for p in range(2):
            for part in range(2):
                left = (2 * p + part) * LANES
                value = out[part * G : (part + 1) * G, p * LANES : (p + 1) * LANES]
                x34[at, left : left + LANES] = value.astype(BF16)

    loads[1].wait()

    many = 5

    @pl.loop(0, KPAD // many)
    def _(m):
        at = pl.ds(pl.multiple_of(m * many * G, 16), many * G)
        factor = kern_v[at, :]
        out = [
            dot(x34[at, 2 * p * LANES : 2 * (p + 1) * LANES], t3[...]).astype(BF16)
            for p in range(2)
        ]
        for part in range(4):
            spectrum = lanes(*[o[:, part * 64 : (part + 1) * 64] for o in out]).astype(F32)
            value = spectrum * factor
            for i in range(many):
                row = (many * m + i) * Z_PITCH
                z[part, pl.ds(row, G), :] = value[i * G : (i + 1) * G]

    @pl.loop(0, G // 4, unroll=3)
    def _(four):
        parts = []
        for e in range(4):
            k2 = 4 * four + e
            mirror = Z_PITCH + jnp.where(k2 == 0, 0, G - k2)
            parts.append(
                stack(
                    z[0, pl.ds(k2, G // 2, stride=Z_PITCH), :].astype(BF16),
                    z[2, pl.ds(mirror, G // 2, stride=Z_PITCH), :].astype(BF16),
                    z[1, pl.ds(k2, G // 2, stride=Z_PITCH), :].astype(BF16),
                    z[3, pl.ds(mirror, G // 2, stride=Z_PITCH), :].astype(BF16),
                )
            )
        out = dot(a1[...], lanes(*parts))
        for e in range(4):
            at = (4 * four + e) * W_PITCH
            yw[pl.ds(at, 2 * G), :] = out[:, e * LANES : (e + 1) * LANES]

    @pl.loop(0, G // 4, unroll=3)
    def _(four):
        parts = []
        for e in range(4):
            x1 = 4 * four + e
            parts.append(
                stack(
                    yw[pl.ds(x1, G, stride=W_PITCH), :].astype(BF16),
                    yw[pl.ds(G + x1, G, stride=W_PITCH), :].astype(BF16),
                )
            )
        out = dot(a2[...], lanes(*parts))
        for r in range(4):
            block = [
                lanes(
                    out[r * QUADS : (r + 1) * QUADS, e * LANES : (e + 1) * LANES],
                    out[G + r * QUADS : G + (r + 1) * QUADS, e * LANES : (e + 1) * LANES],
                )
                for e in range(4)
            ]
            at = pl.multiple_of((r // 2) * G * QUADS + four * 4 * QUADS, 16)
            left = (r % 2) * 2 * LANES
            x34[pl.ds(at, 4 * QUADS), left : left + 2 * LANES] = stack(*block).astype(BF16)

    loads[2].wait()
    loads[3].wait()
    total_ref[...] = jnp.zeros_like(total_ref)
    planes = PLANES
    block_rows = planes * QUADS
    scale = F32(1.0 / NGRID)

    @pl.loop(0, G // planes)
    def _(ch):
        at = pl.multiple_of(ch * block_rows, 16)
        low = x34[pl.ds(at, block_rows), :]
        high = x34[pl.ds(G * QUADS + at, block_rows), :]
        fields = [low, lanes(low[:, 2 * LANES :], high[:, : 2 * LANES]), high]
        flat = pl.ds(pl.multiple_of(ch * planes * PLANE, 16), planes * PLANE)
        own_f[...] = own_v[:, flat, :].astype(F32)
        total = jnp.zeros((QUADS, LANES), F32)
        for third in range(3):
            out = dot(fields[third], a3[third]) * scale
            for i in range(planes):
                plane = ch * planes + i
                partner = par_f[pl.ds(plane * F_PITCH + third, QUADS, stride=3), :]
                here = pl.ds(i * PLANE + third, QUADS, stride=3)
                there = pl.ds(plane * PLANE + third, QUADS, stride=3)
                sent = jnp.zeros((QUADS, LANES), F32)
                for p in range(2):
                    potential = out[i * QUADS : (i + 1) * QUADS, p * LANES : (p + 1) * LANES]
                    own_ov[p, there, :] = potential * partner
                    sent = sent + potential * own_f[p, here, :]
                total = total + sent * partner
                staged[here, :] = sent
        total_ref[...] += total
        par_ov[flat, :] = staged[...].astype(BF16)
        pltpu.make_async_copy(own_ov.at[:, flat, :], own_out.at[:, flat, :], sems.at[4]).start()
        per_piece = G // planes // pieces
        for i, out in enumerate(par_out):

            @pl.when(ch // per_piece == i)
            def _():
                row = pl.multiple_of((ch - i * per_piece) * planes * PLANE, 16)
                there = out.at[pl.ds(row, planes * PLANE), :]
                pltpu.make_async_copy(par_ov.at[flat, :], there, sems.at[5 + i]).start()

    energy = jnp.sum(total_ref[...]) * F32(-2.0 / NGRID)
    energy_out[...] = energy_in[...] + energy
    pltpu.make_async_copy(own_ov, own_out, sems.at[4]).wait()
    for i, out in enumerate(par_out):
        source = par_ov.at[pl.ds(i * out.shape[0], out.shape[0]), :]
        pltpu.make_async_copy(source, out, sems.at[5 + i]).wait()


def pair_terms(own0, own1, own_u, partner, energy, tables, kern, pieces, interpret=False):
    vmem = pl.BlockSpec(memory_space=pltpu.VMEM)
    hbm = pl.BlockSpec(memory_space=pl.ANY)
    return pl.pallas_call(
        functools.partial(pairs_kernel, pieces),
        out_shape=(
            jax.ShapeDtypeStruct((2, ROWS, LANES), F32),
            *[jax.ShapeDtypeStruct((ROWS // pieces, LANES), BF16)] * pieces,
            jax.ShapeDtypeStruct((8, LANES), F32),
        ),
        in_specs=[hbm] * 4 + [vmem] * 9,
        out_specs=(hbm, *[hbm] * pieces, vmem),
        scratch_shapes=[
            pltpu.VMEM((2, ROWS, LANES), BF16),
            pltpu.VMEM((2, G, G, LANES), BF16),
            pltpu.VMEM((KPAD * G, LANES), F32),
            pltpu.VMEM((2, ROWS, LANES), F32),
            pltpu.VMEM((ROWS, LANES), BF16),
            pltpu.VMEM((G * F_PITCH, LANES), F32),
            pltpu.VMEM((G, G, LANES), BF16),
            pltpu.VMEM((2 * G * Y_PITCH, LANES), F32),
            pltpu.VMEM((4, KPAD * Z_PITCH, LANES), F32),
            pltpu.VMEM((KPAD * G, 4 * LANES), BF16),
            pltpu.VMEM((2, PLANES * PLANE, LANES), F32),
            pltpu.VMEM((PLANES * PLANE, LANES), F32),
            pltpu.VMEM((QUADS, LANES), F32),
            pltpu.SemaphoreType.DMA((5 + pieces,)),
        ],
        compiler_params=VMEM_ALL,
        cost_estimate=pl.CostEstimate(
            flops=20_000_000_000, bytes_accessed=20_000_000, transcendentals=0
        ),
        interpret=interpret,
        name="pair_terms",
    )(own0, own1, own_u, kern, partner, energy, *tables)


BLOCK = 576


def add_products(gram_ref, column, own0, own1, exchange):
    for i, own in enumerate((own0, own1)):
        product = (own[...].astype(F32) * exchange).reshape(-1, 8, LANES)
        gram_ref[i, column] += jnp.sum(product, axis=0)


def first_sum_kernel(own0, own1, first, second, back0, exch0, part1, gram_ref):
    @pl.when(pl.program_id(0) == 0)
    def _():
        gram_ref[...] = jnp.zeros_like(gram_ref)

    exchange = first[0] + second[0] + back0[...].astype(F32)
    exch0[...] = exchange
    part1[...] = first[1] + second[1]
    add_products(gram_ref, 0, own0, own1, exchange)


def first_sum(own, first, second, back0, interpret=False):
    flat = pl.BlockSpec((BLOCK, LANES), lambda i: (i, 0))
    both = pl.BlockSpec((2, BLOCK, LANES), lambda i: (0, i, 0))
    return pl.pallas_call(
        first_sum_kernel,
        grid=(ROWS // BLOCK,),
        out_shape=(
            jax.ShapeDtypeStruct((ROWS, LANES), F32),
            jax.ShapeDtypeStruct((ROWS, LANES), F32),
            jax.ShapeDtypeStruct((2, 2, 8, LANES), F32),
        ),
        in_specs=[flat, flat, both, both, flat],
        out_specs=(flat, flat, pl.BlockSpec((2, 2, 8, LANES), lambda i: (0, 0, 0, 0))),
        compiler_params=VMEM_ALL,
        interpret=interpret,
        name="first_sum",
    )(*own, first, second, back0)


def piece_kernel(piece, own0, own1, exch0, part1, back1, gram_in, *rest):
    out_ref, gram_out, gram_ref = rest[-3:]
    step = pl.program_id(0)

    @pl.when(step == 0)
    def _():
        gram_ref[...] = gram_in[...]

    exchange = part1[...] + back1[...].astype(F32)
    out_ref[pl.ds(0, BLOCK, stride=2), :] = exch0[...]
    out_ref[pl.ds(1, BLOCK, stride=2), :] = exchange
    add_products(gram_ref, 1, own0, own1, exchange)

    @pl.when(step == pl.num_programs(0) - 1)
    def _():
        if piece < PIECES - 1:
            gram_out[...] = gram_ref[...]
        else:
            row = lax.broadcasted_iota(jnp.int32, (2, 2), 0)
            column = lax.broadcasted_iota(jnp.int32, (2, 2), 1)
            value = jnp.zeros((2, 2), F32)
            for i in range(2):
                for j in range(2):
                    entry = jnp.sum(gram_ref[i, j]) * F32(1.0 / NGRID)
                    value = jnp.where((row == i) & (column == j), entry, value)
            gram_out[...] = value


def add_piece(piece, own, exch0, part1, back1, gram, out, interpret=False):
    steps = ROWS // PIECES // BLOCK
    here = pl.BlockSpec((BLOCK, LANES), lambda i: (piece * steps + i, 0))
    gram_spec = pl.BlockSpec((2, 2, 8, LANES), lambda i: (0, 0, 0, 0))
    last = piece == PIECES - 1
    earlier = [] if out is None else [out]
    return pl.pallas_call(
        functools.partial(piece_kernel, piece),
        grid=(steps,),
        out_shape=(
            jax.ShapeDtypeStruct((2 * ROWS, LANES), F32),
            jax.ShapeDtypeStruct((2, 2) if last else gram.shape, F32),
        ),
        in_specs=[here] * 4
        + [pl.BlockSpec((BLOCK, LANES), lambda i: (i, 0)), gram_spec]
        + [pl.BlockSpec(memory_space=pl.ANY)] * len(earlier),
        out_specs=(
            pl.BlockSpec((2 * BLOCK, LANES), lambda i: (piece * steps + i, 0)),
            pl.BlockSpec((2, 2), lambda i: (0, 0)) if last else gram_spec,
        ),
        scratch_shapes=[pltpu.VMEM((2, 2, 8, LANES), F32)],
        input_output_aliases={6: 0} if earlier else {},
        compiler_params=VMEM_ALL,
        interpret=interpret,
        name="add_piece",
    )(*own, exch0, part1, back1, gram, *earlier)


def from_behind(block, axis, distance):
    size = lax.axis_size(axis)
    return lax.ppermute(block, axis, [((i - distance) % size, i) for i in range(size)])


def exchange_with(value, axis, bits):
    size = lax.axis_size(axis)
    got = {0: value}
    for flip in sorted({bits[0], bits[-1], sum(bits)}):
        got[flip] = lax.ppermute(value, axis, [(i ^ flip, i) for i in range(size)])
    low = got[0] + got[bits[0]]
    if len(bits) == 1:
        return low
    return low + (got[bits[1]] + got[sum(bits)])


def after(value, other):
    return lax.optimization_barrier((value, other))[0]


def per_device(orbitals):
    tables = section_tables()
    kern = screening()
    size = lax.axis_size("band")
    raw = orbitals.reshape(2, ROWS, LANES).transpose(1, 0, 2).reshape(2 * ROWS, LANES)
    own = [take_band(raw, j) for j in range(2)]
    previous = [from_behind(own[j], "band", 1) for j in range(2)]
    own_u = padded_rows(*own, tables[-1])
    energy = jnp.zeros((8, LANES), F32)
    first, sent0, energy = pair_terms(*own, own_u, previous[0], energy, tables, kern, 1)
    back0 = from_behind(sent0, "band", -1)
    second, *sent1, energy = pair_terms(*own, own_u, previous[1], energy, tables, kern, PIECES)
    back1 = [from_behind(piece, "band", -1) for piece in sent1]
    energy = energy * F32(1.0 / (size * orbitals.shape[0] * 2))

    exch0, part1, gram = first_sum(own, first, second, back0)
    exchange = None
    if size & (size - 1):
        energy = lax.psum(energy, "band")
        groups = []
    else:
        bits = [1 << b for b in range(size.bit_length() - 1)]
        rest = [b for b in bits if b != 2]
        groups = [rest[i : i + 2] for i in range(0, len(rest), 2)] + [[b] for b in bits if b == 2]
    for piece in range(PIECES):
        if groups:
            energy = exchange_with(after(energy, gram) if piece else energy, "band", groups.pop(0))
        exchange, gram = add_piece(piece, own, exch0, part1, back1[piece], gram, exchange)
    for bits in groups:
        energy = exchange_with(energy, "band", bits)
    exchange = exchange.reshape(ROWS, 2, LANES).transpose(1, 0, 2).reshape(2, NGRID)
    return exchange, gram, energy[0, 0]


def solution(mesh):
    return jax.shard_map(
        per_device,
        mesh=mesh,
        in_specs=(P("band", None),),
        out_specs=(P("band", None), P("band", None), P()),
        check_vma=False,
    )
```

```python
import functools

import jax
import jax.numpy as jnp
import ml_dtypes
import numpy as np
from jax import lax
from jax.experimental import pallas as pl
from jax.experimental.pallas import tpu as pltpu
from jax.sharding import PartitionSpec as P

G = 96
HALF = G // 2 + 1
NGRID = G * G * G
LANES = 128
ROWS = NGRID // LANES
PLANE = G * G // LANES
QUADS = G // 4
KPAD = HALF + 1
Y_ROWS = 104
Y_PITCH = Y_ROWS + 1
Z_PITCH = G + 1
W_PITCH = 2 * G + 1
F_PITCH = PLANE + 1
PLANES = 16
PIECES = 3
WAVE_UNIT = 0.05
SCREEN_SQ = 0.0121
VMEM_ALL = pltpu.CompilerParams(vmem_limit_bytes=62 * 1024 * 1024)
BF16 = jnp.bfloat16
F32 = jnp.float32


def dft_tables():
    n = np.arange(G)
    phases = (n[:, None] * n[None, :]) % G
    angles = phases.astype(np.float32) * np.float32(2.0 * np.pi / G)
    rounded = [f(angles).astype(ml_dtypes.bfloat16).astype(np.float32) for f in (np.cos, np.sin)]
    return rounded[0], rounded[1]


def section_tables():
    c, s = dft_tables()
    h = HALF
    t1 = np.zeros((Y_ROWS, G), np.float32)
    t1[:h] = c[:h]
    t1[h : 2 * h] = -s[:h]
    t2 = np.block([[c, s], [-s, c]])
    t3 = np.zeros((2, LANES, 4, 64), np.float32)
    back = (G - np.arange(h)) % G
    t3[0, :G, 0, :h] = c[:h].T
    t3[1, :G, 0, :h] = s[:h].T
    t3[0, :G, 1, :h] = -s[:h].T
    t3[1, :G, 1, :h] = c[:h].T
    t3[0, :G, 2, :h] = c[back].T
    t3[1, :G, 2, :h] = s[back].T
    t3[0, :G, 3, :h] = s[back].T
    t3[1, :G, 3, :h] = -c[back].T
    t3 = t3.reshape(2 * LANES, 4 * 64)
    order = np.concatenate([np.arange(G // 2), G - 1 - np.arange(G // 2)])
    a1 = np.block([[c[:, order], -s[:, order]], [s[:, order], c[:, order]]])
    rows = np.arange(G).reshape(QUADS, 4).T.reshape(-1)
    a2 = np.block([[c[rows], -s[rows]], [s[rows], c[rows]]])
    weight = np.full((h, 1), 2.0, np.float32)
    weight[0] = weight[h - 1] = 1.0
    a3 = np.zeros((3, 2, 2, 2, 64, 2, LANES), np.float32)
    for third in range(3):
        for lane in range(LANES):
            r, x3 = divmod(third * LANES + lane, G)
            for p in range(2):
                a3[third, r - third, 0, p, :h, p, lane] = weight[:, 0] * c[x3, :h]
                a3[third, r - third, 1, p, :h, p, lane] = -weight[:, 0] * s[x3, :h]
    a3 = a3.reshape(3, 4 * LANES, 2 * LANES)
    sel = np.zeros((2, 2 * LANES, 2 * LANES), np.float32)
    for r in range(4):
        for x in range(G):
            sel[r // 2, r * G + x - (r // 2) * LANES, (r % 2) * LANES + x] = 1.0
    return [t.astype(ml_dtypes.bfloat16) for t in (t1, t2, t3, a1, a2, a3, sel)]


def screening():
    n = np.arange(G)
    m = np.where(n <= G // 2, n, n - G).astype(np.float64)
    sq = m * m
    q2 = WAVE_UNIT * (sq[:HALF, None, None] + sq[None, :, None] + sq[None, None, :HALF])
    safe = np.where(q2 > 0, q2, 1.0)
    kern = 4.0 * np.pi * (1.0 - np.exp(-q2 / (4.0 * SCREEN_SQ))) / safe
    kern = np.where(q2 > 0, kern, np.pi / SCREEN_SQ)
    out = np.zeros((KPAD, G, 2, 64), np.float32)
    out[:HALF, :, :, :HALF] = kern[:, :, None, :]
    return out.reshape(KPAD * G, LANES)


def dot(a, b):
    return jnp.dot(a, b, preferred_element_type=F32)


def lanes(*parts):
    return jnp.concatenate(parts, axis=1)


def stack(*parts):
    return jnp.concatenate(parts, axis=0)


def split_rows(src, sel_ref, out, first, count):
    rows = [
        [src[pl.ds(3 * (first + i) + s, G, stride=F_PITCH), :].astype(BF16) for s in range(3)]
        for i in range(count)
    ]
    for half in range(2):
        part = dot(stack(*[lanes(r[half], r[half + 1]) for r in rows]), sel_ref[half])
        for i in range(count):
            for e in range(2):
                value = part[i * G : (i + 1) * G, e * LANES : (e + 1) * LANES]
                out[4 * (first + i) + 2 * half + e] = value.astype(BF16)


def widen_planes(src, dst):
    @pl.loop(0, G // 2, unroll=4)
    def _(i):
        value = src[pl.ds(pl.multiple_of(i * 2 * PLANE, 16), 2 * PLANE), :].astype(F32)
        dst[pl.ds(2 * i * F_PITCH, PLANE), :] = value[:PLANE]
        dst[pl.ds((2 * i + 1) * F_PITCH, PLANE), :] = value[PLANE:]


def rows_of(ref, first, count):
    at = pl.ds(first, count)
    return ref.at[at, :] if len(ref.shape) == 2 else ref.at[:, at, :]


def copy_rows(src, src_row, dst, dst_row, count, sem):
    return pltpu.make_async_copy(rows_of(src, src_row, count), rows_of(dst, dst_row, count), sem)


def band_kernel(raw, pick, out, raw_v, out_v, load_sems, store_sem):
    chunks = load_sems.shape[0]
    rows = out.shape[0] // chunks
    loads = [
        copy_rows(raw, 2 * c * rows, raw_v, 2 * c * rows, 2 * rows, load_sems.at[c])
        for c in range(chunks)
    ]
    for load in loads:
        load.start()
    for c, load in enumerate(loads):
        load.wait()
        for row in range(c * rows, (c + 1) * rows, 2 * LANES):
            top = raw_v[2 * row : 2 * row + 2 * LANES, :]
            low = raw_v[2 * row + 2 * LANES : 2 * row + 4 * LANES, :]
            value = dot(pick[...], lanes(top, low)).astype(BF16)
            out_v[row : row + LANES, :] = value[:, :LANES]
            out_v[row + LANES : row + 2 * LANES, :] = value[:, LANES:]
        copy_rows(out_v, c * rows, out, c * rows, rows, store_sem).start()
    pltpu.make_async_copy(out_v, out, store_sem).wait()


def take_band(raw, p, interpret=False):
    pick = np.zeros((LANES, 2 * LANES), np.float32)
    pick[np.arange(LANES), 2 * np.arange(LANES) + p] = 1.0
    hbm = pl.BlockSpec(memory_space=pl.ANY)
    return pl.pallas_call(
        band_kernel,
        out_shape=jax.ShapeDtypeStruct((ROWS, LANES), BF16),
        in_specs=[hbm, pl.BlockSpec(memory_space=pltpu.VMEM)],
        out_specs=hbm,
        scratch_shapes=[
            pltpu.VMEM((2 * ROWS, LANES), BF16),
            pltpu.VMEM((ROWS, LANES), BF16),
            pltpu.SemaphoreType.DMA((9,)),
            pltpu.SemaphoreType.DMA,
        ],
        compiler_params=VMEM_ALL,
        interpret=interpret,
        name="take_band",
    )(raw, pick.astype(ml_dtypes.bfloat16))


def rows_kernel(own0, own1, sel, out, wide):
    for p, own in enumerate((own0, own1)):
        widen_planes(own, wide)

        @pl.loop(0, QUADS // 4, unroll=2)
        def _(q):
            split_rows(wide, sel, out.at[p], 4 * q, 4)


def padded_rows(own0, own1, sel, interpret=False):
    vmem = pl.BlockSpec(memory_space=pltpu.VMEM)
    return pl.pallas_call(
        rows_kernel,
        out_shape=jax.ShapeDtypeStruct((2, G, G, LANES), BF16),
        in_specs=[vmem] * 3,
        out_specs=vmem,
        scratch_shapes=[pltpu.VMEM((G * F_PITCH, LANES), F32)],
        compiler_params=VMEM_ALL,
        interpret=interpret,
        name="padded_rows",
    )(own0, own1, sel)


def pairs_kernel(
    pieces, own0, own1, own_u, kern, par_ref, energy_in, t1, t2, t3, a1, a2, a3, sel, own_out, *rest
):
    par_out, energy_out = rest[:pieces], rest[pieces]
    own_v, own_uv, kern_v, own_ov, par_ov, par_f, par_u, yw, z, x34 = rest[pieces + 1 : pieces + 11]
    own_f, staged, total_ref, sems = rest[pieces + 11 :]
    loads = [
        pltpu.make_async_copy(own_u, own_uv, sems.at[0]),
        pltpu.make_async_copy(kern, kern_v, sems.at[1]),
        pltpu.make_async_copy(own0, own_v.at[0], sems.at[2]),
        pltpu.make_async_copy(own1, own_v.at[1], sems.at[3]),
    ]
    for load in loads:
        load.start()

    widen_planes(par_ref, par_f)

    @pl.loop(0, QUADS // 4, unroll=2)
    def _(q):
        split_rows(par_f, sel, par_u, 4 * q, 4)

    half_y = G * Y_PITCH
    loads[0].wait()

    @pl.loop(0, G // 2, unroll=8)
    def _(i):
        density = []
        for e in range(2):
            partner = par_u[2 * i + e].astype(F32)
            for p in range(2):
                density.append((own_uv[p, 2 * i + e].astype(F32) * partner).astype(BF16))
        out = dot(t1[...], lanes(*density))
        for e in range(2):
            for p in range(2):
                at = pl.ds(p * half_y + (2 * i + e) * Y_PITCH, Y_ROWS)
                yw[at, :] = out[:, (2 * e + p) * LANES : (2 * e + p + 1) * LANES]

    @pl.loop(0, HALF, unroll=7)
    def _(k1):
        def line(p, part):
            return yw[pl.ds(p * half_y + part * HALF + k1, G, stride=Y_PITCH), :].astype(BF16)

        out = dot(t2[...], stack(lanes(line(0, 0), line(1, 0)), lanes(line(0, 1), line(1, 1))))
        at = pl.ds(pl.multiple_of(k1 * G, 16), G)
        for p in range(2):
            for part in range(2):
                left = (2 * p + part) * LANES
                value = out[part * G : (part + 1) * G, p * LANES : (p + 1) * LANES]
                x34[at, left : left + LANES] = value.astype(BF16)

    loads[1].wait()

    many = 5

    @pl.loop(0, KPAD // many, unroll=2)
    def _(m):
        at = pl.ds(pl.multiple_of(m * many * G, 16), many * G)
        factor = kern_v[at, :]
        out = [
            dot(x34[at, 2 * p * LANES : 2 * (p + 1) * LANES], t3[...]).astype(BF16)
            for p in range(2)
        ]
        for part in range(4):
            spectrum = lanes(*[o[:, part * 64 : (part + 1) * 64] for o in out]).astype(F32)
            value = spectrum * factor
            for i in range(many):
                row = (many * m + i) * Z_PITCH
                z[part, pl.ds(row, G), :] = value[i * G : (i + 1) * G]

    @pl.loop(0, G // 4, unroll=6)
    def _(four):
        parts = []
        for e in range(4):
            k2 = 4 * four + e
            mirror = Z_PITCH + jnp.where(k2 == 0, 0, G - k2)
            parts.append(
                stack(
                    z[0, pl.ds(k2, G // 2, stride=Z_PITCH), :].astype(BF16),
                    z[2, pl.ds(mirror, G // 2, stride=Z_PITCH), :].astype(BF16),
                    z[1, pl.ds(k2, G // 2, stride=Z_PITCH), :].astype(BF16),
                    z[3, pl.ds(mirror, G // 2, stride=Z_PITCH), :].astype(BF16),
                )
            )
        out = dot(a1[...], lanes(*parts))
        for e in range(4):
            at = (4 * four + e) * W_PITCH
            yw[pl.ds(at, 2 * G), :] = out[:, e * LANES : (e + 1) * LANES]

    @pl.loop(0, G // 4, unroll=6)
    def _(four):
        parts = []
        for e in range(4):
            x1 = 4 * four + e
            parts.append(
                stack(
                    yw[pl.ds(x1, G, stride=W_PITCH), :].astype(BF16),
                    yw[pl.ds(G + x1, G, stride=W_PITCH), :].astype(BF16),
                )
            )
        out = dot(a2[...], lanes(*parts))
        for r in range(4):
            block = [
                lanes(
                    out[r * QUADS : (r + 1) * QUADS, e * LANES : (e + 1) * LANES],
                    out[G + r * QUADS : G + (r + 1) * QUADS, e * LANES : (e + 1) * LANES],
                )
                for e in range(4)
            ]
            at = pl.multiple_of((r // 2) * G * QUADS + four * 4 * QUADS, 16)
            left = (r % 2) * 2 * LANES
            x34[pl.ds(at, 4 * QUADS), left : left + 2 * LANES] = stack(*block).astype(BF16)

    loads[2].wait()
    loads[3].wait()
    total_ref[...] = jnp.zeros_like(total_ref)
    planes = PLANES
    block_rows = planes * QUADS
    scale = F32(1.0 / NGRID)

    @pl.loop(0, G // planes, unroll=2)
    def _(ch):
        at = pl.multiple_of(ch * block_rows, 16)
        low = x34[pl.ds(at, block_rows), :]
        high = x34[pl.ds(G * QUADS + at, block_rows), :]
        fields = [low, lanes(low[:, 2 * LANES :], high[:, : 2 * LANES]), high]
        flat = pl.ds(pl.multiple_of(ch * planes * PLANE, 16), planes * PLANE)
        own_f[...] = own_v[:, flat, :].astype(F32)
        total = jnp.zeros((QUADS, LANES), F32)
        for third in range(3):
            out = dot(fields[third], a3[third]) * scale
            for i in range(planes):
                plane = ch * planes + i
                partner = par_f[pl.ds(plane * F_PITCH + third, QUADS, stride=3), :]
                here = pl.ds(i * PLANE + third, QUADS, stride=3)
                there = pl.ds(plane * PLANE + third, QUADS, stride=3)
                sent = jnp.zeros((QUADS, LANES), F32)
                for p in range(2):
                    potential = out[i * QUADS : (i + 1) * QUADS, p * LANES : (p + 1) * LANES]
                    own_ov[p, there, :] = potential * partner
                    sent = sent + potential * own_f[p, here, :]
                total = total + sent * partner
                staged[here, :] = sent
        total_ref[...] += total
        par_ov[flat, :] = staged[...].astype(BF16)
        pltpu.make_async_copy(own_ov.at[:, flat, :], own_out.at[:, flat, :], sems.at[4]).start()
        per_piece = G // planes // pieces
        for i, out in enumerate(par_out):

            @pl.when(ch // per_piece == i)
            def _():
                row = pl.multiple_of((ch - i * per_piece) * planes * PLANE, 16)
                there = out.at[pl.ds(row, planes * PLANE), :]
                pltpu.make_async_copy(par_ov.at[flat, :], there, sems.at[5 + i]).start()

    energy = jnp.sum(total_ref[...]) * F32(-2.0 / NGRID)
    energy_out[...] = energy_in[...] + energy
    pltpu.make_async_copy(own_ov, own_out, sems.at[4]).wait()
    for i, out in enumerate(par_out):
        source = par_ov.at[pl.ds(i * out.shape[0], out.shape[0]), :]
        pltpu.make_async_copy(source, out, sems.at[5 + i]).wait()


def pair_terms(own0, own1, own_u, partner, energy, tables, kern, pieces, interpret=False):
    vmem = pl.BlockSpec(memory_space=pltpu.VMEM)
    hbm = pl.BlockSpec(memory_space=pl.ANY)
    return pl.pallas_call(
        functools.partial(pairs_kernel, pieces),
        out_shape=(
            jax.ShapeDtypeStruct((2, ROWS, LANES), F32),
            *[jax.ShapeDtypeStruct((ROWS // pieces, LANES), BF16)] * pieces,
            jax.ShapeDtypeStruct((8, LANES), F32),
        ),
        in_specs=[hbm] * 4 + [vmem] * 9,
        out_specs=(hbm, *[hbm] * pieces, vmem),
        scratch_shapes=[
            pltpu.VMEM((2, ROWS, LANES), BF16),
            pltpu.VMEM((2, G, G, LANES), BF16),
            pltpu.VMEM((KPAD * G, LANES), F32),
            pltpu.VMEM((2, ROWS, LANES), F32),
            pltpu.VMEM((ROWS, LANES), BF16),
            pltpu.VMEM((G * F_PITCH, LANES), F32),
            pltpu.VMEM((G, G, LANES), BF16),
            pltpu.VMEM((2 * G * Y_PITCH, LANES), F32),
            pltpu.VMEM((4, KPAD * Z_PITCH, LANES), F32),
            pltpu.VMEM((KPAD * G, 4 * LANES), BF16),
            pltpu.VMEM((2, PLANES * PLANE, LANES), F32),
            pltpu.VMEM((PLANES * PLANE, LANES), F32),
            pltpu.VMEM((QUADS, LANES), F32),
            pltpu.SemaphoreType.DMA((5 + pieces,)),
        ],
        compiler_params=VMEM_ALL,
        cost_estimate=pl.CostEstimate(
            flops=20_000_000_000, bytes_accessed=20_000_000, transcendentals=0
        ),
        interpret=interpret,
        name="pair_terms",
    )(own0, own1, own_u, kern, partner, energy, *tables)


def add_products(gram_ref, column, own, exchange):
    for i in range(2):
        product = (own[i].astype(F32) * exchange).reshape(-1, 8, LANES)
        gram_ref[i, column] += jnp.sum(product, axis=0)


def first_sum_kernel(
    own0, own1, first, second, back0, exch0, part1, gram_ref,
    own_v, first_v, second_v, back_v, exch_v, part_v, load_sems, store_sems,
):
    chunks = load_sems.shape[0]
    rows = ROWS // chunks
    arrays = [(own0, own_v.at[0]), (own1, own_v.at[1]), (first, first_v), (second, second_v), (back0, back_v)]

    def loads(c):
        return [
            copy_rows(src, c * rows, dst, c * rows, rows, load_sems.at[c, i])
            for i, (src, dst) in enumerate(arrays)
        ]

    for c in range(chunks):
        for load in loads(c):
            load.start()
    gram_ref[...] = jnp.zeros_like(gram_ref)

    @pl.loop(0, chunks)
    def _(c):
        for load in loads(c):
            load.wait()
        at = pl.ds(pl.multiple_of(c * rows, 16), rows)
        exchange = first_v[0, at, :] + second_v[0, at, :] + back_v[at, :].astype(F32)
        exch_v[at, :] = exchange
        part_v[at, :] = first_v[1, at, :] + second_v[1, at, :]
        add_products(gram_ref, 0, [own_v[i, at, :] for i in range(2)], exchange)
        copy_rows(exch_v, c * rows, exch0, c * rows, rows, store_sems.at[0]).start()
        copy_rows(part_v, c * rows, part1, c * rows, rows, store_sems.at[1]).start()

    pltpu.make_async_copy(exch_v, exch0, store_sems.at[0]).wait()
    pltpu.make_async_copy(part_v, part1, store_sems.at[1]).wait()


def first_sum(own, first, second, back0, interpret=False):
    hbm = pl.BlockSpec(memory_space=pl.ANY)
    chunks = 12
    band = (ROWS, LANES)
    return pl.pallas_call(
        first_sum_kernel,
        out_shape=(
            jax.ShapeDtypeStruct(band, F32),
            jax.ShapeDtypeStruct(band, F32),
            jax.ShapeDtypeStruct((2, 2, 8, LANES), F32),
        ),
        in_specs=[hbm] * 5,
        out_specs=(hbm, hbm, pl.BlockSpec(memory_space=pltpu.VMEM)),
        scratch_shapes=[
            pltpu.VMEM((2, *band), BF16),
            pltpu.VMEM((2, *band), F32),
            pltpu.VMEM((2, *band), F32),
            pltpu.VMEM(band, BF16),
            pltpu.VMEM(band, F32),
            pltpu.VMEM(band, F32),
            pltpu.SemaphoreType.DMA((chunks, 5)),
            pltpu.SemaphoreType.DMA((2,)),
        ],
        compiler_params=VMEM_ALL,
        interpret=interpret,
        name="first_sum",
    )(*own, first, second, back0)


def piece_kernel(piece, own0, own1, exch0, part1, back1, gram_in, *rest):
    out, gram_out, own_v, exch_v, part_v, back_v, out_v, gram_ref, load_sems, store_sem = rest[-10:]
    chunks = load_sems.shape[0]
    size = back1.shape[0]
    rows = size // chunks
    base = piece * size
    arrays = [
        (own0, own_v.at[0], base), (own1, own_v.at[1], base),
        (exch0, exch_v, base), (part1, part_v, base), (back1, back_v, 0),
    ]

    def loads(c):
        return [
            copy_rows(src, start + c * rows, dst, c * rows, rows, load_sems.at[c, i])
            for i, (src, dst, start) in enumerate(arrays)
        ]

    for c in range(chunks):
        for load in loads(c):
            load.start()
    gram_ref[...] = gram_in[...]

    @pl.loop(0, chunks)
    def _(c):
        for load in loads(c):
            load.wait()
        at = pl.ds(pl.multiple_of(c * rows, 16), rows)
        exchange = part_v[at, :] + back_v[at, :].astype(F32)
        out_v[pl.ds(2 * c * rows, rows, stride=2), :] = exch_v[at, :]
        out_v[pl.ds(2 * c * rows + 1, rows, stride=2), :] = exchange
        add_products(gram_ref, 1, [own_v[i, at, :] for i in range(2)], exchange)
        copy_rows(out_v, 2 * c * rows, out, 2 * (base + c * rows), 2 * rows, store_sem).start()

    if piece < PIECES - 1:
        gram_out[...] = gram_ref[...]
    else:
        row = lax.broadcasted_iota(jnp.int32, (2, 2), 0)
        column = lax.broadcasted_iota(jnp.int32, (2, 2), 1)
        value = jnp.zeros((2, 2), F32)
        for i in range(2):
            for j in range(2):
                entry = jnp.sum(gram_ref[i, j]) * F32(1.0 / NGRID)
                value = jnp.where((row == i) & (column == j), entry, value)
        gram_out[...] = value
    copy_rows(out_v, 0, out, 2 * base, 2 * size, store_sem).wait()


def add_piece(piece, own, exch0, part1, back1, gram, out, interpret=False):
    last = piece == PIECES - 1
    earlier = [] if out is None else [out]
    hbm = pl.BlockSpec(memory_space=pl.ANY)
    vmem = pl.BlockSpec(memory_space=pltpu.VMEM)
    band = back1.shape
    return pl.pallas_call(
        functools.partial(piece_kernel, piece),
        out_shape=(
            jax.ShapeDtypeStruct((2 * ROWS, LANES), F32),
            jax.ShapeDtypeStruct((2, 2) if last else gram.shape, F32),
        ),
        in_specs=[hbm] * 5 + [vmem] + [hbm] * len(earlier),
        out_specs=(hbm, vmem),
        scratch_shapes=[
            pltpu.VMEM((2, *band), BF16),
            pltpu.VMEM(band, F32),
            pltpu.VMEM(band, F32),
            pltpu.VMEM(band, BF16),
            pltpu.VMEM((2 * band[0], LANES), F32),
            pltpu.VMEM((2, 2, 8, LANES), F32),
            pltpu.SemaphoreType.DMA((4, 5)),
            pltpu.SemaphoreType.DMA,
        ],
        input_output_aliases={6: 0} if earlier else {},
        compiler_params=VMEM_ALL,
        interpret=interpret,
        name="add_piece",
    )(*own, exch0, part1, back1, gram, *earlier)


def from_behind(block, axis, distance):
    size = lax.axis_size(axis)
    return lax.ppermute(block, axis, [((i - distance) % size, i) for i in range(size)])


def send_to(value, axis, bits):
    size = lax.axis_size(axis)
    flips = sorted({bits[0], bits[-1], sum(bits)})
    return [lax.ppermute(value, axis, [(i ^ flip, i) for i in range(size)]) for flip in flips]


def add_up(value, got):
    if len(got) == 1:
        return value + got[0]
    return (value + got[0]) + (got[1] + got[2])


def after(values, other):
    return lax.optimization_barrier((values, other))[0]


def per_device(orbitals):
    tables = section_tables()
    kern = screening()
    size = lax.axis_size("band")
    raw = orbitals.reshape(2, ROWS, LANES).transpose(1, 0, 2).reshape(2 * ROWS, LANES)
    own = [take_band(raw, j) for j in range(2)]
    previous = [from_behind(own[j], "band", 1) for j in range(2)]
    own_u = padded_rows(*own, tables[-1])
    energy = jnp.zeros((8, LANES), F32)
    first, sent0, energy = pair_terms(*own, own_u, previous[0], energy, tables, kern, 1)
    back0 = from_behind(sent0, "band", -1)
    second, *sent1, energy = pair_terms(*own, own_u, previous[1], energy, tables, kern, PIECES)
    back1 = [from_behind(piece, "band", -1) for piece in sent1]
    energy = energy * F32(1.0 / (size * orbitals.shape[0] * 2))

    exchange = None
    if size & (size - 1):
        energy = lax.psum(energy, "band")
        groups = []
    else:
        bits = [1 << b for b in range(size.bit_length() - 1)]
        rest = [b for b in bits if b != 2]
        groups = [rest[i : i + 2] for i in range(0, len(rest), 2)] + [[b] for b in bits if b == 2]
    got = send_to(energy, "band", groups.pop(0)) if groups else None
    exch0, part1, gram = first_sum(own, first, second, back0)
    for piece in range(PIECES):
        if got is not None:
            energy = add_up(energy, after(got, gram))
            got = send_to(energy, "band", groups.pop(0)) if groups else None
        exchange, gram = add_piece(piece, own, exch0, part1, back1[piece], gram, exchange)
    while got is not None:
        energy = add_up(energy, after(got, gram))
        got = send_to(energy, "band", groups.pop(0)) if groups else None
    exchange = exchange.reshape(ROWS, 2, LANES).transpose(1, 0, 2).reshape(2, NGRID)
    return exchange, gram, energy[0, 0]


def solution(mesh):
    return jax.shard_map(
        per_device,
        mesh=mesh,
        in_specs=(P("band", None),),
        out_specs=(P("band", None), P("band", None), P()),
        check_vma=False,
    )
```

```python
import functools

import jax
import jax.numpy as jnp
import ml_dtypes
import numpy as np
from jax import lax
from jax.experimental import pallas as pl
from jax.experimental.pallas import tpu as pltpu
from jax.sharding import PartitionSpec as P

G = 96
HALF = G // 2 + 1
NGRID = G * G * G
LANES = 128
ROWS = NGRID // LANES
PLANE = G * G // LANES
QUADS = G // 4
KPAD = HALF + 1
Y_ROWS = 104
Y_PITCH = Y_ROWS + 1
Z_PITCH = G + 1
W_PITCH = 2 * G + 1
F_PITCH = PLANE + 1
PLANES = 16
STEP_ROWS = PLANES * PLANE
STEPS = G // PLANES
PIECES = (3, 2, 1)
HEAD = STEP_ROWS
WAVE_UNIT = 0.05
SCREEN_SQ = 0.0121
MIB = 1024 * 1024
BF16 = jnp.bfloat16
F32 = jnp.float32


def dft_tables():
    n = np.arange(G)
    phases = (n[:, None] * n[None, :]) % G
    angles = phases.astype(np.float32) * np.float32(2.0 * np.pi / G)
    rounded = [f(angles).astype(ml_dtypes.bfloat16).astype(np.float32) for f in (np.cos, np.sin)]
    return rounded[0], rounded[1]


def section_tables():
    c, s = dft_tables()
    h = HALF
    t1 = np.zeros((Y_ROWS, G), np.float32)
    t1[:h] = c[:h]
    t1[h : 2 * h] = -s[:h]
    t2 = np.block([[c, s], [-s, c]])
    t3 = np.zeros((2, LANES, 4, 64), np.float32)
    back = (G - np.arange(h)) % G
    t3[0, :G, 0, :h] = c[:h].T
    t3[1, :G, 0, :h] = s[:h].T
    t3[0, :G, 1, :h] = -s[:h].T
    t3[1, :G, 1, :h] = c[:h].T
    t3[0, :G, 2, :h] = c[back].T
    t3[1, :G, 2, :h] = s[back].T
    t3[0, :G, 3, :h] = s[back].T
    t3[1, :G, 3, :h] = -c[back].T
    t3 = t3.reshape(2 * LANES, 4 * 64)
    order = np.concatenate([np.arange(G // 2), G - 1 - np.arange(G // 2)])
    a1 = np.block([[c[:, order], -s[:, order]], [s[:, order], c[:, order]]])
    rows = np.arange(G).reshape(QUADS, 4).T.reshape(-1)
    a2 = np.block([[c[rows], -s[rows]], [s[rows], c[rows]]])
    weight = np.full((h, 1), 2.0, np.float32)
    weight[0] = weight[h - 1] = 1.0
    a3 = np.zeros((3, 2, 2, 2, 64, 2, LANES), np.float32)
    for third in range(3):
        for lane in range(LANES):
            r, x3 = divmod(third * LANES + lane, G)
            for p in range(2):
                a3[third, r - third, 0, p, :h, p, lane] = weight[:, 0] * c[x3, :h]
                a3[third, r - third, 1, p, :h, p, lane] = -weight[:, 0] * s[x3, :h]
    a3 = a3.reshape(3, 4 * LANES, 2 * LANES)
    sel = np.zeros((2, 2 * LANES, 2 * LANES), np.float32)
    for r in range(4):
        for x in range(G):
            sel[r // 2, r * G + x - (r // 2) * LANES, (r % 2) * LANES + x] = 1.0
    return [t.astype(ml_dtypes.bfloat16) for t in (t1, t2, t3, a1, a2, a3, sel)]


def screening():
    n = np.arange(G)
    m = np.where(n <= G // 2, n, n - G).astype(np.float64)
    sq = m * m
    q2 = WAVE_UNIT * (sq[:HALF, None, None] + sq[None, :, None] + sq[None, None, :HALF])
    safe = np.where(q2 > 0, q2, 1.0)
    kern = 4.0 * np.pi * (1.0 - np.exp(-q2 / (4.0 * SCREEN_SQ))) / safe
    kern = np.where(q2 > 0, kern, np.pi / SCREEN_SQ)
    out = np.zeros((KPAD, G, 2, 64), np.float32)
    out[:HALF, :, :, :HALF] = kern[:, :, None, :]
    return out.reshape(KPAD * G, LANES)


def dot(a, b):
    return jnp.dot(a, b, preferred_element_type=F32)


def lanes(*parts):
    return jnp.concatenate(parts, axis=1)


def stack(*parts):
    return jnp.concatenate(parts, axis=0)


def split_rows(src, sel_ref, out, first, count):
    rows = [
        [src[pl.ds(3 * (first + i) + s, G, stride=F_PITCH), :].astype(BF16) for s in range(3)]
        for i in range(count)
    ]
    for half in range(2):
        part = dot(stack(*[lanes(r[half], r[half + 1]) for r in rows]), sel_ref[half])
        for i in range(count):
            for e in range(2):
                value = part[i * G : (i + 1) * G, e * LANES : (e + 1) * LANES]
                out[4 * (first + i) + 2 * half + e] = value.astype(BF16)


def widen_planes(src, dst, first):
    @pl.loop(0, src.shape[0] // (2 * PLANE), unroll=4)
    def _(i):
        value = src[pl.ds(pl.multiple_of(i * 2 * PLANE, 16), 2 * PLANE), :].astype(F32)
        dst[pl.ds((first + 2 * i) * F_PITCH, PLANE), :] = value[:PLANE]
        dst[pl.ds((first + 2 * i + 1) * F_PITCH, PLANE), :] = value[PLANE:]


def rows_of(ref, first, count):
    at = pl.ds(first, count)
    return ref.at[at, :] if len(ref.shape) == 2 else ref.at[:, at, :]


def copy_rows(src, src_row, dst, dst_row, count, sem):
    return pltpu.make_async_copy(rows_of(src, src_row, count), rows_of(dst, dst_row, count), sem)


def band_kernel(first, chunks, raw, pick, out, raw_v, out_v, load_sems, store_sem):
    rows = out.shape[0] // chunks
    loads = [
        copy_rows(raw, 2 * (first + c * rows), raw_v, 2 * c * rows, 2 * rows, load_sems.at[c])
        for c in range(chunks)
    ]
    for load in loads:
        load.start()
    for c, load in enumerate(loads):
        load.wait()
        for row in range(c * rows, (c + 1) * rows, LANES):
            value = dot(pick[...], raw_v[2 * row : 2 * row + 2 * LANES, :])
            out_v[row : row + LANES, :] = value.astype(BF16)
        copy_rows(out_v, c * rows, out, c * rows, rows, store_sem).start()
    pltpu.make_async_copy(out_v, out, store_sem).wait()


def take_band(raw, p, first, rows, chunks, earlier=None, interpret=False):
    pick = np.zeros((LANES, 2 * LANES), np.float32)
    pick[np.arange(LANES), 2 * np.arange(LANES) + p] = 1.0
    pick = jnp.asarray(pick.astype(ml_dtypes.bfloat16))
    if earlier is not None:
        pick = after(pick, earlier)
    hbm = pl.BlockSpec(memory_space=pl.ANY)
    return pl.pallas_call(
        functools.partial(band_kernel, first, chunks),
        out_shape=jax.ShapeDtypeStruct((rows, LANES), BF16),
        in_specs=[hbm, pl.BlockSpec(memory_space=pltpu.VMEM)],
        out_specs=hbm,
        scratch_shapes=[
            pltpu.VMEM((2 * rows, LANES), BF16),
            pltpu.VMEM((rows, LANES), BF16),
            pltpu.SemaphoreType.DMA((chunks,)),
            pltpu.SemaphoreType.DMA,
        ],
        compiler_params=pltpu.CompilerParams(vmem_limit_bytes=56 * MIB),
        interpret=interpret,
        name="take_band",
    )(raw, pick)


def rows_kernel(head, tail, own1, sel, out, wide):
    for p, parts in enumerate(([head, tail], [own1])):
        first = 0
        for part in parts:
            widen_planes(part, wide, first)
            first += part.shape[0] // PLANE

        @pl.loop(0, QUADS // 4, unroll=2)
        def _(q):
            split_rows(wide, sel, out.at[p], 4 * q, 4)


def padded_rows(own, sel, interpret=False):
    vmem = pl.BlockSpec(memory_space=pltpu.VMEM)
    return pl.pallas_call(
        rows_kernel,
        out_shape=jax.ShapeDtypeStruct((2, G, G, LANES), BF16),
        in_specs=[vmem] * 4,
        out_specs=vmem,
        scratch_shapes=[pltpu.VMEM((G * F_PITCH, LANES), F32)],
        compiler_params=pltpu.CompilerParams(vmem_limit_bytes=63 * MIB),
        interpret=interpret,
        name="padded_rows",
    )(*own, sel)


def pairs_kernel(count, pieces, share, head, tail, own1, own_u, kern, *refs):
    refs = list(refs)
    par_refs, refs = refs[:count], refs[count:]
    earlier = []
    if len(pieces) > 1:
        earlier, refs = refs[:2], refs[2:]
    table_refs, own_out = refs[:7], refs[7]
    par_out, energy_out = refs[8 : 8 + len(pieces)], refs[8 + len(pieces)]
    own_v, own_uv, kern_v, own_ov, par_ov, par_f, par_u, yw, z, x34 = refs[9 + len(pieces) : -13]
    own_f, staged, total_ref = refs[-13:-10]
    tables, (par_sems, table_sems, sems) = refs[-10:-3], refs[-3:]
    t1, t2, t3, a1, a2, a3, sel = tables
    par_v = par_ov
    par_loads = []
    first = 0
    for src in par_refs:
        for row in range(0, src.shape[0], STEP_ROWS):
            sem = par_sems.at[first // STEP_ROWS]
            par_loads.append(copy_rows(src, row, par_v, first, STEP_ROWS, sem))
            first += STEP_ROWS
    for load in par_loads:
        load.start()
    table_loads = [
        pltpu.make_async_copy(src, dst, table_sems.at[i])
        for i, (src, dst) in enumerate(zip(table_refs, tables))
    ]
    for i in (6, 0, 1, 2, 3, 4, 5):
        table_loads[i].start()
    loads = [
        pltpu.make_async_copy(own_u, own_uv, sems.at[0]),
        pltpu.make_async_copy(kern, kern_v, sems.at[1]),
        copy_rows(head, 0, own_v.at[0], 0, HEAD, sems.at[2]),
        copy_rows(tail, 0, own_v.at[0], HEAD, ROWS - HEAD, sems.at[3]),
        copy_rows(own1, 0, own_v.at[1], 0, ROWS, sems.at[4]),
    ]
    if earlier:
        loads.append(pltpu.make_async_copy(earlier[0], own_ov, sems.at[5]))
    for load in loads:
        load.start()

    for i, load in enumerate(par_loads):
        load.wait()
        widen_planes(par_v.at[pl.ds(i * STEP_ROWS, STEP_ROWS), :], par_f, i * PLANES)
    table_loads[6].wait()

    @pl.loop(0, QUADS // 4, unroll=2)
    def _(q):
        split_rows(par_f, sel, par_u, 4 * q, 4)

    half_y = G * Y_PITCH
    loads[0].wait()
    table_loads[0].wait()

    @pl.loop(0, G // 2, unroll=8)
    def _(i):
        density = []
        for e in range(2):
            partner = par_u[2 * i + e].astype(F32)
            for p in range(2):
                density.append((own_uv[p, 2 * i + e].astype(F32) * partner).astype(BF16))
        out = dot(t1[...], lanes(*density))
        for e in range(2):
            for p in range(2):
                at = pl.ds(p * half_y + (2 * i + e) * Y_PITCH, Y_ROWS)
                yw[at, :] = out[:, (2 * e + p) * LANES : (2 * e + p + 1) * LANES]

    table_loads[1].wait()

    @pl.loop(0, HALF, unroll=7)
    def _(k1):
        def line(p, part):
            return yw[pl.ds(p * half_y + part * HALF + k1, G, stride=Y_PITCH), :].astype(BF16)

        out = dot(t2[...], stack(lanes(line(0, 0), line(1, 0)), lanes(line(0, 1), line(1, 1))))
        at = pl.ds(pl.multiple_of(k1 * G, 16), G)
        for p in range(2):
            for part in range(2):
                left = (2 * p + part) * LANES
                value = out[part * G : (part + 1) * G, p * LANES : (p + 1) * LANES]
                x34[at, left : left + LANES] = value.astype(BF16)

    loads[1].wait()
    table_loads[2].wait()

    many = 5

    @pl.loop(0, KPAD // many, unroll=2)
    def _(m):
        at = pl.ds(pl.multiple_of(m * many * G, 16), many * G)
        factor = kern_v[at, :]
        out = [
            dot(x34[at, 2 * p * LANES : 2 * (p + 1) * LANES], t3[...]).astype(BF16)
            for p in range(2)
        ]
        for part in range(4):
            spectrum = lanes(*[o[:, part * 64 : (part + 1) * 64] for o in out]).astype(F32)
            value = spectrum * factor
            for i in range(many):
                row = (many * m + i) * Z_PITCH
                z[part, pl.ds(row, G), :] = value[i * G : (i + 1) * G]

    table_loads[3].wait()

    @pl.loop(0, G // 4, unroll=6)
    def _(four):
        parts = []
        for e in range(4):
            k2 = 4 * four + e
            mirror = Z_PITCH + jnp.where(k2 == 0, 0, G - k2)
            parts.append(
                stack(
                    z[0, pl.ds(k2, G // 2, stride=Z_PITCH), :].astype(BF16),
                    z[2, pl.ds(mirror, G // 2, stride=Z_PITCH), :].astype(BF16),
                    z[1, pl.ds(k2, G // 2, stride=Z_PITCH), :].astype(BF16),
                    z[3, pl.ds(mirror, G // 2, stride=Z_PITCH), :].astype(BF16),
                )
            )
        out = dot(a1[...], lanes(*parts))
        for e in range(4):
            at = (4 * four + e) * W_PITCH
            yw[pl.ds(at, 2 * G), :] = out[:, e * LANES : (e + 1) * LANES]

    table_loads[4].wait()

    @pl.loop(0, G // 4, unroll=6)
    def _(four):
        parts = []
        for e in range(4):
            x1 = 4 * four + e
            parts.append(
                stack(
                    yw[pl.ds(x1, G, stride=W_PITCH), :].astype(BF16),
                    yw[pl.ds(G + x1, G, stride=W_PITCH), :].astype(BF16),
                )
            )
        out = dot(a2[...], lanes(*parts))
        for r in range(4):
            block = [
                lanes(
                    out[r * QUADS : (r + 1) * QUADS, e * LANES : (e + 1) * LANES],
                    out[G + r * QUADS : G + (r + 1) * QUADS, e * LANES : (e + 1) * LANES],
                )
                for e in range(4)
            ]
            at = pl.multiple_of((r // 2) * G * QUADS + four * 4 * QUADS, 16)
            left = (r % 2) * 2 * LANES
            x34[pl.ds(at, 4 * QUADS), left : left + 2 * LANES] = stack(*block).astype(BF16)

    table_loads[5].wait()
    for load in loads[2:]:
        load.wait()
    total_ref[...] = jnp.zeros_like(total_ref)
    block_rows = PLANES * QUADS
    scale = F32(1.0 / NGRID)

    def result(ch):
        at = pl.multiple_of(ch * block_rows, 16)
        low = x34[pl.ds(at, block_rows), :]
        high = x34[pl.ds(G * QUADS + at, block_rows), :]
        fields = [low, lanes(low[:, 2 * LANES :], high[:, : 2 * LANES]), high]
        flat = pl.ds(pl.multiple_of(ch * STEP_ROWS, 16), STEP_ROWS)
        own_f[...] = own_v[:, flat, :].astype(F32)
        total = jnp.zeros((QUADS, LANES), F32)
        for third in range(3):
            out = dot(fields[third], a3[third]) * scale
            for i in range(PLANES):
                plane = ch * PLANES + i
                partner = par_f[pl.ds(plane * F_PITCH + third, QUADS, stride=3), :]
                here = pl.ds(i * PLANE + third, QUADS, stride=3)
                there = pl.ds(plane * PLANE + third, QUADS, stride=3)
                sent = jnp.zeros((QUADS, LANES), F32)
                for p in range(2):
                    potential = out[i * QUADS : (i + 1) * QUADS, p * LANES : (p + 1) * LANES]
                    term = potential * partner
                    own_ov[p, there, :] = own_ov[p, there, :] + term if earlier else term
                    sent = sent + potential * own_f[p, here, :]
                total = total + sent * partner
                staged[here, :] = sent
        total_ref[...] += total
        par_ov[flat, :] = staged[...].astype(BF16)
        row = ch * STEP_ROWS
        copy_rows(own_ov, row, own_out, row, STEP_ROWS, sems.at[6]).start()

    first = 0
    for i, steps in enumerate(pieces):

        @pl.loop(0, steps, unroll=2 if steps % 2 == 0 else steps)
        def _(step):
            ch = first + step
            result(ch)
            source, row = ch * STEP_ROWS, step * STEP_ROWS
            copy_rows(par_ov, source, par_out[i], row, STEP_ROWS, sems.at[7 + i]).start()

        first += steps

    energy = jnp.sum(total_ref[...]) * F32(share)
    if earlier:
        energy_out[...] = earlier[1][...] + energy
    else:
        energy_out[...] = jnp.zeros_like(energy_out) + energy
    pltpu.make_async_copy(own_ov, own_out, sems.at[6]).wait()
    first = 0
    for i, steps in enumerate(pieces):
        rows = steps * STEP_ROWS
        copy_rows(par_ov, first, par_out[i], 0, rows, sems.at[7 + i]).wait()
        first += rows


def pair_terms(own, own_u, partner, earlier, tables, kern, pieces, share, interpret=False):
    vmem = pl.BlockSpec(memory_space=pltpu.VMEM)
    hbm = pl.BlockSpec(memory_space=pl.ANY)
    return pl.pallas_call(
        functools.partial(pairs_kernel, len(partner), pieces, share),
        out_shape=(
            jax.ShapeDtypeStruct((2, ROWS, LANES), F32),
            *[jax.ShapeDtypeStruct((steps * STEP_ROWS, LANES), BF16) for steps in pieces],
            jax.ShapeDtypeStruct((8, LANES), F32),
        ),
        in_specs=[hbm] * (5 + len(partner)) + [hbm, vmem][: len(earlier)] + [hbm] * 7,
        out_specs=(hbm, *[hbm] * len(pieces), vmem),
        scratch_shapes=[
            pltpu.VMEM((2, ROWS, LANES), BF16),
            pltpu.VMEM((2, G, G, LANES), BF16),
            pltpu.VMEM((KPAD * G, LANES), F32),
            pltpu.VMEM((2, ROWS, LANES), F32),
            pltpu.VMEM((ROWS, LANES), BF16),
            pltpu.VMEM((G * F_PITCH, LANES), F32),
            pltpu.VMEM((G, G, LANES), BF16),
            pltpu.VMEM((2 * G * Y_PITCH, LANES), F32),
            pltpu.VMEM((4, KPAD * Z_PITCH, LANES), F32),
            pltpu.VMEM((KPAD * G, 4 * LANES), BF16),
            pltpu.VMEM((2, STEP_ROWS, LANES), F32),
            pltpu.VMEM((STEP_ROWS, LANES), F32),
            pltpu.VMEM((QUADS, LANES), F32),
            *[pltpu.VMEM(table.shape, BF16) for table in tables],
            pltpu.SemaphoreType.DMA((STEPS,)),
            pltpu.SemaphoreType.DMA((len(tables),)),
            pltpu.SemaphoreType.DMA((7 + len(pieces),)),
        ],
        compiler_params=pltpu.CompilerParams(vmem_limit_bytes=56 * MIB),
        cost_estimate=pl.CostEstimate(
            flops=20_000_000_000, bytes_accessed=20_000_000, transcendentals=0
        ),
        interpret=interpret,
        name="pair_terms",
    )(*own, own_u, kern, *partner, *earlier, *tables)


def piece_kernel(first, last, head, tail, own1, terms, back0, back1, *rest):
    gram_in = [] if first == 0 else [rest[0]]
    out, gram_out, own_v, terms_v, back_v, out_v, gram_ref, load_sems, store_sem = rest[-9:]
    size = back1.shape[0]
    rows = size // load_sems.shape[0]

    def loads(c):
        start = first + c * rows
        own0 = (head, start) if start < HEAD else (tail, start - HEAD)
        sources = [
            (*own0, own_v.at[0]), (own1, start, own_v.at[1]), (terms, start, terms_v),
            (back0, start, back_v.at[0]), (back1, c * rows, back_v.at[1]),
        ]
        return [
            copy_rows(src, row, dst, c * rows, rows, load_sems.at[c, i])
            for i, (src, row, dst) in enumerate(sources)
        ]

    chunks = [loads(c) for c in range(load_sems.shape[0])]
    for chunk in chunks:
        for load in chunk:
            load.start()
    gram_ref[...] = gram_in[0][...] if gram_in else jnp.zeros_like(gram_ref)
    for c, chunk in enumerate(chunks):
        for load in chunk:
            load.wait()
        at = pl.ds(c * rows, rows)
        own = [own_v[i, at, :].astype(F32) for i in range(2)]
        for p in range(2):
            exchange = terms_v[p, at, :] + back_v[p, at, :].astype(F32)
            out_v[pl.ds(2 * c * rows + p, rows, stride=2), :] = exchange
            for i in range(2):
                product = (own[i] * exchange).reshape(-1, 8, LANES)
                gram_ref[i, p] += jnp.sum(product, axis=0)
        copy_rows(out_v, 2 * c * rows, out, 2 * (first + c * rows), 2 * rows, store_sem).start()

    if not last:
        gram_out[...] = gram_ref[...]
    else:
        row = lax.broadcasted_iota(jnp.int32, (2, 2), 0)
        column = lax.broadcasted_iota(jnp.int32, (2, 2), 1)
        value = jnp.zeros((2, 2), F32)
        for i in range(2):
            for j in range(2):
                entry = jnp.sum(gram_ref[i, j]) * F32(1.0 / NGRID)
                value = jnp.where((row == i) & (column == j), entry, value)
        gram_out[...] = value
    copy_rows(out_v, 0, out, 2 * first, 2 * size, store_sem).wait()


def add_piece(first, own, terms, back0, back1, earlier, interpret=False):
    hbm = pl.BlockSpec(memory_space=pl.ANY)
    vmem = pl.BlockSpec(memory_space=pltpu.VMEM)
    size = back1.shape[0]
    last = first + size == ROWS
    return pl.pallas_call(
        functools.partial(piece_kernel, first, last),
        out_shape=(
            jax.ShapeDtypeStruct((2 * ROWS, LANES), F32),
            jax.ShapeDtypeStruct((2, 2) if last else (2, 2, 8, LANES), F32),
        ),
        in_specs=[hbm] * 6 + [vmem, hbm][: len(earlier)],
        out_specs=(hbm, vmem),
        scratch_shapes=[
            pltpu.VMEM((2, size, LANES), BF16),
            pltpu.VMEM((2, size, LANES), F32),
            pltpu.VMEM((2, size, LANES), BF16),
            pltpu.VMEM((2 * size, LANES), F32),
            pltpu.VMEM((2, 2, 8, LANES), F32),
            pltpu.SemaphoreType.DMA((2 * size // STEP_ROWS, 5)),
            pltpu.SemaphoreType.DMA,
        ],
        input_output_aliases={7: 0} if earlier else {},
        compiler_params=pltpu.CompilerParams(vmem_limit_bytes=44 * MIB),
        interpret=interpret,
        name="add_piece",
    )(*own, terms, back0, back1, *earlier)


def from_behind(block, axis, distance):
    size = lax.axis_size(axis)
    return lax.ppermute(block, axis, [((i - distance) % size, i) for i in range(size)])


def send_to(value, axis, bits):
    size = lax.axis_size(axis)
    flips = sorted({bits[0], bits[-1], sum(bits)})
    return [lax.ppermute(value, axis, [(i ^ flip, i) for i in range(size)]) for flip in flips]


def add_up(value, got):
    if len(got) == 1:
        return value + got[0]
    return (value + got[0]) + (got[1] + got[2])


def after(values, other):
    return lax.optimization_barrier((values, other))[0]


def per_device(orbitals):
    tables = section_tables()
    kern = screening()
    size = lax.axis_size("band")
    share = -2.0 / (NGRID * 2 * size * orbitals.shape[0])
    raw = orbitals.reshape(2, ROWS, LANES).transpose(1, 0, 2).reshape(2 * ROWS, LANES)
    head = take_band(raw, 0, 0, HEAD, 3)
    tail = take_band(raw, 0, HEAD, ROWS - HEAD, 9, head)
    own = [head, tail, take_band(raw, 1, 0, ROWS, 9, tail)]
    previous = [from_behind(part, "band", 1) for part in own]
    own_u = padded_rows(own, tables[-1])
    terms, back0, energy = pair_terms(
        own, own_u, previous[:2], (), tables, kern, (STEPS,), share
    )
    back0 = from_behind(back0, "band", -1)
    terms, *sent, energy = pair_terms(
        own, own_u, previous[2:], (terms, energy), tables, kern, PIECES, share
    )
    back1 = [from_behind(piece, "band", -1) for piece in sent]

    if size & (size - 1):
        energy = lax.psum(energy, "band")
        groups = []
    else:
        bits = [1 << b for b in range(size.bit_length() - 1)]
        rest = [b for b in bits if b != 2]
        groups = [rest[i : i + 2] for i in range(0, len(rest), 2)]
    for group in groups:
        energy = add_up(energy, send_to(energy, "band", group))
    result = ()
    first = 0
    for i, piece in enumerate(back1):
        if groups and i == len(back1) - 1:
            got = send_to(after(energy, result[1]), "band", [2])
        result = add_piece(first, own, terms, back0, piece, result[::-1])
        first += piece.shape[0]
    exchange, gram = result
    if groups:
        energy = add_up(energy, after(got, gram))
    exchange = exchange.reshape(ROWS, 2, LANES).transpose(1, 0, 2).reshape(2, NGRID)
    return exchange, gram, energy[0, 0]


def solution(mesh):
    return jax.shard_map(
        per_device,
        mesh=mesh,
        in_specs=(P("band", None),),
        out_specs=(P("band", None), P("band", None), P()),
        check_vma=False,
    )
```

```python
import functools

import jax
import jax.numpy as jnp
import ml_dtypes
import numpy as np
from jax import lax
from jax.experimental import pallas as pl
from jax.experimental.pallas import tpu as pltpu
from jax.sharding import PartitionSpec as P

G = 96
HALF = G // 2 + 1
NGRID = G * G * G
LANES = 128
ROWS = NGRID // LANES
PLANE = G * G // LANES
QUADS = G // 4
KPAD = HALF + 1
Y_ROWS = 104
Y_PITCH = Y_ROWS + 1
Z_PITCH = G + 1
W_PITCH = 2 * G + 1
F_PITCH = PLANE + 1
PLANES = 16
STEP_ROWS = PLANES * PLANE
STEPS = G // PLANES
PIECES = (3, 2, 1)
RIDER = 16
WAVE_UNIT = 0.05
SCREEN_SQ = 0.0121
MIB = 1024 * 1024
BF16 = jnp.bfloat16
F32 = jnp.float32


def dft_tables():
    n = np.arange(G)
    phases = (n[:, None] * n[None, :]) % G
    angles = phases.astype(np.float32) * np.float32(2.0 * np.pi / G)
    rounded = [f(angles).astype(ml_dtypes.bfloat16).astype(np.float32) for f in (np.cos, np.sin)]
    return rounded[0], rounded[1]


def section_tables():
    c, s = dft_tables()
    h = HALF
    t1 = np.zeros((Y_ROWS, G), np.float32)
    t1[:h] = c[:h]
    t1[h : 2 * h] = -s[:h]
    t2 = np.block([[c, s], [-s, c]])
    t3 = np.zeros((2, LANES, 4, 64), np.float32)
    back = (G - np.arange(h)) % G
    t3[0, :G, 0, :h] = c[:h].T
    t3[1, :G, 0, :h] = s[:h].T
    t3[0, :G, 1, :h] = -s[:h].T
    t3[1, :G, 1, :h] = c[:h].T
    t3[0, :G, 2, :h] = c[back].T
    t3[1, :G, 2, :h] = s[back].T
    t3[0, :G, 3, :h] = s[back].T
    t3[1, :G, 3, :h] = -c[back].T
    t3 = t3.reshape(2 * LANES, 4 * 64)
    order = np.concatenate([np.arange(G // 2), G - 1 - np.arange(G // 2)])
    a1 = np.block([[c[:, order], -s[:, order]], [s[:, order], c[:, order]]])
    rows = np.arange(G).reshape(QUADS, 4).T.reshape(-1)
    a2 = np.block([[c[rows], -s[rows]], [s[rows], c[rows]]])
    weight = np.full((h, 1), 2.0, np.float32)
    weight[0] = weight[h - 1] = 1.0
    a3 = np.zeros((3, 2, 2, 2, 64, 2, LANES), np.float32)
    for third in range(3):
        for lane in range(LANES):
            r, x3 = divmod(third * LANES + lane, G)
            for p in range(2):
                a3[third, r - third, 0, p, :h, p, lane] = weight[:, 0] * c[x3, :h]
                a3[third, r - third, 1, p, :h, p, lane] = -weight[:, 0] * s[x3, :h]
    a3 = a3.reshape(3, 4 * LANES, 2 * LANES)
    sel = np.zeros((2, 2 * LANES, 2 * LANES), np.float32)
    for r in range(4):
        for x in range(G):
            sel[r // 2, r * G + x - (r // 2) * LANES, (r % 2) * LANES + x] = 1.0
    return [t.astype(ml_dtypes.bfloat16) for t in (t1, t2, t3, a1, a2, a3, sel)]


def screening():
    n = np.arange(G)
    m = np.where(n <= G // 2, n, n - G).astype(np.float64)
    sq = m * m
    q2 = WAVE_UNIT * (sq[:HALF, None, None] + sq[None, :, None] + sq[None, None, :HALF])
    safe = np.where(q2 > 0, q2, 1.0)
    kern = 4.0 * np.pi * (1.0 - np.exp(-q2 / (4.0 * SCREEN_SQ))) / safe
    kern = np.where(q2 > 0, kern, np.pi / SCREEN_SQ)
    out = np.zeros((KPAD, G, 2, 64), np.float32)
    out[:HALF, :, :, :HALF] = kern[:, :, None, :]
    return out.reshape(KPAD * G, LANES)


def cost(size):
    return pl.CostEstimate(flops=0, bytes_accessed=size, transcendentals=0)


def dot(a, b):
    return jnp.dot(a, b, preferred_element_type=F32)


def lanes(*parts):
    return jnp.concatenate(parts, axis=1)


def stack(*parts):
    return jnp.concatenate(parts, axis=0)


def split_rows(src, sel_ref, out, first, count):
    rows = [
        [src[pl.ds(3 * (first + i) + s, G, stride=F_PITCH), :].astype(BF16) for s in range(3)]
        for i in range(count)
    ]
    for half in range(2):
        part = dot(stack(*[lanes(r[half], r[half + 1]) for r in rows]), sel_ref[half])
        for i in range(count):
            for e in range(2):
                value = part[i * G : (i + 1) * G, e * LANES : (e + 1) * LANES]
                out[4 * (first + i) + 2 * half + e] = value.astype(BF16)


def widen_planes(src, dst, first):
    @pl.loop(0, src.shape[0] // (2 * PLANE), unroll=4)
    def _(i):
        value = src[pl.ds(pl.multiple_of(i * 2 * PLANE, 16), 2 * PLANE), :].astype(F32)
        dst[pl.ds((first + 2 * i) * F_PITCH, PLANE), :] = value[:PLANE]
        dst[pl.ds((first + 2 * i + 1) * F_PITCH, PLANE), :] = value[PLANE:]


def rows_of(ref, first, count):
    at = pl.ds(first, count)
    return ref.at[at, :] if len(ref.shape) == 2 else ref.at[:, at, :]


def copy_rows(src, src_row, dst, dst_row, count, sem):
    return pltpu.make_async_copy(rows_of(src, src_row, count), rows_of(dst, dst_row, count), sem)


def band_kernel(p, raw, *refs):
    out, raw_v, out_v, load_sems, store_sem = refs[-5:]
    chunks = load_sems.shape[0]
    rows = out.shape[0] // chunks
    loads = [
        copy_rows(raw, 2 * c * rows, raw_v, 2 * c * rows, 2 * rows, load_sems.at[c])
        for c in range(chunks)
    ]
    for load in loads:
        load.start()
    shape = (LANES, 2 * LANES)
    row = lax.broadcasted_iota(jnp.int32, shape, 0)
    column = lax.broadcasted_iota(jnp.int32, shape, 1)
    pick = jnp.where(column == 2 * row + p, F32(1.0), F32(0.0)).astype(BF16)
    for c, load in enumerate(loads):
        load.wait()
        for row in range(c * rows, (c + 1) * rows, LANES):
            value = dot(pick, raw_v[2 * row : 2 * row + 2 * LANES, :])
            out_v[row : row + LANES, :] = value.astype(BF16)
        copy_rows(out_v, c * rows, out, c * rows, rows, store_sem).start()
    pltpu.make_async_copy(out_v, out, store_sem).wait()


def take_band(raw, p, earlier=(), interpret=False):
    hbm = pl.BlockSpec(memory_space=pl.ANY)
    return pl.pallas_call(
        functools.partial(band_kernel, p),
        out_shape=jax.ShapeDtypeStruct((ROWS, LANES), BF16),
        in_specs=[hbm] * (1 + len(earlier)),
        out_specs=hbm,
        scratch_shapes=[
            pltpu.VMEM((2 * ROWS, LANES), BF16),
            pltpu.VMEM((ROWS, LANES), BF16),
            pltpu.SemaphoreType.DMA((9,)),
            pltpu.SemaphoreType.DMA,
        ],
        compiler_params=pltpu.CompilerParams(vmem_limit_bytes=56 * MIB),
        cost_estimate=cost(6 * ROWS * LANES),
        interpret=interpret,
        name="take_band",
    )(raw, *earlier)


def rows_kernel(own0, own1, sel, out, wide):
    for p, own in enumerate((own0, own1)):
        widen_planes(own, wide, 0)

        @pl.loop(0, QUADS // 4, unroll=2)
        def _(q):
            split_rows(wide, sel, out.at[p], 4 * q, 4)


def padded_rows(own, sel, interpret=False):
    vmem = pl.BlockSpec(memory_space=pltpu.VMEM)
    return pl.pallas_call(
        rows_kernel,
        out_shape=jax.ShapeDtypeStruct((2, G, G, LANES), BF16),
        in_specs=[vmem] * 3,
        out_specs=vmem,
        scratch_shapes=[pltpu.VMEM((G * F_PITCH, LANES), F32)],
        compiler_params=pltpu.CompilerParams(vmem_limit_bytes=63 * MIB),
        cost_estimate=cost(16 * NGRID),
        interpret=interpret,
        name="padded_rows",
    )(*own, sel)


def pairs_kernel(pieces, share, own0, own1, own_u, kern, par, *refs):
    earlier = []
    if len(pieces) > 1:
        earlier, refs = refs[:2], refs[2:]
    table_refs, own_out = refs[:7], refs[7]
    par_out, energy_out = refs[8 : 8 + len(pieces)], refs[8 + len(pieces)]
    own_v, own_uv, kern_v, own_ov, par_ov, par_f, par_u, yw, z, x34 = refs[9 + len(pieces) : -16]
    own_f, staged, total_ref = refs[-16:-13]
    energy_v, before_v, parts_v = refs[-13:-10]
    tables, (par_sems, table_sems, sems) = refs[-10:-3], refs[-3:]
    t1, t2, t3, a1, a2, a3, sel = tables
    par_v = par_ov
    par_loads = []
    for first in (0, ROWS // 2):
        sem = par_sems.at[len(par_loads)]
        par_loads.append(copy_rows(par, first, par_v, first, ROWS // 2, sem))
    for load in par_loads:
        load.start()
    table_loads = [
        pltpu.make_async_copy(src, dst, table_sems.at[i])
        for i, (src, dst) in enumerate(zip(table_refs, tables))
    ]
    for i in (6, 0, 1, 2, 3, 4, 5):
        table_loads[i].start()
    loads = [
        pltpu.make_async_copy(own_u, own_uv, sems.at[0]),
        pltpu.make_async_copy(kern, kern_v, sems.at[1]),
        copy_rows(own0, 0, own_v.at[0], 0, ROWS, sems.at[2]),
        copy_rows(own1, 0, own_v.at[1], 0, ROWS, sems.at[3]),
    ]
    if earlier:
        loads.append(pltpu.make_async_copy(earlier[0], own_ov, sems.at[5]))
        loads.append(pltpu.make_async_copy(earlier[1], before_v, sems.at[8 + len(pieces)]))
    for load in loads:
        load.start()

    for i, load in enumerate(par_loads):
        load.wait()
        widen_planes(par_v.at[pl.ds(i * ROWS // 2, ROWS // 2), :], par_f, i * G // 2)
    table_loads[6].wait()

    @pl.loop(0, QUADS // 4, unroll=2)
    def _(q):
        split_rows(par_f, sel, par_u, 4 * q, 4)

    half_y = G * Y_PITCH
    loads[0].wait()
    table_loads[0].wait()

    @pl.loop(0, G // 2, unroll=8)
    def _(i):
        density = []
        for e in range(2):
            partner = par_u[2 * i + e].astype(F32)
            for p in range(2):
                density.append((own_uv[p, 2 * i + e].astype(F32) * partner).astype(BF16))
        out = dot(t1[...], lanes(*density))
        for e in range(2):
            for p in range(2):
                at = pl.ds(p * half_y + (2 * i + e) * Y_PITCH, Y_ROWS)
                yw[at, :] = out[:, (2 * e + p) * LANES : (2 * e + p + 1) * LANES]

    table_loads[1].wait()

    @pl.loop(0, HALF, unroll=7)
    def _(k1):
        def line(p, part):
            return yw[pl.ds(p * half_y + part * HALF + k1, G, stride=Y_PITCH), :].astype(BF16)

        out = dot(t2[...], stack(lanes(line(0, 0), line(1, 0)), lanes(line(0, 1), line(1, 1))))
        at = pl.ds(pl.multiple_of(k1 * G, 16), G)
        for p in range(2):
            for part in range(2):
                left = (2 * p + part) * LANES
                value = out[part * G : (part + 1) * G, p * LANES : (p + 1) * LANES]
                x34[at, left : left + LANES] = value.astype(BF16)

    loads[1].wait()
    table_loads[2].wait()

    many = 5

    @pl.loop(0, KPAD // many, unroll=2)
    def _(m):
        at = pl.ds(pl.multiple_of(m * many * G, 16), many * G)
        factor = kern_v[at, :]
        out = [
            dot(x34[at, 2 * p * LANES : 2 * (p + 1) * LANES], t3[...]).astype(BF16)
            for p in range(2)
        ]
        for part in range(4):
            spectrum = lanes(*[o[:, part * 64 : (part + 1) * 64] for o in out]).astype(F32)
            value = spectrum * factor
            for i in range(many):
                row = (many * m + i) * Z_PITCH
                z[part, pl.ds(row, G), :] = value[i * G : (i + 1) * G]

    table_loads[3].wait()

    @pl.loop(0, G // 4, unroll=6)
    def _(four):
        parts = []
        for e in range(4):
            k2 = 4 * four + e
            mirror = Z_PITCH + jnp.where(k2 == 0, 0, G - k2)
            parts.append(
                stack(
                    z[0, pl.ds(k2, G // 2, stride=Z_PITCH), :].astype(BF16),
                    z[2, pl.ds(mirror, G // 2, stride=Z_PITCH), :].astype(BF16),
                    z[1, pl.ds(k2, G // 2, stride=Z_PITCH), :].astype(BF16),
                    z[3, pl.ds(mirror, G // 2, stride=Z_PITCH), :].astype(BF16),
                )
            )
        out = dot(a1[...], lanes(*parts))
        for e in range(4):
            at = (4 * four + e) * W_PITCH
            yw[pl.ds(at, 2 * G), :] = out[:, e * LANES : (e + 1) * LANES]

    table_loads[4].wait()

    @pl.loop(0, G // 4, unroll=6)
    def _(four):
        parts = []
        for e in range(4):
            x1 = 4 * four + e
            parts.append(
                stack(
                    yw[pl.ds(x1, G, stride=W_PITCH), :].astype(BF16),
                    yw[pl.ds(G + x1, G, stride=W_PITCH), :].astype(BF16),
                )
            )
        out = dot(a2[...], lanes(*parts))
        for r in range(4):
            block = [
                lanes(
                    out[r * QUADS : (r + 1) * QUADS, e * LANES : (e + 1) * LANES],
                    out[G + r * QUADS : G + (r + 1) * QUADS, e * LANES : (e + 1) * LANES],
                )
                for e in range(4)
            ]
            at = pl.multiple_of((r // 2) * G * QUADS + four * 4 * QUADS, 16)
            left = (r % 2) * 2 * LANES
            x34[pl.ds(at, 4 * QUADS), left : left + 2 * LANES] = stack(*block).astype(BF16)

    table_loads[5].wait()
    for load in loads[2:]:
        load.wait()
    total_ref[...] = jnp.zeros_like(total_ref)
    block_rows = PLANES * QUADS
    scale = F32(1.0 / NGRID)

    def result(ch):
        at = pl.multiple_of(ch * block_rows, 16)
        low = x34[pl.ds(at, block_rows), :]
        high = x34[pl.ds(G * QUADS + at, block_rows), :]
        fields = [low, lanes(low[:, 2 * LANES :], high[:, : 2 * LANES]), high]
        flat = pl.ds(pl.multiple_of(ch * STEP_ROWS, 16), STEP_ROWS)
        own_f[...] = own_v[:, flat, :].astype(F32)
        total = jnp.zeros((QUADS, LANES), F32)
        for third in range(3):
            out = dot(fields[third], a3[third]) * scale
            for i in range(PLANES):
                plane = ch * PLANES + i
                partner = par_f[pl.ds(plane * F_PITCH + third, QUADS, stride=3), :]
                here = pl.ds(i * PLANE + third, QUADS, stride=3)
                there = pl.ds(plane * PLANE + third, QUADS, stride=3)
                sent = jnp.zeros((QUADS, LANES), F32)
                for p in range(2):
                    potential = out[i * QUADS : (i + 1) * QUADS, p * LANES : (p + 1) * LANES]
                    term = potential * partner
                    own_ov[p, there, :] = own_ov[p, there, :] + term if earlier else term
                    sent = sent + potential * own_f[p, here, :]
                total = total + sent * partner
                staged[here, :] = sent
        total_ref[...] += total
        par_ov[flat, :] = staged[...].astype(BF16)
        row = ch * STEP_ROWS
        copy_rows(own_ov, row, own_out, row, STEP_ROWS, sems.at[6]).start()

    first = 0
    for i, steps in enumerate(pieces):

        @pl.loop(0, steps, unroll=2 if steps % 2 == 0 else steps)
        def _(step):
            ch = first + step
            result(ch)
            source, row = ch * STEP_ROWS, step * STEP_ROWS
            copy_rows(par_ov, source, par_out[i], row, STEP_ROWS, sems.at[7 + i]).start()

        first += steps

    energy = jnp.zeros((8, LANES), F32) + jnp.sum(total_ref[...]) * F32(share)
    if earlier:
        energy = energy + before_v[...]
        row = lax.broadcasted_iota(jnp.int32, (8, LANES), 0)
        rest, parts = energy, jnp.zeros_like(energy)
        for i in range(3):
            part = rest.astype(BF16).astype(F32)
            parts = jnp.where(row == i, part, parts)
            rest = rest - part
        parts_v[...] = stack(parts, jnp.zeros_like(parts)).astype(BF16)
        rider = copy_rows(parts_v, 0, par_out[0], pieces[0] * STEP_ROWS, RIDER, sems.at[9 + len(pieces)])
        rider.start()
    energy_v[...] = energy
    report = pltpu.make_async_copy(energy_v, energy_out, sems.at[7 + len(pieces)])
    report.start()
    pltpu.make_async_copy(own_ov, own_out, sems.at[6]).wait()
    first = 0
    for i, steps in enumerate(pieces):
        rows = steps * STEP_ROWS
        copy_rows(par_ov, first, par_out[i], 0, rows, sems.at[7 + i]).wait()
        first += rows
    report.wait()
    if earlier:
        rider.wait()


def pair_terms(own, own_u, partner, earlier, tables, kern, pieces, share, interpret=False):
    hbm = pl.BlockSpec(memory_space=pl.ANY)
    return pl.pallas_call(
        functools.partial(pairs_kernel, pieces, share),
        out_shape=(
            jax.ShapeDtypeStruct((2, ROWS, LANES), F32),
            *[
                jax.ShapeDtypeStruct((steps * STEP_ROWS + (RIDER if earlier and i == 0 else 0), LANES), BF16)
                for i, steps in enumerate(pieces)
            ],
            jax.ShapeDtypeStruct((8, LANES), F32),
        ),
        in_specs=[hbm] * (5 + len(earlier) + len(tables)),
        out_specs=(hbm,) * (2 + len(pieces)),
        scratch_shapes=[
            pltpu.VMEM((2, ROWS, LANES), BF16),
            pltpu.VMEM((2, G, G, LANES), BF16),
            pltpu.VMEM((KPAD * G, LANES), F32),
            pltpu.VMEM((2, ROWS, LANES), F32),
            pltpu.VMEM((ROWS, LANES), BF16),
            pltpu.VMEM((G * F_PITCH, LANES), F32),
            pltpu.VMEM((G, G, LANES), BF16),
            pltpu.VMEM((2 * G * Y_PITCH, LANES), F32),
            pltpu.VMEM((4, KPAD * Z_PITCH, LANES), F32),
            pltpu.VMEM((KPAD * G, 4 * LANES), BF16),
            pltpu.VMEM((2, STEP_ROWS, LANES), F32),
            pltpu.VMEM((STEP_ROWS, LANES), F32),
            pltpu.VMEM((QUADS, LANES), F32),
            pltpu.VMEM((8, LANES), F32),
            pltpu.VMEM((8, LANES), F32),
            pltpu.VMEM((RIDER, LANES), BF16),
            *[pltpu.VMEM(table.shape, BF16) for table in tables],
            pltpu.SemaphoreType.DMA((2,)),
            pltpu.SemaphoreType.DMA((len(tables),)),
            pltpu.SemaphoreType.DMA((10 + len(pieces),)),
        ],
        compiler_params=pltpu.CompilerParams(vmem_limit_bytes=56 * MIB),
        cost_estimate=pl.CostEstimate(
            flops=20_000_000_000, bytes_accessed=20_000_000, transcendentals=0
        ),
        interpret=interpret,
        name="pair_terms",
    )(*own, own_u, kern, partner, *earlier, *tables)


def piece_kernel(first, size, own0, own1, terms, back0, back1, *rest):
    last = first + size == ROWS
    earlier = rest[: len(rest) - 12]
    out, gram_out, own_v, terms_v, back_v, out_v, gram_ref, gram_v, value_ref = rest[-12:-3]
    load_sems, gram_sems, store_sems = rest[-3:]
    rows = size // load_sems.shape[0]

    def loads(c):
        start = first + c * rows
        sources = [
            (own0, start, own_v.at[0]), (own1, start, own_v.at[1]), (terms, start, terms_v),
            (back0, start, back_v.at[0]), (back1, c * rows, back_v.at[1]),
        ]
        return [
            copy_rows(src, row, dst, c * rows, rows, load_sems.at[c, i])
            for i, (src, row, dst) in enumerate(sources)
        ]

    chunks = [loads(c) for c in range(load_sems.shape[0])]
    for chunk in chunks:
        for load in chunk:
            load.start()
    gram_loads = []
    if last:
        gram_loads = [
            pltpu.make_async_copy(src, gram_v.at[i], gram_sems.at[i])
            for i, src in enumerate(earlier[:-1])
        ]
        for load in gram_loads:
            load.start()
    gram_ref[...] = jnp.zeros_like(gram_ref)
    for c, chunk in enumerate(chunks):
        for load in chunk:
            load.wait()
        at = pl.ds(c * rows, rows)
        own = [own_v[i, at, :].astype(F32) for i in range(2)]
        for p in range(2):
            exchange = terms_v[p, at, :] + back_v[p, at, :].astype(F32)
            out_v[pl.ds(2 * c * rows + p, rows, stride=2), :] = exchange
            for i in range(2):
                product = (own[i] * exchange).reshape(-1, 8, LANES)
                gram_ref[i, p] += jnp.sum(product, axis=0)
        copy_rows(out_v, 2 * c * rows, out, 2 * (first + c * rows), 2 * rows, store_sems.at[0]).start()

    result = gram_ref
    if last:
        for load in gram_loads:
            load.wait()
        row = lax.broadcasted_iota(jnp.int32, (2, 2), 0)
        column = lax.broadcasted_iota(jnp.int32, (2, 2), 1)
        value = jnp.zeros((2, 2), F32)
        for i in range(2):
            for j in range(2):
                entry = gram_ref[i, j]
                for k in range(len(gram_loads)):
                    entry = entry + gram_v[k, i, j]
                value = jnp.where((row == i) & (column == j), jnp.sum(entry) * F32(1.0 / NGRID), value)
        value_ref[...] = value
        result = value_ref
    report = pltpu.make_async_copy(result, gram_out, store_sems.at[1])
    report.start()
    copy_rows(out_v, 0, out, 2 * first, 2 * size, store_sems.at[0]).wait()
    report.wait()


def add_piece(first, size, own, terms, back0, back1, grams, out, interpret=False):
    hbm = pl.BlockSpec(memory_space=pl.ANY)
    last = first + size == ROWS
    earlier = [] if out is None else [*(grams if last else []), out]
    gram_shape = (2, 2, 8, LANES)
    return pl.pallas_call(
        functools.partial(piece_kernel, first, size),
        out_shape=(
            jax.ShapeDtypeStruct((2 * ROWS, LANES), F32),
            jax.ShapeDtypeStruct((2, 2) if last else gram_shape, F32),
        ),
        in_specs=[hbm] * (5 + len(earlier)),
        out_specs=(hbm, hbm),
        scratch_shapes=[
            pltpu.VMEM((2, size, LANES), BF16),
            pltpu.VMEM((2, size, LANES), F32),
            pltpu.VMEM((2, size, LANES), BF16),
            pltpu.VMEM((2 * size, LANES), F32),
            pltpu.VMEM(gram_shape, F32),
            pltpu.VMEM((len(PIECES), *gram_shape), F32),
            pltpu.VMEM((2, 2), F32),
            pltpu.SemaphoreType.DMA((2 * size // STEP_ROWS, 5)),
            pltpu.SemaphoreType.DMA((len(PIECES),)),
            pltpu.SemaphoreType.DMA((2,)),
        ],
        input_output_aliases={4 + len(earlier): 0} if earlier else {},
        compiler_params=pltpu.CompilerParams(vmem_limit_bytes=44 * MIB),
        cost_estimate=cost(24 * size * LANES),
        interpret=interpret,
        name="add_piece",
    )(*own, terms, back0, back1, *earlier)


def from_behind(block, axis, distance):
    size = lax.axis_size(axis)
    return lax.ppermute(block, axis, [((i - distance) % size, i) for i in range(size)])


def send_to(value, axis, bits):
    size = lax.axis_size(axis)
    flips = sorted({bits[0], bits[-1], sum(bits)})
    return [lax.ppermute(value, axis, [(i ^ flip, i) for i in range(1, size, 2)]) for flip in flips]


def add_up(value, got):
    if len(got) == 1:
        return value + got[0]
    return (value + got[0]) + (got[1] + got[2])


def after(values, other):
    return lax.optimization_barrier((values, other))[0]


def per_device(orbitals):
    tables = section_tables()
    kern = screening()
    size = lax.axis_size("band")
    share = -2.0 / (NGRID * 2 * size * orbitals.shape[0])
    raw = orbitals.reshape(2, ROWS, LANES).transpose(1, 0, 2).reshape(2 * ROWS, LANES)
    own = [take_band(raw, 0)]
    own.append(take_band(raw, 1, own))
    previous = [from_behind(part, "band", 1) for part in own]
    own_u = padded_rows(own, tables[-1])
    terms, back0, energy = pair_terms(
        own, own_u, previous[0], (), tables, kern, (STEPS,), share
    )
    back0 = from_behind(back0, "band", -1)
    terms, *sent, energy = pair_terms(
        own, own_u, previous[1], (terms, energy), tables, kern, PIECES, share
    )
    back1 = [from_behind(piece, "band", -1) for piece in sent]

    power = size & (size - 1) == 0
    rounds = []
    if power:
        bits = [1 << b for b in range(2, size.bit_length() - 1)] + [2][: size // 4]
        rounds = [bits[i : i + 2] for i in range(0, len(bits), 2)]
        energy = energy + jnp.sum(back1[0][-RIDER:, :1].astype(F32))
    else:
        energy = lax.psum(energy, "band")
    exchange, grams = None, []
    first = 0
    for steps, piece in zip(PIECES, back1):
        sent, got = bool(rounds), None
        if rounds:
            got = send_to(energy, "band", rounds.pop(0))
        elif power and len(grams) == len(PIECES) - 1:
            total = lax.ppermute(energy, "band", [(i + 1, i) for i in range(0, size, 2)])
        size_rows = steps * STEP_ROWS
        exchange, gram = add_piece(first, size_rows, own, terms, back0, piece, grams, exchange)
        grams.append(gram)
        first += size_rows
        if got:
            energy = add_up(energy, after(got, gram))
    if power:
        for bits in rounds:
            energy = add_up(energy, send_to(energy, "band", bits))
        if sent:
            total = lax.ppermute(energy, "band", [(i + 1, i) for i in range(0, size, 2)])
        odd = lax.axis_index("band") % 2 == 1
        energy = jnp.where(odd, energy, after(total, gram))
    exchange = exchange.reshape(ROWS, 2, LANES).transpose(1, 0, 2).reshape(2, NGRID)
    return exchange, gram, energy[0, 0]


def solution(mesh):
    return jax.shard_map(
        per_device,
        mesh=mesh,
        in_specs=(P("band", None),),
        out_specs=(P("band", None), P("band", None), P()),
        check_vma=False,
    )
```

```python
import functools

import jax
import jax.numpy as jnp
import ml_dtypes
import numpy as np
from jax import lax
from jax.experimental import pallas as pl
from jax.experimental.pallas import tpu as pltpu
from jax.sharding import PartitionSpec as P

G = 96
HALF = G // 2 + 1
NGRID = G * G * G
LANES = 128
ROWS = NGRID // LANES
PLANE = G * G // LANES
QUADS = G // 4
KPAD = HALF + 1
Y_ROWS = 104
Y_PITCH = Y_ROWS + 1
Z_PITCH = G + 1
W_PITCH = 2 * G + 1
Z_ROWS = KPAD * Z_PITCH
F_PITCH = PLANE + 1
PLANES = 16
STEP_ROWS = PLANES * PLANE
STEPS = G // PLANES
PIECES = (3, 2, 1)
WAVE_UNIT = 0.05
SCREEN_SQ = 0.0121
MIB = 1024 * 1024
BF16 = jnp.bfloat16
F32 = jnp.float32


def dft_tables():
    n = np.arange(G)
    phases = (n[:, None] * n[None, :]) % G
    angles = phases.astype(np.float32) * np.float32(2.0 * np.pi / G)
    rounded = [f(angles).astype(ml_dtypes.bfloat16).astype(np.float32) for f in (np.cos, np.sin)]
    return rounded[0], rounded[1]


def section_tables():
    c, s = dft_tables()
    h = HALF
    t1 = np.zeros((Y_ROWS, G), np.float32)
    t1[:h] = c[:h]
    t1[h : 2 * h] = -s[:h]
    t2 = np.block([[c, s], [-s, c]])
    t3 = np.zeros((2, LANES, 4, 64), np.float32)
    back = (G - np.arange(h)) % G
    t3[0, :G, 0, :h] = c[:h].T
    t3[1, :G, 0, :h] = s[:h].T
    t3[0, :G, 1, :h] = -s[:h].T
    t3[1, :G, 1, :h] = c[:h].T
    t3[0, :G, 2, :h] = c[back].T
    t3[1, :G, 2, :h] = s[back].T
    t3[0, :G, 3, :h] = s[back].T
    t3[1, :G, 3, :h] = -c[back].T
    t3 = t3.reshape(2 * LANES, 4 * 64)
    order = np.concatenate([np.arange(G // 2), G - 1 - np.arange(G // 2)])
    a1 = np.block([[c[:, order], -s[:, order]], [s[:, order], c[:, order]]])
    rows = np.arange(G).reshape(QUADS, 4).T.reshape(-1)
    a2 = np.block([[c[rows], -s[rows]], [s[rows], c[rows]]])
    weight = np.full((h, 1), 2.0, np.float32)
    weight[0] = weight[h - 1] = 1.0
    a3 = np.zeros((3, 2, 2, 2, 64, 2, LANES), np.float32)
    for third in range(3):
        for lane in range(LANES):
            r, x3 = divmod(third * LANES + lane, G)
            for p in range(2):
                a3[third, r - third, 0, p, :h, p, lane] = weight[:, 0] * c[x3, :h]
                a3[third, r - third, 1, p, :h, p, lane] = -weight[:, 0] * s[x3, :h]
    a3 = a3.reshape(3, 4 * LANES, 2 * LANES)
    sel = np.zeros((2, 2 * LANES, 2 * LANES), np.float32)
    for r in range(4):
        for x in range(G):
            sel[r // 2, r * G + x - (r // 2) * LANES, (r % 2) * LANES + x] = 1.0
    return [t.astype(ml_dtypes.bfloat16) for t in (t1, t2, t3, a1, a2, a3, sel)]


def screening():
    n = np.arange(G)
    m = np.where(n <= G // 2, n, n - G).astype(np.float64)
    sq = m * m
    q2 = WAVE_UNIT * (sq[:HALF, None, None] + sq[None, :, None] + sq[None, None, :HALF])
    safe = np.where(q2 > 0, q2, 1.0)
    kern = 4.0 * np.pi * (1.0 - np.exp(-q2 / (4.0 * SCREEN_SQ))) / safe
    kern = np.where(q2 > 0, kern, np.pi / SCREEN_SQ)
    out = np.zeros((KPAD, G, 2, 64), np.float32)
    out[:HALF, :, :, :HALF] = kern[:, :, None, :]
    return out.reshape(KPAD * G, LANES)


def cost(size):
    return pl.CostEstimate(flops=0, bytes_accessed=size, transcendentals=0)


def dot(a, b):
    return jnp.dot(a, b, preferred_element_type=F32)


def lanes(*parts):
    return jnp.concatenate(parts, axis=1)


def stack(*parts):
    return jnp.concatenate(parts, axis=0)


def split_rows(src, sel_ref, out, first, count):
    rows = [
        [src[pl.ds(3 * (first + i) + s, G, stride=F_PITCH), :].astype(BF16) for s in range(3)]
        for i in range(count)
    ]
    for half in range(2):
        part = dot(stack(*[lanes(r[half], r[half + 1]) for r in rows]), sel_ref[half])
        for i in range(count):
            for e in range(2):
                value = part[i * G : (i + 1) * G, e * LANES : (e + 1) * LANES]
                out[4 * (first + i) + 2 * half + e] = value.astype(BF16)


def widen_planes(src, dst, first):
    @pl.loop(0, src.shape[0] // (2 * PLANE), unroll=4)
    def _(i):
        value = src[pl.ds(pl.multiple_of(i * 2 * PLANE, 16), 2 * PLANE), :].astype(F32)
        dst[pl.ds((first + 2 * i) * F_PITCH, PLANE), :] = value[:PLANE]
        dst[pl.ds((first + 2 * i + 1) * F_PITCH, PLANE), :] = value[PLANE:]


def rows_of(ref, first, count):
    at = pl.ds(first, count)
    return ref.at[at, :] if len(ref.shape) == 2 else ref.at[:, at, :]


def copy_rows(src, src_row, dst, dst_row, count, sem):
    return pltpu.make_async_copy(rows_of(src, src_row, count), rows_of(dst, dst_row, count), sem)


def band_kernel(p, raw, *refs):
    out, raw_v, out_v, load_sems, store_sem = refs[-5:]
    chunks = load_sems.shape[0]
    rows = out.shape[0] // chunks
    loads = [
        copy_rows(raw, 2 * c * rows, raw_v, 2 * c * rows, 2 * rows, load_sems.at[c])
        for c in range(chunks)
    ]
    for load in loads:
        load.start()
    shape = (LANES, 2 * LANES)
    row = lax.broadcasted_iota(jnp.int32, shape, 0)
    column = lax.broadcasted_iota(jnp.int32, shape, 1)
    pick = jnp.where(column == 2 * row + p, F32(1.0), F32(0.0)).astype(BF16)
    for c, load in enumerate(loads):
        load.wait()
        for row in range(c * rows, (c + 1) * rows, LANES):
            value = dot(pick, raw_v[2 * row : 2 * row + 2 * LANES, :])
            out_v[row : row + LANES, :] = value.astype(BF16)
        copy_rows(out_v, c * rows, out, c * rows, rows, store_sem).start()
    pltpu.make_async_copy(out_v, out, store_sem).wait()


def take_band(raw, p, earlier=(), interpret=False):
    hbm = pl.BlockSpec(memory_space=pl.ANY)
    return pl.pallas_call(
        functools.partial(band_kernel, p),
        out_shape=jax.ShapeDtypeStruct((ROWS, LANES), BF16),
        in_specs=[hbm] * (1 + len(earlier)),
        out_specs=hbm,
        scratch_shapes=[
            pltpu.VMEM((2 * ROWS, LANES), BF16),
            pltpu.VMEM((ROWS, LANES), BF16),
            pltpu.SemaphoreType.DMA((9,)),
            pltpu.SemaphoreType.DMA,
        ],
        compiler_params=pltpu.CompilerParams(vmem_limit_bytes=63 * MIB),
        cost_estimate=cost(6 * ROWS * LANES),
        interpret=interpret,
        name="take_band",
    )(raw, *earlier)


def rows_kernel(own0, own1, sel, out, wide):
    for p, own in enumerate((own0, own1)):
        widen_planes(own, wide, 0)

        @pl.loop(0, QUADS // 4, unroll=2)
        def _(q):
            split_rows(wide, sel, out.at[p], 4 * q, 4)


def padded_rows(own, sel, interpret=False):
    vmem = pl.BlockSpec(memory_space=pltpu.VMEM)
    return pl.pallas_call(
        rows_kernel,
        out_shape=jax.ShapeDtypeStruct((2, G, G, LANES), BF16),
        in_specs=[vmem] * 3,
        out_specs=vmem,
        scratch_shapes=[pltpu.VMEM((G * F_PITCH, LANES), F32)],
        compiler_params=pltpu.CompilerParams(vmem_limit_bytes=63 * MIB),
        cost_estimate=cost(16 * NGRID),
        interpret=interpret,
        name="padded_rows",
    )(*own, sel)


def pairs_kernel(pieces, share, own0, own1, own_u, kern, par, *refs):
    earlier = []
    if len(pieces) > 1:
        earlier, refs = refs[:2], refs[2:]
    table_refs, own_out = refs[:7], refs[7]
    par_out, energy_out = refs[8 : 8 + len(pieces)], refs[8 + len(pieces)]
    own_v, own_uv, kern_v, own_ov, par_ov, par_f, par_u, yw, z, x34 = refs[9 + len(pieces) : -15]
    own_f, staged, total_ref, energy_v, before_v = refs[-15:-10]
    tables, (par_sems, table_sems, sems) = refs[-10:-3], refs[-3:]
    t1, t2, t3, a1, a2, a3, sel = tables
    par_v = par_ov
    par_loads = []
    for first in (0, ROWS // 2):
        sem = par_sems.at[len(par_loads)]
        par_loads.append(copy_rows(par, first, par_v, first, ROWS // 2, sem))
    for load in par_loads:
        load.start()
    table_loads = [
        pltpu.make_async_copy(src, dst, table_sems.at[i])
        for i, (src, dst) in enumerate(zip(table_refs, tables))
    ]
    table_loads[6].start()
    table_loads[0].start()
    loads = [
        pltpu.make_async_copy(own_u, own_uv, sems.at[0]),
        pltpu.make_async_copy(kern, kern_v, sems.at[1]),
        copy_rows(own0, 0, own_v.at[0], 0, ROWS, sems.at[2]),
        copy_rows(own1, 0, own_v.at[1], 0, ROWS, sems.at[3]),
    ]
    later = []
    if earlier:
        later = [copy_rows(earlier[0].at[p], 0, z, p * ROWS, ROWS, sems.at[4 + p]) for p in range(2)]
        loads.append(pltpu.make_async_copy(earlier[1], before_v, sems.at[8 + len(pieces)]))

    for i, load in enumerate(par_loads):
        load.wait()
        for other in ([loads[0]], table_loads[1:5])[i]:
            other.start()
        widen_planes(par_v.at[pl.ds(i * ROWS // 2, ROWS // 2), :], par_f, i * G // 2)
    table_loads[6].wait()

    @pl.loop(0, QUADS // 4, unroll=2)
    def _(q):
        split_rows(par_f, sel, par_u, 4 * q, 4)

    half_y = G * Y_PITCH
    loads[0].wait()
    for load in loads[1:]:
        load.start()
    table_loads[5].start()
    table_loads[0].wait()

    @pl.loop(0, G // 2, unroll=8)
    def _(i):
        density = []
        for e in range(2):
            partner = par_u[2 * i + e].astype(F32)
            for p in range(2):
                density.append((own_uv[p, 2 * i + e].astype(F32) * partner).astype(BF16))
        out = dot(t1[...], lanes(*density))
        for e in range(2):
            for p in range(2):
                at = pl.ds(p * half_y + (2 * i + e) * Y_PITCH, Y_ROWS)
                yw[at, :] = out[:, (2 * e + p) * LANES : (2 * e + p + 1) * LANES]

    table_loads[1].wait()

    @pl.loop(0, HALF, unroll=7)
    def _(k1):
        def line(p, part):
            return yw[pl.ds(p * half_y + part * HALF + k1, G, stride=Y_PITCH), :].astype(BF16)

        out = dot(t2[...], stack(lanes(line(0, 0), line(1, 0)), lanes(line(0, 1), line(1, 1))))
        at = pl.ds(pl.multiple_of(k1 * G, 16), G)
        for p in range(2):
            for part in range(2):
                left = (2 * p + part) * LANES
                value = out[part * G : (part + 1) * G, p * LANES : (p + 1) * LANES]
                x34[at, left : left + LANES] = value.astype(BF16)

    loads[1].wait()
    table_loads[2].wait()

    many = 5

    @pl.loop(0, KPAD // many, unroll=2)
    def _(m):
        at = pl.ds(pl.multiple_of(m * many * G, 16), many * G)
        factor = kern_v[at, :]
        out = [
            dot(x34[at, 2 * p * LANES : 2 * (p + 1) * LANES], t3[...]).astype(BF16)
            for p in range(2)
        ]
        for part in range(4):
            spectrum = lanes(*[o[:, part * 64 : (part + 1) * 64] for o in out]).astype(F32)
            value = spectrum * factor
            for i in range(many):
                row = part * Z_ROWS + (many * m + i) * Z_PITCH
                z[pl.ds(row, G), :] = value[i * G : (i + 1) * G]

    table_loads[3].wait()

    @pl.loop(0, G // 4, unroll=6)
    def _(four):
        parts = []
        for e in range(4):
            k2 = 4 * four + e
            mirror = Z_PITCH + jnp.where(k2 == 0, 0, G - k2)
            parts.append(
                stack(
                    z[pl.ds(k2, G // 2, stride=Z_PITCH), :].astype(BF16),
                    z[pl.ds(2 * Z_ROWS + mirror, G // 2, stride=Z_PITCH), :].astype(BF16),
                    z[pl.ds(1 * Z_ROWS + k2, G // 2, stride=Z_PITCH), :].astype(BF16),
                    z[pl.ds(3 * Z_ROWS + mirror, G // 2, stride=Z_PITCH), :].astype(BF16),
                )
            )
        out = dot(a1[...], lanes(*parts))
        for e in range(4):
            at = (4 * four + e) * W_PITCH
            yw[pl.ds(at, 2 * G), :] = out[:, e * LANES : (e + 1) * LANES]

    for load in later:
        load.start()
    table_loads[4].wait()

    @pl.loop(0, G // 4, unroll=6)
    def _(four):
        parts = []
        for e in range(4):
            x1 = 4 * four + e
            parts.append(
                stack(
                    yw[pl.ds(x1, G, stride=W_PITCH), :].astype(BF16),
                    yw[pl.ds(G + x1, G, stride=W_PITCH), :].astype(BF16),
                )
            )
        out = dot(a2[...], lanes(*parts))
        for r in range(4):
            block = [
                lanes(
                    out[r * QUADS : (r + 1) * QUADS, e * LANES : (e + 1) * LANES],
                    out[G + r * QUADS : G + (r + 1) * QUADS, e * LANES : (e + 1) * LANES],
                )
                for e in range(4)
            ]
            at = pl.multiple_of((r // 2) * G * QUADS + four * 4 * QUADS, 16)
            left = (r % 2) * 2 * LANES
            x34[pl.ds(at, 4 * QUADS), left : left + 2 * LANES] = stack(*block).astype(BF16)

    table_loads[5].wait()
    for load in loads[2:] + later:
        load.wait()
    total_ref[...] = jnp.zeros_like(total_ref)
    block_rows = PLANES * QUADS
    scale = F32(1.0 / NGRID)

    def result(ch):
        at = pl.multiple_of(ch * block_rows, 16)
        low = x34[pl.ds(at, block_rows), :]
        high = x34[pl.ds(G * QUADS + at, block_rows), :]
        fields = [low, lanes(low[:, 2 * LANES :], high[:, : 2 * LANES]), high]
        flat = pl.ds(pl.multiple_of(ch * STEP_ROWS, 16), STEP_ROWS)
        own_f[...] = own_v[:, flat, :].astype(F32)
        total = jnp.zeros((QUADS, LANES), F32)
        for third in range(3):
            out = dot(fields[third], a3[third]) * scale
            for i in range(PLANES):
                plane = ch * PLANES + i
                partner = par_f[pl.ds(plane * F_PITCH + third, QUADS, stride=3), :]
                here = pl.ds(i * PLANE + third, QUADS, stride=3)
                there = pl.ds(plane * PLANE + third, QUADS, stride=3)
                sent = jnp.zeros((QUADS, LANES), F32)
                for p in range(2):
                    potential = out[i * QUADS : (i + 1) * QUADS, p * LANES : (p + 1) * LANES]
                    term = potential * partner
                    if earlier:
                        at = p * ROWS + plane * PLANE + third
                        term = term + z[pl.ds(at, QUADS, stride=3), :]
                    own_ov[p, there, :] = term
                    sent = sent + potential * own_f[p, here, :]
                total = total + sent * partner
                staged[here, :] = sent
        total_ref[...] += total
        par_ov[flat, :] = staged[...].astype(BF16)
        row = ch * STEP_ROWS
        copy_rows(own_ov, row, own_out, row, STEP_ROWS, sems.at[6]).start()

    first = 0
    for i, steps in enumerate(pieces):

        @pl.loop(0, steps, unroll=2 if steps % 2 == 0 else steps)
        def _(step):
            ch = first + step
            result(ch)
            source, row = ch * STEP_ROWS, step * STEP_ROWS
            copy_rows(par_ov, source, par_out[i], row, STEP_ROWS, sems.at[7 + i]).start()

        first += steps

    energy = jnp.zeros((8, LANES), F32) + jnp.sum(total_ref[...]) * F32(share)
    if earlier:
        energy = energy + before_v[...]
    energy_v[...] = energy
    report = pltpu.make_async_copy(energy_v, energy_out, sems.at[7 + len(pieces)])
    report.start()
    pltpu.make_async_copy(own_ov, own_out, sems.at[6]).wait()
    first = 0
    for i, steps in enumerate(pieces):
        rows = steps * STEP_ROWS
        copy_rows(par_ov, first, par_out[i], 0, rows, sems.at[7 + i]).wait()
        first += rows
    report.wait()


def pair_terms(own, own_u, partner, earlier, tables, kern, pieces, share, interpret=False):
    hbm = pl.BlockSpec(memory_space=pl.ANY)
    return pl.pallas_call(
        functools.partial(pairs_kernel, pieces, share),
        out_shape=(
            jax.ShapeDtypeStruct((2, ROWS, LANES), F32),
            *[jax.ShapeDtypeStruct((steps * STEP_ROWS, LANES), BF16) for steps in pieces],
            jax.ShapeDtypeStruct((8, LANES), F32),
        ),
        in_specs=[hbm] * (5 + len(earlier) + len(tables)),
        out_specs=(hbm,) * (2 + len(pieces)),
        scratch_shapes=[
            pltpu.VMEM((2, ROWS, LANES), BF16),
            pltpu.VMEM((2, G, G, LANES), BF16),
            pltpu.VMEM((KPAD * G, LANES), F32),
            pltpu.VMEM((2, ROWS, LANES), F32),
            pltpu.VMEM((ROWS, LANES), BF16),
            pltpu.VMEM((G * F_PITCH, LANES), F32),
            pltpu.VMEM((G, G, LANES), BF16),
            pltpu.VMEM((2 * G * Y_PITCH, LANES), F32),
            pltpu.VMEM((4 * Z_ROWS, LANES), F32),
            pltpu.VMEM((KPAD * G, 4 * LANES), BF16),
            pltpu.VMEM((2, STEP_ROWS, LANES), F32),
            pltpu.VMEM((STEP_ROWS, LANES), F32),
            pltpu.VMEM((QUADS, LANES), F32),
            pltpu.VMEM((8, LANES), F32),
            pltpu.VMEM((8, LANES), F32),
            *[pltpu.VMEM(table.shape, BF16) for table in tables],
            pltpu.SemaphoreType.DMA((2,)),
            pltpu.SemaphoreType.DMA((len(tables),)),
            pltpu.SemaphoreType.DMA((9 + len(pieces),)),
        ],
        compiler_params=pltpu.CompilerParams(vmem_limit_bytes=63 * MIB),
        cost_estimate=pl.CostEstimate(
            flops=20_000_000_000, bytes_accessed=20_000_000, transcendentals=0
        ),
        interpret=interpret,
        name="pair_terms",
    )(*own, own_u, kern, partner, *earlier, *tables)


def piece_kernel(first, size, own0, own1, terms, back0, back1, *rest):
    last = first + size == ROWS
    earlier = rest[: len(rest) - 12]
    out, gram_out, own_v, terms_v, back_v, out_v, gram_ref, gram_v, value_ref = rest[-12:-3]
    load_sems, gram_sems, store_sems = rest[-3:]
    rows = size // load_sems.shape[0]

    def loads(c):
        start = first + c * rows
        sources = [
            (own0, start, own_v.at[0]), (own1, start, own_v.at[1]), (terms, start, terms_v),
            (back0, start, back_v.at[0]), (back1, c * rows, back_v.at[1]),
        ]
        return [
            copy_rows(src, row, dst, c * rows, rows, load_sems.at[c, i])
            for i, (src, row, dst) in enumerate(sources)
        ]

    chunks = [loads(c) for c in range(load_sems.shape[0])]
    for chunk in chunks:
        for load in chunk:
            load.start()
    gram_loads = []
    if last:
        gram_loads = [
            pltpu.make_async_copy(src, gram_v.at[i], gram_sems.at[i])
            for i, src in enumerate(earlier[:-1])
        ]
        for load in gram_loads:
            load.start()
    gram_ref[...] = jnp.zeros_like(gram_ref)
    for c, chunk in enumerate(chunks):
        for load in chunk:
            load.wait()
        at = pl.ds(c * rows, rows)
        own = [own_v[i, at, :].astype(F32) for i in range(2)]
        for p in range(2):
            exchange = terms_v[p, at, :] + back_v[p, at, :].astype(F32)
            out_v[pl.ds(2 * c * rows + p, rows, stride=2), :] = exchange
            for i in range(2):
                product = (own[i] * exchange).reshape(-1, 8, LANES)
                gram_ref[i, p] += jnp.sum(product, axis=0)
        copy_rows(out_v, 2 * c * rows, out, 2 * (first + c * rows), 2 * rows, store_sems.at[0]).start()

    result = gram_ref
    if last:
        for load in gram_loads:
            load.wait()
        row = lax.broadcasted_iota(jnp.int32, (2, 2), 0)
        column = lax.broadcasted_iota(jnp.int32, (2, 2), 1)
        value = jnp.zeros((2, 2), F32)
        for i in range(2):
            for j in range(2):
                entry = gram_ref[i, j]
                for k in range(len(gram_loads)):
                    entry = entry + gram_v[k, i, j]
                value = jnp.where((row == i) & (column == j), jnp.sum(entry) * F32(1.0 / NGRID), value)
        value_ref[...] = value
        result = value_ref
    report = pltpu.make_async_copy(result, gram_out, store_sems.at[1])
    report.start()
    copy_rows(out_v, 0, out, 2 * first, 2 * size, store_sems.at[0]).wait()
    report.wait()


def add_piece(first, size, own, terms, back0, back1, grams, out, interpret=False):
    hbm = pl.BlockSpec(memory_space=pl.ANY)
    last = first + size == ROWS
    earlier = [] if out is None else [*(grams if last else []), out]
    gram_shape = (2, 2, 8, LANES)
    return pl.pallas_call(
        functools.partial(piece_kernel, first, size),
        out_shape=(
            jax.ShapeDtypeStruct((2 * ROWS, LANES), F32),
            jax.ShapeDtypeStruct((2, 2) if last else gram_shape, F32),
        ),
        in_specs=[hbm] * (5 + len(earlier)),
        out_specs=(hbm, hbm),
        scratch_shapes=[
            pltpu.VMEM((2, size, LANES), BF16),
            pltpu.VMEM((2, size, LANES), F32),
            pltpu.VMEM((2, size, LANES), BF16),
            pltpu.VMEM((2 * size, LANES), F32),
            pltpu.VMEM(gram_shape, F32),
            pltpu.VMEM((len(PIECES), *gram_shape), F32),
            pltpu.VMEM((2, 2), F32),
            pltpu.SemaphoreType.DMA((2 * size // STEP_ROWS, 5)),
            pltpu.SemaphoreType.DMA((len(PIECES),)),
            pltpu.SemaphoreType.DMA((2,)),
        ],
        input_output_aliases={4 + len(earlier): 0} if earlier else {},
        compiler_params=pltpu.CompilerParams(vmem_limit_bytes=44 * MIB),
        cost_estimate=cost(24 * size * LANES),
        interpret=interpret,
        name="add_piece",
    )(*own, terms, back0, back1, *earlier)


def from_behind(block, axis, distance):
    size = lax.axis_size(axis)
    return lax.ppermute(block, axis, [((i - distance) % size, i) for i in range(size)])


def after(values, other):
    return lax.optimization_barrier((values, other))[0]


def per_device(orbitals):
    tables = section_tables()
    kern = screening()
    size = lax.axis_size("band")
    share = -2.0 / (NGRID * 2 * size * orbitals.shape[0])
    raw = orbitals.reshape(2, ROWS, LANES).transpose(1, 0, 2).reshape(2 * ROWS, LANES)
    own = [take_band(raw, 0)]
    own.append(take_band(raw, 1, own))
    previous = [from_behind(part, "band", 1) for part in own]
    own_u = padded_rows(own, tables[-1])
    terms, back0, energy = pair_terms(
        own, own_u, previous[0], (), tables, kern, (STEPS,), share
    )
    back0 = from_behind(back0, "band", -1)
    terms, *sent, energy = pair_terms(
        own, own_u, previous[1], (terms, energy), tables, kern, PIECES, share
    )
    back1 = [from_behind(piece, "band", -1) for piece in sent]

    energies = lax.all_gather(energy, "band")

    exchange, grams = None, []
    first = 0
    for steps, piece in zip(PIECES, back1):
        count = steps * STEP_ROWS
        exchange, gram = add_piece(first, count, own, terms, back0, piece, grams, exchange)
        grams.append(gram)
        first += count
    energy = jnp.sum(after(energies, gram)[:, 0, 0])
    exchange = exchange.reshape(ROWS, 2, LANES).transpose(1, 0, 2).reshape(2, NGRID)
    return exchange, gram, energy


def solution(mesh):
    return jax.shard_map(
        per_device,
        mesh=mesh,
        in_specs=(P("band", None),),
        out_specs=(P("band", None), P("band", None), P()),
        check_vma=False,
    )
```

```python
import functools

import jax
import jax.numpy as jnp
import ml_dtypes
import numpy as np
from jax import lax
from jax.experimental import pallas as pl
from jax.experimental.pallas import tpu as pltpu
from jax.sharding import PartitionSpec as P

G = 96
HALF = G // 2 + 1
NGRID = G * G * G
LANES = 128
ROWS = NGRID // LANES
PLANE = G * G // LANES
QUADS = G // 4
KPAD = HALF + 1
Y_ROWS = 104
Y_PITCH = Y_ROWS + 1
Z_PITCH = G + 1
W_PITCH = 2 * G + 1
Z_ROWS = KPAD * Z_PITCH
F_PITCH = PLANE + 1
PLANES = 16
STEP_ROWS = PLANES * PLANE
STEPS = G // PLANES
PIECES = (4, 2)
WAVE_UNIT = 0.05
SCREEN_SQ = 0.0121
MIB = 1024 * 1024
BF16 = jnp.bfloat16
F32 = jnp.float32


def dft_tables():
    n = np.arange(G)
    phases = (n[:, None] * n[None, :]) % G
    angles = phases.astype(np.float32) * np.float32(2.0 * np.pi / G)
    rounded = [f(angles).astype(ml_dtypes.bfloat16).astype(np.float32) for f in (np.cos, np.sin)]
    return rounded[0], rounded[1]


def section_tables():
    c, s = dft_tables()
    h = HALF
    t1 = np.zeros((Y_ROWS, G), np.float32)
    t1[:h] = c[:h]
    t1[h : 2 * h] = -s[:h]
    t2 = np.block([[c, s], [-s, c]])
    t3 = np.zeros((2, LANES, 4, 64), np.float32)
    back = (G - np.arange(h)) % G
    t3[0, :G, 0, :h] = c[:h].T
    t3[1, :G, 0, :h] = s[:h].T
    t3[0, :G, 1, :h] = -s[:h].T
    t3[1, :G, 1, :h] = c[:h].T
    t3[0, :G, 2, :h] = c[back].T
    t3[1, :G, 2, :h] = s[back].T
    t3[0, :G, 3, :h] = s[back].T
    t3[1, :G, 3, :h] = -c[back].T
    t3 = t3.reshape(2 * LANES, 4 * 64)
    order = np.concatenate([np.arange(G // 2), G - 1 - np.arange(G // 2)])
    a1 = np.block([[c[:, order], -s[:, order]], [s[:, order], c[:, order]]])
    rows = np.arange(G).reshape(QUADS, 4).T.reshape(-1)
    a2 = np.block([[c[rows], -s[rows]], [s[rows], c[rows]]])
    weight = np.full((h, 1), 2.0, np.float32)
    weight[0] = weight[h - 1] = 1.0
    a3 = np.zeros((3, 2, 2, 2, 64, 2, LANES), np.float32)
    for third in range(3):
        for lane in range(LANES):
            r, x3 = divmod(third * LANES + lane, G)
            for p in range(2):
                a3[third, r - third, 0, p, :h, p, lane] = weight[:, 0] * c[x3, :h]
                a3[third, r - third, 1, p, :h, p, lane] = -weight[:, 0] * s[x3, :h]
    a3 = a3.reshape(3, 4 * LANES, 2 * LANES)
    sel = np.zeros((2, 2 * LANES, 2 * LANES), np.float32)
    for r in range(4):
        for x in range(G):
            sel[r // 2, r * G + x - (r // 2) * LANES, (r % 2) * LANES + x] = 1.0
    return [t.astype(ml_dtypes.bfloat16) for t in (t1, t2, t3, a1, a2, a3, sel)]


def screening():
    n = np.arange(G)
    m = np.where(n <= G // 2, n, n - G).astype(np.float64)
    sq = m * m
    q2 = WAVE_UNIT * (sq[:HALF, None, None] + sq[None, :, None] + sq[None, None, :HALF])
    safe = np.where(q2 > 0, q2, 1.0)
    kern = 4.0 * np.pi * (1.0 - np.exp(-q2 / (4.0 * SCREEN_SQ))) / safe
    kern = np.where(q2 > 0, kern, np.pi / SCREEN_SQ)
    out = np.zeros((KPAD, G, 2, 64), np.float32)
    out[:HALF, :, :, :HALF] = kern[:, :, None, :]
    return out.reshape(KPAD * G, LANES)


def cost(size):
    return pl.CostEstimate(flops=0, bytes_accessed=size, transcendentals=0)


def dot(a, b):
    return jnp.dot(a, b, preferred_element_type=F32)


def lanes(*parts):
    return jnp.concatenate(parts, axis=1)


def stack(*parts):
    return jnp.concatenate(parts, axis=0)


def split_rows(src, sel_ref, out, first, count):
    rows = [
        [src[pl.ds(3 * (first + i) + s, G, stride=F_PITCH), :].astype(BF16) for s in range(3)]
        for i in range(count)
    ]
    for half in range(2):
        part = dot(stack(*[lanes(r[half], r[half + 1]) for r in rows]), sel_ref[half])
        for i in range(count):
            for e in range(2):
                value = part[i * G : (i + 1) * G, e * LANES : (e + 1) * LANES]
                out[4 * (first + i) + 2 * half + e] = value.astype(BF16)


def widen_planes(src, dst, first):
    @pl.loop(0, src.shape[0] // (2 * PLANE), unroll=4)
    def _(i):
        value = src[pl.ds(pl.multiple_of(i * 2 * PLANE, 16), 2 * PLANE), :].astype(F32)
        dst[pl.ds((first + 2 * i) * F_PITCH, PLANE), :] = value[:PLANE]
        dst[pl.ds((first + 2 * i + 1) * F_PITCH, PLANE), :] = value[PLANE:]


def rows_of(ref, first, count):
    at = pl.ds(first, count)
    return ref.at[at, :] if len(ref.shape) == 2 else ref.at[:, at, :]


def copy_rows(src, src_row, dst, dst_row, count, sem):
    return pltpu.make_async_copy(rows_of(src, src_row, count), rows_of(dst, dst_row, count), sem)


def band_kernel(p, raw, *refs):
    out, raw_v, out_v, load_sems, store_sem = refs[-5:]
    chunks = load_sems.shape[0]
    rows = out.shape[0] // chunks
    loads = [
        copy_rows(raw, 2 * c * rows, raw_v, 2 * c * rows, 2 * rows, load_sems.at[c])
        for c in range(chunks)
    ]
    for load in loads:
        load.start()
    shape = (LANES, 2 * LANES)
    row = lax.broadcasted_iota(jnp.int32, shape, 0)
    column = lax.broadcasted_iota(jnp.int32, shape, 1)
    pick = jnp.where(column == 2 * row + p, F32(1.0), F32(0.0)).astype(BF16)
    for c, load in enumerate(loads):
        load.wait()
        for row in range(c * rows, (c + 1) * rows, LANES):
            value = dot(pick, raw_v[2 * row : 2 * row + 2 * LANES, :])
            out_v[row : row + LANES, :] = value.astype(BF16)
        copy_rows(out_v, c * rows, out, c * rows, rows, store_sem).start()
    pltpu.make_async_copy(out_v, out, store_sem).wait()


def take_band(raw, p, earlier=(), interpret=False):
    hbm = pl.BlockSpec(memory_space=pl.ANY)
    return pl.pallas_call(
        functools.partial(band_kernel, p),
        out_shape=jax.ShapeDtypeStruct((ROWS, LANES), BF16),
        in_specs=[hbm] * (1 + len(earlier)),
        out_specs=hbm,
        scratch_shapes=[
            pltpu.VMEM((2 * ROWS, LANES), BF16),
            pltpu.VMEM((ROWS, LANES), BF16),
            pltpu.SemaphoreType.DMA((9,)),
            pltpu.SemaphoreType.DMA,
        ],
        compiler_params=pltpu.CompilerParams(vmem_limit_bytes=63 * MIB),
        cost_estimate=cost(6 * ROWS * LANES),
        interpret=interpret,
        name="take_band",
    )(raw, *earlier)


def rows_kernel(own0, own1, sel, out, wide):
    for p, own in enumerate((own0, own1)):
        widen_planes(own, wide, 0)

        @pl.loop(0, QUADS // 4, unroll=2)
        def _(q):
            split_rows(wide, sel, out.at[p], 4 * q, 4)


def padded_rows(own, sel, interpret=False):
    vmem = pl.BlockSpec(memory_space=pltpu.VMEM)
    return pl.pallas_call(
        rows_kernel,
        out_shape=jax.ShapeDtypeStruct((2, G, G, LANES), BF16),
        in_specs=[vmem] * 3,
        out_specs=vmem,
        scratch_shapes=[pltpu.VMEM((G * F_PITCH, LANES), F32)],
        compiler_params=pltpu.CompilerParams(vmem_limit_bytes=63 * MIB),
        cost_estimate=cost(16 * NGRID),
        interpret=interpret,
        name="padded_rows",
    )(*own, sel)


def pairs_kernel(pieces, share, own0, own1, own_u, kern, par, *refs):
    earlier = []
    if len(pieces) > 1:
        earlier, refs = refs[:2], refs[2:]
    table_refs, own_out = refs[:7], refs[7]
    par_out, energy_out = refs[8 : 8 + len(pieces)], refs[8 + len(pieces)]
    own_v, own_uv, kern_v, own_ov, par_ov, par_f, par_u, yw, z, x34 = refs[9 + len(pieces) : -15]
    own_f, staged, total_ref, energy_v, before_v = refs[-15:-10]
    tables, (par_sems, table_sems, sems) = refs[-10:-3], refs[-3:]
    t1, t2, t3, a1, a2, a3, sel = tables
    par_v = par_ov
    par_loads = []
    for first in (0, ROWS // 2):
        sem = par_sems.at[len(par_loads)]
        par_loads.append(copy_rows(par, first, par_v, first, ROWS // 2, sem))
    for load in par_loads:
        load.start()
    table_loads = [
        pltpu.make_async_copy(src, dst, table_sems.at[i])
        for i, (src, dst) in enumerate(zip(table_refs, tables))
    ]
    table_loads[6].start()
    table_loads[0].start()
    loads = [
        pltpu.make_async_copy(own_u, own_uv, sems.at[0]),
        pltpu.make_async_copy(kern, kern_v, sems.at[1]),
        copy_rows(own0, 0, own_v.at[0], 0, ROWS, sems.at[2]),
        copy_rows(own1, 0, own_v.at[1], 0, ROWS, sems.at[3]),
    ]
    later = []
    if earlier:
        later = [copy_rows(earlier[0].at[p], 0, z, p * ROWS, ROWS, sems.at[4 + p]) for p in range(2)]
        loads.append(pltpu.make_async_copy(earlier[1], before_v, sems.at[8 + len(pieces)]))

    for i, load in enumerate(par_loads):
        load.wait()
        for other in ([loads[0]], table_loads[1:5])[i]:
            other.start()
        widen_planes(par_v.at[pl.ds(i * ROWS // 2, ROWS // 2), :], par_f, i * G // 2)
    table_loads[6].wait()

    @pl.loop(0, QUADS // 4, unroll=2)
    def _(q):
        split_rows(par_f, sel, par_u, 4 * q, 4)

    half_y = G * Y_PITCH
    loads[0].wait()
    for load in loads[1:]:
        load.start()
    table_loads[5].start()
    table_loads[0].wait()

    @pl.loop(0, G // 2, unroll=8)
    def _(i):
        density = []
        for e in range(2):
            partner = par_u[2 * i + e].astype(F32)
            for p in range(2):
                density.append((own_uv[p, 2 * i + e].astype(F32) * partner).astype(BF16))
        out = dot(t1[...], lanes(*density))
        for e in range(2):
            for p in range(2):
                at = pl.ds(p * half_y + (2 * i + e) * Y_PITCH, Y_ROWS)
                yw[at, :] = out[:, (2 * e + p) * LANES : (2 * e + p + 1) * LANES]

    table_loads[1].wait()

    @pl.loop(0, HALF, unroll=7)
    def _(k1):
        def line(p, part):
            return yw[pl.ds(p * half_y + part * HALF + k1, G, stride=Y_PITCH), :].astype(BF16)

        out = dot(t2[...], stack(lanes(line(0, 0), line(1, 0)), lanes(line(0, 1), line(1, 1))))
        at = pl.ds(pl.multiple_of(k1 * G, 16), G)
        for p in range(2):
            for part in range(2):
                left = (2 * p + part) * LANES
                value = out[part * G : (part + 1) * G, p * LANES : (p + 1) * LANES]
                x34[at, left : left + LANES] = value.astype(BF16)

    loads[1].wait()
    table_loads[2].wait()

    many = 5

    @pl.loop(0, KPAD // many, unroll=2)
    def _(m):
        at = pl.ds(pl.multiple_of(m * many * G, 16), many * G)
        factor = kern_v[at, :]
        out = [
            dot(x34[at, 2 * p * LANES : 2 * (p + 1) * LANES], t3[...]).astype(BF16)
            for p in range(2)
        ]
        for part in range(4):
            spectrum = lanes(*[o[:, part * 64 : (part + 1) * 64] for o in out]).astype(F32)
            value = spectrum * factor
            for i in range(many):
                row = part * Z_ROWS + (many * m + i) * Z_PITCH
                z[pl.ds(row, G), :] = value[i * G : (i + 1) * G]

    table_loads[3].wait()

    @pl.loop(0, G // 4, unroll=6)
    def _(four):
        parts = []
        for e in range(4):
            k2 = 4 * four + e
            mirror = Z_PITCH + jnp.where(k2 == 0, 0, G - k2)
            parts.append(
                stack(
                    z[pl.ds(k2, G // 2, stride=Z_PITCH), :].astype(BF16),
                    z[pl.ds(2 * Z_ROWS + mirror, G // 2, stride=Z_PITCH), :].astype(BF16),
                    z[pl.ds(1 * Z_ROWS + k2, G // 2, stride=Z_PITCH), :].astype(BF16),
                    z[pl.ds(3 * Z_ROWS + mirror, G // 2, stride=Z_PITCH), :].astype(BF16),
                )
            )
        out = dot(a1[...], lanes(*parts))
        for e in range(4):
            at = (4 * four + e) * W_PITCH
            yw[pl.ds(at, 2 * G), :] = out[:, e * LANES : (e + 1) * LANES]

    for load in later:
        load.start()
    table_loads[4].wait()

    @pl.loop(0, G // 4, unroll=6)
    def _(four):
        parts = []
        for e in range(4):
            x1 = 4 * four + e
            parts.append(
                stack(
                    yw[pl.ds(x1, G, stride=W_PITCH), :].astype(BF16),
                    yw[pl.ds(G + x1, G, stride=W_PITCH), :].astype(BF16),
                )
            )
        out = dot(a2[...], lanes(*parts))
        for r in range(4):
            block = [
                lanes(
                    out[r * QUADS : (r + 1) * QUADS, e * LANES : (e + 1) * LANES],
                    out[G + r * QUADS : G + (r + 1) * QUADS, e * LANES : (e + 1) * LANES],
                )
                for e in range(4)
            ]
            at = pl.multiple_of((r // 2) * G * QUADS + four * 4 * QUADS, 16)
            left = (r % 2) * 2 * LANES
            x34[pl.ds(at, 4 * QUADS), left : left + 2 * LANES] = stack(*block).astype(BF16)

    table_loads[5].wait()
    for load in loads[2:] + later:
        load.wait()
    total_ref[...] = jnp.zeros_like(total_ref)
    block_rows = PLANES * QUADS
    scale = F32(1.0 / NGRID)

    def result(ch):
        at = pl.multiple_of(ch * block_rows, 16)
        low = x34[pl.ds(at, block_rows), :]
        high = x34[pl.ds(G * QUADS + at, block_rows), :]
        fields = [low, lanes(low[:, 2 * LANES :], high[:, : 2 * LANES]), high]
        flat = pl.ds(pl.multiple_of(ch * STEP_ROWS, 16), STEP_ROWS)
        own_f[...] = own_v[:, flat, :].astype(F32)
        total = jnp.zeros((QUADS, LANES), F32)
        for third in range(3):
            out = dot(fields[third], a3[third]) * scale
            for i in range(PLANES):
                plane = ch * PLANES + i
                partner = par_f[pl.ds(plane * F_PITCH + third, QUADS, stride=3), :]
                here = pl.ds(i * PLANE + third, QUADS, stride=3)
                there = pl.ds(plane * PLANE + third, QUADS, stride=3)
                sent = jnp.zeros((QUADS, LANES), F32)
                for p in range(2):
                    potential = out[i * QUADS : (i + 1) * QUADS, p * LANES : (p + 1) * LANES]
                    term = potential * partner
                    if earlier:
                        at = p * ROWS + plane * PLANE + third
                        term = term + z[pl.ds(at, QUADS, stride=3), :]
                    own_ov[p, there, :] = term
                    sent = sent + potential * own_f[p, here, :]
                total = total + sent * partner
                staged[here, :] = sent
        total_ref[...] += total
        par_ov[flat, :] = staged[...].astype(BF16)
        row = ch * STEP_ROWS
        copy_rows(own_ov, row, own_out, row, STEP_ROWS, sems.at[6]).start()

    first = 0
    for i, steps in enumerate(pieces):

        @pl.loop(0, steps, unroll=2 if steps % 2 == 0 else steps)
        def _(step):
            ch = first + step
            result(ch)
            source, row = ch * STEP_ROWS, step * STEP_ROWS
            copy_rows(par_ov, source, par_out[i], row, STEP_ROWS, sems.at[7 + i]).start()

        first += steps

    energy = jnp.zeros((8, LANES), F32) + jnp.sum(total_ref[...]) * F32(share)
    if earlier:
        energy = energy + before_v[...]
    energy_v[...] = energy
    report = pltpu.make_async_copy(energy_v, energy_out, sems.at[7 + len(pieces)])
    report.start()
    pltpu.make_async_copy(own_ov, own_out, sems.at[6]).wait()
    first = 0
    for i, steps in enumerate(pieces):
        rows = steps * STEP_ROWS
        copy_rows(par_ov, first, par_out[i], 0, rows, sems.at[7 + i]).wait()
        first += rows
    report.wait()


def pair_terms(own, own_u, partner, earlier, tables, kern, pieces, share, interpret=False):
    hbm = pl.BlockSpec(memory_space=pl.ANY)
    return pl.pallas_call(
        functools.partial(pairs_kernel, pieces, share),
        out_shape=(
            jax.ShapeDtypeStruct((2, ROWS, LANES), F32),
            *[jax.ShapeDtypeStruct((steps * STEP_ROWS, LANES), BF16) for steps in pieces],
            jax.ShapeDtypeStruct((8, LANES), F32),
        ),
        in_specs=[hbm] * (5 + len(earlier) + len(tables)),
        out_specs=(hbm,) * (2 + len(pieces)),
        scratch_shapes=[
            pltpu.VMEM((2, ROWS, LANES), BF16),
            pltpu.VMEM((2, G, G, LANES), BF16),
            pltpu.VMEM((KPAD * G, LANES), F32),
            pltpu.VMEM((2, ROWS, LANES), F32),
            pltpu.VMEM((ROWS, LANES), BF16),
            pltpu.VMEM((G * F_PITCH, LANES), F32),
            pltpu.VMEM((G, G, LANES), BF16),
            pltpu.VMEM((2 * G * Y_PITCH, LANES), F32),
            pltpu.VMEM((4 * Z_ROWS, LANES), F32),
            pltpu.VMEM((KPAD * G, 4 * LANES), BF16),
            pltpu.VMEM((2, STEP_ROWS, LANES), F32),
            pltpu.VMEM((STEP_ROWS, LANES), F32),
            pltpu.VMEM((QUADS, LANES), F32),
            pltpu.VMEM((8, LANES), F32),
            pltpu.VMEM((8, LANES), F32),
            *[pltpu.VMEM(table.shape, BF16) for table in tables],
            pltpu.SemaphoreType.DMA((2,)),
            pltpu.SemaphoreType.DMA((len(tables),)),
            pltpu.SemaphoreType.DMA((9 + len(pieces),)),
        ],
        compiler_params=pltpu.CompilerParams(vmem_limit_bytes=63 * MIB),
        cost_estimate=pl.CostEstimate(
            flops=20_000_000_000, bytes_accessed=20_000_000, transcendentals=0
        ),
        interpret=interpret,
        name="pair_terms",
    )(*own, own_u, kern, partner, *earlier, *tables)


def piece_kernel(first, size, own0, own1, terms, back0, back1, *rest):
    last = first + size == ROWS
    earlier = rest[: len(rest) - 12]
    out, gram_out, own_v, terms_v, back_v, out_v, gram_ref, gram_v, value_ref = rest[-12:-3]
    load_sems, gram_sems, store_sems = rest[-3:]
    rows = size // load_sems.shape[0]

    def loads(c):
        start = first + c * rows
        sources = [
            (own0, start, own_v.at[0]), (own1, start, own_v.at[1]), (terms, start, terms_v),
            (back0, start, back_v.at[0]), (back1, c * rows, back_v.at[1]),
        ]
        return [
            copy_rows(src, row, dst, c * rows, rows, load_sems.at[c, i])
            for i, (src, row, dst) in enumerate(sources)
        ]

    chunks = [loads(c) for c in range(load_sems.shape[0])]
    for chunk in chunks:
        for load in chunk:
            load.start()
    gram_loads = []
    if last:
        gram_loads = [
            pltpu.make_async_copy(src, gram_v.at[i], gram_sems.at[i])
            for i, src in enumerate(earlier[:-1])
        ]
        for load in gram_loads:
            load.start()
    gram_ref[...] = jnp.zeros_like(gram_ref)
    for c, chunk in enumerate(chunks):
        for load in chunk:
            load.wait()
        at = pl.ds(c * rows, rows)
        own = [own_v[i, at, :].astype(F32) for i in range(2)]
        for p in range(2):
            exchange = terms_v[p, at, :] + back_v[p, at, :].astype(F32)
            out_v[pl.ds(2 * c * rows + p, rows, stride=2), :] = exchange
            for i in range(2):
                product = (own[i] * exchange).reshape(-1, 8, LANES)
                gram_ref[i, p] += jnp.sum(product, axis=0)
        copy_rows(out_v, 2 * c * rows, out, 2 * (first + c * rows), 2 * rows, store_sems.at[0]).start()

    result = gram_ref
    if last:
        for load in gram_loads:
            load.wait()
        row = lax.broadcasted_iota(jnp.int32, (2, 2), 0)
        column = lax.broadcasted_iota(jnp.int32, (2, 2), 1)
        value = jnp.zeros((2, 2), F32)
        for i in range(2):
            for j in range(2):
                entry = gram_ref[i, j]
                for k in range(len(gram_loads)):
                    entry = entry + gram_v[k, i, j]
                value = jnp.where((row == i) & (column == j), jnp.sum(entry) * F32(1.0 / NGRID), value)
        value_ref[...] = value
        result = value_ref
    report = pltpu.make_async_copy(result, gram_out, store_sems.at[1])
    report.start()
    copy_rows(out_v, 0, out, 2 * first, 2 * size, store_sems.at[0]).wait()
    report.wait()


def add_piece(first, size, own, terms, back0, back1, grams, out, interpret=False):
    hbm = pl.BlockSpec(memory_space=pl.ANY)
    last = first + size == ROWS
    earlier = [] if out is None else [*(grams if last else []), out]
    gram_shape = (2, 2, 8, LANES)
    return pl.pallas_call(
        functools.partial(piece_kernel, first, size),
        out_shape=(
            jax.ShapeDtypeStruct((2 * ROWS, LANES), F32),
            jax.ShapeDtypeStruct((2, 2) if last else gram_shape, F32),
        ),
        in_specs=[hbm] * (5 + len(earlier)),
        out_specs=(hbm, hbm),
        scratch_shapes=[
            pltpu.VMEM((2, size, LANES), BF16),
            pltpu.VMEM((2, size, LANES), F32),
            pltpu.VMEM((2, size, LANES), BF16),
            pltpu.VMEM((2 * size, LANES), F32),
            pltpu.VMEM(gram_shape, F32),
            pltpu.VMEM((len(PIECES), *gram_shape), F32),
            pltpu.VMEM((2, 2), F32),
            pltpu.SemaphoreType.DMA((2 * size // STEP_ROWS, 5)),
            pltpu.SemaphoreType.DMA((len(PIECES),)),
            pltpu.SemaphoreType.DMA((2,)),
        ],
        input_output_aliases={4 + len(earlier): 0} if earlier else {},
        compiler_params=pltpu.CompilerParams(vmem_limit_bytes=52 * MIB),
        cost_estimate=cost(24 * size * LANES),
        interpret=interpret,
        name="add_piece",
    )(*own, terms, back0, back1, *earlier)


def from_behind(block, axis, distance):
    size = lax.axis_size(axis)
    return lax.ppermute(block, axis, [((i - distance) % size, i) for i in range(size)])


def send_to(value, axis, flip):
    size = lax.axis_size(axis)
    return lax.ppermute(value, axis, [(i ^ flip, i) for i in range(size)])


def after(values, other):
    return lax.optimization_barrier((values, other))[0]


def per_device(orbitals):
    tables = section_tables()
    kern = screening()
    size = lax.axis_size("band")
    share = -2.0 / (NGRID * 2 * size * orbitals.shape[0])
    raw = orbitals.reshape(2, ROWS, LANES).transpose(1, 0, 2).reshape(2 * ROWS, LANES)
    own = [take_band(raw, 0)]
    own.append(take_band(raw, 1, own))
    previous = [from_behind(part, "band", 1) for part in own]
    own_u = padded_rows(own, tables[-1])
    terms, back0, energy = pair_terms(
        own, own_u, previous[0], (), tables, kern, (STEPS,), share
    )
    back0 = from_behind(back0, "band", -1)
    terms, *sent, energy = pair_terms(
        own, own_u, previous[1], (terms, energy), tables, kern, PIECES, share
    )
    back1 = [from_behind(piece, "band", -1) for piece in sent]

    steps = []
    if size & (size - 1):
        energy = lax.psum(energy, "band")
    else:
        steps = [1 << b for b in range(size.bit_length() - 1)]
        steps = [b for b in steps if b != 2] + [b for b in steps if b == 2]
    while len(steps) > len(back1):
        energy = energy + send_to(energy, "band", steps.pop(0))
    exchange, grams, got = None, [], None
    first = 0
    for count, piece in zip(PIECES, back1):
        count *= STEP_ROWS
        if steps:
            got = send_to(energy, "band", steps.pop(0))
        exchange, gram = add_piece(first, count, own, terms, back0, piece, grams, exchange)
        if got is not None:
            energy = energy + after(got, gram)
            got = None
        grams.append(gram)
        first += count
    exchange = exchange.reshape(ROWS, 2, LANES).transpose(1, 0, 2).reshape(2, NGRID)
    return exchange, gram, energy[0, 0]


def solution(mesh):
    return jax.shard_map(
        per_device,
        mesh=mesh,
        in_specs=(P("band", None),),
        out_specs=(P("band", None), P("band", None), P()),
        check_vma=False,
    )
```

```python
import functools

import jax
import jax.numpy as jnp
import ml_dtypes
import numpy as np
from jax import lax
from jax.experimental import pallas as pl
from jax.experimental.pallas import tpu as pltpu
from jax.sharding import PartitionSpec as P

G = 96
HALF = G // 2 + 1
NGRID = G * G * G
LANES = 128
ROWS = NGRID // LANES
PLANE = G * G // LANES
QUADS = G // 4
KPAD = HALF + 1
Y_ROWS = 104
Y_PITCH = Y_ROWS + 1
Z_PITCH = G + 1
W_PITCH = 2 * G + 1
Z_ROWS = KPAD * Z_PITCH
F_PITCH = PLANE + 1
PLANES = 16
STEP_ROWS = PLANES * PLANE
STEPS = G // PLANES
PIECES = (4, 2)
WAVE_UNIT = 0.05
SCREEN_SQ = 0.0121
MIB = 1024 * 1024
BF16 = jnp.bfloat16
F32 = jnp.float32


def dft_tables():
    n = np.arange(G)
    phases = (n[:, None] * n[None, :]) % G
    angles = phases.astype(np.float32) * np.float32(2.0 * np.pi / G)
    rounded = [f(angles).astype(ml_dtypes.bfloat16).astype(np.float32) for f in (np.cos, np.sin)]
    return rounded[0], rounded[1]


def section_tables():
    c, s = dft_tables()
    h = HALF
    t1 = np.zeros((Y_ROWS, G), np.float32)
    t1[:h] = c[:h]
    t1[h : 2 * h] = -s[:h]
    t2 = np.block([[c, s], [-s, c]])
    t3 = np.zeros((2, LANES, 4, 64), np.float32)
    back = (G - np.arange(h)) % G
    t3[0, :G, 0, :h] = c[:h].T
    t3[1, :G, 0, :h] = s[:h].T
    t3[0, :G, 1, :h] = -s[:h].T
    t3[1, :G, 1, :h] = c[:h].T
    t3[0, :G, 2, :h] = c[back].T
    t3[1, :G, 2, :h] = s[back].T
    t3[0, :G, 3, :h] = s[back].T
    t3[1, :G, 3, :h] = -c[back].T
    t3 = t3.reshape(2 * LANES, 4 * 64)
    order = np.concatenate([np.arange(G // 2), G - 1 - np.arange(G // 2)])
    a1 = np.block([[c[:, order], -s[:, order]], [s[:, order], c[:, order]]])
    rows = np.arange(G).reshape(QUADS, 4).T.reshape(-1)
    a2 = np.block([[c[rows], -s[rows]], [s[rows], c[rows]]])
    weight = np.full((h, 1), 2.0, np.float32)
    weight[0] = weight[h - 1] = 1.0
    a3 = np.zeros((3, 2, 2, 2, 64, 2, LANES), np.float32)
    for third in range(3):
        for lane in range(LANES):
            r, x3 = divmod(third * LANES + lane, G)
            for p in range(2):
                a3[third, r - third, 0, p, :h, p, lane] = weight[:, 0] * c[x3, :h]
                a3[third, r - third, 1, p, :h, p, lane] = -weight[:, 0] * s[x3, :h]
    a3 = a3.reshape(3, 4 * LANES, 2 * LANES)
    sel = np.zeros((2, 2 * LANES, 2 * LANES), np.float32)
    for r in range(4):
        for x in range(G):
            sel[r // 2, r * G + x - (r // 2) * LANES, (r % 2) * LANES + x] = 1.0
    return [t.astype(ml_dtypes.bfloat16) for t in (t1, t2, t3, a1, a2, a3, sel)]


def screening():
    n = np.arange(G)
    m = np.where(n <= G // 2, n, n - G).astype(np.float64)
    sq = m * m
    q2 = WAVE_UNIT * (sq[:HALF, None, None] + sq[None, :, None] + sq[None, None, :HALF])
    safe = np.where(q2 > 0, q2, 1.0)
    kern = 4.0 * np.pi * (1.0 - np.exp(-q2 / (4.0 * SCREEN_SQ))) / safe
    kern = np.where(q2 > 0, kern, np.pi / SCREEN_SQ)
    out = np.zeros((KPAD, G, 2, 64), np.float32)
    out[:HALF, :, :, :HALF] = kern[:, :, None, :]
    return out.reshape(KPAD * G, LANES)


def cost(size):
    return pl.CostEstimate(flops=0, bytes_accessed=size, transcendentals=0)


def dot(a, b):
    return jnp.dot(a, b, preferred_element_type=F32)


def lanes(*parts):
    return jnp.concatenate(parts, axis=1)


def stack(*parts):
    return jnp.concatenate(parts, axis=0)


def split_rows(src, sel_ref, out, first, count):
    rows = [
        [src[pl.ds(3 * (first + i) + s, G, stride=F_PITCH), :].astype(BF16) for s in range(3)]
        for i in range(count)
    ]
    for half in range(2):
        part = dot(stack(*[lanes(r[half], r[half + 1]) for r in rows]), sel_ref[half])
        for i in range(count):
            for e in range(2):
                value = part[i * G : (i + 1) * G, e * LANES : (e + 1) * LANES]
                out[4 * (first + i) + 2 * half + e] = value.astype(BF16)


def widen_planes(src, dst, first):
    @pl.loop(0, src.shape[0] // (2 * PLANE), unroll=4)
    def _(i):
        value = src[pl.ds(pl.multiple_of(i * 2 * PLANE, 16), 2 * PLANE), :].astype(F32)
        dst[pl.ds((first + 2 * i) * F_PITCH, PLANE), :] = value[:PLANE]
        dst[pl.ds((first + 2 * i + 1) * F_PITCH, PLANE), :] = value[PLANE:]


def rows_of(ref, first, count):
    at = pl.ds(first, count)
    return ref.at[at, :] if len(ref.shape) == 2 else ref.at[:, at, :]


def copy_rows(src, src_row, dst, dst_row, count, sem):
    return pltpu.make_async_copy(rows_of(src, src_row, count), rows_of(dst, dst_row, count), sem)


def band_kernel(p, raw, *refs):
    out, raw_v, out_v, load_sems, store_sem = refs[-5:]
    chunks = load_sems.shape[0]
    rows = out.shape[0] // chunks
    loads = [
        copy_rows(raw, 2 * c * rows, raw_v, 2 * c * rows, 2 * rows, load_sems.at[c])
        for c in range(chunks)
    ]
    for load in loads:
        load.start()
    shape = (LANES, 2 * LANES)
    row = lax.broadcasted_iota(jnp.int32, shape, 0)
    column = lax.broadcasted_iota(jnp.int32, shape, 1)
    pick = jnp.where(column == 2 * row + p, F32(1.0), F32(0.0)).astype(BF16)
    for c, load in enumerate(loads):
        load.wait()
        for row in range(c * rows, (c + 1) * rows, LANES):
            value = dot(pick, raw_v[2 * row : 2 * row + 2 * LANES, :])
            out_v[row : row + LANES, :] = value.astype(BF16)
        copy_rows(out_v, c * rows, out, c * rows, rows, store_sem).start()
    pltpu.make_async_copy(out_v, out, store_sem).wait()


def take_band(raw, p, earlier=(), interpret=False):
    hbm = pl.BlockSpec(memory_space=pl.ANY)
    return pl.pallas_call(
        functools.partial(band_kernel, p),
        out_shape=jax.ShapeDtypeStruct((ROWS, LANES), BF16),
        in_specs=[hbm] * (1 + len(earlier)),
        out_specs=hbm,
        scratch_shapes=[
            pltpu.VMEM((2 * ROWS, LANES), BF16),
            pltpu.VMEM((ROWS, LANES), BF16),
            pltpu.SemaphoreType.DMA((9,)),
            pltpu.SemaphoreType.DMA,
        ],
        compiler_params=pltpu.CompilerParams(vmem_limit_bytes=63 * MIB),
        cost_estimate=cost(6 * ROWS * LANES),
        interpret=interpret,
        name="take_band",
    )(raw, *earlier)


def rows_kernel(own0, own1, sel, out, wide):
    for p, own in enumerate((own0, own1)):
        widen_planes(own, wide, 0)

        @pl.loop(0, QUADS // 4, unroll=2)
        def _(q):
            split_rows(wide, sel, out.at[p], 4 * q, 4)


def padded_rows(own, sel, interpret=False):
    vmem = pl.BlockSpec(memory_space=pltpu.VMEM)
    return pl.pallas_call(
        rows_kernel,
        out_shape=jax.ShapeDtypeStruct((2, G, G, LANES), BF16),
        in_specs=[vmem] * 3,
        out_specs=vmem,
        scratch_shapes=[pltpu.VMEM((G * F_PITCH, LANES), F32)],
        compiler_params=pltpu.CompilerParams(vmem_limit_bytes=63 * MIB),
        cost_estimate=cost(16 * NGRID),
        interpret=interpret,
        name="padded_rows",
    )(*own, sel)


def pairs_kernel(pieces, share, own0, own1, own_u, kern, par, *refs):
    earlier = []
    if len(pieces) > 1:
        earlier, refs = refs[:2], refs[2:]
    table_refs, own_out = refs[:7], refs[7]
    par_out, energy_out = refs[8 : 8 + len(pieces)], refs[8 + len(pieces)]
    own_v, own_uv, kern_v, own_ov, par_ov, par_f, par_u, yw, z, x34 = refs[9 + len(pieces) : -15]
    own_f, staged, total_ref, energy_v, before_v = refs[-15:-10]
    tables, (par_sems, table_sems, sems) = refs[-10:-3], refs[-3:]
    t1, t2, t3, a1, a2, a3, sel = tables
    par_v = par_ov
    par_loads = []
    for first in (0, ROWS // 2):
        sem = par_sems.at[len(par_loads)]
        par_loads.append(copy_rows(par, first, par_v, first, ROWS // 2, sem))
    for load in par_loads:
        load.start()
    table_loads = [
        pltpu.make_async_copy(src, dst, table_sems.at[i])
        for i, (src, dst) in enumerate(zip(table_refs, tables))
    ]
    table_loads[6].start()
    table_loads[0].start()
    loads = [
        pltpu.make_async_copy(own_u, own_uv, sems.at[0]),
        pltpu.make_async_copy(kern, kern_v, sems.at[1]),
        copy_rows(own0, 0, own_v.at[0], 0, ROWS, sems.at[2]),
        copy_rows(own1, 0, own_v.at[1], 0, ROWS, sems.at[3]),
    ]
    later = []
    if earlier:
        later = [copy_rows(earlier[0].at[p], 0, z, p * ROWS, ROWS, sems.at[4 + p]) for p in range(2)]
        loads.append(pltpu.make_async_copy(earlier[1], before_v, sems.at[8 + len(pieces)]))

    for i, load in enumerate(par_loads):
        load.wait()
        for other in ([loads[0]], table_loads[1:5])[i]:
            other.start()
        widen_planes(par_v.at[pl.ds(i * ROWS // 2, ROWS // 2), :], par_f, i * G // 2)
    table_loads[6].wait()

    @pl.loop(0, QUADS // 4, unroll=2)
    def _(q):
        split_rows(par_f, sel, par_u, 4 * q, 4)

    half_y = G * Y_PITCH
    loads[0].wait()
    for load in loads[1:]:
        load.start()
    table_loads[5].start()
    table_loads[0].wait()

    @pl.loop(0, G // 2, unroll=8)
    def _(i):
        density = []
        for e in range(2):
            partner = par_u[2 * i + e].astype(F32)
            for p in range(2):
                density.append((own_uv[p, 2 * i + e].astype(F32) * partner).astype(BF16))
        out = dot(t1[...], lanes(*density))
        for e in range(2):
            for p in range(2):
                at = pl.ds(p * half_y + (2 * i + e) * Y_PITCH, Y_ROWS)
                yw[at, :] = out[:, (2 * e + p) * LANES : (2 * e + p + 1) * LANES]

    table_loads[1].wait()

    @pl.loop(0, HALF, unroll=7)
    def _(k1):
        def line(p, part):
            return yw[pl.ds(p * half_y + part * HALF + k1, G, stride=Y_PITCH), :].astype(BF16)

        out = dot(t2[...], stack(lanes(line(0, 0), line(1, 0)), lanes(line(0, 1), line(1, 1))))
        at = pl.ds(pl.multiple_of(k1 * G, 16), G)
        for p in range(2):
            for part in range(2):
                left = (2 * p + part) * LANES
                value = out[part * G : (part + 1) * G, p * LANES : (p + 1) * LANES]
                x34[at, left : left + LANES] = value.astype(BF16)

    loads[1].wait()
    table_loads[2].wait()

    many = 5

    @pl.loop(0, KPAD // many, unroll=2)
    def _(m):
        at = pl.ds(pl.multiple_of(m * many * G, 16), many * G)
        factor = kern_v[at, :]
        out = [
            dot(x34[at, 2 * p * LANES : 2 * (p + 1) * LANES], t3[...]).astype(BF16)
            for p in range(2)
        ]
        for part in range(4):
            spectrum = lanes(*[o[:, part * 64 : (part + 1) * 64] for o in out]).astype(F32)
            value = spectrum * factor
            for i in range(many):
                row = part * Z_ROWS + (many * m + i) * Z_PITCH
                z[pl.ds(row, G), :] = value[i * G : (i + 1) * G]

    table_loads[3].wait()

    @pl.loop(0, G // 4, unroll=6)
    def _(four):
        parts = []
        for e in range(4):
            k2 = 4 * four + e
            mirror = Z_PITCH + jnp.where(k2 == 0, 0, G - k2)
            parts.append(
                stack(
                    z[pl.ds(k2, G // 2, stride=Z_PITCH), :].astype(BF16),
                    z[pl.ds(2 * Z_ROWS + mirror, G // 2, stride=Z_PITCH), :].astype(BF16),
                    z[pl.ds(1 * Z_ROWS + k2, G // 2, stride=Z_PITCH), :].astype(BF16),
                    z[pl.ds(3 * Z_ROWS + mirror, G // 2, stride=Z_PITCH), :].astype(BF16),
                )
            )
        out = dot(a1[...], lanes(*parts))
        for e in range(4):
            at = (4 * four + e) * W_PITCH
            yw[pl.ds(at, 2 * G), :] = out[:, e * LANES : (e + 1) * LANES]

    for load in later:
        load.start()
    table_loads[4].wait()

    @pl.loop(0, G // 4, unroll=6)
    def _(four):
        parts = []
        for e in range(4):
            x1 = 4 * four + e
            parts.append(
                stack(
                    yw[pl.ds(x1, G, stride=W_PITCH), :].astype(BF16),
                    yw[pl.ds(G + x1, G, stride=W_PITCH), :].astype(BF16),
                )
            )
        out = dot(a2[...], lanes(*parts))
        for r in range(4):
            block = [
                lanes(
                    out[r * QUADS : (r + 1) * QUADS, e * LANES : (e + 1) * LANES],
                    out[G + r * QUADS : G + (r + 1) * QUADS, e * LANES : (e + 1) * LANES],
                )
                for e in range(4)
            ]
            at = pl.multiple_of((r // 2) * G * QUADS + four * 4 * QUADS, 16)
            left = (r % 2) * 2 * LANES
            x34[pl.ds(at, 4 * QUADS), left : left + 2 * LANES] = stack(*block).astype(BF16)

    table_loads[5].wait()
    for load in loads[2:] + later:
        load.wait()
    total_ref[...] = jnp.zeros_like(total_ref)
    block_rows = PLANES * QUADS
    scale = F32(1.0 / NGRID)

    def result(ch):
        at = pl.multiple_of(ch * block_rows, 16)
        low = x34[pl.ds(at, block_rows), :]
        high = x34[pl.ds(G * QUADS + at, block_rows), :]
        fields = [low, lanes(low[:, 2 * LANES :], high[:, : 2 * LANES]), high]
        flat = pl.ds(pl.multiple_of(ch * STEP_ROWS, 16), STEP_ROWS)
        own_f[...] = own_v[:, flat, :].astype(F32)
        total = jnp.zeros((QUADS, LANES), F32)
        for third in range(3):
            out = dot(fields[third], a3[third]) * scale
            for i in range(PLANES):
                plane = ch * PLANES + i
                partner = par_f[pl.ds(plane * F_PITCH + third, QUADS, stride=3), :]
                here = pl.ds(i * PLANE + third, QUADS, stride=3)
                there = pl.ds(plane * PLANE + third, QUADS, stride=3)
                sent = jnp.zeros((QUADS, LANES), F32)
                for p in range(2):
                    potential = out[i * QUADS : (i + 1) * QUADS, p * LANES : (p + 1) * LANES]
                    term = potential * partner
                    if earlier:
                        at = p * ROWS + plane * PLANE + third
                        term = term + z[pl.ds(at, QUADS, stride=3), :]
                    own_ov[p, there, :] = term
                    sent = sent + potential * own_f[p, here, :]
                total = total + sent * partner
                staged[here, :] = sent
        total_ref[...] += total
        par_ov[flat, :] = staged[...].astype(BF16)
        row = ch * STEP_ROWS
        copy_rows(own_ov, row, own_out, row, STEP_ROWS, sems.at[6]).start()

    first = 0
    for i, steps in enumerate(pieces):

        @pl.loop(0, steps, unroll=2 if steps % 2 == 0 else steps)
        def _(step):
            ch = first + step
            result(ch)
            source, row = ch * STEP_ROWS, step * STEP_ROWS
            copy_rows(par_ov, source, par_out[i], row, STEP_ROWS, sems.at[7 + i]).start()

        first += steps

    energy = jnp.zeros((8, LANES), F32) + jnp.sum(total_ref[...]) * F32(share)
    if earlier:
        energy = energy + before_v[...]
    energy_v[...] = energy
    report = pltpu.make_async_copy(energy_v, energy_out, sems.at[7 + len(pieces)])
    report.start()
    pltpu.make_async_copy(own_ov, own_out, sems.at[6]).wait()
    first = 0
    for i, steps in enumerate(pieces):
        rows = steps * STEP_ROWS
        copy_rows(par_ov, first, par_out[i], 0, rows, sems.at[7 + i]).wait()
        first += rows
    report.wait()


def pair_terms(own, own_u, partner, earlier, tables, kern, pieces, share, interpret=False):
    hbm = pl.BlockSpec(memory_space=pl.ANY)
    return pl.pallas_call(
        functools.partial(pairs_kernel, pieces, share),
        out_shape=(
            jax.ShapeDtypeStruct((2, ROWS, LANES), F32),
            *[jax.ShapeDtypeStruct((steps * STEP_ROWS, LANES), BF16) for steps in pieces],
            jax.ShapeDtypeStruct((8, LANES), F32),
        ),
        in_specs=[hbm] * (5 + len(earlier) + len(tables)),
        out_specs=(hbm,) * (2 + len(pieces)),
        scratch_shapes=[
            pltpu.VMEM((2, ROWS, LANES), BF16),
            pltpu.VMEM((2, G, G, LANES), BF16),
            pltpu.VMEM((KPAD * G, LANES), F32),
            pltpu.VMEM((2, ROWS, LANES), F32),
            pltpu.VMEM((ROWS, LANES), BF16),
            pltpu.VMEM((G * F_PITCH, LANES), F32),
            pltpu.VMEM((G, G, LANES), BF16),
            pltpu.VMEM((2 * G * Y_PITCH, LANES), F32),
            pltpu.VMEM((4 * Z_ROWS, LANES), F32),
            pltpu.VMEM((KPAD * G, 4 * LANES), BF16),
            pltpu.VMEM((2, STEP_ROWS, LANES), F32),
            pltpu.VMEM((STEP_ROWS, LANES), F32),
            pltpu.VMEM((QUADS, LANES), F32),
            pltpu.VMEM((8, LANES), F32),
            pltpu.VMEM((8, LANES), F32),
            *[pltpu.VMEM(table.shape, BF16) for table in tables],
            pltpu.SemaphoreType.DMA((2,)),
            pltpu.SemaphoreType.DMA((len(tables),)),
            pltpu.SemaphoreType.DMA((9 + len(pieces),)),
        ],
        compiler_params=pltpu.CompilerParams(vmem_limit_bytes=63 * MIB),
        cost_estimate=pl.CostEstimate(
            flops=20_000_000_000, bytes_accessed=20_000_000, transcendentals=0
        ),
        interpret=interpret,
        name="pair_terms",
    )(*own, own_u, kern, partner, *earlier, *tables)


def piece_kernel(first, size, own0, own1, terms, back0, back1, *rest):
    last = first + size == ROWS
    earlier = rest[: len(rest) - 12]
    out, gram_out, own_v, terms_v, back_v, out_v, gram_ref, gram_v, value_ref = rest[-12:-3]
    load_sems, gram_sems, store_sems = rest[-3:]
    rows = size // load_sems.shape[0]

    def loads(c):
        start = first + c * rows
        sources = [
            (own0, start, own_v.at[0]), (own1, start, own_v.at[1]), (terms, start, terms_v),
            (back0, start, back_v.at[0]), (back1, c * rows, back_v.at[1]),
        ]
        return [
            copy_rows(src, row, dst, c * rows, rows, load_sems.at[c, i])
            for i, (src, row, dst) in enumerate(sources)
        ]

    chunks = [loads(c) for c in range(load_sems.shape[0])]
    for chunk in chunks:
        for load in chunk:
            load.start()
    gram_loads = []
    if last:
        gram_loads = [
            pltpu.make_async_copy(src, gram_v.at[i], gram_sems.at[i])
            for i, src in enumerate(earlier[:-1])
        ]
        for load in gram_loads:
            load.start()
    gram_ref[...] = jnp.zeros_like(gram_ref)
    for c, chunk in enumerate(chunks):
        for load in chunk:
            load.wait()
        at = pl.ds(c * rows, rows)
        own = [own_v[i, at, :].astype(F32) for i in range(2)]
        for p in range(2):
            exchange = terms_v[p, at, :] + back_v[p, at, :].astype(F32)
            out_v[pl.ds(2 * c * rows + p, rows, stride=2), :] = exchange
            for i in range(2):
                product = (own[i] * exchange).reshape(-1, 8, LANES)
                gram_ref[i, p] += jnp.sum(product, axis=0)
        copy_rows(out_v, 2 * c * rows, out, 2 * (first + c * rows), 2 * rows, store_sems.at[0]).start()

    result = gram_ref
    if last:
        for load in gram_loads:
            load.wait()
        row = lax.broadcasted_iota(jnp.int32, (2, 2), 0)
        column = lax.broadcasted_iota(jnp.int32, (2, 2), 1)
        value = jnp.zeros((2, 2), F32)
        for i in range(2):
            for j in range(2):
                entry = gram_ref[i, j]
                for k in range(len(gram_loads)):
                    entry = entry + gram_v[k, i, j]
                value = jnp.where((row == i) & (column == j), jnp.sum(entry) * F32(1.0 / NGRID), value)
        value_ref[...] = value
        result = value_ref
    report = pltpu.make_async_copy(result, gram_out, store_sems.at[1])
    report.start()
    copy_rows(out_v, 0, out, 2 * first, 2 * size, store_sems.at[0]).wait()
    report.wait()


def add_piece(first, size, own, terms, back0, back1, grams, out, interpret=False):
    hbm = pl.BlockSpec(memory_space=pl.ANY)
    last = first + size == ROWS
    earlier = [] if out is None else [*(grams if last else []), out]
    gram_shape = (2, 2, 8, LANES)
    return pl.pallas_call(
        functools.partial(piece_kernel, first, size),
        out_shape=(
            jax.ShapeDtypeStruct((2 * ROWS, LANES), F32),
            jax.ShapeDtypeStruct((2, 2) if last else gram_shape, F32),
        ),
        in_specs=[hbm] * (5 + len(earlier)),
        out_specs=(hbm, hbm),
        scratch_shapes=[
            pltpu.VMEM((2, size, LANES), BF16),
            pltpu.VMEM((2, size, LANES), F32),
            pltpu.VMEM((2, size, LANES), BF16),
            pltpu.VMEM((2 * size, LANES), F32),
            pltpu.VMEM(gram_shape, F32),
            pltpu.VMEM((len(PIECES), *gram_shape), F32),
            pltpu.VMEM((2, 2), F32),
            pltpu.SemaphoreType.DMA((2 * size // STEP_ROWS, 5)),
            pltpu.SemaphoreType.DMA((len(PIECES),)),
            pltpu.SemaphoreType.DMA((2,)),
        ],
        input_output_aliases={4 + len(earlier): 0} if earlier else {},
        compiler_params=pltpu.CompilerParams(vmem_limit_bytes=52 * MIB),
        cost_estimate=cost(24 * size * LANES),
        interpret=interpret,
        name="add_piece",
    )(*own, terms, back0, back1, *earlier)


def from_behind(block, axis, distance):
    size = lax.axis_size(axis)
    return lax.ppermute(block, axis, [((i - distance) % size, i) for i in range(size)])


def after(values, other):
    return lax.optimization_barrier((values, other))[0]


def per_device(orbitals):
    tables = section_tables()
    kern = screening()
    size = lax.axis_size("band")
    share = -2.0 / (NGRID * 2 * size * orbitals.shape[0])
    raw = orbitals.reshape(2, ROWS, LANES).transpose(1, 0, 2).reshape(2 * ROWS, LANES)
    own = [take_band(raw, 0)]
    own.append(take_band(raw, 1, own))
    previous = [from_behind(part, "band", 1) for part in own]
    own_u = padded_rows(own, tables[-1])
    terms, back0, energy = pair_terms(
        own, own_u, previous[0], (), tables, kern, (STEPS,), share
    )
    back0 = from_behind(back0, "band", -1)
    terms, *sent, energy = pair_terms(
        own, own_u, previous[1], (terms, energy), tables, kern, PIECES, share
    )
    back1 = [from_behind(piece, "band", -1) for piece in sent]

    steps = []
    if size & (size - 1):
        energy = lax.psum(energy, "band")
    else:
        energy = energy + lax.ppermute(energy, "band", [(i, i + 1) for i in range(0, size, 2)])
        steps = [1 << b for b in range(1, size.bit_length() - 1)]
        steps = [b for b in steps if b != 2] + [b for b in steps if b == 2]
        steps = [[(i, i ^ b) for i in range(1, size, 2)] for b in steps]
    while len(steps) > len(back1) - 1:
        energy = energy + lax.ppermute(energy, "band", steps.pop(0))
    exchange, grams = None, []
    first = 0
    for count, piece in zip(PIECES, back1):
        count *= STEP_ROWS
        got, last = None, piece is back1[-1]
        if last and size & (size - 1) == 0:
            got = lax.ppermute(energy, "band", [(i + 1, i) for i in range(0, size, 2)])
        elif steps:
            got = lax.ppermute(energy, "band", steps.pop(0))
        exchange, gram = add_piece(first, count, own, terms, back0, piece, grams, exchange)
        if got is not None and last:
            odd = lax.axis_index("band") % 2 == 1
            energy = jnp.where(odd, energy[:1, :1], after(got, gram)[:1, :1])
        elif got is not None:
            energy = energy + after(got, gram)
        grams.append(gram)
        first += count
    exchange = exchange.reshape(ROWS, 2, LANES).transpose(1, 0, 2).reshape(2, NGRID)
    return exchange, gram, energy[0, 0]


def solution(mesh):
    return jax.shard_map(
        per_device,
        mesh=mesh,
        in_specs=(P("band", None),),
        out_specs=(P("band", None), P("band", None), P()),
        check_vma=False,
    )
```

```python
import functools

import jax
import jax.numpy as jnp
import ml_dtypes
import numpy as np
from jax import lax
from jax.experimental import pallas as pl
from jax.experimental.pallas import tpu as pltpu
from jax.sharding import PartitionSpec as P

G = 96
HALF = G // 2 + 1
NGRID = G * G * G
LANES = 128
ROWS = NGRID // LANES
PLANE = G * G // LANES
QUADS = G // 4
KPAD = HALF + 1
Y_ROWS = 104
Y_PITCH = Y_ROWS + 1
Z_PITCH = G + 1
W_PITCH = 2 * G + 1
Z_ROWS = KPAD * Z_PITCH
F_PITCH = PLANE + 1
PLANES = 16
STEP_ROWS = PLANES * PLANE
STEPS = G // PLANES
PIECES = (4, 2)
WAVE_UNIT = 0.05
SCREEN_SQ = 0.0121
MIB = 1024 * 1024
BF16 = jnp.bfloat16
F32 = jnp.float32


def dft_tables():
    n = np.arange(G)
    phases = (n[:, None] * n[None, :]) % G
    angles = phases.astype(np.float32) * np.float32(2.0 * np.pi / G)
    rounded = [f(angles).astype(ml_dtypes.bfloat16).astype(np.float32) for f in (np.cos, np.sin)]
    return rounded[0], rounded[1]


def section_tables():
    c, s = dft_tables()
    h = HALF
    t1 = np.zeros((Y_ROWS, G), np.float32)
    t1[:h] = c[:h]
    t1[h : 2 * h] = -s[:h]
    t2 = np.block([[c, s], [-s, c]])
    t3 = np.zeros((2, LANES, 4, 64), np.float32)
    back = (G - np.arange(h)) % G
    t3[0, :G, 0, :h] = c[:h].T
    t3[1, :G, 0, :h] = s[:h].T
    t3[0, :G, 1, :h] = -s[:h].T
    t3[1, :G, 1, :h] = c[:h].T
    t3[0, :G, 2, :h] = c[back].T
    t3[1, :G, 2, :h] = s[back].T
    t3[0, :G, 3, :h] = s[back].T
    t3[1, :G, 3, :h] = -c[back].T
    t3 = t3.reshape(2 * LANES, 4 * 64)
    order = np.concatenate([np.arange(G // 2), G - 1 - np.arange(G // 2)])
    a1 = np.block([[c[:, order], -s[:, order]], [s[:, order], c[:, order]]])
    rows = np.arange(G).reshape(QUADS, 4).T.reshape(-1)
    a2 = np.block([[c[rows], -s[rows]], [s[rows], c[rows]]])
    weight = np.full((h, 1), 2.0, np.float32)
    weight[0] = weight[h - 1] = 1.0
    a3 = np.zeros((3, 2, 2, 2, 64, 2, LANES), np.float32)
    for third in range(3):
        for lane in range(LANES):
            r, x3 = divmod(third * LANES + lane, G)
            for p in range(2):
                a3[third, r - third, 0, p, :h, p, lane] = weight[:, 0] * c[x3, :h]
                a3[third, r - third, 1, p, :h, p, lane] = -weight[:, 0] * s[x3, :h]
    a3 = a3.reshape(3, 4 * LANES, 2 * LANES)
    sel = np.zeros((2, 2 * LANES, 2 * LANES), np.float32)
    for r in range(4):
        for x in range(G):
            sel[r // 2, r * G + x - (r // 2) * LANES, (r % 2) * LANES + x] = 1.0
    return [t.astype(ml_dtypes.bfloat16) for t in (t1, t2, t3, a1, a2, a3, sel)]


def screening():
    n = np.arange(G)
    m = np.where(n <= G // 2, n, n - G).astype(np.float64)
    sq = m * m
    q2 = WAVE_UNIT * (sq[:HALF, None, None] + sq[None, :, None] + sq[None, None, :HALF])
    safe = np.where(q2 > 0, q2, 1.0)
    kern = 4.0 * np.pi * (1.0 - np.exp(-q2 / (4.0 * SCREEN_SQ))) / safe
    kern = np.where(q2 > 0, kern, np.pi / SCREEN_SQ)
    out = np.zeros((KPAD, G, 2, 64), np.float32)
    out[:HALF, :, :, :HALF] = kern[:, :, None, :]
    return out.reshape(KPAD * G, LANES)


def cost(size):
    return pl.CostEstimate(flops=0, bytes_accessed=size, transcendentals=0)


def dot(a, b):
    return jnp.dot(a, b, preferred_element_type=F32)


def lanes(*parts):
    return jnp.concatenate(parts, axis=1)


def stack(*parts):
    return jnp.concatenate(parts, axis=0)


def split_rows(src, sel_ref, out, first, count):
    rows = [
        [src[pl.ds(3 * (first + i) + s, G, stride=F_PITCH), :].astype(BF16) for s in range(3)]
        for i in range(count)
    ]
    for half in range(2):
        part = dot(stack(*[lanes(r[half], r[half + 1]) for r in rows]), sel_ref[half])
        for i in range(count):
            for e in range(2):
                value = part[i * G : (i + 1) * G, e * LANES : (e + 1) * LANES]
                out[4 * (first + i) + 2 * half + e] = value.astype(BF16)


def widen_planes(src, dst, first):
    @pl.loop(0, src.shape[0] // (2 * PLANE), unroll=4)
    def _(i):
        value = src[pl.ds(pl.multiple_of(i * 2 * PLANE, 16), 2 * PLANE), :].astype(F32)
        dst[pl.ds((first + 2 * i) * F_PITCH, PLANE), :] = value[:PLANE]
        dst[pl.ds((first + 2 * i + 1) * F_PITCH, PLANE), :] = value[PLANE:]


def rows_of(ref, first, count):
    at = pl.ds(first, count)
    return ref.at[at, :] if len(ref.shape) == 2 else ref.at[:, at, :]


def copy_rows(src, src_row, dst, dst_row, count, sem):
    return pltpu.make_async_copy(rows_of(src, src_row, count), rows_of(dst, dst_row, count), sem)


def band_kernel(p, raw, *refs):
    out, raw_v, out_v, load_sems, store_sem = refs[-5:]
    chunks = load_sems.shape[0]
    rows = out.shape[0] // chunks
    loads = [
        copy_rows(raw, 2 * c * rows, raw_v, 2 * c * rows, 2 * rows, load_sems.at[c])
        for c in range(chunks)
    ]
    for load in loads:
        load.start()
    shape = (LANES, 2 * LANES)
    row = lax.broadcasted_iota(jnp.int32, shape, 0)
    column = lax.broadcasted_iota(jnp.int32, shape, 1)
    pick = jnp.where(column == 2 * row + p, F32(1.0), F32(0.0)).astype(BF16)
    for c, load in enumerate(loads):
        load.wait()
        for row in range(c * rows, (c + 1) * rows, LANES):
            value = dot(pick, raw_v[2 * row : 2 * row + 2 * LANES, :])
            out_v[row : row + LANES, :] = value.astype(BF16)
        copy_rows(out_v, c * rows, out, c * rows, rows, store_sem).start()
    pltpu.make_async_copy(out_v, out, store_sem).wait()


def take_band(raw, p, earlier=(), interpret=False):
    hbm = pl.BlockSpec(memory_space=pl.ANY)
    return pl.pallas_call(
        functools.partial(band_kernel, p),
        out_shape=jax.ShapeDtypeStruct((ROWS, LANES), BF16),
        in_specs=[hbm] * (1 + len(earlier)),
        out_specs=hbm,
        scratch_shapes=[
            pltpu.VMEM((2 * ROWS, LANES), BF16),
            pltpu.VMEM((ROWS, LANES), BF16),
            pltpu.SemaphoreType.DMA((9,)),
            pltpu.SemaphoreType.DMA,
        ],
        compiler_params=pltpu.CompilerParams(vmem_limit_bytes=63 * MIB),
        cost_estimate=cost(6 * ROWS * LANES),
        interpret=interpret,
        name="take_band",
    )(raw, *earlier)


def rows_kernel(own0, own1, sel, out, wide):
    for p, own in enumerate((own0, own1)):
        widen_planes(own, wide, 0)

        @pl.loop(0, QUADS // 4, unroll=2)
        def _(q):
            split_rows(wide, sel, out.at[p], 4 * q, 4)


def padded_rows(own, sel, interpret=False):
    vmem = pl.BlockSpec(memory_space=pltpu.VMEM)
    return pl.pallas_call(
        rows_kernel,
        out_shape=jax.ShapeDtypeStruct((2, G, G, LANES), BF16),
        in_specs=[vmem] * 3,
        out_specs=vmem,
        scratch_shapes=[pltpu.VMEM((G * F_PITCH, LANES), F32)],
        compiler_params=pltpu.CompilerParams(vmem_limit_bytes=63 * MIB),
        cost_estimate=cost(16 * NGRID),
        interpret=interpret,
        name="padded_rows",
    )(*own, sel)


def pairs_kernel(pieces, share, own0, own1, own_u, kern, par, *refs):
    earlier = []
    if len(pieces) > 1:
        earlier, refs = refs[:2], refs[2:]
    table_refs, own_out = refs[:7], refs[7]
    par_out, energy_out = refs[8 : 8 + len(pieces)], refs[8 + len(pieces)]
    own_v, own_uv, kern_v, own_ov, par_ov, par_f, par_u, yw, z, x34 = refs[9 + len(pieces) : -15]
    own_f, staged, total_ref, energy_v, before_v = refs[-15:-10]
    tables, (par_sems, table_sems, sems) = refs[-10:-3], refs[-3:]
    t1, t2, t3, a1, a2, a3, sel = tables
    par_v = par_ov
    par_loads = []
    for first in (0, ROWS // 2):
        sem = par_sems.at[len(par_loads)]
        par_loads.append(copy_rows(par, first, par_v, first, ROWS // 2, sem))
    for load in par_loads:
        load.start()
    table_loads = [
        pltpu.make_async_copy(src, dst, table_sems.at[i])
        for i, (src, dst) in enumerate(zip(table_refs, tables))
    ]
    table_loads[6].start()
    table_loads[0].start()
    loads = [
        pltpu.make_async_copy(own_u, own_uv, sems.at[0]),
        pltpu.make_async_copy(kern, kern_v, sems.at[1]),
        copy_rows(own0, 0, own_v.at[0], 0, ROWS, sems.at[2]),
        copy_rows(own1, 0, own_v.at[1], 0, ROWS, sems.at[3]),
    ]
    later = []
    if earlier:
        later = [copy_rows(earlier[0].at[p], 0, z, p * ROWS, ROWS, sems.at[4 + p]) for p in range(2)]
        loads.append(pltpu.make_async_copy(earlier[1], before_v, sems.at[8 + len(pieces)]))

    for i, load in enumerate(par_loads):
        load.wait()
        for other in ([loads[0]], table_loads[1:5])[i]:
            other.start()
        widen_planes(par_v.at[pl.ds(i * ROWS // 2, ROWS // 2), :], par_f, i * G // 2)
    table_loads[6].wait()

    @pl.loop(0, QUADS // 4, unroll=2)
    def _(q):
        split_rows(par_f, sel, par_u, 4 * q, 4)

    half_y = G * Y_PITCH
    loads[0].wait()
    for load in loads[1:]:
        load.start()
    table_loads[5].start()
    table_loads[0].wait()

    @pl.loop(0, G // 2, unroll=8)
    def _(i):
        density = []
        for e in range(2):
            partner = par_u[2 * i + e].astype(F32)
            for p in range(2):
                density.append((own_uv[p, 2 * i + e].astype(F32) * partner).astype(BF16))
        out = dot(t1[...], lanes(*density))
        for e in range(2):
            for p in range(2):
                at = pl.ds(p * half_y + (2 * i + e) * Y_PITCH, Y_ROWS)
                yw[at, :] = out[:, (2 * e + p) * LANES : (2 * e + p + 1) * LANES]

    table_loads[1].wait()

    @pl.loop(0, HALF, unroll=7)
    def _(k1):
        def line(p, part):
            return yw[pl.ds(p * half_y + part * HALF + k1, G, stride=Y_PITCH), :].astype(BF16)

        out = dot(t2[...], stack(lanes(line(0, 0), line(1, 0)), lanes(line(0, 1), line(1, 1))))
        at = pl.ds(pl.multiple_of(k1 * G, 16), G)
        for p in range(2):
            for part in range(2):
                left = (2 * p + part) * LANES
                value = out[part * G : (part + 1) * G, p * LANES : (p + 1) * LANES]
                x34[at, left : left + LANES] = value.astype(BF16)

    loads[1].wait()
    table_loads[2].wait()

    many = 5

    @pl.loop(0, KPAD // many, unroll=2)
    def _(m):
        at = pl.ds(pl.multiple_of(m * many * G, 16), many * G)
        factor = kern_v[at, :]
        out = [
            dot(x34[at, 2 * p * LANES : 2 * (p + 1) * LANES], t3[...]).astype(BF16)
            for p in range(2)
        ]
        for part in range(4):
            spectrum = lanes(*[o[:, part * 64 : (part + 1) * 64] for o in out]).astype(F32)
            value = spectrum * factor
            for i in range(many):
                row = part * Z_ROWS + (many * m + i) * Z_PITCH
                z[pl.ds(row, G), :] = value[i * G : (i + 1) * G]

    table_loads[3].wait()

    @pl.loop(0, G // 4, unroll=6)
    def _(four):
        parts = []
        for e in range(4):
            k2 = 4 * four + e
            mirror = Z_PITCH + jnp.where(k2 == 0, 0, G - k2)
            parts.append(
                stack(
                    z[pl.ds(k2, G // 2, stride=Z_PITCH), :].astype(BF16),
                    z[pl.ds(2 * Z_ROWS + mirror, G // 2, stride=Z_PITCH), :].astype(BF16),
                    z[pl.ds(1 * Z_ROWS + k2, G // 2, stride=Z_PITCH), :].astype(BF16),
                    z[pl.ds(3 * Z_ROWS + mirror, G // 2, stride=Z_PITCH), :].astype(BF16),
                )
            )
        out = dot(a1[...], lanes(*parts))
        for e in range(4):
            at = (4 * four + e) * W_PITCH
            yw[pl.ds(at, 2 * G), :] = out[:, e * LANES : (e + 1) * LANES]

    for load in later:
        load.start()
    table_loads[4].wait()

    @pl.loop(0, G // 4, unroll=6)
    def _(four):
        parts = []
        for e in range(4):
            x1 = 4 * four + e
            parts.append(
                stack(
                    yw[pl.ds(x1, G, stride=W_PITCH), :].astype(BF16),
                    yw[pl.ds(G + x1, G, stride=W_PITCH), :].astype(BF16),
                )
            )
        out = dot(a2[...], lanes(*parts))
        for r in range(4):
            block = [
                lanes(
                    out[r * QUADS : (r + 1) * QUADS, e * LANES : (e + 1) * LANES],
                    out[G + r * QUADS : G + (r + 1) * QUADS, e * LANES : (e + 1) * LANES],
                )
                for e in range(4)
            ]
            at = pl.multiple_of((r // 2) * G * QUADS + four * 4 * QUADS, 16)
            left = (r % 2) * 2 * LANES
            x34[pl.ds(at, 4 * QUADS), left : left + 2 * LANES] = stack(*block).astype(BF16)

    table_loads[5].wait()
    for load in loads[2:] + later:
        load.wait()
    total_ref[...] = jnp.zeros_like(total_ref)
    block_rows = PLANES * QUADS
    scale = F32(1.0 / NGRID)

    def result(ch):
        at = pl.multiple_of(ch * block_rows, 16)
        low = x34[pl.ds(at, block_rows), :]
        high = x34[pl.ds(G * QUADS + at, block_rows), :]
        fields = [low, lanes(low[:, 2 * LANES :], high[:, : 2 * LANES]), high]
        flat = pl.ds(pl.multiple_of(ch * STEP_ROWS, 16), STEP_ROWS)
        own_f[...] = own_v[:, flat, :].astype(F32)
        total = jnp.zeros((QUADS, LANES), F32)
        for third in range(3):
            out = dot(fields[third], a3[third]) * scale
            for i in range(PLANES):
                plane = ch * PLANES + i
                partner = par_f[pl.ds(plane * F_PITCH + third, QUADS, stride=3), :]
                here = pl.ds(i * PLANE + third, QUADS, stride=3)
                there = pl.ds(plane * PLANE + third, QUADS, stride=3)
                sent = jnp.zeros((QUADS, LANES), F32)
                for p in range(2):
                    potential = out[i * QUADS : (i + 1) * QUADS, p * LANES : (p + 1) * LANES]
                    term = potential * partner
                    if earlier:
                        at = p * ROWS + plane * PLANE + third
                        term = term + z[pl.ds(at, QUADS, stride=3), :]
                    own_ov[p, there, :] = term
                    sent = sent + potential * own_f[p, here, :]
                total = total + sent * partner
                staged[here, :] = sent
        total_ref[...] += total
        par_ov[flat, :] = staged[...].astype(BF16)
        row = ch * STEP_ROWS
        copy_rows(own_ov, row, own_out, row, STEP_ROWS, sems.at[6]).start()

    first = 0
    for i, steps in enumerate(pieces):

        @pl.loop(0, steps, unroll=2 if steps % 2 == 0 else steps)
        def _(step):
            ch = first + step
            result(ch)
            source, row = ch * STEP_ROWS, step * STEP_ROWS
            copy_rows(par_ov, source, par_out[i], row, STEP_ROWS, sems.at[7 + i]).start()

        first += steps

    energy = jnp.zeros((8, LANES), F32) + jnp.sum(total_ref[...]) * F32(share)
    if earlier:
        energy = energy + before_v[...]
    energy_v[...] = energy
    report = pltpu.make_async_copy(energy_v, energy_out, sems.at[7 + len(pieces)])
    report.start()
    pltpu.make_async_copy(own_ov, own_out, sems.at[6]).wait()
    first = 0
    for i, steps in enumerate(pieces):
        rows = steps * STEP_ROWS
        copy_rows(par_ov, first, par_out[i], 0, rows, sems.at[7 + i]).wait()
        first += rows
    report.wait()


def pair_terms(own, own_u, partner, earlier, tables, kern, pieces, share, interpret=False):
    hbm = pl.BlockSpec(memory_space=pl.ANY)
    return pl.pallas_call(
        functools.partial(pairs_kernel, pieces, share),
        out_shape=(
            jax.ShapeDtypeStruct((2, ROWS, LANES), F32),
            *[jax.ShapeDtypeStruct((steps * STEP_ROWS, LANES), BF16) for steps in pieces],
            jax.ShapeDtypeStruct((8, LANES), F32),
        ),
        in_specs=[hbm] * (5 + len(earlier) + len(tables)),
        out_specs=(hbm,) * (2 + len(pieces)),
        scratch_shapes=[
            pltpu.VMEM((2, ROWS, LANES), BF16),
            pltpu.VMEM((2, G, G, LANES), BF16),
            pltpu.VMEM((KPAD * G, LANES), F32),
            pltpu.VMEM((2, ROWS, LANES), F32),
            pltpu.VMEM((ROWS, LANES), BF16),
            pltpu.VMEM((G * F_PITCH, LANES), F32),
            pltpu.VMEM((G, G, LANES), BF16),
            pltpu.VMEM((2 * G * Y_PITCH, LANES), F32),
            pltpu.VMEM((4 * Z_ROWS, LANES), F32),
            pltpu.VMEM((KPAD * G, 4 * LANES), BF16),
            pltpu.VMEM((2, STEP_ROWS, LANES), F32),
            pltpu.VMEM((STEP_ROWS, LANES), F32),
            pltpu.VMEM((QUADS, LANES), F32),
            pltpu.VMEM((8, LANES), F32),
            pltpu.VMEM((8, LANES), F32),
            *[pltpu.VMEM(table.shape, BF16) for table in tables],
            pltpu.SemaphoreType.DMA((2,)),
            pltpu.SemaphoreType.DMA((len(tables),)),
            pltpu.SemaphoreType.DMA((9 + len(pieces),)),
        ],
        compiler_params=pltpu.CompilerParams(vmem_limit_bytes=63 * MIB),
        cost_estimate=pl.CostEstimate(
            flops=20_000_000_000, bytes_accessed=20_000_000, transcendentals=0
        ),
        interpret=interpret,
        name="pair_terms",
    )(*own, own_u, kern, partner, *earlier, *tables)


def piece_kernel(first, size, own0, own1, terms, back0, back1, *rest):
    last = first + size == ROWS
    earlier = rest[: len(rest) - 12]
    out, gram_out, own_v, terms_v, back_v, out_v, gram_ref, gram_v, value_ref = rest[-12:-3]
    load_sems, gram_sems, store_sems = rest[-3:]
    rows = size // load_sems.shape[0]

    def loads(c):
        start = first + c * rows
        sources = [
            (own0, start, own_v.at[0]), (own1, start, own_v.at[1]), (terms, start, terms_v),
            (back0, start, back_v.at[0]), (back1, c * rows, back_v.at[1]),
        ]
        return [
            copy_rows(src, row, dst, c * rows, rows, load_sems.at[c, i])
            for i, (src, row, dst) in enumerate(sources)
        ]

    chunks = [loads(c) for c in range(load_sems.shape[0])]
    for chunk in chunks:
        for load in chunk:
            load.start()
    gram_loads = []
    if last:
        gram_loads = [
            pltpu.make_async_copy(src, gram_v.at[i], gram_sems.at[i])
            for i, src in enumerate(earlier[:-1])
        ]
        for load in gram_loads:
            load.start()
    gram_ref[...] = jnp.zeros_like(gram_ref)
    for c, chunk in enumerate(chunks):
        for load in chunk:
            load.wait()
        at = pl.ds(c * rows, rows)
        own = [own_v[i, at, :].astype(F32) for i in range(2)]
        for p in range(2):
            exchange = terms_v[p, at, :] + back_v[p, at, :].astype(F32)
            out_v[pl.ds(2 * c * rows + p, rows, stride=2), :] = exchange
            for i in range(2):
                product = (own[i] * exchange).reshape(-1, 8, LANES)
                gram_ref[i, p] += jnp.sum(product, axis=0)
        copy_rows(out_v, 2 * c * rows, out, 2 * (first + c * rows), 2 * rows, store_sems.at[0]).start()

    result = gram_ref
    if last:
        for load in gram_loads:
            load.wait()
        row = lax.broadcasted_iota(jnp.int32, (2, 2), 0)
        column = lax.broadcasted_iota(jnp.int32, (2, 2), 1)
        value = jnp.zeros((2, 2), F32)
        for i in range(2):
            for j in range(2):
                entry = gram_ref[i, j]
                for k in range(len(gram_loads)):
                    entry = entry + gram_v[k, i, j]
                value = jnp.where((row == i) & (column == j), jnp.sum(entry) * F32(1.0 / NGRID), value)
        value_ref[...] = value
        result = value_ref
    report = pltpu.make_async_copy(result, gram_out, store_sems.at[1])
    report.start()
    copy_rows(out_v, 0, out, 2 * first, 2 * size, store_sems.at[0]).wait()
    report.wait()


def add_piece(first, size, own, terms, back0, back1, grams, out, interpret=False):
    hbm = pl.BlockSpec(memory_space=pl.ANY)
    last = first + size == ROWS
    earlier = [] if out is None else [*(grams if last else []), out]
    gram_shape = (2, 2, 8, LANES)
    return pl.pallas_call(
        functools.partial(piece_kernel, first, size),
        out_shape=(
            jax.ShapeDtypeStruct((2 * ROWS, LANES), F32),
            jax.ShapeDtypeStruct((2, 2) if last else gram_shape, F32),
        ),
        in_specs=[hbm] * (5 + len(earlier)),
        out_specs=(hbm, hbm),
        scratch_shapes=[
            pltpu.VMEM((2, size, LANES), BF16),
            pltpu.VMEM((2, size, LANES), F32),
            pltpu.VMEM((2, size, LANES), BF16),
            pltpu.VMEM((2 * size, LANES), F32),
            pltpu.VMEM(gram_shape, F32),
            pltpu.VMEM((len(PIECES), *gram_shape), F32),
            pltpu.VMEM((2, 2), F32),
            pltpu.SemaphoreType.DMA((2 * size // STEP_ROWS, 5)),
            pltpu.SemaphoreType.DMA((len(PIECES),)),
            pltpu.SemaphoreType.DMA((2,)),
        ],
        input_output_aliases={4 + len(earlier): 0} if earlier else {},
        compiler_params=pltpu.CompilerParams(vmem_limit_bytes=52 * MIB),
        cost_estimate=cost(24 * size * LANES),
        interpret=interpret,
        name="add_piece",
    )(*own, terms, back0, back1, *earlier)


def from_behind(block, axis, distance):
    size = lax.axis_size(axis)
    return lax.ppermute(block, axis, [((i - distance) % size, i) for i in range(size)])


def after(values, other):
    return lax.optimization_barrier((values, other))[0]


def per_device(orbitals):
    tables = section_tables()
    kern = screening()
    size = lax.axis_size("band")
    share = -2.0 / (NGRID * 2 * size * orbitals.shape[0])
    raw = orbitals.reshape(2, ROWS, LANES).transpose(1, 0, 2).reshape(2 * ROWS, LANES)
    own = [take_band(raw, 0)]
    own.append(take_band(raw, 1, own))
    previous = [from_behind(part, "band", 1) for part in own]
    own_u = padded_rows(own, tables[-1])
    terms, back0, energy = pair_terms(
        own, own_u, previous[0], (), tables, kern, (STEPS,), share
    )
    back0 = from_behind(back0, "band", -1)
    terms, *sent, energy = pair_terms(
        own, own_u, previous[1], (terms, energy), tables, kern, PIECES, share
    )
    back1 = [from_behind(piece, "band", -1) for piece in sent]

    steps = []
    if size & (size - 1):
        energy = lax.psum(energy, "band")
    else:
        swap = [(i, i ^ 1) for i in range(size)]
        energy = energy + lax.ppermute(energy, "band", swap)
        steps = [1 << b for b in range(1, size.bit_length() - 1)]
        steps = [b for b in steps if b != 2] + [b for b in steps if b == 2]
        steps = [[(i, i ^ b if i % 2 else i) for i in range(size)] for b in steps]
    while len(steps) > len(back1) - 1:
        energy = energy + lax.ppermute(energy, "band", steps.pop(0))
    exchange, grams = None, []
    first = 0
    for count, piece in zip(PIECES, back1):
        count *= STEP_ROWS
        got, last = None, piece is back1[-1]
        if last and size & (size - 1) == 0:
            got = lax.ppermute(energy, "band", swap)
        elif steps:
            got = lax.ppermute(energy, "band", steps.pop(0))
        exchange, gram = add_piece(first, count, own, terms, back0, piece, grams, exchange)
        if got is not None and last:
            odd = lax.axis_index("band") % 2 == 1
            energy = jnp.where(odd, energy[:1, :1], after(got, gram)[:1, :1])
        elif got is not None:
            energy = energy + after(got, gram)
        grams.append(gram)
        first += count
    exchange = exchange.reshape(ROWS, 2, LANES).transpose(1, 0, 2).reshape(2, NGRID)
    return exchange, gram, energy[0, 0]


def solution(mesh):
    return jax.shard_map(
        per_device,
        mesh=mesh,
        in_specs=(P("band", None),),
        out_specs=(P("band", None), P("band", None), P()),
        check_vma=False,
    )
```

```python
import functools

import jax
import jax.numpy as jnp
import ml_dtypes
import numpy as np
from jax import lax
from jax.experimental import pallas as pl
from jax.experimental.pallas import tpu as pltpu
from jax.sharding import PartitionSpec as P

G = 96
HALF = G // 2 + 1
NGRID = G * G * G
LANES = 128
ROWS = NGRID // LANES
PLANE = G * G // LANES
QUADS = G // 4
KPAD = HALF + 1
Y_ROWS = 104
Y_PITCH = Y_ROWS + 1
Z_PITCH = G + 1
W_PITCH = 2 * G + 1
Z_ROWS = KPAD * Z_PITCH
F_PITCH = PLANE + 1
PLANES = 16
STEP_ROWS = PLANES * PLANE
STEPS = G // PLANES
PIECES = (4, 2)
WAVE_UNIT = 0.05
SCREEN_SQ = 0.0121
MIB = 1024 * 1024
BF16 = jnp.bfloat16
F32 = jnp.float32


def dft_tables():
    n = np.arange(G)
    phases = (n[:, None] * n[None, :]) % G
    angles = phases.astype(np.float32) * np.float32(2.0 * np.pi / G)
    rounded = [f(angles).astype(ml_dtypes.bfloat16).astype(np.float32) for f in (np.cos, np.sin)]
    return rounded[0], rounded[1]


def section_tables():
    c, s = dft_tables()
    h = HALF
    t1 = np.zeros((Y_ROWS, G), np.float32)
    t1[:h] = c[:h]
    t1[h : 2 * h] = -s[:h]
    t2 = np.block([[c, s], [-s, c]])
    t3 = np.zeros((2, LANES, 4, 64), np.float32)
    back = (G - np.arange(h)) % G
    t3[0, :G, 0, :h] = c[:h].T
    t3[1, :G, 0, :h] = s[:h].T
    t3[0, :G, 1, :h] = -s[:h].T
    t3[1, :G, 1, :h] = c[:h].T
    t3[0, :G, 2, :h] = c[back].T
    t3[1, :G, 2, :h] = s[back].T
    t3[0, :G, 3, :h] = s[back].T
    t3[1, :G, 3, :h] = -c[back].T
    t3 = t3.reshape(2 * LANES, 4 * 64)
    order = np.concatenate([np.arange(G // 2), G - 1 - np.arange(G // 2)])
    a1 = np.block([[c[:, order], -s[:, order]], [s[:, order], c[:, order]]])
    rows = np.arange(G).reshape(QUADS, 4).T.reshape(-1)
    a2 = np.block([[c[rows], -s[rows]], [s[rows], c[rows]]])
    weight = np.full((h, 1), 2.0, np.float32)
    weight[0] = weight[h - 1] = 1.0
    a3 = np.zeros((3, 2, 2, 2, 64, 2, LANES), np.float32)
    for third in range(3):
        for lane in range(LANES):
            r, x3 = divmod(third * LANES + lane, G)
            for p in range(2):
                a3[third, r - third, 0, p, :h, p, lane] = weight[:, 0] * c[x3, :h]
                a3[third, r - third, 1, p, :h, p, lane] = -weight[:, 0] * s[x3, :h]
    a3 = a3.reshape(3, 4 * LANES, 2 * LANES)
    sel = np.zeros((2, 2 * LANES, 2 * LANES), np.float32)
    for r in range(4):
        for x in range(G):
            sel[r // 2, r * G + x - (r // 2) * LANES, (r % 2) * LANES + x] = 1.0
    return [t.astype(ml_dtypes.bfloat16) for t in (t1, t2, t3, a1, a2, a3, sel)]


def screening():
    n = np.arange(G)
    m = np.where(n <= G // 2, n, n - G).astype(np.float64)
    sq = m * m
    q2 = WAVE_UNIT * (sq[:HALF, None, None] + sq[None, :, None] + sq[None, None, :HALF])
    safe = np.where(q2 > 0, q2, 1.0)
    kern = 4.0 * np.pi * (1.0 - np.exp(-q2 / (4.0 * SCREEN_SQ))) / safe
    kern = np.where(q2 > 0, kern, np.pi / SCREEN_SQ)
    out = np.zeros((KPAD, G, 2, 64), np.float32)
    out[:HALF, :, :, :HALF] = kern[:, :, None, :]
    return out.reshape(KPAD * G, LANES)


def cost(size):
    return pl.CostEstimate(flops=0, bytes_accessed=size, transcendentals=0)


def dot(a, b):
    return jnp.dot(a, b, preferred_element_type=F32)


def lanes(*parts):
    return jnp.concatenate(parts, axis=1)


def stack(*parts):
    return jnp.concatenate(parts, axis=0)


def split_rows(src, sel_ref, out, first, count):
    rows = [
        [src[pl.ds(3 * (first + i) + s, G, stride=F_PITCH), :].astype(BF16) for s in range(3)]
        for i in range(count)
    ]
    for half in range(2):
        part = dot(stack(*[lanes(r[half], r[half + 1]) for r in rows]), sel_ref[half])
        for i in range(count):
            for e in range(2):
                value = part[i * G : (i + 1) * G, e * LANES : (e + 1) * LANES]
                out[4 * (first + i) + 2 * half + e] = value.astype(BF16)


def widen_planes(src, dst, first):
    @pl.loop(0, src.shape[0] // (2 * PLANE), unroll=4)
    def _(i):
        value = src[pl.ds(pl.multiple_of(i * 2 * PLANE, 16), 2 * PLANE), :].astype(F32)
        dst[pl.ds((first + 2 * i) * F_PITCH, PLANE), :] = value[:PLANE]
        dst[pl.ds((first + 2 * i + 1) * F_PITCH, PLANE), :] = value[PLANE:]


def rows_of(ref, first, count):
    at = pl.ds(first, count)
    return ref.at[at, :] if len(ref.shape) == 2 else ref.at[:, at, :]


def copy_rows(src, src_row, dst, dst_row, count, sem):
    return pltpu.make_async_copy(rows_of(src, src_row, count), rows_of(dst, dst_row, count), sem)


def band_kernel(p, raw, *refs):
    out, raw_v, out_v, load_sems, store_sem = refs[-5:]
    chunks = load_sems.shape[0]
    rows = out.shape[0] // chunks
    loads = [
        copy_rows(raw, 2 * c * rows, raw_v, 2 * c * rows, 2 * rows, load_sems.at[c])
        for c in range(chunks)
    ]
    for load in loads:
        load.start()
    shape = (LANES, 2 * LANES)
    row = lax.broadcasted_iota(jnp.int32, shape, 0)
    column = lax.broadcasted_iota(jnp.int32, shape, 1)
    pick = jnp.where(column == 2 * row + p, F32(1.0), F32(0.0)).astype(BF16)
    for c, load in enumerate(loads):
        load.wait()
        for row in range(c * rows, (c + 1) * rows, LANES):
            value = dot(pick, raw_v[2 * row : 2 * row + 2 * LANES, :])
            out_v[row : row + LANES, :] = value.astype(BF16)
        copy_rows(out_v, c * rows, out, c * rows, rows, store_sem).start()
    pltpu.make_async_copy(out_v, out, store_sem).wait()


def take_band(raw, p, earlier=(), interpret=False):
    hbm = pl.BlockSpec(memory_space=pl.ANY)
    return pl.pallas_call(
        functools.partial(band_kernel, p),
        out_shape=jax.ShapeDtypeStruct((ROWS, LANES), BF16),
        in_specs=[hbm] * (1 + len(earlier)),
        out_specs=hbm,
        scratch_shapes=[
            pltpu.VMEM((2 * ROWS, LANES), BF16),
            pltpu.VMEM((ROWS, LANES), BF16),
            pltpu.SemaphoreType.DMA((9,)),
            pltpu.SemaphoreType.DMA,
        ],
        compiler_params=pltpu.CompilerParams(vmem_limit_bytes=63 * MIB),
        cost_estimate=cost(6 * ROWS * LANES),
        interpret=interpret,
        name="take_band",
    )(raw, *earlier)


def rows_kernel(own0, own1, sel, out, wide):
    for p, own in enumerate((own0, own1)):
        widen_planes(own, wide, 0)

        @pl.loop(0, QUADS // 4, unroll=2)
        def _(q):
            split_rows(wide, sel, out.at[p], 4 * q, 4)


def padded_rows(own, sel, interpret=False):
    vmem = pl.BlockSpec(memory_space=pltpu.VMEM)
    return pl.pallas_call(
        rows_kernel,
        out_shape=jax.ShapeDtypeStruct((2, G, G, LANES), BF16),
        in_specs=[vmem] * 3,
        out_specs=vmem,
        scratch_shapes=[pltpu.VMEM((G * F_PITCH, LANES), F32)],
        compiler_params=pltpu.CompilerParams(vmem_limit_bytes=63 * MIB),
        cost_estimate=cost(16 * NGRID),
        interpret=interpret,
        name="padded_rows",
    )(*own, sel)


def pairs_kernel(pieces, share, own0, own1, own_u, kern, par, *refs):
    earlier = []
    if len(pieces) > 1:
        earlier, refs = refs[:2], refs[2:]
    table_refs, own_out = refs[:7], refs[7]
    par_out, energy_out = refs[8 : 8 + len(pieces)], refs[8 + len(pieces)]
    own_v, own_uv, kern_v, own_ov, par_ov, par_f, par_u, yw, z, x34 = refs[9 + len(pieces) : -15]
    own_f, staged, total_ref, energy_v, before_v = refs[-15:-10]
    tables, (par_sems, table_sems, sems) = refs[-10:-3], refs[-3:]
    t1, t2, t3, a1, a2, a3, sel = tables
    par_v = par_ov
    par_loads = []
    for first in (0, ROWS // 2):
        sem = par_sems.at[len(par_loads)]
        par_loads.append(copy_rows(par, first, par_v, first, ROWS // 2, sem))
    for load in par_loads:
        load.start()
    table_loads = [
        pltpu.make_async_copy(src, dst, table_sems.at[i])
        for i, (src, dst) in enumerate(zip(table_refs, tables))
    ]
    table_loads[6].start()
    table_loads[0].start()
    loads = [
        pltpu.make_async_copy(own_u, own_uv, sems.at[0]),
        pltpu.make_async_copy(kern, kern_v, sems.at[1]),
        copy_rows(own0, 0, own_v.at[0], 0, ROWS, sems.at[2]),
        copy_rows(own1, 0, own_v.at[1], 0, ROWS, sems.at[3]),
    ]
    later = []
    if earlier:
        later = [copy_rows(earlier[0].at[p], 0, z, p * ROWS, ROWS, sems.at[4 + p]) for p in range(2)]
        loads.append(pltpu.make_async_copy(earlier[1], before_v, sems.at[8 + len(pieces)]))

    for i, load in enumerate(par_loads):
        load.wait()
        for other in ([loads[0]], table_loads[1:5])[i]:
            other.start()
        widen_planes(par_v.at[pl.ds(i * ROWS // 2, ROWS // 2), :], par_f, i * G // 2)
    table_loads[6].wait()

    @pl.loop(0, QUADS // 4, unroll=2)
    def _(q):
        split_rows(par_f, sel, par_u, 4 * q, 4)

    half_y = G * Y_PITCH
    loads[0].wait()
    for load in loads[1:]:
        load.start()
    table_loads[5].start()
    table_loads[0].wait()

    @pl.loop(0, G // 2, unroll=8)
    def _(i):
        density = []
        for e in range(2):
            partner = par_u[2 * i + e].astype(F32)
            for p in range(2):
                density.append((own_uv[p, 2 * i + e].astype(F32) * partner).astype(BF16))
        out = dot(t1[...], lanes(*density))
        for e in range(2):
            for p in range(2):
                at = pl.ds(p * half_y + (2 * i + e) * Y_PITCH, Y_ROWS)
                yw[at, :] = out[:, (2 * e + p) * LANES : (2 * e + p + 1) * LANES]

    table_loads[1].wait()

    @pl.loop(0, HALF, unroll=7)
    def _(k1):
        def line(p, part):
            return yw[pl.ds(p * half_y + part * HALF + k1, G, stride=Y_PITCH), :].astype(BF16)

        out = dot(t2[...], stack(lanes(line(0, 0), line(1, 0)), lanes(line(0, 1), line(1, 1))))
        at = pl.ds(pl.multiple_of(k1 * G, 16), G)
        for p in range(2):
            for part in range(2):
                left = (2 * p + part) * LANES
                value = out[part * G : (part + 1) * G, p * LANES : (p + 1) * LANES]
                x34[at, left : left + LANES] = value.astype(BF16)

    loads[1].wait()
    table_loads[2].wait()

    many = 5

    @pl.loop(0, KPAD // many, unroll=2)
    def _(m):
        at = pl.ds(pl.multiple_of(m * many * G, 16), many * G)
        factor = kern_v[at, :]
        out = [
            dot(x34[at, 2 * p * LANES : 2 * (p + 1) * LANES], t3[...]).astype(BF16)
            for p in range(2)
        ]
        for part in range(4):
            spectrum = lanes(*[o[:, part * 64 : (part + 1) * 64] for o in out]).astype(F32)
            value = spectrum * factor
            for i in range(many):
                row = part * Z_ROWS + (many * m + i) * Z_PITCH
                z[pl.ds(row, G), :] = value[i * G : (i + 1) * G]

    table_loads[3].wait()

    @pl.loop(0, G // 4, unroll=6)
    def _(four):
        parts = []
        for e in range(4):
            k2 = 4 * four + e
            mirror = Z_PITCH + jnp.where(k2 == 0, 0, G - k2)
            parts.append(
                stack(
                    z[pl.ds(k2, G // 2, stride=Z_PITCH), :].astype(BF16),
                    z[pl.ds(2 * Z_ROWS + mirror, G // 2, stride=Z_PITCH), :].astype(BF16),
                    z[pl.ds(1 * Z_ROWS + k2, G // 2, stride=Z_PITCH), :].astype(BF16),
                    z[pl.ds(3 * Z_ROWS + mirror, G // 2, stride=Z_PITCH), :].astype(BF16),
                )
            )
        out = dot(a1[...], lanes(*parts))
        for e in range(4):
            at = (4 * four + e) * W_PITCH
            yw[pl.ds(at, 2 * G), :] = out[:, e * LANES : (e + 1) * LANES]

    for load in later:
        load.start()
    table_loads[4].wait()

    @pl.loop(0, G // 4, unroll=6)
    def _(four):
        parts = []
        for e in range(4):
            x1 = 4 * four + e
            parts.append(
                stack(
                    yw[pl.ds(x1, G, stride=W_PITCH), :].astype(BF16),
                    yw[pl.ds(G + x1, G, stride=W_PITCH), :].astype(BF16),
                )
            )
        out = dot(a2[...], lanes(*parts))
        for r in range(4):
            block = [
                lanes(
                    out[r * QUADS : (r + 1) * QUADS, e * LANES : (e + 1) * LANES],
                    out[G + r * QUADS : G + (r + 1) * QUADS, e * LANES : (e + 1) * LANES],
                )
                for e in range(4)
            ]
            at = pl.multiple_of((r // 2) * G * QUADS + four * 4 * QUADS, 16)
            left = (r % 2) * 2 * LANES
            x34[pl.ds(at, 4 * QUADS), left : left + 2 * LANES] = stack(*block).astype(BF16)

    table_loads[5].wait()
    for load in loads[2:] + later:
        load.wait()
    total_ref[...] = jnp.zeros_like(total_ref)
    block_rows = PLANES * QUADS
    scale = F32(1.0 / NGRID)

    def result(ch):
        at = pl.multiple_of(ch * block_rows, 16)
        low = x34[pl.ds(at, block_rows), :]
        high = x34[pl.ds(G * QUADS + at, block_rows), :]
        fields = [low, lanes(low[:, 2 * LANES :], high[:, : 2 * LANES]), high]
        flat = pl.ds(pl.multiple_of(ch * STEP_ROWS, 16), STEP_ROWS)
        own_f[...] = own_v[:, flat, :].astype(F32)
        total = jnp.zeros((QUADS, LANES), F32)
        for third in range(3):
            out = dot(fields[third], a3[third]) * scale
            for i in range(PLANES):
                plane = ch * PLANES + i
                partner = par_f[pl.ds(plane * F_PITCH + third, QUADS, stride=3), :]
                here = pl.ds(i * PLANE + third, QUADS, stride=3)
                there = pl.ds(plane * PLANE + third, QUADS, stride=3)
                sent = jnp.zeros((QUADS, LANES), F32)
                for p in range(2):
                    potential = out[i * QUADS : (i + 1) * QUADS, p * LANES : (p + 1) * LANES]
                    term = potential * partner
                    if earlier:
                        at = p * ROWS + plane * PLANE + third
                        term = term + z[pl.ds(at, QUADS, stride=3), :]
                    own_ov[p, there, :] = term
                    sent = sent + potential * own_f[p, here, :]
                total = total + sent * partner
                staged[here, :] = sent
        total_ref[...] += total
        par_ov[flat, :] = staged[...].astype(BF16)
        row = ch * STEP_ROWS
        copy_rows(own_ov, row, own_out, row, STEP_ROWS, sems.at[6]).start()

    first = 0
    for i, steps in enumerate(pieces):

        @pl.loop(0, steps, unroll=2 if steps % 2 == 0 else steps)
        def _(step):
            ch = first + step
            result(ch)
            source, row = ch * STEP_ROWS, step * STEP_ROWS
            copy_rows(par_ov, source, par_out[i], row, STEP_ROWS, sems.at[7 + i]).start()

        first += steps

    energy = jnp.zeros((8, LANES), F32) + jnp.sum(total_ref[...]) * F32(share)
    if earlier:
        energy = energy + before_v[...]
    energy_v[...] = energy
    report = pltpu.make_async_copy(energy_v, energy_out, sems.at[7 + len(pieces)])
    report.start()
    pltpu.make_async_copy(own_ov, own_out, sems.at[6]).wait()
    first = 0
    for i, steps in enumerate(pieces):
        rows = steps * STEP_ROWS
        copy_rows(par_ov, first, par_out[i], 0, rows, sems.at[7 + i]).wait()
        first += rows
    report.wait()


def pair_terms(own, own_u, partner, earlier, tables, kern, pieces, share, interpret=False):
    hbm = pl.BlockSpec(memory_space=pl.ANY)
    return pl.pallas_call(
        functools.partial(pairs_kernel, pieces, share),
        out_shape=(
            jax.ShapeDtypeStruct((2, ROWS, LANES), F32),
            *[jax.ShapeDtypeStruct((steps * STEP_ROWS, LANES), BF16) for steps in pieces],
            jax.ShapeDtypeStruct((8, LANES), F32),
        ),
        in_specs=[hbm] * (5 + len(earlier) + len(tables)),
        out_specs=(hbm,) * (2 + len(pieces)),
        scratch_shapes=[
            pltpu.VMEM((2, ROWS, LANES), BF16),
            pltpu.VMEM((2, G, G, LANES), BF16),
            pltpu.VMEM((KPAD * G, LANES), F32),
            pltpu.VMEM((2, ROWS, LANES), F32),
            pltpu.VMEM((ROWS, LANES), BF16),
            pltpu.VMEM((G * F_PITCH, LANES), F32),
            pltpu.VMEM((G, G, LANES), BF16),
            pltpu.VMEM((2 * G * Y_PITCH, LANES), F32),
            pltpu.VMEM((4 * Z_ROWS, LANES), F32),
            pltpu.VMEM((KPAD * G, 4 * LANES), BF16),
            pltpu.VMEM((2, STEP_ROWS, LANES), F32),
            pltpu.VMEM((STEP_ROWS, LANES), F32),
            pltpu.VMEM((QUADS, LANES), F32),
            pltpu.VMEM((8, LANES), F32),
            pltpu.VMEM((8, LANES), F32),
            *[pltpu.VMEM(table.shape, BF16) for table in tables],
            pltpu.SemaphoreType.DMA((2,)),
            pltpu.SemaphoreType.DMA((len(tables),)),
            pltpu.SemaphoreType.DMA((9 + len(pieces),)),
        ],
        compiler_params=pltpu.CompilerParams(vmem_limit_bytes=63 * MIB),
        cost_estimate=pl.CostEstimate(
            flops=20_000_000_000, bytes_accessed=20_000_000, transcendentals=0
        ),
        interpret=interpret,
        name="pair_terms",
    )(*own, own_u, kern, partner, *earlier, *tables)


def piece_kernel(first, size, own0, own1, terms, back0, back1, *rest):
    last = first + size == ROWS
    earlier = rest[: len(rest) - 12]
    out, gram_out, own_v, terms_v, back_v, out_v, gram_ref, gram_v, value_ref = rest[-12:-3]
    load_sems, gram_sems, store_sems = rest[-3:]
    rows = size // load_sems.shape[0]

    def loads(c):
        start = first + c * rows
        sources = [
            (own0, start, own_v.at[0]), (own1, start, own_v.at[1]), (terms, start, terms_v),
            (back0, start, back_v.at[0]), (back1, c * rows, back_v.at[1]),
        ]
        return [
            copy_rows(src, row, dst, c * rows, rows, load_sems.at[c, i])
            for i, (src, row, dst) in enumerate(sources)
        ]

    chunks = [loads(c) for c in range(load_sems.shape[0])]
    for chunk in chunks:
        for load in chunk:
            load.start()
    gram_loads = []
    if last:
        gram_loads = [
            pltpu.make_async_copy(src, gram_v.at[i], gram_sems.at[i])
            for i, src in enumerate(earlier[:-1])
        ]
        for load in gram_loads:
            load.start()
    gram_ref[...] = jnp.zeros_like(gram_ref)
    for c, chunk in enumerate(chunks):
        for load in chunk:
            load.wait()
        at = pl.ds(c * rows, rows)
        own = [own_v[i, at, :].astype(F32) for i in range(2)]
        for p in range(2):
            exchange = terms_v[p, at, :] + back_v[p, at, :].astype(F32)
            out_v[pl.ds(2 * c * rows + p, rows, stride=2), :] = exchange
            for i in range(2):
                product = (own[i] * exchange).reshape(-1, 8, LANES)
                gram_ref[i, p] += jnp.sum(product, axis=0)
        copy_rows(out_v, 2 * c * rows, out, 2 * (first + c * rows), 2 * rows, store_sems.at[0]).start()

    result = gram_ref
    if last:
        for load in gram_loads:
            load.wait()
        row = lax.broadcasted_iota(jnp.int32, (2, 2), 0)
        column = lax.broadcasted_iota(jnp.int32, (2, 2), 1)
        value = jnp.zeros((2, 2), F32)
        for i in range(2):
            for j in range(2):
                entry = gram_ref[i, j]
                for k in range(len(gram_loads)):
                    entry = entry + gram_v[k, i, j]
                value = jnp.where((row == i) & (column == j), jnp.sum(entry) * F32(1.0 / NGRID), value)
        value_ref[...] = value
        result = value_ref
    report = pltpu.make_async_copy(result, gram_out, store_sems.at[1])
    report.start()
    copy_rows(out_v, 0, out, 2 * first, 2 * size, store_sems.at[0]).wait()
    report.wait()


def add_piece(first, size, own, terms, back0, back1, grams, out, interpret=False):
    hbm = pl.BlockSpec(memory_space=pl.ANY)
    last = first + size == ROWS
    earlier = [] if out is None else [*(grams if last else []), out]
    gram_shape = (2, 2, 8, LANES)
    return pl.pallas_call(
        functools.partial(piece_kernel, first, size),
        out_shape=(
            jax.ShapeDtypeStruct((2 * ROWS, LANES), F32),
            jax.ShapeDtypeStruct((2, 2) if last else gram_shape, F32),
        ),
        in_specs=[hbm] * (5 + len(earlier)),
        out_specs=(hbm, hbm),
        scratch_shapes=[
            pltpu.VMEM((2, size, LANES), BF16),
            pltpu.VMEM((2, size, LANES), F32),
            pltpu.VMEM((2, size, LANES), BF16),
            pltpu.VMEM((2 * size, LANES), F32),
            pltpu.VMEM(gram_shape, F32),
            pltpu.VMEM((len(PIECES), *gram_shape), F32),
            pltpu.VMEM((2, 2), F32),
            pltpu.SemaphoreType.DMA((2 * size // STEP_ROWS, 5)),
            pltpu.SemaphoreType.DMA((len(PIECES),)),
            pltpu.SemaphoreType.DMA((2,)),
        ],
        input_output_aliases={4 + len(earlier): 0} if earlier else {},
        compiler_params=pltpu.CompilerParams(vmem_limit_bytes=52 * MIB),
        cost_estimate=cost(24 * size * LANES),
        interpret=interpret,
        name="add_piece",
    )(*own, terms, back0, back1, *earlier)


def from_behind(block, axis, distance):
    size = lax.axis_size(axis)
    return lax.ppermute(block, axis, [((i - distance) % size, i) for i in range(size)])


def after(values, other):
    return lax.optimization_barrier((values, other))[0]


def per_device(orbitals):
    tables = section_tables()
    kern = screening()
    size = lax.axis_size("band")
    share = -2.0 / (NGRID * 2 * size * orbitals.shape[0])
    raw = orbitals.reshape(2, ROWS, LANES).transpose(1, 0, 2).reshape(2 * ROWS, LANES)
    own = [take_band(raw, 0)]
    own.append(take_band(raw, 1, own))
    previous = [from_behind(part, "band", 1) for part in own]
    own_u = padded_rows(own, tables[-1])
    terms, back0, energy = pair_terms(
        own, own_u, previous[0], (), tables, kern, (STEPS,), share
    )
    back0 = from_behind(back0, "band", -1)
    terms, *sent, energy = pair_terms(
        own, own_u, previous[1], (terms, energy), tables, kern, PIECES, share
    )
    back1 = [from_behind(piece, "band", -1) for piece in sent]

    steps = []
    if size & (size - 1):
        energy = lax.psum(energy, "band")
    else:
        swap = [(i, i ^ 1) for i in range(size)]
        energy = energy + lax.ppermute(energy, "band", swap)
        steps = [1 << b for b in range(1, size.bit_length() - 1)]
        steps = [b for b in steps if b != 2] + [b for b in steps if b == 2]
        steps = [[(i, i ^ (b if i % 2 else steps[0])) for i in range(size)] for b in steps]
    while len(steps) > len(back1) - 1:
        energy = energy + lax.ppermute(energy, "band", steps.pop(0))
    exchange, grams = None, []
    first = 0
    for count, piece in zip(PIECES, back1):
        count *= STEP_ROWS
        got, last = None, piece is back1[-1]
        if last and size & (size - 1) == 0:
            got = lax.ppermute(energy, "band", swap)
        elif steps:
            got = lax.ppermute(energy, "band", steps.pop(0))
        exchange, gram = add_piece(first, count, own, terms, back0, piece, grams, exchange)
        if got is not None and last:
            odd = lax.axis_index("band") % 2 == 1
            energy = jnp.where(odd, energy[:1, :1], after(got, gram)[:1, :1])
        elif got is not None:
            energy = energy + after(got, gram)
        grams.append(gram)
        first += count
    exchange = exchange.reshape(ROWS, 2, LANES).transpose(1, 0, 2).reshape(2, NGRID)
    return exchange, gram, energy[0, 0]


def solution(mesh):
    return jax.shard_map(
        per_device,
        mesh=mesh,
        in_specs=(P("band", None),),
        out_specs=(P("band", None), P("band", None), P()),
        check_vma=False,
    )
```

```python
import functools

import jax
import jax.numpy as jnp
import ml_dtypes
import numpy as np
from jax import lax
from jax.experimental import pallas as pl
from jax.experimental.pallas import tpu as pltpu
from jax.sharding import PartitionSpec as P

G = 96
HALF = G // 2 + 1
NGRID = G * G * G
LANES = 128
ROWS = NGRID // LANES
PLANE = G * G // LANES
QUADS = G // 4
KPAD = HALF + 1
Y_ROWS = 104
Y_PITCH = Y_ROWS + 1
Z_PITCH = G + 1
W_PITCH = 2 * G + 1
Z_ROWS = KPAD * Z_PITCH
F_PITCH = PLANE + 1
PLANES = 16
STEP_ROWS = PLANES * PLANE
STEPS = G // PLANES
PIECES = (4, 2)
WAVE_UNIT = 0.05
SCREEN_SQ = 0.0121
MIB = 1024 * 1024
BF16 = jnp.bfloat16
F32 = jnp.float32


def dft_tables():
    n = np.arange(G)
    phases = (n[:, None] * n[None, :]) % G
    angles = phases.astype(np.float32) * np.float32(2.0 * np.pi / G)
    rounded = [f(angles).astype(ml_dtypes.bfloat16).astype(np.float32) for f in (np.cos, np.sin)]
    return rounded[0], rounded[1]


def section_tables():
    c, s = dft_tables()
    h = HALF
    t1 = np.zeros((Y_ROWS, G), np.float32)
    t1[:h] = c[:h]
    t1[h : 2 * h] = -s[:h]
    t2 = np.block([[c, s], [-s, c]])
    t3 = np.zeros((2, LANES, 4, 64), np.float32)
    back = (G - np.arange(h)) % G
    t3[0, :G, 0, :h] = c[:h].T
    t3[1, :G, 0, :h] = s[:h].T
    t3[0, :G, 1, :h] = -s[:h].T
    t3[1, :G, 1, :h] = c[:h].T
    t3[0, :G, 2, :h] = c[back].T
    t3[1, :G, 2, :h] = s[back].T
    t3[0, :G, 3, :h] = s[back].T
    t3[1, :G, 3, :h] = -c[back].T
    t3 = t3.reshape(2 * LANES, 4 * 64)
    order = np.concatenate([np.arange(G // 2), G - 1 - np.arange(G // 2)])
    a1 = np.block([[c[:, order], -s[:, order]], [s[:, order], c[:, order]]])
    rows = np.arange(G).reshape(QUADS, 4).T.reshape(-1)
    a2 = np.block([[c[rows], -s[rows]], [s[rows], c[rows]]])
    weight = np.full((h, 1), 2.0, np.float32)
    weight[0] = weight[h - 1] = 1.0
    a3 = np.zeros((3, 2, 2, 2, 64, 2, LANES), np.float32)
    for third in range(3):
        for lane in range(LANES):
            r, x3 = divmod(third * LANES + lane, G)
            for p in range(2):
                a3[third, r - third, 0, p, :h, p, lane] = weight[:, 0] * c[x3, :h]
                a3[third, r - third, 1, p, :h, p, lane] = -weight[:, 0] * s[x3, :h]
    a3 = a3.reshape(3, 4 * LANES, 2 * LANES)
    sel = np.zeros((2, 2 * LANES, 2 * LANES), np.float32)
    for r in range(4):
        for x in range(G):
            sel[r // 2, r * G + x - (r // 2) * LANES, (r % 2) * LANES + x] = 1.0
    return [t.astype(ml_dtypes.bfloat16) for t in (t1, t2, t3, a1, a2, a3, sel)]


def screening():
    n = np.arange(G)
    m = np.where(n <= G // 2, n, n - G).astype(np.float64)
    sq = m * m
    q2 = WAVE_UNIT * (sq[:HALF, None, None] + sq[None, :, None] + sq[None, None, :HALF])
    safe = np.where(q2 > 0, q2, 1.0)
    kern = 4.0 * np.pi * (1.0 - np.exp(-q2 / (4.0 * SCREEN_SQ))) / safe
    kern = np.where(q2 > 0, kern, np.pi / SCREEN_SQ)
    out = np.zeros((KPAD, G, 2, 64), np.float32)
    out[:HALF, :, :, :HALF] = kern[:, :, None, :]
    return out.reshape(KPAD * G, LANES)


def cost(size):
    return pl.CostEstimate(flops=0, bytes_accessed=size, transcendentals=0)


def dot(a, b):
    return jnp.dot(a, b, preferred_element_type=F32)


def lanes(*parts):
    return jnp.concatenate(parts, axis=1)


def stack(*parts):
    return jnp.concatenate(parts, axis=0)


def split_rows(src, sel_ref, out, first, count):
    rows = [
        [src[pl.ds(3 * (first + i) + s, G, stride=F_PITCH), :].astype(BF16) for s in range(3)]
        for i in range(count)
    ]
    for half in range(2):
        part = dot(stack(*[lanes(r[half], r[half + 1]) for r in rows]), sel_ref[half])
        for i in range(count):
            for e in range(2):
                value = part[i * G : (i + 1) * G, e * LANES : (e + 1) * LANES]
                out[4 * (first + i) + 2 * half + e] = value.astype(BF16)


def widen_planes(src, dst, first):
    @pl.loop(0, src.shape[0] // (2 * PLANE), unroll=4)
    def _(i):
        value = src[pl.ds(pl.multiple_of(i * 2 * PLANE, 16), 2 * PLANE), :].astype(F32)
        dst[pl.ds((first + 2 * i) * F_PITCH, PLANE), :] = value[:PLANE]
        dst[pl.ds((first + 2 * i + 1) * F_PITCH, PLANE), :] = value[PLANE:]


def rows_of(ref, first, count):
    at = pl.ds(first, count)
    return ref.at[at, :] if len(ref.shape) == 2 else ref.at[:, at, :]


def copy_rows(src, src_row, dst, dst_row, count, sem):
    return pltpu.make_async_copy(rows_of(src, src_row, count), rows_of(dst, dst_row, count), sem)


def band_kernel(p, raw, *refs):
    out, raw_v, out_v, load_sems, store_sem = refs[-5:]
    chunks = load_sems.shape[0]
    rows = out.shape[0] // chunks
    loads = [
        copy_rows(raw, 2 * c * rows, raw_v, 2 * c * rows, 2 * rows, load_sems.at[c])
        for c in range(chunks)
    ]
    for load in loads:
        load.start()
    shape = (LANES, 2 * LANES)
    row = lax.broadcasted_iota(jnp.int32, shape, 0)
    column = lax.broadcasted_iota(jnp.int32, shape, 1)
    pick = jnp.where(column == 2 * row + p, F32(1.0), F32(0.0)).astype(BF16)
    for c, load in enumerate(loads):
        load.wait()
        for row in range(c * rows, (c + 1) * rows, LANES):
            value = dot(pick, raw_v[2 * row : 2 * row + 2 * LANES, :])
            out_v[row : row + LANES, :] = value.astype(BF16)
        copy_rows(out_v, c * rows, out, c * rows, rows, store_sem).start()
    pltpu.make_async_copy(out_v, out, store_sem).wait()


def take_band(raw, p, earlier=(), interpret=False):
    hbm = pl.BlockSpec(memory_space=pl.ANY)
    return pl.pallas_call(
        functools.partial(band_kernel, p),
        out_shape=jax.ShapeDtypeStruct((ROWS, LANES), BF16),
        in_specs=[hbm] * (1 + len(earlier)),
        out_specs=hbm,
        scratch_shapes=[
            pltpu.VMEM((2 * ROWS, LANES), BF16),
            pltpu.VMEM((ROWS, LANES), BF16),
            pltpu.SemaphoreType.DMA((9,)),
            pltpu.SemaphoreType.DMA,
        ],
        compiler_params=pltpu.CompilerParams(vmem_limit_bytes=63 * MIB),
        cost_estimate=cost(6 * ROWS * LANES),
        interpret=interpret,
        name="take_band",
    )(raw, *earlier)


def rows_kernel(own0, own1, sel, out, wide):
    for p, own in enumerate((own0, own1)):
        widen_planes(own, wide, 0)

        @pl.loop(0, QUADS // 4, unroll=2)
        def _(q):
            split_rows(wide, sel, out.at[p], 4 * q, 4)


def padded_rows(own, sel, interpret=False):
    vmem = pl.BlockSpec(memory_space=pltpu.VMEM)
    return pl.pallas_call(
        rows_kernel,
        out_shape=jax.ShapeDtypeStruct((2, G, G, LANES), BF16),
        in_specs=[vmem] * 3,
        out_specs=vmem,
        scratch_shapes=[pltpu.VMEM((G * F_PITCH, LANES), F32)],
        compiler_params=pltpu.CompilerParams(vmem_limit_bytes=63 * MIB),
        cost_estimate=cost(16 * NGRID),
        interpret=interpret,
        name="padded_rows",
    )(*own, sel)


def pairs_kernel(pieces, share, own0, own1, own_u, kern, par, *refs):
    earlier = []
    if len(pieces) > 1:
        earlier, refs = refs[:2], refs[2:]
    table_refs, own_out = refs[:7], refs[7]
    par_out, energy_out = refs[8 : 8 + len(pieces)], refs[8 + len(pieces)]
    own_v, own_uv, kern_v, own_ov, par_ov, par_f, par_u, yw, z, x34 = refs[9 + len(pieces) : -15]
    own_f, staged, total_ref, energy_v, before_v = refs[-15:-10]
    tables, (par_sems, table_sems, sems) = refs[-10:-3], refs[-3:]
    t1, t2, t3, a1, a2, a3, sel = tables
    par_v = par_ov
    par_loads = []
    for first in (0, ROWS // 2):
        sem = par_sems.at[len(par_loads)]
        par_loads.append(copy_rows(par, first, par_v, first, ROWS // 2, sem))
    for load in par_loads:
        load.start()
    table_loads = [
        pltpu.make_async_copy(src, dst, table_sems.at[i])
        for i, (src, dst) in enumerate(zip(table_refs, tables))
    ]
    table_loads[6].start()
    table_loads[0].start()
    loads = [
        pltpu.make_async_copy(own_u, own_uv, sems.at[0]),
        pltpu.make_async_copy(kern, kern_v, sems.at[1]),
        copy_rows(own0, 0, own_v.at[0], 0, ROWS, sems.at[2]),
        copy_rows(own1, 0, own_v.at[1], 0, ROWS, sems.at[3]),
    ]
    later = []
    if earlier:
        later = [copy_rows(earlier[0].at[p], 0, z, p * ROWS, ROWS, sems.at[4 + p]) for p in range(2)]
        loads.append(pltpu.make_async_copy(earlier[1], before_v, sems.at[8 + len(pieces)]))

    for i, load in enumerate(par_loads):
        load.wait()
        for other in ([loads[0]], table_loads[1:5])[i]:
            other.start()
        widen_planes(par_v.at[pl.ds(i * ROWS // 2, ROWS // 2), :], par_f, i * G // 2)
    table_loads[6].wait()

    @pl.loop(0, QUADS // 4, unroll=2)
    def _(q):
        split_rows(par_f, sel, par_u, 4 * q, 4)

    half_y = G * Y_PITCH
    loads[0].wait()
    for load in loads[1:]:
        load.start()
    table_loads[5].start()
    table_loads[0].wait()

    @pl.loop(0, G // 2, unroll=8)
    def _(i):
        density = []
        for e in range(2):
            partner = par_u[2 * i + e].astype(F32)
            for p in range(2):
                density.append((own_uv[p, 2 * i + e].astype(F32) * partner).astype(BF16))
        out = dot(t1[...], lanes(*density))
        for e in range(2):
            for p in range(2):
                at = pl.ds(p * half_y + (2 * i + e) * Y_PITCH, Y_ROWS)
                yw[at, :] = out[:, (2 * e + p) * LANES : (2 * e + p + 1) * LANES]

    table_loads[1].wait()

    @pl.loop(0, HALF, unroll=7)
    def _(k1):
        def line(p, part):
            return yw[pl.ds(p * half_y + part * HALF + k1, G, stride=Y_PITCH), :].astype(BF16)

        out = dot(t2[...], stack(lanes(line(0, 0), line(1, 0)), lanes(line(0, 1), line(1, 1))))
        at = pl.ds(pl.multiple_of(k1 * G, 16), G)
        for p in range(2):
            for part in range(2):
                left = (2 * p + part) * LANES
                value = out[part * G : (part + 1) * G, p * LANES : (p + 1) * LANES]
                x34[at, left : left + LANES] = value.astype(BF16)

    loads[1].wait()
    table_loads[2].wait()

    many = 5

    @pl.loop(0, KPAD // many, unroll=2)
    def _(m):
        at = pl.ds(pl.multiple_of(m * many * G, 16), many * G)
        factor = kern_v[at, :]
        out = [
            dot(x34[at, 2 * p * LANES : 2 * (p + 1) * LANES], t3[...]).astype(BF16)
            for p in range(2)
        ]
        for part in range(4):
            spectrum = lanes(*[o[:, part * 64 : (part + 1) * 64] for o in out]).astype(F32)
            value = spectrum * factor
            for i in range(many):
                row = part * Z_ROWS + (many * m + i) * Z_PITCH
                z[pl.ds(row, G), :] = value[i * G : (i + 1) * G]

    table_loads[3].wait()

    @pl.loop(0, G // 4, unroll=6)
    def _(four):
        parts = []
        for e in range(4):
            k2 = 4 * four + e
            mirror = Z_PITCH + jnp.where(k2 == 0, 0, G - k2)
            parts.append(
                stack(
                    z[pl.ds(k2, G // 2, stride=Z_PITCH), :].astype(BF16),
                    z[pl.ds(2 * Z_ROWS + mirror, G // 2, stride=Z_PITCH), :].astype(BF16),
                    z[pl.ds(1 * Z_ROWS + k2, G // 2, stride=Z_PITCH), :].astype(BF16),
                    z[pl.ds(3 * Z_ROWS + mirror, G // 2, stride=Z_PITCH), :].astype(BF16),
                )
            )
        out = dot(a1[...], lanes(*parts))
        for e in range(4):
            at = (4 * four + e) * W_PITCH
            yw[pl.ds(at, 2 * G), :] = out[:, e * LANES : (e + 1) * LANES]

    for load in later:
        load.start()
    table_loads[4].wait()

    @pl.loop(0, G // 4, unroll=6)
    def _(four):
        parts = []
        for e in range(4):
            x1 = 4 * four + e
            parts.append(
                stack(
                    yw[pl.ds(x1, G, stride=W_PITCH), :].astype(BF16),
                    yw[pl.ds(G + x1, G, stride=W_PITCH), :].astype(BF16),
                )
            )
        out = dot(a2[...], lanes(*parts))
        for r in range(4):
            block = [
                lanes(
                    out[r * QUADS : (r + 1) * QUADS, e * LANES : (e + 1) * LANES],
                    out[G + r * QUADS : G + (r + 1) * QUADS, e * LANES : (e + 1) * LANES],
                )
                for e in range(4)
            ]
            at = pl.multiple_of((r // 2) * G * QUADS + four * 4 * QUADS, 16)
            left = (r % 2) * 2 * LANES
            x34[pl.ds(at, 4 * QUADS), left : left + 2 * LANES] = stack(*block).astype(BF16)

    table_loads[5].wait()
    for load in loads[2:] + later:
        load.wait()
    total_ref[...] = jnp.zeros_like(total_ref)
    block_rows = PLANES * QUADS
    scale = F32(1.0 / NGRID)

    def result(ch):
        at = pl.multiple_of(ch * block_rows, 16)
        low = x34[pl.ds(at, block_rows), :]
        high = x34[pl.ds(G * QUADS + at, block_rows), :]
        fields = [low, lanes(low[:, 2 * LANES :], high[:, : 2 * LANES]), high]
        flat = pl.ds(pl.multiple_of(ch * STEP_ROWS, 16), STEP_ROWS)
        own_f[...] = own_v[:, flat, :].astype(F32)
        total = jnp.zeros((QUADS, LANES), F32)
        for third in range(3):
            out = dot(fields[third], a3[third]) * scale
            for i in range(PLANES):
                plane = ch * PLANES + i
                partner = par_f[pl.ds(plane * F_PITCH + third, QUADS, stride=3), :]
                here = pl.ds(i * PLANE + third, QUADS, stride=3)
                there = pl.ds(plane * PLANE + third, QUADS, stride=3)
                sent = jnp.zeros((QUADS, LANES), F32)
                for p in range(2):
                    potential = out[i * QUADS : (i + 1) * QUADS, p * LANES : (p + 1) * LANES]
                    term = potential * partner
                    if earlier:
                        at = p * ROWS + plane * PLANE + third
                        term = term + z[pl.ds(at, QUADS, stride=3), :]
                    own_ov[p, there, :] = term
                    sent = sent + potential * own_f[p, here, :]
                total = total + sent * partner
                staged[here, :] = sent
        total_ref[...] += total
        par_ov[flat, :] = staged[...].astype(BF16)
        row = ch * STEP_ROWS
        copy_rows(own_ov, row, own_out, row, STEP_ROWS, sems.at[6]).start()

    first = 0
    for i, steps in enumerate(pieces):

        @pl.loop(0, steps, unroll=2 if steps % 2 == 0 else steps)
        def _(step):
            ch = first + step
            result(ch)
            source, row = ch * STEP_ROWS, step * STEP_ROWS
            copy_rows(par_ov, source, par_out[i], row, STEP_ROWS, sems.at[7 + i]).start()

        first += steps

    energy = jnp.zeros((8, LANES), F32) + jnp.sum(total_ref[...]) * F32(share)
    if earlier:
        energy = energy + before_v[...]
    energy_v[...] = energy
    report = pltpu.make_async_copy(energy_v, energy_out, sems.at[7 + len(pieces)])
    report.start()
    pltpu.make_async_copy(own_ov, own_out, sems.at[6]).wait()
    first = 0
    for i, steps in enumerate(pieces):
        rows = steps * STEP_ROWS
        copy_rows(par_ov, first, par_out[i], 0, rows, sems.at[7 + i]).wait()
        first += rows
    report.wait()


def pair_terms(own, own_u, partner, earlier, tables, kern, pieces, share, interpret=False):
    hbm = pl.BlockSpec(memory_space=pl.ANY)
    return pl.pallas_call(
        functools.partial(pairs_kernel, pieces, share),
        out_shape=(
            jax.ShapeDtypeStruct((2, ROWS, LANES), F32),
            *[jax.ShapeDtypeStruct((steps * STEP_ROWS, LANES), BF16) for steps in pieces],
            jax.ShapeDtypeStruct((8, LANES), F32),
        ),
        in_specs=[hbm] * (5 + len(earlier) + len(tables)),
        out_specs=(hbm,) * (2 + len(pieces)),
        scratch_shapes=[
            pltpu.VMEM((2, ROWS, LANES), BF16),
            pltpu.VMEM((2, G, G, LANES), BF16),
            pltpu.VMEM((KPAD * G, LANES), F32),
            pltpu.VMEM((2, ROWS, LANES), F32),
            pltpu.VMEM((ROWS, LANES), BF16),
            pltpu.VMEM((G * F_PITCH, LANES), F32),
            pltpu.VMEM((G, G, LANES), BF16),
            pltpu.VMEM((2 * G * Y_PITCH, LANES), F32),
            pltpu.VMEM((4 * Z_ROWS, LANES), F32),
            pltpu.VMEM((KPAD * G, 4 * LANES), BF16),
            pltpu.VMEM((2, STEP_ROWS, LANES), F32),
            pltpu.VMEM((STEP_ROWS, LANES), F32),
            pltpu.VMEM((QUADS, LANES), F32),
            pltpu.VMEM((8, LANES), F32),
            pltpu.VMEM((8, LANES), F32),
            *[pltpu.VMEM(table.shape, BF16) for table in tables],
            pltpu.SemaphoreType.DMA((2,)),
            pltpu.SemaphoreType.DMA((len(tables),)),
            pltpu.SemaphoreType.DMA((9 + len(pieces),)),
        ],
        compiler_params=pltpu.CompilerParams(vmem_limit_bytes=63 * MIB),
        cost_estimate=pl.CostEstimate(
            flops=20_000_000_000, bytes_accessed=20_000_000, transcendentals=0
        ),
        interpret=interpret,
        name="pair_terms",
    )(*own, own_u, kern, partner, *earlier, *tables)


def piece_kernel(first, size, own0, own1, terms, back0, back1, *rest):
    last = first + size == ROWS
    earlier = rest[: len(rest) - 12]
    out, gram_out, own_v, terms_v, back_v, out_v, gram_ref, gram_v, value_ref = rest[-12:-3]
    load_sems, gram_sems, store_sems = rest[-3:]
    rows = size // load_sems.shape[0]

    def loads(c):
        start = first + c * rows
        sources = [
            (own0, start, own_v.at[0]), (own1, start, own_v.at[1]), (terms, start, terms_v),
            (back0, start, back_v.at[0]), (back1, c * rows, back_v.at[1]),
        ]
        return [
            copy_rows(src, row, dst, c * rows, rows, load_sems.at[c, i])
            for i, (src, row, dst) in enumerate(sources)
        ]

    chunks = [loads(c) for c in range(load_sems.shape[0])]
    for chunk in chunks:
        for load in chunk:
            load.start()
    gram_loads = []
    if last:
        gram_loads = [
            pltpu.make_async_copy(src, gram_v.at[i], gram_sems.at[i])
            for i, src in enumerate(earlier[:-1])
        ]
        for load in gram_loads:
            load.start()
    gram_ref[...] = jnp.zeros_like(gram_ref)
    for c, chunk in enumerate(chunks):
        for load in chunk:
            load.wait()
        at = pl.ds(c * rows, rows)
        own = [own_v[i, at, :].astype(F32) for i in range(2)]
        for p in range(2):
            exchange = terms_v[p, at, :] + back_v[p, at, :].astype(F32)
            out_v[pl.ds(2 * c * rows + p, rows, stride=2), :] = exchange
            for i in range(2):
                product = (own[i] * exchange).reshape(-1, 8, LANES)
                gram_ref[i, p] += jnp.sum(product, axis=0)
        copy_rows(out_v, 2 * c * rows, out, 2 * (first + c * rows), 2 * rows, store_sems.at[0]).start()

    result = gram_ref
    if last:
        for load in gram_loads:
            load.wait()
        row = lax.broadcasted_iota(jnp.int32, (2, 2), 0)
        column = lax.broadcasted_iota(jnp.int32, (2, 2), 1)
        value = jnp.zeros((2, 2), F32)
        for i in range(2):
            for j in range(2):
                entry = gram_ref[i, j]
                for k in range(len(gram_loads)):
                    entry = entry + gram_v[k, i, j]
                value = jnp.where((row == i) & (column == j), jnp.sum(entry) * F32(1.0 / NGRID), value)
        value_ref[...] = value
        result = value_ref
    report = pltpu.make_async_copy(result, gram_out, store_sems.at[1])
    report.start()
    copy_rows(out_v, 0, out, 2 * first, 2 * size, store_sems.at[0]).wait()
    report.wait()


def add_piece(first, size, own, terms, back0, back1, grams, out, interpret=False):
    hbm = pl.BlockSpec(memory_space=pl.ANY)
    last = first + size == ROWS
    earlier = [] if out is None else [*(grams if last else []), out]
    gram_shape = (2, 2, 8, LANES)
    return pl.pallas_call(
        functools.partial(piece_kernel, first, size),
        out_shape=(
            jax.ShapeDtypeStruct((2 * ROWS, LANES), F32),
            jax.ShapeDtypeStruct((2, 2) if last else gram_shape, F32),
        ),
        in_specs=[hbm] * (5 + len(earlier)),
        out_specs=(hbm, hbm),
        scratch_shapes=[
            pltpu.VMEM((2, size, LANES), BF16),
            pltpu.VMEM((2, size, LANES), F32),
            pltpu.VMEM((2, size, LANES), BF16),
            pltpu.VMEM((2 * size, LANES), F32),
            pltpu.VMEM(gram_shape, F32),
            pltpu.VMEM((len(PIECES), *gram_shape), F32),
            pltpu.VMEM((2, 2), F32),
            pltpu.SemaphoreType.DMA((2 * size // STEP_ROWS, 5)),
            pltpu.SemaphoreType.DMA((len(PIECES),)),
            pltpu.SemaphoreType.DMA((2,)),
        ],
        input_output_aliases={4 + len(earlier): 0} if earlier else {},
        compiler_params=pltpu.CompilerParams(vmem_limit_bytes=52 * MIB),
        cost_estimate=cost(24 * size * LANES),
        interpret=interpret,
        name="add_piece",
    )(*own, terms, back0, back1, *earlier)


def from_behind(block, axis, distance):
    size = lax.axis_size(axis)
    return lax.ppermute(block, axis, [((i - distance) % size, i) for i in range(size)])


def after(values, other):
    return lax.optimization_barrier((values, other))[0]


def per_device(orbitals):
    tables = section_tables()
    kern = screening()
    size = lax.axis_size("band")
    share = -2.0 / (NGRID * 2 * size * orbitals.shape[0])
    raw = orbitals.reshape(2, ROWS, LANES).transpose(1, 0, 2).reshape(2 * ROWS, LANES)
    own = [take_band(raw, 0)]
    own.append(take_band(raw, 1, own))
    previous = [from_behind(part, "band", 1) for part in own]
    own_u = padded_rows(own, tables[-1])
    terms, back0, energy = pair_terms(
        own, own_u, previous[0], (), tables, kern, (STEPS,), share
    )
    back0 = from_behind(back0, "band", -1)
    terms, *sent, energy = pair_terms(
        own, own_u, previous[1], (terms, energy), tables, kern, PIECES, share
    )
    back1 = [from_behind(piece, "band", -1) for piece in sent]

    steps = []
    if size & (size - 1):
        energy = lax.psum(energy, "band")
    else:
        swap = [(i, i ^ 1) for i in range(size)]
        energy = energy + lax.ppermute(energy, "band", swap)
        steps = [1 << b for b in range(1, size.bit_length() - 1)]
        steps = [b for b in steps if b != 2] + [b for b in steps if b == 2]
        steps = [[(i, i ^ b) for i in range(size) if i % 2 or b == 4] for b in steps]
    while len(steps) > len(back1):
        energy = energy + lax.ppermute(energy, "band", steps.pop(0))
    exchange, grams = None, []
    first = 0
    for count, piece in zip(PIECES, back1):
        count *= STEP_ROWS
        got, last = None, piece is back1[-1]
        if last and size & (size - 1) == 0:
            got = lax.ppermute(energy, "band", swap)
        elif steps:
            got = lax.ppermute(energy, "band", steps.pop(0))
        exchange, gram = add_piece(first, count, own, terms, back0, piece, grams, exchange)
        while not last and steps:
            energy = energy + after(got, gram)
            got = lax.ppermute(energy, "band", steps.pop(0))
        if got is not None and last:
            odd = lax.axis_index("band") % 2 == 1
            energy = jnp.where(odd, energy[:1, :1], after(got, gram)[:1, :1])
        elif got is not None:
            energy = energy + after(got, gram)
        grams.append(gram)
        first += count
    exchange = exchange.reshape(ROWS, 2, LANES).transpose(1, 0, 2).reshape(2, NGRID)
    return exchange, gram, energy[0, 0]


def solution(mesh):
    return jax.shard_map(
        per_device,
        mesh=mesh,
        in_specs=(P("band", None),),
        out_specs=(P("band", None), P("band", None), P()),
        check_vma=False,
    )
```

```python
import functools

import jax
import jax.numpy as jnp
import ml_dtypes
import numpy as np
from jax import lax
from jax.experimental import pallas as pl
from jax.experimental.pallas import tpu as pltpu
from jax.sharding import PartitionSpec as P

G = 96
HALF = G // 2 + 1
NGRID = G * G * G
LANES = 128
ROWS = NGRID // LANES
PLANE = G * G // LANES
QUADS = G // 4
KPAD = HALF + 1
Y_ROWS = 104
Y_PITCH = Y_ROWS + 1
Z_PITCH = G + 1
W_PITCH = 2 * G + 1
Z_ROWS = KPAD * Z_PITCH
F_PITCH = PLANE + 1
PLANES = 16
STEP_ROWS = PLANES * PLANE
STEPS = G // PLANES
PIECES = (4, 2)
WAVE_UNIT = 0.05
SCREEN_SQ = 0.0121
MIB = 1024 * 1024
BF16 = jnp.bfloat16
F32 = jnp.float32


def dft_tables():
    n = np.arange(G)
    phases = (n[:, None] * n[None, :]) % G
    angles = phases.astype(np.float32) * np.float32(2.0 * np.pi / G)
    rounded = [f(angles).astype(ml_dtypes.bfloat16).astype(np.float32) for f in (np.cos, np.sin)]
    return rounded[0], rounded[1]


def section_tables():
    c, s = dft_tables()
    h = HALF
    t1 = np.zeros((Y_ROWS, G), np.float32)
    t1[:h] = c[:h]
    t1[h : 2 * h] = -s[:h]
    t2 = np.block([[c, s], [-s, c]])
    t3 = np.zeros((2, LANES, 4, 64), np.float32)
    back = (G - np.arange(h)) % G
    t3[0, :G, 0, :h] = c[:h].T
    t3[1, :G, 0, :h] = s[:h].T
    t3[0, :G, 1, :h] = -s[:h].T
    t3[1, :G, 1, :h] = c[:h].T
    t3[0, :G, 2, :h] = c[back].T
    t3[1, :G, 2, :h] = s[back].T
    t3[0, :G, 3, :h] = s[back].T
    t3[1, :G, 3, :h] = -c[back].T
    t3 = t3.reshape(2 * LANES, 4 * 64)
    order = np.concatenate([np.arange(G // 2), G - 1 - np.arange(G // 2)])
    a1 = np.block([[c[:, order], -s[:, order]], [s[:, order], c[:, order]]])
    rows = np.arange(G).reshape(QUADS, 4).T.reshape(-1)
    a2 = np.block([[c[rows], -s[rows]], [s[rows], c[rows]]])
    weight = np.full((h, 1), 2.0, np.float32)
    weight[0] = weight[h - 1] = 1.0
    a3 = np.zeros((3, 2, 2, 2, 64, 2, LANES), np.float32)
    for third in range(3):
        for lane in range(LANES):
            r, x3 = divmod(third * LANES + lane, G)
            for p in range(2):
                a3[third, r - third, 0, p, :h, p, lane] = weight[:, 0] * c[x3, :h]
                a3[third, r - third, 1, p, :h, p, lane] = -weight[:, 0] * s[x3, :h]
    a3 = a3.reshape(3, 4 * LANES, 2 * LANES)
    sel = np.zeros((2, 2 * LANES, 2 * LANES), np.float32)
    for r in range(4):
        for x in range(G):
            sel[r // 2, r * G + x - (r // 2) * LANES, (r % 2) * LANES + x] = 1.0
    return [t.astype(ml_dtypes.bfloat16) for t in (t1, t2, t3, a1, a2, a3, sel)]


def screening():
    n = np.arange(G)
    m = np.where(n <= G // 2, n, n - G).astype(np.float64)
    sq = m * m
    q2 = WAVE_UNIT * (sq[:HALF, None, None] + sq[None, :, None] + sq[None, None, :HALF])
    safe = np.where(q2 > 0, q2, 1.0)
    kern = 4.0 * np.pi * (1.0 - np.exp(-q2 / (4.0 * SCREEN_SQ))) / safe
    kern = np.where(q2 > 0, kern, np.pi / SCREEN_SQ)
    out = np.zeros((KPAD, G, 2, 64), np.float32)
    out[:HALF, :, :, :HALF] = kern[:, :, None, :]
    return out.reshape(KPAD * G, LANES)


def cost(size):
    return pl.CostEstimate(flops=0, bytes_accessed=size, transcendentals=0)


def dot(a, b):
    return jnp.dot(a, b, preferred_element_type=F32)


def lanes(*parts):
    return jnp.concatenate(parts, axis=1)


def stack(*parts):
    return jnp.concatenate(parts, axis=0)


def split_rows(src, sel_ref, out, first, count):
    rows = [
        [src[pl.ds(3 * (first + i) + s, G, stride=F_PITCH), :].astype(BF16) for s in range(3)]
        for i in range(count)
    ]
    for half in range(2):
        part = dot(stack(*[lanes(r[half], r[half + 1]) for r in rows]), sel_ref[half])
        for i in range(count):
            for e in range(2):
                value = part[i * G : (i + 1) * G, e * LANES : (e + 1) * LANES]
                out[4 * (first + i) + 2 * half + e] = value.astype(BF16)


def widen_planes(src, dst, first):
    @pl.loop(0, src.shape[0] // (2 * PLANE), unroll=8)
    def _(i):
        value = src[pl.ds(pl.multiple_of(i * 2 * PLANE, 16), 2 * PLANE), :].astype(F32)
        dst[pl.ds((first + 2 * i) * F_PITCH, PLANE), :] = value[:PLANE]
        dst[pl.ds((first + 2 * i + 1) * F_PITCH, PLANE), :] = value[PLANE:]


def rows_of(ref, first, count):
    at = pl.ds(first, count)
    return ref.at[at, :] if len(ref.shape) == 2 else ref.at[:, at, :]


def copy_rows(src, src_row, dst, dst_row, count, sem):
    return pltpu.make_async_copy(rows_of(src, src_row, count), rows_of(dst, dst_row, count), sem)


def band_kernel(p, raw, *refs):
    out, raw_v, out_v, load_sems, store_sem = refs[-5:]
    chunks = load_sems.shape[0]
    rows = out.shape[0] // chunks
    loads = [
        copy_rows(raw, 2 * c * rows, raw_v, 2 * c * rows, 2 * rows, load_sems.at[c])
        for c in range(chunks)
    ]
    for load in loads:
        load.start()
    shape = (LANES, 2 * LANES)
    row = lax.broadcasted_iota(jnp.int32, shape, 0)
    column = lax.broadcasted_iota(jnp.int32, shape, 1)
    pick = jnp.where(column == 2 * row + p, F32(1.0), F32(0.0)).astype(BF16)
    for c, load in enumerate(loads):
        load.wait()
        for row in range(c * rows, (c + 1) * rows, LANES):
            value = dot(pick, raw_v[2 * row : 2 * row + 2 * LANES, :])
            out_v[row : row + LANES, :] = value.astype(BF16)
        copy_rows(out_v, c * rows, out, c * rows, rows, store_sem).start()
    pltpu.make_async_copy(out_v, out, store_sem).wait()


def take_band(raw, p, earlier=(), interpret=False):
    hbm = pl.BlockSpec(memory_space=pl.ANY)
    return pl.pallas_call(
        functools.partial(band_kernel, p),
        out_shape=jax.ShapeDtypeStruct((ROWS, LANES), BF16),
        in_specs=[hbm] * (1 + len(earlier)),
        out_specs=hbm,
        scratch_shapes=[
            pltpu.VMEM((2 * ROWS, LANES), BF16),
            pltpu.VMEM((ROWS, LANES), BF16),
            pltpu.SemaphoreType.DMA((9,)),
            pltpu.SemaphoreType.DMA,
        ],
        compiler_params=pltpu.CompilerParams(vmem_limit_bytes=63 * MIB),
        cost_estimate=cost(6 * ROWS * LANES),
        interpret=interpret,
        name="take_band",
    )(raw, *earlier)


def rows_kernel(own0, own1, sel, out, wide):
    for p, own in enumerate((own0, own1)):
        widen_planes(own, wide, 0)

        @pl.loop(0, QUADS // 4, unroll=2)
        def _(q):
            split_rows(wide, sel, out.at[p], 4 * q, 4)


def padded_rows(own, sel, interpret=False):
    vmem = pl.BlockSpec(memory_space=pltpu.VMEM)
    return pl.pallas_call(
        rows_kernel,
        out_shape=jax.ShapeDtypeStruct((2, G, G, LANES), BF16),
        in_specs=[vmem] * 3,
        out_specs=vmem,
        scratch_shapes=[pltpu.VMEM((G * F_PITCH, LANES), F32)],
        compiler_params=pltpu.CompilerParams(vmem_limit_bytes=63 * MIB),
        cost_estimate=cost(16 * NGRID),
        interpret=interpret,
        name="padded_rows",
    )(*own, sel)


def pairs_kernel(pieces, share, own0, own1, own_u, kern, par, *refs):
    earlier = []
    if len(pieces) > 1:
        earlier, refs = refs[:2], refs[2:]
    table_refs, own_out = refs[:7], refs[7]
    par_out, energy_out = refs[8 : 8 + len(pieces)], refs[8 + len(pieces)]
    own_v, own_uv, kern_v, own_ov, par_ov, par_f, par_u, yw, z, x34 = refs[9 + len(pieces) : -15]
    own_f, staged, total_ref, energy_v, before_v = refs[-15:-10]
    tables, (par_sems, table_sems, sems) = refs[-10:-3], refs[-3:]
    t1, t2, t3, a1, a2, a3, sel = tables
    par_v = par_ov
    par_loads = []
    for first in (0, ROWS // 2):
        sem = par_sems.at[len(par_loads)]
        par_loads.append(copy_rows(par, first, par_v, first, ROWS // 2, sem))
    for load in par_loads:
        load.start()
    table_loads = [
        pltpu.make_async_copy(src, dst, table_sems.at[i])
        for i, (src, dst) in enumerate(zip(table_refs, tables))
    ]
    table_loads[6].start()
    table_loads[0].start()
    loads = [
        pltpu.make_async_copy(own_u, own_uv, sems.at[0]),
        pltpu.make_async_copy(kern, kern_v, sems.at[1]),
        copy_rows(own0, 0, own_v.at[0], 0, ROWS, sems.at[2]),
        copy_rows(own1, 0, own_v.at[1], 0, ROWS, sems.at[3]),
    ]
    later = []
    if earlier:
        later = [copy_rows(earlier[0].at[p], 0, z, p * ROWS, ROWS, sems.at[4 + p]) for p in range(2)]
        loads.append(pltpu.make_async_copy(earlier[1], before_v, sems.at[8 + len(pieces)]))

    for i, load in enumerate(par_loads):
        load.wait()
        for other in ([loads[0]], table_loads[1:5])[i]:
            other.start()
        widen_planes(par_v.at[pl.ds(i * ROWS // 2, ROWS // 2), :], par_f, i * G // 2)
    table_loads[6].wait()

    @pl.loop(0, QUADS // 4, unroll=3)
    def _(q):
        split_rows(par_f, sel, par_u, 4 * q, 4)

    half_y = G * Y_PITCH
    loads[0].wait()
    for load in loads[1:]:
        load.start()
    table_loads[5].start()
    table_loads[0].wait()

    @pl.loop(0, G // 2, unroll=16)
    def _(i):
        density = []
        for e in range(2):
            partner = par_u[2 * i + e].astype(F32)
            for p in range(2):
                density.append((own_uv[p, 2 * i + e].astype(F32) * partner).astype(BF16))
        out = dot(t1[...], lanes(*density))
        for e in range(2):
            for p in range(2):
                at = pl.ds(p * half_y + (2 * i + e) * Y_PITCH, Y_ROWS)
                yw[at, :] = out[:, (2 * e + p) * LANES : (2 * e + p + 1) * LANES]

    table_loads[1].wait()

    @pl.loop(0, KPAD // 2, unroll=5)
    def _(pair):
        def line(k1, part):
            first = part * HALF + k1
            rows = [yw[pl.ds(p * half_y + first, G, stride=Y_PITCH), :].astype(BF16) for p in range(2)]
            return lanes(*rows)

        both = [2 * pair, 2 * pair + 1]
        out = dot(t2[...], lanes(*[stack(line(k1, 0), line(k1, 1)) for k1 in both]))
        for e, k1 in enumerate(both):
            at = pl.ds(pl.multiple_of(k1 * G, 16), G)
            for p in range(2):
                for part in range(2):
                    left = (2 * p + part) * LANES
                    right = (2 * e + p) * LANES
                    value = out[part * G : (part + 1) * G, right : right + LANES]
                    x34[at, left : left + LANES] = value.astype(BF16)

    loads[1].wait()
    table_loads[2].wait()

    many = 5

    @pl.loop(0, KPAD // many, unroll=5)
    def _(m):
        at = pl.ds(pl.multiple_of(m * many * G, 16), many * G)
        factor = kern_v[at, :]
        out = [
            dot(x34[at, 2 * p * LANES : 2 * (p + 1) * LANES], t3[...]).astype(BF16)
            for p in range(2)
        ]
        for part in range(4):
            spectrum = lanes(*[o[:, part * 64 : (part + 1) * 64] for o in out]).astype(F32)
            value = spectrum * factor
            for i in range(many):
                row = part * Z_ROWS + (many * m + i) * Z_PITCH
                z[pl.ds(row, G), :] = value[i * G : (i + 1) * G]

    table_loads[3].wait()

    @pl.loop(0, G // 4, unroll=12)
    def _(four):
        parts = []
        for e in range(4):
            k2 = 4 * four + e
            mirror = Z_PITCH + jnp.where(k2 == 0, 0, G - k2)
            parts.append(
                stack(
                    z[pl.ds(k2, G // 2, stride=Z_PITCH), :].astype(BF16),
                    z[pl.ds(2 * Z_ROWS + mirror, G // 2, stride=Z_PITCH), :].astype(BF16),
                    z[pl.ds(1 * Z_ROWS + k2, G // 2, stride=Z_PITCH), :].astype(BF16),
                    z[pl.ds(3 * Z_ROWS + mirror, G // 2, stride=Z_PITCH), :].astype(BF16),
                )
            )
        out = dot(a1[...], lanes(*parts))
        for e in range(4):
            at = (4 * four + e) * W_PITCH
            yw[pl.ds(at, 2 * G), :] = out[:, e * LANES : (e + 1) * LANES]

    for load in later:
        load.start()
    table_loads[4].wait()

    @pl.loop(0, G // 4, unroll=12)
    def _(four):
        parts = []
        for e in range(4):
            x1 = 4 * four + e
            parts.append(
                stack(
                    yw[pl.ds(x1, G, stride=W_PITCH), :].astype(BF16),
                    yw[pl.ds(G + x1, G, stride=W_PITCH), :].astype(BF16),
                )
            )
        out = dot(a2[...], lanes(*parts))
        for r in range(4):
            block = [
                lanes(
                    out[r * QUADS : (r + 1) * QUADS, e * LANES : (e + 1) * LANES],
                    out[G + r * QUADS : G + (r + 1) * QUADS, e * LANES : (e + 1) * LANES],
                )
                for e in range(4)
            ]
            at = pl.multiple_of((r // 2) * G * QUADS + four * 4 * QUADS, 16)
            left = (r % 2) * 2 * LANES
            x34[pl.ds(at, 4 * QUADS), left : left + 2 * LANES] = stack(*block).astype(BF16)

    table_loads[5].wait()
    for load in loads[2:] + later:
        load.wait()
    total_ref[...] = jnp.zeros_like(total_ref)
    block_rows = PLANES * QUADS
    scale = F32(1.0 / NGRID)

    def result(ch):
        at = pl.multiple_of(ch * block_rows, 16)
        low = x34[pl.ds(at, block_rows), :]
        high = x34[pl.ds(G * QUADS + at, block_rows), :]
        fields = [low, lanes(low[:, 2 * LANES :], high[:, : 2 * LANES]), high]
        flat = pl.ds(pl.multiple_of(ch * STEP_ROWS, 16), STEP_ROWS)
        own_f[...] = own_v[:, flat, :].astype(F32)
        total = jnp.zeros((QUADS, LANES), F32)
        for third in range(3):
            out = dot(fields[third], a3[third]) * scale
            for i in range(PLANES):
                plane = ch * PLANES + i
                partner = par_f[pl.ds(plane * F_PITCH + third, QUADS, stride=3), :]
                here = pl.ds(i * PLANE + third, QUADS, stride=3)
                there = pl.ds(plane * PLANE + third, QUADS, stride=3)
                sent = jnp.zeros((QUADS, LANES), F32)
                for p in range(2):
                    potential = out[i * QUADS : (i + 1) * QUADS, p * LANES : (p + 1) * LANES]
                    term = potential * partner
                    if earlier:
                        at = p * ROWS + plane * PLANE + third
                        term = term + z[pl.ds(at, QUADS, stride=3), :]
                    own_ov[p, there, :] = term
                    sent = sent + potential * own_f[p, here, :]
                total = total + sent * partner
                staged[here, :] = sent
        total_ref[...] += total
        par_ov[flat, :] = staged[...].astype(BF16)
        row = ch * STEP_ROWS
        copy_rows(own_ov, row, own_out, row, STEP_ROWS, sems.at[6]).start()

    first = 0
    for i, steps in enumerate(pieces):

        @pl.loop(0, steps, unroll=2 if steps % 2 == 0 else steps)
        def _(step):
            ch = first + step
            result(ch)
            source, row = ch * STEP_ROWS, step * STEP_ROWS
            copy_rows(par_ov, source, par_out[i], row, STEP_ROWS, sems.at[7 + i]).start()

        first += steps

    energy = jnp.zeros((8, LANES), F32) + jnp.sum(total_ref[...]) * F32(share)
    if earlier:
        energy = energy + before_v[...]
    energy_v[...] = energy
    report = pltpu.make_async_copy(energy_v, energy_out, sems.at[7 + len(pieces)])
    report.start()
    pltpu.make_async_copy(own_ov, own_out, sems.at[6]).wait()
    first = 0
    for i, steps in enumerate(pieces):
        rows = steps * STEP_ROWS
        copy_rows(par_ov, first, par_out[i], 0, rows, sems.at[7 + i]).wait()
        first += rows
    report.wait()


def pair_terms(own, own_u, partner, earlier, tables, kern, pieces, share, interpret=False):
    hbm = pl.BlockSpec(memory_space=pl.ANY)
    return pl.pallas_call(
        functools.partial(pairs_kernel, pieces, share),
        out_shape=(
            jax.ShapeDtypeStruct((2, ROWS, LANES), F32),
            *[jax.ShapeDtypeStruct((steps * STEP_ROWS, LANES), BF16) for steps in pieces],
            jax.ShapeDtypeStruct((8, LANES), F32),
        ),
        in_specs=[hbm] * (5 + len(earlier) + len(tables)),
        out_specs=(hbm,) * (2 + len(pieces)),
        scratch_shapes=[
            pltpu.VMEM((2, ROWS, LANES), BF16),
            pltpu.VMEM((2, G, G, LANES), BF16),
            pltpu.VMEM((KPAD * G, LANES), F32),
            pltpu.VMEM((2, ROWS, LANES), F32),
            pltpu.VMEM((ROWS, LANES), BF16),
            pltpu.VMEM((G * F_PITCH, LANES), F32),
            pltpu.VMEM((G, G, LANES), BF16),
            pltpu.VMEM((2 * G * Y_PITCH, LANES), F32),
            pltpu.VMEM((4 * Z_ROWS, LANES), F32),
            pltpu.VMEM((KPAD * G, 4 * LANES), BF16),
            pltpu.VMEM((2, STEP_ROWS, LANES), F32),
            pltpu.VMEM((STEP_ROWS, LANES), F32),
            pltpu.VMEM((QUADS, LANES), F32),
            pltpu.VMEM((8, LANES), F32),
            pltpu.VMEM((8, LANES), F32),
            *[pltpu.VMEM(table.shape, BF16) for table in tables],
            pltpu.SemaphoreType.DMA((2,)),
            pltpu.SemaphoreType.DMA((len(tables),)),
            pltpu.SemaphoreType.DMA((9 + len(pieces),)),
        ],
        compiler_params=pltpu.CompilerParams(vmem_limit_bytes=63 * MIB),
        cost_estimate=pl.CostEstimate(
            flops=20_000_000_000, bytes_accessed=20_000_000, transcendentals=0
        ),
        interpret=interpret,
        name="pair_terms",
    )(*own, own_u, kern, partner, *earlier, *tables)


def piece_kernel(first, size, own0, own1, terms, back0, back1, *rest):
    last = first + size == ROWS
    earlier = rest[: len(rest) - 12]
    out, gram_out, own_v, terms_v, back_v, out_v, gram_ref, gram_v, value_ref = rest[-12:-3]
    load_sems, gram_sems, store_sems = rest[-3:]
    rows = size // load_sems.shape[0]

    def loads(c):
        start = first + c * rows
        sources = [
            (own0, start, own_v.at[0]), (own1, start, own_v.at[1]), (terms, start, terms_v),
            (back0, start, back_v.at[0]), (back1, c * rows, back_v.at[1]),
        ]
        return [
            copy_rows(src, row, dst, c * rows, rows, load_sems.at[c, i])
            for i, (src, row, dst) in enumerate(sources)
        ]

    chunks = [loads(c) for c in range(load_sems.shape[0])]
    for chunk in chunks:
        for load in chunk:
            load.start()
    gram_loads = []
    if last:
        gram_loads = [
            pltpu.make_async_copy(src, gram_v.at[i], gram_sems.at[i])
            for i, src in enumerate(earlier[:-1])
        ]
        for load in gram_loads:
            load.start()
    gram_ref[...] = jnp.zeros_like(gram_ref)
    for c, chunk in enumerate(chunks):
        for load in chunk:
            load.wait()
        at = pl.ds(c * rows, rows)
        own = [own_v[i, at, :].astype(F32) for i in range(2)]
        for p in range(2):
            exchange = terms_v[p, at, :] + back_v[p, at, :].astype(F32)
            out_v[pl.ds(2 * c * rows + p, rows, stride=2), :] = exchange
            for i in range(2):
                product = (own[i] * exchange).reshape(-1, 8, LANES)
                gram_ref[i, p] += jnp.sum(product, axis=0)
        copy_rows(out_v, 2 * c * rows, out, 2 * (first + c * rows), 2 * rows, store_sems.at[0]).start()

    result = gram_ref
    if last:
        for load in gram_loads:
            load.wait()
        row = lax.broadcasted_iota(jnp.int32, (2, 2), 0)
        column = lax.broadcasted_iota(jnp.int32, (2, 2), 1)
        value = jnp.zeros((2, 2), F32)
        for i in range(2):
            for j in range(2):
                entry = gram_ref[i, j]
                for k in range(len(gram_loads)):
                    entry = entry + gram_v[k, i, j]
                value = jnp.where((row == i) & (column == j), jnp.sum(entry) * F32(1.0 / NGRID), value)
        value_ref[...] = value
        result = value_ref
    report = pltpu.make_async_copy(result, gram_out, store_sems.at[1])
    report.start()
    copy_rows(out_v, 0, out, 2 * first, 2 * size, store_sems.at[0]).wait()
    report.wait()


def add_piece(first, size, own, terms, back0, back1, grams, out, interpret=False):
    hbm = pl.BlockSpec(memory_space=pl.ANY)
    last = first + size == ROWS
    earlier = [] if out is None else [*(grams if last else []), out]
    gram_shape = (2, 2, 8, LANES)
    return pl.pallas_call(
        functools.partial(piece_kernel, first, size),
        out_shape=(
            jax.ShapeDtypeStruct((2 * ROWS, LANES), F32),
            jax.ShapeDtypeStruct((2, 2) if last else gram_shape, F32),
        ),
        in_specs=[hbm] * (5 + len(earlier)),
        out_specs=(hbm, hbm),
        scratch_shapes=[
            pltpu.VMEM((2, size, LANES), BF16),
            pltpu.VMEM((2, size, LANES), F32),
            pltpu.VMEM((2, size, LANES), BF16),
            pltpu.VMEM((2 * size, LANES), F32),
            pltpu.VMEM(gram_shape, F32),
            pltpu.VMEM((len(PIECES), *gram_shape), F32),
            pltpu.VMEM((2, 2), F32),
            pltpu.SemaphoreType.DMA((2 * size // STEP_ROWS, 5)),
            pltpu.SemaphoreType.DMA((len(PIECES),)),
            pltpu.SemaphoreType.DMA((2,)),
        ],
        input_output_aliases={4 + len(earlier): 0} if earlier else {},
        compiler_params=pltpu.CompilerParams(vmem_limit_bytes=52 * MIB),
        cost_estimate=cost(24 * size * LANES),
        interpret=interpret,
        name="add_piece",
    )(*own, terms, back0, back1, *earlier)


def from_behind(block, axis, distance):
    size = lax.axis_size(axis)
    return lax.ppermute(block, axis, [((i - distance) % size, i) for i in range(size)])


def after(values, other):
    return lax.optimization_barrier((values, other))[0]


def per_device(orbitals):
    tables = section_tables()
    kern = screening()
    size = lax.axis_size("band")
    share = -2.0 / (NGRID * 2 * size * orbitals.shape[0])
    raw = orbitals.reshape(2, ROWS, LANES).transpose(1, 0, 2).reshape(2 * ROWS, LANES)
    own = [take_band(raw, 0)]
    own.append(take_band(raw, 1, own))
    previous = [from_behind(part, "band", 1) for part in own]
    own_u = padded_rows(own, tables[-1])
    terms, back0, energy = pair_terms(
        own, own_u, previous[0], (), tables, kern, (STEPS,), share
    )
    back0 = from_behind(back0, "band", -1)
    terms, *sent, energy = pair_terms(
        own, own_u, previous[1], (terms, energy), tables, kern, PIECES, share
    )
    back1 = [from_behind(piece, "band", -1) for piece in sent]

    steps = []
    if size & (size - 1):
        energy = lax.psum(energy, "band")
    else:
        swap = [(i, i ^ 1) for i in range(size)]
        energy = energy + lax.ppermute(energy, "band", swap)
        steps = [1 << b for b in range(1, size.bit_length() - 1)]
        steps = [b for b in steps if b != 2] + [b for b in steps if b == 2]
        aside = [4 if size > 4 else 2, 8 if size > 8 else 2]
        steps = [[(i, i ^ (b if i % 2 else aside[i // 2 % 2])) for i in range(size)] for b in steps]
    while len(steps) > len(back1) - 1:
        energy = energy + lax.ppermute(energy, "band", steps.pop(0))
    exchange, grams = None, []
    first = 0
    for count, piece in zip(PIECES, back1):
        count *= STEP_ROWS
        got, last = None, piece is back1[-1]
        if last and size & (size - 1) == 0:
            got = lax.ppermute(energy, "band", swap)
        elif steps:
            got = lax.ppermute(energy, "band", steps.pop(0))
        exchange, gram = add_piece(first, count, own, terms, back0, piece, grams, exchange)
        if got is not None and last:
            odd = lax.axis_index("band") % 2 == 1
            energy = jnp.where(odd, energy[:1, :1], after(got, gram)[:1, :1])
        elif got is not None:
            energy = energy + after(got, gram)
        grams.append(gram)
        first += count
    exchange = exchange.reshape(ROWS, 2, LANES).transpose(1, 0, 2).reshape(2, NGRID)
    return exchange, gram, energy[0, 0]


def solution(mesh):
    return jax.shard_map(
        per_device,
        mesh=mesh,
        in_specs=(P("band", None),),
        out_specs=(P("band", None), P("band", None), P()),
        check_vma=False,
    )
```

```python
import functools

import jax
import jax.numpy as jnp
import ml_dtypes
import numpy as np
from jax import lax
from jax.experimental import pallas as pl
from jax.experimental.pallas import tpu as pltpu
from jax.sharding import PartitionSpec as P

G = 96
HALF = G // 2 + 1
NGRID = G * G * G
LANES = 128
ROWS = NGRID // LANES
PLANE = G * G // LANES
QUADS = G // 4
KPAD = HALF + 1
Y_ROWS = 104
Y_PITCH = Y_ROWS + 1
Z_PITCH = G + 1
W_PITCH = 2 * G + 1
Z_ROWS = KPAD * Z_PITCH
F_PITCH = PLANE + 1
PLANES = 16
STEP_ROWS = PLANES * PLANE
STEPS = G // PLANES
PIECES = (4, 2)
WAVE_UNIT = 0.05
SCREEN_SQ = 0.0121
MIB = 1024 * 1024
BF16 = jnp.bfloat16
F32 = jnp.float32


def dft_tables():
    n = np.arange(G)
    phases = (n[:, None] * n[None, :]) % G
    angles = phases.astype(np.float32) * np.float32(2.0 * np.pi / G)
    rounded = [f(angles).astype(ml_dtypes.bfloat16).astype(np.float32) for f in (np.cos, np.sin)]
    return rounded[0], rounded[1]


def section_tables():
    c, s = dft_tables()
    h = HALF
    t1 = np.zeros((Y_ROWS, G), np.float32)
    t1[:h] = c[:h]
    t1[h : 2 * h] = -s[:h]
    t2 = np.block([[c, s], [-s, c]])
    t3 = np.zeros((2, LANES, 4, 64), np.float32)
    back = (G - np.arange(h)) % G
    t3[0, :G, 0, :h] = c[:h].T
    t3[1, :G, 0, :h] = s[:h].T
    t3[0, :G, 1, :h] = -s[:h].T
    t3[1, :G, 1, :h] = c[:h].T
    t3[0, :G, 2, :h] = c[back].T
    t3[1, :G, 2, :h] = s[back].T
    t3[0, :G, 3, :h] = s[back].T
    t3[1, :G, 3, :h] = -c[back].T
    t3 = t3.reshape(2 * LANES, 4 * 64)
    order = np.concatenate([np.arange(G // 2), G - 1 - np.arange(G // 2)])
    a1 = np.block([[c[:, order], -s[:, order]], [s[:, order], c[:, order]]])
    rows = np.arange(G).reshape(QUADS, 4).T.reshape(-1)
    a2 = np.block([[c[rows], -s[rows]], [s[rows], c[rows]]])
    weight = np.full((h, 1), 2.0, np.float32)
    weight[0] = weight[h - 1] = 1.0
    a3 = np.zeros((3, 2, 2, 2, 64, 2, LANES), np.float32)
    for third in range(3):
        for lane in range(LANES):
            r, x3 = divmod(third * LANES + lane, G)
            for p in range(2):
                a3[third, r - third, 0, p, :h, p, lane] = weight[:, 0] * c[x3, :h]
                a3[third, r - third, 1, p, :h, p, lane] = -weight[:, 0] * s[x3, :h]
    a3 = a3.reshape(3, 4 * LANES, 2 * LANES)
    sel = np.zeros((2, 2 * LANES, 2 * LANES), np.float32)
    for r in range(4):
        for x in range(G):
            sel[r // 2, r * G + x - (r // 2) * LANES, (r % 2) * LANES + x] = 1.0
    return [t.astype(ml_dtypes.bfloat16) for t in (t1, t2, t3, a1, a2, a3, sel)]


def screening():
    n = np.arange(G)
    m = np.where(n <= G // 2, n, n - G).astype(np.float64)
    sq = m * m
    q2 = WAVE_UNIT * (sq[:HALF, None, None] + sq[None, :, None] + sq[None, None, :HALF])
    safe = np.where(q2 > 0, q2, 1.0)
    kern = 4.0 * np.pi * (1.0 - np.exp(-q2 / (4.0 * SCREEN_SQ))) / safe
    kern = np.where(q2 > 0, kern, np.pi / SCREEN_SQ)
    out = np.zeros((KPAD, G, 2, 64), np.float32)
    out[:HALF, :, :, :HALF] = kern[:, :, None, :]
    return out.reshape(KPAD * G, LANES)


def cost(size):
    return pl.CostEstimate(flops=0, bytes_accessed=size, transcendentals=0)


def dot(a, b):
    return jnp.dot(a, b, preferred_element_type=F32)


def lanes(*parts):
    return jnp.concatenate(parts, axis=1)


def stack(*parts):
    return jnp.concatenate(parts, axis=0)


def split_rows(src, sel_ref, out, first, count):
    rows = [
        [src[pl.ds(3 * (first + i) + s, G, stride=F_PITCH), :].astype(BF16) for s in range(3)]
        for i in range(count)
    ]
    for half in range(2):
        part = dot(stack(*[lanes(r[half], r[half + 1]) for r in rows]), sel_ref[half])
        for i in range(count):
            for e in range(2):
                value = part[i * G : (i + 1) * G, e * LANES : (e + 1) * LANES]
                out[4 * (first + i) + 2 * half + e] = value.astype(BF16)


def widen_planes(src, dst, first):
    @pl.loop(0, src.shape[0] // (2 * PLANE), unroll=8)
    def _(i):
        value = src[pl.ds(pl.multiple_of(i * 2 * PLANE, 16), 2 * PLANE), :].astype(F32)
        dst[pl.ds((first + 2 * i) * F_PITCH, PLANE), :] = value[:PLANE]
        dst[pl.ds((first + 2 * i + 1) * F_PITCH, PLANE), :] = value[PLANE:]


def rows_of(ref, first, count):
    at = pl.ds(first, count)
    return ref.at[at, :] if len(ref.shape) == 2 else ref.at[:, at, :]


def copy_rows(src, src_row, dst, dst_row, count, sem):
    return pltpu.make_async_copy(rows_of(src, src_row, count), rows_of(dst, dst_row, count), sem)


def band_kernel(p, raw, *refs):
    out, raw_v, out_v, load_sems, store_sem = refs[-5:]
    chunks = load_sems.shape[0]
    rows = out.shape[0] // chunks
    loads = [
        copy_rows(raw, 2 * c * rows, raw_v, 2 * c * rows, 2 * rows, load_sems.at[c])
        for c in range(chunks)
    ]
    for load in loads:
        load.start()
    shape = (LANES, 2 * LANES)
    row = lax.broadcasted_iota(jnp.int32, shape, 0)
    column = lax.broadcasted_iota(jnp.int32, shape, 1)
    pick = jnp.where(column == 2 * row + p, F32(1.0), F32(0.0)).astype(BF16)
    for c, load in enumerate(loads):
        load.wait()
        for row in range(c * rows, (c + 1) * rows, 2 * LANES):
            blocks = [raw_v[2 * at : 2 * at + 2 * LANES, :] for at in (row, row + LANES)]
            value = dot(pick, lanes(*blocks)).astype(BF16)
            out_v[row : row + LANES, :] = value[:, :LANES]
            out_v[row + LANES : row + 2 * LANES, :] = value[:, LANES:]
        copy_rows(out_v, c * rows, out, c * rows, rows, store_sem).start()
    pltpu.make_async_copy(out_v, out, store_sem).wait()


def take_band(raw, p, earlier=(), interpret=False):
    hbm = pl.BlockSpec(memory_space=pl.ANY)
    return pl.pallas_call(
        functools.partial(band_kernel, p),
        out_shape=jax.ShapeDtypeStruct((ROWS, LANES), BF16),
        in_specs=[hbm] * (1 + len(earlier)),
        out_specs=hbm,
        scratch_shapes=[
            pltpu.VMEM((2 * ROWS, LANES), BF16),
            pltpu.VMEM((ROWS, LANES), BF16),
            pltpu.SemaphoreType.DMA((9,)),
            pltpu.SemaphoreType.DMA,
        ],
        compiler_params=pltpu.CompilerParams(vmem_limit_bytes=63 * MIB),
        cost_estimate=cost(6 * ROWS * LANES),
        interpret=interpret,
        name="take_band",
    )(raw, *earlier)


def rows_kernel(own0, own1, sel, out, wide):
    for p, own in enumerate((own0, own1)):
        widen_planes(own, wide, 0)

        @pl.loop(0, QUADS // 4, unroll=2)
        def _(q):
            split_rows(wide, sel, out.at[p], 4 * q, 4)


def padded_rows(own, sel, interpret=False):
    vmem = pl.BlockSpec(memory_space=pltpu.VMEM)
    return pl.pallas_call(
        rows_kernel,
        out_shape=jax.ShapeDtypeStruct((2, G, G, LANES), BF16),
        in_specs=[vmem] * 3,
        out_specs=vmem,
        scratch_shapes=[pltpu.VMEM((G * F_PITCH, LANES), F32)],
        compiler_params=pltpu.CompilerParams(vmem_limit_bytes=63 * MIB),
        cost_estimate=cost(16 * NGRID),
        interpret=interpret,
        name="padded_rows",
    )(*own, sel)


def pairs_kernel(pieces, share, own0, own1, own_u, kern, par, *refs):
    earlier = []
    if len(pieces) > 1:
        earlier, refs = refs[:2], refs[2:]
    table_refs, own_out = refs[:7], refs[7]
    par_out, energy_out = refs[8 : 8 + len(pieces)], refs[8 + len(pieces)]
    own_v, own_uv, kern_v, own_ov, par_ov, par_f, par_u, yw, z, x34 = refs[9 + len(pieces) : -15]
    own_f, staged, total_ref, energy_v, before_v = refs[-15:-10]
    tables, (par_sems, table_sems, sems) = refs[-10:-3], refs[-3:]
    t1, t2, t3, a1, a2, a3, sel = tables
    par_v = par_ov
    par_loads = []
    for first in (0, ROWS // 2):
        sem = par_sems.at[len(par_loads)]
        par_loads.append(copy_rows(par, first, par_v, first, ROWS // 2, sem))
    for load in par_loads:
        load.start()
    table_loads = [
        pltpu.make_async_copy(src, dst, table_sems.at[i])
        for i, (src, dst) in enumerate(zip(table_refs, tables))
    ]
    table_loads[6].start()
    table_loads[0].start()
    loads = [
        pltpu.make_async_copy(own_u, own_uv, sems.at[0]),
        pltpu.make_async_copy(kern, kern_v, sems.at[1]),
        copy_rows(own0, 0, own_v.at[0], 0, ROWS, sems.at[2]),
        copy_rows(own1, 0, own_v.at[1], 0, ROWS, sems.at[3]),
    ]
    later = []
    if earlier:
        later = [copy_rows(earlier[0].at[p], 0, z, p * ROWS, ROWS, sems.at[4 + p]) for p in range(2)]
        loads.append(pltpu.make_async_copy(earlier[1], before_v, sems.at[8 + len(pieces)]))

    for i, load in enumerate(par_loads):
        load.wait()
        for other in ([loads[0]], table_loads[1:5])[i]:
            other.start()
        widen_planes(par_v.at[pl.ds(i * ROWS // 2, ROWS // 2), :], par_f, i * G // 2)
    table_loads[6].wait()

    @pl.loop(0, QUADS // 4, unroll=6)
    def _(q):
        split_rows(par_f, sel, par_u, 4 * q, 4)

    half_y = G * Y_PITCH
    loads[0].wait()
    for load in loads[1:]:
        load.start()
    table_loads[5].start()
    table_loads[0].wait()

    @pl.loop(0, G // 2, unroll=24)
    def _(i):
        density = []
        for e in range(2):
            partner = par_u[2 * i + e].astype(F32)
            for p in range(2):
                density.append((own_uv[p, 2 * i + e].astype(F32) * partner).astype(BF16))
        out = dot(t1[...], lanes(*density))
        for e in range(2):
            for p in range(2):
                at = pl.ds(p * half_y + (2 * i + e) * Y_PITCH, Y_ROWS)
                yw[at, :] = out[:, (2 * e + p) * LANES : (2 * e + p + 1) * LANES]

    table_loads[1].wait()

    @pl.loop(0, KPAD // 2, unroll=25)
    def _(pair):
        def line(k1, part):
            first = part * HALF + k1
            rows = [yw[pl.ds(p * half_y + first, G, stride=Y_PITCH), :].astype(BF16) for p in range(2)]
            return lanes(*rows)

        both = [2 * pair, 2 * pair + 1]
        out = dot(t2[...], lanes(*[stack(line(k1, 0), line(k1, 1)) for k1 in both]))
        for e, k1 in enumerate(both):
            at = pl.ds(pl.multiple_of(k1 * G, 16), G)
            for p in range(2):
                for part in range(2):
                    left = (2 * p + part) * LANES
                    right = (2 * e + p) * LANES
                    value = out[part * G : (part + 1) * G, right : right + LANES]
                    x34[at, left : left + LANES] = value.astype(BF16)

    loads[1].wait()
    table_loads[2].wait()

    many = 5

    @pl.loop(0, KPAD // many, unroll=10)
    def _(m):
        at = pl.ds(pl.multiple_of(m * many * G, 16), many * G)
        factor = kern_v[at, :]
        out = [
            dot(x34[at, 2 * p * LANES : 2 * (p + 1) * LANES], t3[...]).astype(BF16)
            for p in range(2)
        ]
        for part in range(4):
            spectrum = lanes(*[o[:, part * 64 : (part + 1) * 64] for o in out]).astype(F32)
            value = spectrum * factor
            for i in range(many):
                row = part * Z_ROWS + (many * m + i) * Z_PITCH
                z[pl.ds(row, G), :] = value[i * G : (i + 1) * G]

    table_loads[3].wait()

    @pl.loop(0, G // 4, unroll=24)
    def _(four):
        parts = []
        for e in range(4):
            k2 = 4 * four + e
            mirror = Z_PITCH + jnp.where(k2 == 0, 0, G - k2)
            parts.append(
                stack(
                    z[pl.ds(k2, G // 2, stride=Z_PITCH), :].astype(BF16),
                    z[pl.ds(2 * Z_ROWS + mirror, G // 2, stride=Z_PITCH), :].astype(BF16),
                    z[pl.ds(1 * Z_ROWS + k2, G // 2, stride=Z_PITCH), :].astype(BF16),
                    z[pl.ds(3 * Z_ROWS + mirror, G // 2, stride=Z_PITCH), :].astype(BF16),
                )
            )
        out = dot(a1[...], lanes(*parts))
        for e in range(4):
            at = (4 * four + e) * W_PITCH
            yw[pl.ds(at, 2 * G), :] = out[:, e * LANES : (e + 1) * LANES]

    for load in later:
        load.start()
    table_loads[4].wait()

    @pl.loop(0, G // 4, unroll=24)
    def _(four):
        parts = []
        for e in range(4):
            x1 = 4 * four + e
            parts.append(
                stack(
                    yw[pl.ds(x1, G, stride=W_PITCH), :].astype(BF16),
                    yw[pl.ds(G + x1, G, stride=W_PITCH), :].astype(BF16),
                )
            )
        out = dot(a2[...], lanes(*parts))
        for r in range(4):
            block = [
                lanes(
                    out[r * QUADS : (r + 1) * QUADS, e * LANES : (e + 1) * LANES],
                    out[G + r * QUADS : G + (r + 1) * QUADS, e * LANES : (e + 1) * LANES],
                )
                for e in range(4)
            ]
            at = pl.multiple_of((r // 2) * G * QUADS + four * 4 * QUADS, 16)
            left = (r % 2) * 2 * LANES
            x34[pl.ds(at, 4 * QUADS), left : left + 2 * LANES] = stack(*block).astype(BF16)

    table_loads[5].wait()
    for load in loads[2:] + later:
        load.wait()
    total_ref[...] = jnp.zeros_like(total_ref)
    block_rows = PLANES * QUADS
    scale = F32(1.0 / NGRID)

    def result(ch):
        at = pl.multiple_of(ch * block_rows, 16)
        low = x34[pl.ds(at, block_rows), :]
        high = x34[pl.ds(G * QUADS + at, block_rows), :]
        fields = [low, lanes(low[:, 2 * LANES :], high[:, : 2 * LANES]), high]
        flat = pl.ds(pl.multiple_of(ch * STEP_ROWS, 16), STEP_ROWS)
        own_f[...] = own_v[:, flat, :].astype(F32)
        total = jnp.zeros((QUADS, LANES), F32)
        for third in range(3):
            out = dot(fields[third], a3[third]) * scale
            for i in range(PLANES):
                plane = ch * PLANES + i
                partner = par_f[pl.ds(plane * F_PITCH + third, QUADS, stride=3), :]
                here = pl.ds(i * PLANE + third, QUADS, stride=3)
                there = pl.ds(plane * PLANE + third, QUADS, stride=3)
                sent = jnp.zeros((QUADS, LANES), F32)
                for p in range(2):
                    potential = out[i * QUADS : (i + 1) * QUADS, p * LANES : (p + 1) * LANES]
                    term = potential * partner
                    if earlier:
                        at = p * ROWS + plane * PLANE + third
                        term = term + z[pl.ds(at, QUADS, stride=3), :]
                    own_ov[p, there, :] = term
                    sent = sent + potential * own_f[p, here, :]
                total = total + sent * partner
                staged[here, :] = sent
        total_ref[...] += total
        par_ov[flat, :] = staged[...].astype(BF16)
        row = ch * STEP_ROWS
        copy_rows(own_ov, row, own_out, row, STEP_ROWS, sems.at[6]).start()

    first = 0
    for i, steps in enumerate(pieces):

        @pl.loop(0, steps, unroll=3 if steps % 3 == 0 else 2)
        def _(step):
            ch = first + step
            result(ch)
            source, row = ch * STEP_ROWS, step * STEP_ROWS
            copy_rows(par_ov, source, par_out[i], row, STEP_ROWS, sems.at[7 + i]).start()

        first += steps

    energy = jnp.zeros((8, LANES), F32) + jnp.sum(total_ref[...]) * F32(share)
    if earlier:
        energy = energy + before_v[...]
    energy_v[...] = energy
    report = pltpu.make_async_copy(energy_v, energy_out, sems.at[7 + len(pieces)])
    report.start()
    pltpu.make_async_copy(own_ov, own_out, sems.at[6]).wait()
    first = 0
    for i, steps in enumerate(pieces):
        rows = steps * STEP_ROWS
        copy_rows(par_ov, first, par_out[i], 0, rows, sems.at[7 + i]).wait()
        first += rows
    report.wait()


def pair_terms(own, own_u, partner, earlier, tables, kern, pieces, share, interpret=False):
    hbm = pl.BlockSpec(memory_space=pl.ANY)
    return pl.pallas_call(
        functools.partial(pairs_kernel, pieces, share),
        out_shape=(
            jax.ShapeDtypeStruct((2, ROWS, LANES), F32),
            *[jax.ShapeDtypeStruct((steps * STEP_ROWS, LANES), BF16) for steps in pieces],
            jax.ShapeDtypeStruct((8, LANES), F32),
        ),
        in_specs=[hbm] * (5 + len(earlier) + len(tables)),
        out_specs=(hbm,) * (2 + len(pieces)),
        scratch_shapes=[
            pltpu.VMEM((2, ROWS, LANES), BF16),
            pltpu.VMEM((2, G, G, LANES), BF16),
            pltpu.VMEM((KPAD * G, LANES), F32),
            pltpu.VMEM((2, ROWS, LANES), F32),
            pltpu.VMEM((ROWS, LANES), BF16),
            pltpu.VMEM((G * F_PITCH, LANES), F32),
            pltpu.VMEM((G, G, LANES), BF16),
            pltpu.VMEM((2 * G * Y_PITCH, LANES), F32),
            pltpu.VMEM((4 * Z_ROWS, LANES), F32),
            pltpu.VMEM((KPAD * G, 4 * LANES), BF16),
            pltpu.VMEM((2, STEP_ROWS, LANES), F32),
            pltpu.VMEM((STEP_ROWS, LANES), F32),
            pltpu.VMEM((QUADS, LANES), F32),
            pltpu.VMEM((8, LANES), F32),
            pltpu.VMEM((8, LANES), F32),
            *[pltpu.VMEM(table.shape, BF16) for table in tables],
            pltpu.SemaphoreType.DMA((2,)),
            pltpu.SemaphoreType.DMA((len(tables),)),
            pltpu.SemaphoreType.DMA((9 + len(pieces),)),
        ],
        compiler_params=pltpu.CompilerParams(vmem_limit_bytes=63 * MIB),
        cost_estimate=pl.CostEstimate(
            flops=20_000_000_000, bytes_accessed=20_000_000, transcendentals=0
        ),
        interpret=interpret,
        name="pair_terms",
    )(*own, own_u, kern, partner, *earlier, *tables)


def piece_kernel(first, size, own0, own1, terms, back0, back1, *rest):
    last = first + size == ROWS
    earlier = rest[: len(rest) - 12]
    out, gram_out, own_v, terms_v, back_v, out_v, gram_ref, gram_v, value_ref = rest[-12:-3]
    load_sems, gram_sems, store_sems = rest[-3:]
    rows = size // load_sems.shape[0]

    def loads(c):
        start = first + c * rows
        sources = [
            (own0, start, own_v.at[0]), (own1, start, own_v.at[1]), (terms, start, terms_v),
            (back0, start, back_v.at[0]), (back1, c * rows, back_v.at[1]),
        ]
        return [
            copy_rows(src, row, dst, c * rows, rows, load_sems.at[c, i])
            for i, (src, row, dst) in enumerate(sources)
        ]

    chunks = [loads(c) for c in range(load_sems.shape[0])]
    for chunk in chunks:
        for load in chunk:
            load.start()
    gram_loads = []
    if last:
        gram_loads = [
            pltpu.make_async_copy(src, gram_v.at[i], gram_sems.at[i])
            for i, src in enumerate(earlier[:-1])
        ]
        for load in gram_loads:
            load.start()
    gram_ref[...] = jnp.zeros_like(gram_ref)
    for c, chunk in enumerate(chunks):
        for load in chunk:
            load.wait()
        at = pl.ds(c * rows, rows)
        own = [own_v[i, at, :].astype(F32) for i in range(2)]
        for p in range(2):
            exchange = terms_v[p, at, :] + back_v[p, at, :].astype(F32)
            out_v[pl.ds(2 * c * rows + p, rows, stride=2), :] = exchange
            for i in range(2):
                product = (own[i] * exchange).reshape(-1, 8, LANES)
                gram_ref[i, p] += jnp.sum(product, axis=0)
        copy_rows(out_v, 2 * c * rows, out, 2 * (first + c * rows), 2 * rows, store_sems.at[0]).start()

    result = gram_ref
    if last:
        for load in gram_loads:
            load.wait()
        row = lax.broadcasted_iota(jnp.int32, (2, 2), 0)
        column = lax.broadcasted_iota(jnp.int32, (2, 2), 1)
        value = jnp.zeros((2, 2), F32)
        for i in range(2):
            for j in range(2):
                entry = gram_ref[i, j]
                for k in range(len(gram_loads)):
                    entry = entry + gram_v[k, i, j]
                value = jnp.where((row == i) & (column == j), jnp.sum(entry) * F32(1.0 / NGRID), value)
        value_ref[...] = value
        result = value_ref
    report = pltpu.make_async_copy(result, gram_out, store_sems.at[1])
    report.start()
    copy_rows(out_v, 0, out, 2 * first, 2 * size, store_sems.at[0]).wait()
    report.wait()


def add_piece(first, size, own, terms, back0, back1, grams, out, interpret=False):
    hbm = pl.BlockSpec(memory_space=pl.ANY)
    last = first + size == ROWS
    earlier = [] if out is None else [*(grams if last else []), out]
    gram_shape = (2, 2, 8, LANES)
    return pl.pallas_call(
        functools.partial(piece_kernel, first, size),
        out_shape=(
            jax.ShapeDtypeStruct((2 * ROWS, LANES), F32),
            jax.ShapeDtypeStruct((2, 2) if last else gram_shape, F32),
        ),
        in_specs=[hbm] * (5 + len(earlier)),
        out_specs=(hbm, hbm),
        scratch_shapes=[
            pltpu.VMEM((2, size, LANES), BF16),
            pltpu.VMEM((2, size, LANES), F32),
            pltpu.VMEM((2, size, LANES), BF16),
            pltpu.VMEM((2 * size, LANES), F32),
            pltpu.VMEM(gram_shape, F32),
            pltpu.VMEM((len(PIECES), *gram_shape), F32),
            pltpu.VMEM((2, 2), F32),
            pltpu.SemaphoreType.DMA((2 * size // STEP_ROWS, 5)),
            pltpu.SemaphoreType.DMA((len(PIECES),)),
            pltpu.SemaphoreType.DMA((2,)),
        ],
        input_output_aliases={4 + len(earlier): 0} if earlier else {},
        compiler_params=pltpu.CompilerParams(vmem_limit_bytes=52 * MIB),
        cost_estimate=cost(24 * size * LANES),
        interpret=interpret,
        name="add_piece",
    )(*own, terms, back0, back1, *earlier)


def from_behind(block, axis, distance):
    size = lax.axis_size(axis)
    return lax.ppermute(block, axis, [((i - distance) % size, i) for i in range(size)])


def after(values, other):
    return lax.optimization_barrier((values, other))[0]


def per_device(orbitals):
    tables = section_tables()
    kern = screening()
    size = lax.axis_size("band")
    share = -2.0 / (NGRID * 2 * size * orbitals.shape[0])
    raw = orbitals.reshape(2, ROWS, LANES).transpose(1, 0, 2).reshape(2 * ROWS, LANES)
    own = [take_band(raw, 0)]
    own.append(take_band(raw, 1, own))
    previous = [from_behind(part, "band", 1) for part in own]
    own_u = padded_rows(own, tables[-1])
    terms, back0, energy = pair_terms(
        own, own_u, previous[0], (), tables, kern, (STEPS,), share
    )
    back0 = from_behind(back0, "band", -1)
    terms, *sent, energy = pair_terms(
        own, own_u, previous[1], (terms, energy), tables, kern, PIECES, share
    )
    back1 = [from_behind(piece, "band", -1) for piece in sent]

    steps = []
    if size & (size - 1):
        energy = lax.psum(energy, "band")
    else:
        swap = [(i, i ^ 1) for i in range(size)]
        energy = energy + lax.ppermute(energy, "band", swap)
        steps = [1 << b for b in range(1, size.bit_length() - 1)]
        steps = [b for b in steps if b != 2] + [b for b in steps if b == 2]
        aside = [4 if size > 4 else 2, 8 if size > 8 else 2]
        steps = [[(i, i ^ (b if i % 2 else aside[i // 2 % 2])) for i in range(size)] for b in steps]
    while len(steps) > len(back1) - 1:
        energy = energy + lax.ppermute(energy, "band", steps.pop(0))
    exchange, grams = None, []
    first = 0
    for count, piece in zip(PIECES, back1):
        count *= STEP_ROWS
        got, last = None, piece is back1[-1]
        if last and size & (size - 1) == 0:
            got = lax.ppermute(energy, "band", swap)
        elif steps:
            got = lax.ppermute(energy, "band", steps.pop(0))
        exchange, gram = add_piece(first, count, own, terms, back0, piece, grams, exchange)
        if got is not None and last:
            odd = lax.axis_index("band") % 2 == 1
            energy = jnp.where(odd, energy[:1, :1], after(got, gram)[:1, :1])
        elif got is not None:
            energy = energy + after(got, gram)
        grams.append(gram)
        first += count
    exchange = exchange.reshape(ROWS, 2, LANES).transpose(1, 0, 2).reshape(2, NGRID)
    return exchange, gram, energy[0, 0]


def solution(mesh):
    return jax.shard_map(
        per_device,
        mesh=mesh,
        in_specs=(P("band", None),),
        out_specs=(P("band", None), P("band", None), P()),
        check_vma=False,
    )
```

```python
import functools

import jax
import jax.numpy as jnp
import ml_dtypes
import numpy as np
from jax import lax
from jax.experimental import pallas as pl
from jax.experimental.pallas import tpu as pltpu
from jax.sharding import PartitionSpec as P

G = 96
HALF = G // 2 + 1
NGRID = G * G * G
LANES = 128
ROWS = NGRID // LANES
PLANE = G * G // LANES
QUADS = G // 4
KPAD = HALF + 1
Y_ROWS = 104
Y_PITCH = Y_ROWS + 1
Z_PITCH = G + 1
W_PITCH = 2 * G + 1
Z_ROWS = KPAD * Z_PITCH
F_PITCH = PLANE + 1
PLANES = 16
STEP_ROWS = PLANES * PLANE
STEPS = G // PLANES
PIECES = (3, 2, 1)
WAVE_UNIT = 0.05
SCREEN_SQ = 0.0121
MIB = 1024 * 1024
BF16 = jnp.bfloat16
F32 = jnp.float32


def dft_tables():
    n = np.arange(G)
    phases = (n[:, None] * n[None, :]) % G
    angles = phases.astype(np.float32) * np.float32(2.0 * np.pi / G)
    rounded = [f(angles).astype(ml_dtypes.bfloat16).astype(np.float32) for f in (np.cos, np.sin)]
    return rounded[0], rounded[1]


def section_tables():
    c, s = dft_tables()
    h = HALF
    t1 = np.zeros((Y_ROWS, G), np.float32)
    t1[:h] = c[:h]
    t1[h : 2 * h] = -s[:h]
    t2 = np.block([[c, s], [-s, c]])
    t3 = np.zeros((2, LANES, 4, 64), np.float32)
    back = (G - np.arange(h)) % G
    t3[0, :G, 0, :h] = c[:h].T
    t3[1, :G, 0, :h] = s[:h].T
    t3[0, :G, 1, :h] = -s[:h].T
    t3[1, :G, 1, :h] = c[:h].T
    t3[0, :G, 2, :h] = c[back].T
    t3[1, :G, 2, :h] = s[back].T
    t3[0, :G, 3, :h] = s[back].T
    t3[1, :G, 3, :h] = -c[back].T
    t3 = t3.reshape(2 * LANES, 4 * 64)
    order = np.concatenate([np.arange(G // 2), G - 1 - np.arange(G // 2)])
    a1 = np.block([[c[:, order], -s[:, order]], [s[:, order], c[:, order]]])
    rows = np.arange(G).reshape(QUADS, 4).T.reshape(-1)
    a2 = np.block([[c[rows], -s[rows]], [s[rows], c[rows]]])
    weight = np.full((h, 1), 2.0, np.float32)
    weight[0] = weight[h - 1] = 1.0
    a3 = np.zeros((3, 2, 2, 2, 64, 2, LANES), np.float32)
    for third in range(3):
        for lane in range(LANES):
            r, x3 = divmod(third * LANES + lane, G)
            for p in range(2):
                a3[third, r - third, 0, p, :h, p, lane] = weight[:, 0] * c[x3, :h]
                a3[third, r - third, 1, p, :h, p, lane] = -weight[:, 0] * s[x3, :h]
    a3 = a3.reshape(3, 4 * LANES, 2 * LANES)
    sel = np.zeros((2, 2 * LANES, 2 * LANES), np.float32)
    for r in range(4):
        for x in range(G):
            sel[r // 2, r * G + x - (r // 2) * LANES, (r % 2) * LANES + x] = 1.0
    return [t.astype(ml_dtypes.bfloat16) for t in (t1, t2, t3, a1, a2, a3, sel)]


def screening():
    n = np.arange(G)
    m = np.where(n <= G // 2, n, n - G).astype(np.float64)
    sq = m * m
    q2 = WAVE_UNIT * (sq[:HALF, None, None] + sq[None, :, None] + sq[None, None, :HALF])
    safe = np.where(q2 > 0, q2, 1.0)
    kern = 4.0 * np.pi * (1.0 - np.exp(-q2 / (4.0 * SCREEN_SQ))) / safe
    kern = np.where(q2 > 0, kern, np.pi / SCREEN_SQ)
    out = np.zeros((KPAD, G, 2, 64), np.float32)
    out[:HALF, :, :, :HALF] = kern[:, :, None, :]
    return out.reshape(KPAD * G, LANES)


def cost(size):
    return pl.CostEstimate(flops=0, bytes_accessed=size, transcendentals=0)


def dot(a, b):
    return jnp.dot(a, b, preferred_element_type=F32)


def lanes(*parts):
    return jnp.concatenate(parts, axis=1)


def stack(*parts):
    return jnp.concatenate(parts, axis=0)


def split_rows(src, sel_ref, out, first, count):
    rows = [
        [src[pl.ds(3 * (first + i) + s, G, stride=F_PITCH), :].astype(BF16) for s in range(3)]
        for i in range(count)
    ]
    for half in range(2):
        part = dot(stack(*[lanes(r[half], r[half + 1]) for r in rows]), sel_ref[half])
        for i in range(count):
            for e in range(2):
                value = part[i * G : (i + 1) * G, e * LANES : (e + 1) * LANES]
                out[4 * (first + i) + 2 * half + e] = value.astype(BF16)


def widen_planes(src, dst, first):
    @pl.loop(0, src.shape[0] // (2 * PLANE), unroll=8)
    def _(i):
        value = src[pl.ds(pl.multiple_of(i * 2 * PLANE, 16), 2 * PLANE), :].astype(F32)
        dst[pl.ds((first + 2 * i) * F_PITCH, PLANE), :] = value[:PLANE]
        dst[pl.ds((first + 2 * i + 1) * F_PITCH, PLANE), :] = value[PLANE:]


def rows_of(ref, first, count):
    at = pl.ds(first, count)
    return ref.at[at, :] if len(ref.shape) == 2 else ref.at[:, at, :]


def copy_rows(src, src_row, dst, dst_row, count, sem):
    return pltpu.make_async_copy(rows_of(src, src_row, count), rows_of(dst, dst_row, count), sem)


def band_kernel(p, raw, *refs):
    out, raw_v, out_v, load_sems, store_sem = refs[-5:]
    chunks = load_sems.shape[0]
    rows = out.shape[0] // chunks
    loads = [
        copy_rows(raw, 2 * c * rows, raw_v, 2 * c * rows, 2 * rows, load_sems.at[c])
        for c in range(chunks)
    ]
    for load in loads:
        load.start()
    shape = (LANES, 2 * LANES)
    row = lax.broadcasted_iota(jnp.int32, shape, 0)
    column = lax.broadcasted_iota(jnp.int32, shape, 1)
    pick = jnp.where(column == 2 * row + p, F32(1.0), F32(0.0)).astype(BF16)
    for c, load in enumerate(loads):
        load.wait()
        for row in range(c * rows, (c + 1) * rows, 2 * LANES):
            blocks = [raw_v[2 * at : 2 * at + 2 * LANES, :] for at in (row, row + LANES)]
            value = dot(pick, lanes(*blocks)).astype(BF16)
            out_v[row : row + LANES, :] = value[:, :LANES]
            out_v[row + LANES : row + 2 * LANES, :] = value[:, LANES:]
        copy_rows(out_v, c * rows, out, c * rows, rows, store_sem).start()
    pltpu.make_async_copy(out_v, out, store_sem).wait()


def take_band(raw, p, earlier=(), interpret=False):
    hbm = pl.BlockSpec(memory_space=pl.ANY)
    return pl.pallas_call(
        functools.partial(band_kernel, p),
        out_shape=jax.ShapeDtypeStruct((ROWS, LANES), BF16),
        in_specs=[hbm] * (1 + len(earlier)),
        out_specs=hbm,
        scratch_shapes=[
            pltpu.VMEM((2 * ROWS, LANES), BF16),
            pltpu.VMEM((ROWS, LANES), BF16),
            pltpu.SemaphoreType.DMA((9,)),
            pltpu.SemaphoreType.DMA,
        ],
        compiler_params=pltpu.CompilerParams(vmem_limit_bytes=63 * MIB),
        cost_estimate=cost(6 * ROWS * LANES),
        interpret=interpret,
        name="take_band",
    )(raw, *earlier)


def rows_kernel(own0, own1, sel, out, wide):
    for p, own in enumerate((own0, own1)):
        widen_planes(own, wide, 0)

        @pl.loop(0, QUADS // 4, unroll=2)
        def _(q):
            split_rows(wide, sel, out.at[p], 4 * q, 4)


def padded_rows(own, sel, interpret=False):
    vmem = pl.BlockSpec(memory_space=pltpu.VMEM)
    return pl.pallas_call(
        rows_kernel,
        out_shape=jax.ShapeDtypeStruct((2, G, G, LANES), BF16),
        in_specs=[vmem] * 3,
        out_specs=vmem,
        scratch_shapes=[pltpu.VMEM((G * F_PITCH, LANES), F32)],
        compiler_params=pltpu.CompilerParams(vmem_limit_bytes=63 * MIB),
        cost_estimate=cost(16 * NGRID),
        interpret=interpret,
        name="padded_rows",
    )(*own, sel)


def pairs_kernel(pieces, share, own0, own1, own_u, kern, par, *refs):
    earlier = []
    if len(pieces) > 1:
        earlier, refs = refs[:2], refs[2:]
    table_refs, own_out = refs[:7], refs[7]
    par_out, energy_out = refs[8 : 8 + len(pieces)], refs[8 + len(pieces)]
    own_v, own_uv, kern_v, own_ov, par_ov, par_f, par_u, yw, z, x34 = refs[9 + len(pieces) : -15]
    own_f, staged, total_ref, energy_v, before_v = refs[-15:-10]
    tables, (par_sems, table_sems, sems) = refs[-10:-3], refs[-3:]
    t1, t2, t3, a1, a2, a3, sel = tables
    par_v = par_ov
    par_loads = []
    for first in (0, ROWS // 2):
        sem = par_sems.at[len(par_loads)]
        par_loads.append(copy_rows(par, first, par_v, first, ROWS // 2, sem))
    for load in par_loads:
        load.start()
    table_loads = [
        pltpu.make_async_copy(src, dst, table_sems.at[i])
        for i, (src, dst) in enumerate(zip(table_refs, tables))
    ]
    table_loads[6].start()
    table_loads[0].start()
    loads = [
        pltpu.make_async_copy(own_u, own_uv, sems.at[0]),
        pltpu.make_async_copy(kern, kern_v, sems.at[1]),
        copy_rows(own0, 0, own_v.at[0], 0, ROWS, sems.at[2]),
        copy_rows(own1, 0, own_v.at[1], 0, ROWS, sems.at[3]),
    ]
    later = []
    if earlier:
        later = [copy_rows(earlier[0].at[p], 0, z, p * ROWS, ROWS, sems.at[4 + p]) for p in range(2)]
        loads.append(pltpu.make_async_copy(earlier[1], before_v, sems.at[8 + len(pieces)]))

    for i, load in enumerate(par_loads):
        load.wait()
        for other in ([loads[0]], table_loads[1:5])[i]:
            other.start()
        widen_planes(par_v.at[pl.ds(i * ROWS // 2, ROWS // 2), :], par_f, i * G // 2)
    table_loads[6].wait()

    @pl.loop(0, QUADS // 4, unroll=6)
    def _(q):
        split_rows(par_f, sel, par_u, 4 * q, 4)

    half_y = G * Y_PITCH
    loads[0].wait()
    for load in loads[1:]:
        load.start()
    table_loads[5].start()
    table_loads[0].wait()

    @pl.loop(0, G // 2, unroll=24)
    def _(i):
        density = []
        for e in range(2):
            partner = par_u[2 * i + e].astype(F32)
            for p in range(2):
                density.append((own_uv[p, 2 * i + e].astype(F32) * partner).astype(BF16))
        out = dot(t1[...], lanes(*density))
        for e in range(2):
            for p in range(2):
                at = pl.ds(p * half_y + (2 * i + e) * Y_PITCH, Y_ROWS)
                yw[at, :] = out[:, (2 * e + p) * LANES : (2 * e + p + 1) * LANES]

    table_loads[1].wait()

    @pl.loop(0, KPAD // 2, unroll=25)
    def _(pair):
        def line(k1, part):
            first = part * HALF + k1
            rows = [yw[pl.ds(p * half_y + first, G, stride=Y_PITCH), :].astype(BF16) for p in range(2)]
            return lanes(*rows)

        both = [2 * pair, 2 * pair + 1]
        out = dot(t2[...], lanes(*[stack(line(k1, 0), line(k1, 1)) for k1 in both]))
        for e, k1 in enumerate(both):
            at = pl.ds(pl.multiple_of(k1 * G, 16), G)
            for p in range(2):
                for part in range(2):
                    left = (2 * p + part) * LANES
                    right = (2 * e + p) * LANES
                    value = out[part * G : (part + 1) * G, right : right + LANES]
                    x34[at, left : left + LANES] = value.astype(BF16)

    loads[1].wait()
    table_loads[2].wait()

    many = 5

    @pl.loop(0, KPAD // many, unroll=10)
    def _(m):
        at = pl.ds(pl.multiple_of(m * many * G, 16), many * G)
        factor = kern_v[at, :]
        out = [
            dot(x34[at, 2 * p * LANES : 2 * (p + 1) * LANES], t3[...]).astype(BF16)
            for p in range(2)
        ]
        for part in range(4):
            spectrum = lanes(*[o[:, part * 64 : (part + 1) * 64] for o in out]).astype(F32)
            value = spectrum * factor
            for i in range(many):
                row = part * Z_ROWS + (many * m + i) * Z_PITCH
                z[pl.ds(row, G), :] = value[i * G : (i + 1) * G]

    table_loads[3].wait()

    @pl.loop(0, G // 4, unroll=24)
    def _(four):
        parts = []
        for e in range(4):
            k2 = 4 * four + e
            mirror = Z_PITCH + jnp.where(k2 == 0, 0, G - k2)
            parts.append(
                stack(
                    z[pl.ds(k2, G // 2, stride=Z_PITCH), :].astype(BF16),
                    z[pl.ds(2 * Z_ROWS + mirror, G // 2, stride=Z_PITCH), :].astype(BF16),
                    z[pl.ds(1 * Z_ROWS + k2, G // 2, stride=Z_PITCH), :].astype(BF16),
                    z[pl.ds(3 * Z_ROWS + mirror, G // 2, stride=Z_PITCH), :].astype(BF16),
                )
            )
        out = dot(a1[...], lanes(*parts))
        for e in range(4):
            at = (4 * four + e) * W_PITCH
            yw[pl.ds(at, 2 * G), :] = out[:, e * LANES : (e + 1) * LANES]

    for load in later:
        load.start()
    table_loads[4].wait()

    @pl.loop(0, G // 4, unroll=24)
    def _(four):
        parts = []
        for e in range(4):
            x1 = 4 * four + e
            parts.append(
                stack(
                    yw[pl.ds(x1, G, stride=W_PITCH), :].astype(BF16),
                    yw[pl.ds(G + x1, G, stride=W_PITCH), :].astype(BF16),
                )
            )
        out = dot(a2[...], lanes(*parts))
        for r in range(4):
            block = [
                lanes(
                    out[r * QUADS : (r + 1) * QUADS, e * LANES : (e + 1) * LANES],
                    out[G + r * QUADS : G + (r + 1) * QUADS, e * LANES : (e + 1) * LANES],
                )
                for e in range(4)
            ]
            at = pl.multiple_of((r // 2) * G * QUADS + four * 4 * QUADS, 16)
            left = (r % 2) * 2 * LANES
            x34[pl.ds(at, 4 * QUADS), left : left + 2 * LANES] = stack(*block).astype(BF16)

    table_loads[5].wait()
    for load in loads[2:] + later:
        load.wait()
    total_ref[...] = jnp.zeros_like(total_ref)
    block_rows = PLANES * QUADS
    scale = F32(1.0 / NGRID)

    def result(ch):
        at = pl.multiple_of(ch * block_rows, 16)
        low = x34[pl.ds(at, block_rows), :]
        high = x34[pl.ds(G * QUADS + at, block_rows), :]
        fields = [low, lanes(low[:, 2 * LANES :], high[:, : 2 * LANES]), high]
        flat = pl.ds(pl.multiple_of(ch * STEP_ROWS, 16), STEP_ROWS)
        own_f[...] = own_v[:, flat, :].astype(F32)
        total = jnp.zeros((QUADS, LANES), F32)
        for third in range(3):
            out = dot(fields[third], a3[third]) * scale
            for i in range(PLANES):
                plane = ch * PLANES + i
                partner = par_f[pl.ds(plane * F_PITCH + third, QUADS, stride=3), :]
                here = pl.ds(i * PLANE + third, QUADS, stride=3)
                there = pl.ds(plane * PLANE + third, QUADS, stride=3)
                sent = jnp.zeros((QUADS, LANES), F32)
                for p in range(2):
                    potential = out[i * QUADS : (i + 1) * QUADS, p * LANES : (p + 1) * LANES]
                    term = potential * partner
                    if earlier:
                        at = p * ROWS + plane * PLANE + third
                        term = term + z[pl.ds(at, QUADS, stride=3), :]
                    own_ov[p, there, :] = term
                    sent = sent + potential * own_f[p, here, :]
                total = total + sent * partner
                staged[here, :] = sent
        total_ref[...] += total
        par_ov[flat, :] = staged[...].astype(BF16)
        row = ch * STEP_ROWS
        copy_rows(own_ov, row, own_out, row, STEP_ROWS, sems.at[6]).start()

    first = 0
    for i, steps in enumerate(pieces):

        @pl.loop(0, steps, unroll=min(steps, 3))
        def _(step):
            ch = first + step
            result(ch)
            source, row = ch * STEP_ROWS, step * STEP_ROWS
            copy_rows(par_ov, source, par_out[i], row, STEP_ROWS, sems.at[7 + i]).start()

        first += steps

    energy = jnp.zeros((8, LANES), F32) + jnp.sum(total_ref[...]) * F32(share)
    if earlier:
        energy = energy + before_v[...]
    energy_v[...] = energy
    report = pltpu.make_async_copy(energy_v, energy_out, sems.at[7 + len(pieces)])
    report.start()
    pltpu.make_async_copy(own_ov, own_out, sems.at[6]).wait()
    first = 0
    for i, steps in enumerate(pieces):
        rows = steps * STEP_ROWS
        copy_rows(par_ov, first, par_out[i], 0, rows, sems.at[7 + i]).wait()
        first += rows
    report.wait()


def pair_terms(own, own_u, partner, earlier, tables, kern, pieces, share, interpret=False):
    hbm = pl.BlockSpec(memory_space=pl.ANY)
    return pl.pallas_call(
        functools.partial(pairs_kernel, pieces, share),
        out_shape=(
            jax.ShapeDtypeStruct((2, ROWS, LANES), F32),
            *[jax.ShapeDtypeStruct((steps * STEP_ROWS, LANES), BF16) for steps in pieces],
            jax.ShapeDtypeStruct((8, LANES), F32),
        ),
        in_specs=[hbm] * (5 + len(earlier) + len(tables)),
        out_specs=(hbm,) * (2 + len(pieces)),
        scratch_shapes=[
            pltpu.VMEM((2, ROWS, LANES), BF16),
            pltpu.VMEM((2, G, G, LANES), BF16),
            pltpu.VMEM((KPAD * G, LANES), F32),
            pltpu.VMEM((2, ROWS, LANES), F32),
            pltpu.VMEM((ROWS, LANES), BF16),
            pltpu.VMEM((G * F_PITCH, LANES), F32),
            pltpu.VMEM((G, G, LANES), BF16),
            pltpu.VMEM((2 * G * Y_PITCH, LANES), F32),
            pltpu.VMEM((4 * Z_ROWS, LANES), F32),
            pltpu.VMEM((KPAD * G, 4 * LANES), BF16),
            pltpu.VMEM((2, STEP_ROWS, LANES), F32),
            pltpu.VMEM((STEP_ROWS, LANES), F32),
            pltpu.VMEM((QUADS, LANES), F32),
            pltpu.VMEM((8, LANES), F32),
            pltpu.VMEM((8, LANES), F32),
            *[pltpu.VMEM(table.shape, BF16) for table in tables],
            pltpu.SemaphoreType.DMA((2,)),
            pltpu.SemaphoreType.DMA((len(tables),)),
            pltpu.SemaphoreType.DMA((9 + len(pieces),)),
        ],
        compiler_params=pltpu.CompilerParams(vmem_limit_bytes=63 * MIB),
        cost_estimate=pl.CostEstimate(
            flops=20_000_000_000, bytes_accessed=20_000_000, transcendentals=0
        ),
        interpret=interpret,
        name="pair_terms",
    )(*own, own_u, kern, partner, *earlier, *tables)


def piece_kernel(first, size, own0, own1, terms, back0, back1, *rest):
    last = first + size == ROWS
    earlier = rest[: len(rest) - 12]
    out, gram_out, own_v, terms_v, back_v, out_v, gram_ref, gram_v, value_ref = rest[-12:-3]
    load_sems, gram_sems, store_sems = rest[-3:]
    rows = size // load_sems.shape[0]

    def loads(c):
        start = first + c * rows
        sources = [
            (own0, start, own_v.at[0]), (own1, start, own_v.at[1]), (terms, start, terms_v),
            (back0, start, back_v.at[0]), (back1, c * rows, back_v.at[1]),
        ]
        return [
            copy_rows(src, row, dst, c * rows, rows, load_sems.at[c, i])
            for i, (src, row, dst) in enumerate(sources)
        ]

    chunks = [loads(c) for c in range(load_sems.shape[0])]
    for chunk in chunks:
        for load in chunk:
            load.start()
    gram_loads = []
    if last:
        gram_loads = [
            pltpu.make_async_copy(src, gram_v.at[i], gram_sems.at[i])
            for i, src in enumerate(earlier[:-1])
        ]
        for load in gram_loads:
            load.start()
    gram_ref[...] = jnp.zeros_like(gram_ref)
    for c, chunk in enumerate(chunks):
        for load in chunk:
            load.wait()
        at = pl.ds(c * rows, rows)
        own = [own_v[i, at, :].astype(F32) for i in range(2)]
        for p in range(2):
            exchange = terms_v[p, at, :] + back_v[p, at, :].astype(F32)
            out_v[pl.ds(2 * c * rows + p, rows, stride=2), :] = exchange
            for i in range(2):
                product = (own[i] * exchange).reshape(-1, 8, LANES)
                gram_ref[i, p] += jnp.sum(product, axis=0)
        copy_rows(out_v, 2 * c * rows, out, 2 * (first + c * rows), 2 * rows, store_sems.at[0]).start()

    result = gram_ref
    if last:
        for load in gram_loads:
            load.wait()
        row = lax.broadcasted_iota(jnp.int32, (2, 2), 0)
        column = lax.broadcasted_iota(jnp.int32, (2, 2), 1)
        value = jnp.zeros((2, 2), F32)
        for i in range(2):
            for j in range(2):
                entry = gram_ref[i, j]
                for k in range(len(gram_loads)):
                    entry = entry + gram_v[k, i, j]
                value = jnp.where((row == i) & (column == j), jnp.sum(entry) * F32(1.0 / NGRID), value)
        value_ref[...] = value
        result = value_ref
    report = pltpu.make_async_copy(result, gram_out, store_sems.at[1])
    report.start()
    copy_rows(out_v, 0, out, 2 * first, 2 * size, store_sems.at[0]).wait()
    report.wait()


def add_piece(first, size, own, terms, back0, back1, grams, out, interpret=False):
    hbm = pl.BlockSpec(memory_space=pl.ANY)
    last = first + size == ROWS
    earlier = [] if out is None else [*(grams if last else []), out]
    gram_shape = (2, 2, 8, LANES)
    return pl.pallas_call(
        functools.partial(piece_kernel, first, size),
        out_shape=(
            jax.ShapeDtypeStruct((2 * ROWS, LANES), F32),
            jax.ShapeDtypeStruct((2, 2) if last else gram_shape, F32),
        ),
        in_specs=[hbm] * (5 + len(earlier)),
        out_specs=(hbm, hbm),
        scratch_shapes=[
            pltpu.VMEM((2, size, LANES), BF16),
            pltpu.VMEM((2, size, LANES), F32),
            pltpu.VMEM((2, size, LANES), BF16),
            pltpu.VMEM((2 * size, LANES), F32),
            pltpu.VMEM(gram_shape, F32),
            pltpu.VMEM((len(PIECES), *gram_shape), F32),
            pltpu.VMEM((2, 2), F32),
            pltpu.SemaphoreType.DMA((2 * size // STEP_ROWS, 5)),
            pltpu.SemaphoreType.DMA((len(PIECES),)),
            pltpu.SemaphoreType.DMA((2,)),
        ],
        input_output_aliases={4 + len(earlier): 0} if earlier else {},
        compiler_params=pltpu.CompilerParams(vmem_limit_bytes=52 * MIB),
        cost_estimate=cost(24 * size * LANES),
        interpret=interpret,
        name="add_piece",
    )(*own, terms, back0, back1, *earlier)


def from_behind(block, axis, distance):
    size = lax.axis_size(axis)
    return lax.ppermute(block, axis, [((i - distance) % size, i) for i in range(size)])


def after(values, other):
    return lax.optimization_barrier((values, other))[0]


def per_device(orbitals):
    tables = section_tables()
    kern = screening()
    size = lax.axis_size("band")
    share = -2.0 / (NGRID * 2 * size * orbitals.shape[0])
    raw = orbitals.reshape(2, ROWS, LANES).transpose(1, 0, 2).reshape(2 * ROWS, LANES)
    own = [take_band(raw, 0)]
    own.append(take_band(raw, 1, own))
    previous = [from_behind(part, "band", 1) for part in own]
    own_u = padded_rows(own, tables[-1])
    terms, back0, energy = pair_terms(
        own, own_u, previous[0], (), tables, kern, (STEPS,), share
    )
    back0 = from_behind(back0, "band", -1)
    terms, *sent, energy = pair_terms(
        own, own_u, previous[1], (terms, energy), tables, kern, PIECES, share
    )
    back1 = [from_behind(piece, "band", -1) for piece in sent]

    steps = []
    if size & (size - 1):
        energy = lax.psum(energy, "band")
    else:
        swap = [(i, i ^ 1) for i in range(size)]
        energy = energy + lax.ppermute(energy, "band", swap)
        steps = [1 << b for b in range(1, size.bit_length() - 1)]
        steps = [b for b in steps if b != 2] + [b for b in steps if b == 2]
        aside = [4 if size > 4 else 2, 8 if size > 8 else 2]
        steps = [[(i, i ^ (b if i % 2 else aside[i // 2 % 2])) for i in range(size)] for b in steps]
    while len(steps) > len(back1) - 1:
        energy = energy + lax.ppermute(energy, "band", steps.pop(0))
    exchange, grams = None, []
    first = 0
    for count, piece in zip(PIECES, back1):
        count *= STEP_ROWS
        got, last = None, piece is back1[-1]
        if last and size & (size - 1) == 0:
            got = lax.ppermute(energy, "band", swap)
        elif steps:
            got = lax.ppermute(energy, "band", steps.pop(0))
        exchange, gram = add_piece(first, count, own, terms, back0, piece, grams, exchange)
        if got is not None and last:
            odd = lax.axis_index("band") % 2 == 1
            energy = jnp.where(odd, energy[:1, :1], after(got, gram)[:1, :1])
        elif got is not None:
            energy = energy + after(got, gram)
        grams.append(gram)
        first += count
    exchange = exchange.reshape(ROWS, 2, LANES).transpose(1, 0, 2).reshape(2, NGRID)
    return exchange, gram, energy[0, 0]


def solution(mesh):
    return jax.shard_map(
        per_device,
        mesh=mesh,
        in_specs=(P("band", None),),
        out_specs=(P("band", None), P("band", None), P()),
        check_vma=False,
    )
```

```python
import functools

import jax
import jax.numpy as jnp
import ml_dtypes
import numpy as np
from jax import lax
from jax.experimental import pallas as pl
from jax.experimental.pallas import tpu as pltpu
from jax.sharding import PartitionSpec as P

G = 96
HALF = G // 2 + 1
NGRID = G * G * G
LANES = 128
ROWS = NGRID // LANES
PLANE = G * G // LANES
QUADS = G // 4
KPAD = HALF + 1
Y_ROWS = 104
Y_PITCH = Y_ROWS + 1
Z_PITCH = G + 1
W_PITCH = 2 * G + 1
Z_ROWS = KPAD * Z_PITCH
F_PITCH = PLANE + 1
PLANES = 16
STEP_ROWS = PLANES * QUADS
THIRD = G * QUADS
STEPS = G // PLANES
PIECES = (3, 2, 1)
WAVE_UNIT = 0.05
SCREEN_SQ = 0.0121
MIB = 1024 * 1024
BF16 = jnp.bfloat16
F32 = jnp.float32


def dft_tables():
    n = np.arange(G)
    phases = (n[:, None] * n[None, :]) % G
    angles = phases.astype(np.float32) * np.float32(2.0 * np.pi / G)
    rounded = [f(angles).astype(ml_dtypes.bfloat16).astype(np.float32) for f in (np.cos, np.sin)]
    return rounded[0], rounded[1]


def section_tables():
    c, s = dft_tables()
    h = HALF
    t1 = np.zeros((Y_ROWS, G), np.float32)
    t1[:h] = c[:h]
    t1[h : 2 * h] = -s[:h]
    t2 = np.block([[c, s], [-s, c]])
    t3 = np.zeros((2, LANES, 4, 64), np.float32)
    back = (G - np.arange(h)) % G
    t3[0, :G, 0, :h] = c[:h].T
    t3[1, :G, 0, :h] = s[:h].T
    t3[0, :G, 1, :h] = -s[:h].T
    t3[1, :G, 1, :h] = c[:h].T
    t3[0, :G, 2, :h] = c[back].T
    t3[1, :G, 2, :h] = s[back].T
    t3[0, :G, 3, :h] = s[back].T
    t3[1, :G, 3, :h] = -c[back].T
    t3 = t3.reshape(2 * LANES, 4 * 64)
    order = np.concatenate([np.arange(G // 2), G - 1 - np.arange(G // 2)])
    a1 = np.block([[c[:, order], -s[:, order]], [s[:, order], c[:, order]]])
    rows = np.arange(G).reshape(QUADS, 4).T.reshape(-1)
    a2 = np.block([[c[rows], -s[rows]], [s[rows], c[rows]]])
    weight = np.full((h, 1), 2.0, np.float32)
    weight[0] = weight[h - 1] = 1.0
    a3 = np.zeros((3, 2, 2, 2, 64, 2, LANES), np.float32)
    for third in range(3):
        for lane in range(LANES):
            r, x3 = divmod(third * LANES + lane, G)
            for p in range(2):
                a3[third, r - third, 0, p, :h, p, lane] = weight[:, 0] * c[x3, :h]
                a3[third, r - third, 1, p, :h, p, lane] = -weight[:, 0] * s[x3, :h]
    a3 = a3.reshape(3, 4 * LANES, 2 * LANES)
    sel = np.zeros((2, 2 * LANES, 2 * LANES), np.float32)
    for r in range(4):
        for x in range(G):
            sel[r // 2, r * G + x - (r // 2) * LANES, (r % 2) * LANES + x] = 1.0
    return [t.astype(ml_dtypes.bfloat16) for t in (t1, t2, t3, a1, a2, a3, sel)]


def screening():
    n = np.arange(G)
    m = np.where(n <= G // 2, n, n - G).astype(np.float64)
    sq = m * m
    q2 = WAVE_UNIT * (sq[:HALF, None, None] + sq[None, :, None] + sq[None, None, :HALF])
    safe = np.where(q2 > 0, q2, 1.0)
    kern = 4.0 * np.pi * (1.0 - np.exp(-q2 / (4.0 * SCREEN_SQ))) / safe
    kern = np.where(q2 > 0, kern, np.pi / SCREEN_SQ)
    out = np.zeros((KPAD, G, 2, 64), np.float32)
    out[:HALF, :, :, :HALF] = kern[:, :, None, :]
    return out.reshape(KPAD * G, LANES)


def cost(size):
    return pl.CostEstimate(flops=0, bytes_accessed=size, transcendentals=0)


def dot(a, b):
    return jnp.dot(a, b, preferred_element_type=F32)


def lanes(*parts):
    return jnp.concatenate(parts, axis=1)


def stack(*parts):
    return jnp.concatenate(parts, axis=0)


def split_rows(src, sel_ref, out, first, count):
    rows = [
        [src[pl.ds(3 * (first + i) + s, G, stride=F_PITCH), :].astype(BF16) for s in range(3)]
        for i in range(count)
    ]
    for half in range(2):
        part = dot(stack(*[lanes(r[half], r[half + 1]) for r in rows]), sel_ref[half])
        for i in range(count):
            for e in range(2):
                value = part[i * G : (i + 1) * G, e * LANES : (e + 1) * LANES]
                out[4 * (first + i) + 2 * half + e] = value.astype(BF16)


def widen_planes(src, dst, first):
    @pl.loop(0, src.shape[0] // (2 * PLANE), unroll=8)
    def _(i):
        value = src[pl.ds(pl.multiple_of(i * 2 * PLANE, 16), 2 * PLANE), :].astype(F32)
        dst[pl.ds((first + 2 * i) * F_PITCH, PLANE), :] = value[:PLANE]
        dst[pl.ds((first + 2 * i + 1) * F_PITCH, PLANE), :] = value[PLANE:]


def rows_of(ref, first, count):
    return ref.at[(slice(None),) * (len(ref.shape) - 2) + (pl.ds(first, count), slice(None))]


def copy_rows(src, src_row, dst, dst_row, count, sem):
    return pltpu.make_async_copy(rows_of(src, src_row, count), rows_of(dst, dst_row, count), sem)


def band_kernel(p, raw, *refs):
    out, raw_v, out_v, load_sems, store_sem = refs[-5:]
    chunks = load_sems.shape[0]
    rows = out.shape[0] // chunks
    loads = [
        copy_rows(raw, 2 * c * rows, raw_v, 2 * c * rows, 2 * rows, load_sems.at[c])
        for c in range(chunks)
    ]
    for load in loads:
        load.start()
    shape = (LANES, 2 * LANES)
    row = lax.broadcasted_iota(jnp.int32, shape, 0)
    column = lax.broadcasted_iota(jnp.int32, shape, 1)
    pick = jnp.where(column == 2 * row + p, F32(1.0), F32(0.0)).astype(BF16)
    for c, load in enumerate(loads):
        load.wait()
        for row in range(c * rows, (c + 1) * rows, 2 * LANES):
            blocks = [raw_v[2 * at : 2 * at + 2 * LANES, :] for at in (row, row + LANES)]
            value = dot(pick, lanes(*blocks)).astype(BF16)
            out_v[row : row + LANES, :] = value[:, :LANES]
            out_v[row + LANES : row + 2 * LANES, :] = value[:, LANES:]
        copy_rows(out_v, c * rows, out, c * rows, rows, store_sem).start()
    pltpu.make_async_copy(out_v, out, store_sem).wait()


def take_band(raw, p, earlier=(), interpret=False):
    hbm = pl.BlockSpec(memory_space=pl.ANY)
    return pl.pallas_call(
        functools.partial(band_kernel, p),
        out_shape=jax.ShapeDtypeStruct((ROWS, LANES), BF16),
        in_specs=[hbm] * (1 + len(earlier)),
        out_specs=hbm,
        scratch_shapes=[
            pltpu.VMEM((2 * ROWS, LANES), BF16),
            pltpu.VMEM((ROWS, LANES), BF16),
            pltpu.SemaphoreType.DMA((9,)),
            pltpu.SemaphoreType.DMA,
        ],
        compiler_params=pltpu.CompilerParams(vmem_limit_bytes=63 * MIB),
        cost_estimate=cost(6 * ROWS * LANES),
        interpret=interpret,
        name="take_band",
    )(raw, *earlier)


def rows_kernel(own0, own1, sel, out, thirds, wide):
    for p, own in enumerate((own0, own1)):
        widen_planes(own, wide, 0)

        @pl.loop(0, QUADS // 4, unroll=2)
        def _(q):
            split_rows(wide, sel, out.at[p], 4 * q, 4)

        @pl.loop(0, G // 2, unroll=4)
        def _(i):
            for s in range(3):
                rows = [wide[pl.ds((2 * i + e) * F_PITCH + s, QUADS, stride=3), :] for e in range(2)]
                at = pl.multiple_of(2 * i * QUADS, 16)
                thirds[p, s, pl.ds(at, 2 * QUADS), :] = stack(*rows).astype(BF16)


def padded_rows(own, sel, interpret=False):
    vmem = pl.BlockSpec(memory_space=pltpu.VMEM)
    return pl.pallas_call(
        rows_kernel,
        out_shape=(
            jax.ShapeDtypeStruct((2, G, G, LANES), BF16),
            jax.ShapeDtypeStruct((2, 3, THIRD, LANES), BF16),
        ),
        in_specs=[vmem] * 3,
        out_specs=(vmem, vmem),
        scratch_shapes=[pltpu.VMEM((G * F_PITCH, LANES), F32)],
        compiler_params=pltpu.CompilerParams(vmem_limit_bytes=63 * MIB),
        cost_estimate=cost(16 * NGRID),
        interpret=interpret,
        name="padded_rows",
    )(*own, sel)


def pairs_kernel(pieces, share, own, own_u, kern, par, *refs):
    earlier = []
    if len(pieces) > 1:
        earlier, refs = refs[:2], refs[2:]
    table_refs, own_out = refs[:7], refs[7]
    par_out, energy_out = refs[8 : 8 + len(pieces)], refs[8 + len(pieces)]
    own_v, own_uv, kern_v, own_ov, par_ov, par_f, par_u, yw, z, x34 = refs[9 + len(pieces) : -15]
    par_v, total_ref, energy_v, before_v = refs[-15:-11]
    tables, (par_sems, table_sems, before_sems, sems) = refs[-11:-4], refs[-4:]
    t1, t2, t3, a1, a2, a3, sel = tables
    par_loads = []
    for first in (0, ROWS // 2):
        sem = par_sems.at[len(par_loads)]
        par_loads.append(copy_rows(par, first, par_v, first, ROWS // 2, sem))
    for load in par_loads:
        load.start()
    table_loads = [
        pltpu.make_async_copy(src, dst, table_sems.at[i])
        for i, (src, dst) in enumerate(zip(table_refs, tables))
    ]
    table_loads[6].start()
    table_loads[0].start()
    loads = [
        pltpu.make_async_copy(own_u, own_uv, sems.at[0]),
        pltpu.make_async_copy(kern, kern_v, sems.at[1]),
        pltpu.make_async_copy(own, own_v, sems.at[2]),
    ]
    later = []
    if earlier:
        later = [
            copy_rows(earlier[0].at[p, s], 0, z, (3 * p + s) * THIRD, THIRD, before_sems.at[3 * p + s])
            for p in range(2)
            for s in range(3)
        ]
        loads.append(pltpu.make_async_copy(earlier[1], before_v, sems.at[3]))

    for i, load in enumerate(par_loads):
        load.wait()
        for other in ([loads[0]], table_loads[1:5])[i]:
            other.start()
        widen_planes(par_v.at[pl.ds(i * ROWS // 2, ROWS // 2), :], par_f, i * G // 2)
    table_loads[6].wait()

    @pl.loop(0, QUADS // 4, unroll=6)
    def _(q):
        split_rows(par_f, sel, par_u, 4 * q, 4)

    half_y = G * Y_PITCH
    loads[0].wait()
    for load in loads[1:]:
        load.start()
    table_loads[5].start()
    table_loads[0].wait()

    @pl.loop(0, G // 2, unroll=24)
    def _(i):
        density = []
        for e in range(2):
            partner = par_u[2 * i + e].astype(F32)
            for p in range(2):
                density.append((own_uv[p, 2 * i + e].astype(F32) * partner).astype(BF16))
        out = dot(t1[...], lanes(*density))
        for e in range(2):
            for p in range(2):
                at = pl.ds(p * half_y + (2 * i + e) * Y_PITCH, Y_ROWS)
                yw[at, :] = out[:, (2 * e + p) * LANES : (2 * e + p + 1) * LANES]

    table_loads[1].wait()

    @pl.loop(0, KPAD // 2, unroll=25)
    def _(pair):
        def line(k1, part):
            first = part * HALF + k1
            rows = [yw[pl.ds(p * half_y + first, G, stride=Y_PITCH), :].astype(BF16) for p in range(2)]
            return lanes(*rows)

        both = [2 * pair, 2 * pair + 1]
        out = dot(t2[...], lanes(*[stack(line(k1, 0), line(k1, 1)) for k1 in both]))
        for e, k1 in enumerate(both):
            at = pl.ds(pl.multiple_of(k1 * G, 16), G)
            for p in range(2):
                for part in range(2):
                    left = (2 * p + part) * LANES
                    right = (2 * e + p) * LANES
                    value = out[part * G : (part + 1) * G, right : right + LANES]
                    x34[at, left : left + LANES] = value.astype(BF16)

    loads[1].wait()
    table_loads[2].wait()

    many = 5

    @pl.loop(0, KPAD // many, unroll=10)
    def _(m):
        at = pl.ds(pl.multiple_of(m * many * G, 16), many * G)
        factor = kern_v[at, :]
        out = [
            dot(x34[at, 2 * p * LANES : 2 * (p + 1) * LANES], t3[...]).astype(BF16)
            for p in range(2)
        ]
        for part in range(4):
            spectrum = lanes(*[o[:, part * 64 : (part + 1) * 64] for o in out]).astype(F32)
            value = spectrum * factor
            for i in range(many):
                row = part * Z_ROWS + (many * m + i) * Z_PITCH
                z[pl.ds(row, G), :] = value[i * G : (i + 1) * G]

    table_loads[3].wait()

    @pl.loop(0, G // 4, unroll=24)
    def _(four):
        parts = []
        for e in range(4):
            k2 = 4 * four + e
            mirror = Z_PITCH + jnp.where(k2 == 0, 0, G - k2)
            parts.append(
                stack(
                    z[pl.ds(k2, G // 2, stride=Z_PITCH), :].astype(BF16),
                    z[pl.ds(2 * Z_ROWS + mirror, G // 2, stride=Z_PITCH), :].astype(BF16),
                    z[pl.ds(1 * Z_ROWS + k2, G // 2, stride=Z_PITCH), :].astype(BF16),
                    z[pl.ds(3 * Z_ROWS + mirror, G // 2, stride=Z_PITCH), :].astype(BF16),
                )
            )
        out = dot(a1[...], lanes(*parts))
        for e in range(4):
            at = (4 * four + e) * W_PITCH
            yw[pl.ds(at, 2 * G), :] = out[:, e * LANES : (e + 1) * LANES]

    for load in later:
        load.start()
    table_loads[4].wait()

    @pl.loop(0, G // 4, unroll=24)
    def _(four):
        parts = []
        for e in range(4):
            x1 = 4 * four + e
            parts.append(
                stack(
                    yw[pl.ds(x1, G, stride=W_PITCH), :].astype(BF16),
                    yw[pl.ds(G + x1, G, stride=W_PITCH), :].astype(BF16),
                )
            )
        out = dot(a2[...], lanes(*parts))
        for r in range(4):
            block = [
                lanes(
                    out[r * QUADS : (r + 1) * QUADS, e * LANES : (e + 1) * LANES],
                    out[G + r * QUADS : G + (r + 1) * QUADS, e * LANES : (e + 1) * LANES],
                )
                for e in range(4)
            ]
            at = pl.multiple_of((r // 2) * G * QUADS + four * 4 * QUADS, 16)
            left = (r % 2) * 2 * LANES
            x34[pl.ds(at, 4 * QUADS), left : left + 2 * LANES] = stack(*block).astype(BF16)

    table_loads[5].wait()
    for load in loads[2:] + later:
        load.wait()
    total_ref[...] = jnp.zeros_like(total_ref)
    scale = F32(1.0 / NGRID)

    def result(ch):
        at = pl.multiple_of(ch * STEP_ROWS, 16)
        rows = pl.ds(at, STEP_ROWS)
        low = x34[rows, :]
        high = x34[pl.ds(THIRD + at, STEP_ROWS), :]
        fields = [low, lanes(low[:, 2 * LANES :], high[:, : 2 * LANES]), high]
        total = jnp.zeros((8, LANES), F32)
        for third in range(3):
            out = dot(fields[third], a3[third]) * scale
            first = ch * PLANES * F_PITCH + third
            partner = stack(
                *[par_f[pl.ds(first + i * F_PITCH, QUADS, stride=3), :] for i in range(PLANES)]
            )
            sent = None
            for p in range(2):
                potential = out[:, p * LANES : (p + 1) * LANES]
                term = potential * partner
                if earlier:
                    term = term + z[pl.ds((3 * p + third) * THIRD + at, STEP_ROWS), :]
                own_ov[p, third, rows, :] = term
                part = potential * own_v[p, third, rows, :].astype(F32)
                sent = part if sent is None else sent + part
            total = total + jnp.sum((sent * partner).reshape(-1, 8, LANES), axis=0)
            par_ov[third, rows, :] = sent.astype(BF16)
        total_ref[...] += total
        copy_rows(own_ov, at, own_out, at, STEP_ROWS, sems.at[4]).start()

    first = 0
    for i, steps in enumerate(pieces):

        @pl.loop(0, steps, unroll=min(steps, 3))
        def _(step):
            ch = first + step
            result(ch)
            source, row = ch * STEP_ROWS, step * STEP_ROWS
            copy_rows(par_ov, source, par_out[i], row, STEP_ROWS, sems.at[6 + i]).start()

        first += steps

    energy = jnp.zeros((8, LANES), F32) + jnp.sum(total_ref[...]) * F32(share)
    if earlier:
        energy = energy + before_v[...]
    energy_v[...] = energy
    report = pltpu.make_async_copy(energy_v, energy_out, sems.at[5])
    report.start()
    pltpu.make_async_copy(own_ov, own_out, sems.at[4]).wait()
    first = 0
    for i, steps in enumerate(pieces):
        rows = steps * STEP_ROWS
        copy_rows(par_ov, first, par_out[i], 0, rows, sems.at[6 + i]).wait()
        first += rows
    report.wait()


def pair_terms(own, own_u, partner, earlier, tables, kern, pieces, share, interpret=False):
    hbm = pl.BlockSpec(memory_space=pl.ANY)
    return pl.pallas_call(
        functools.partial(pairs_kernel, pieces, share),
        out_shape=(
            jax.ShapeDtypeStruct((2, 3, THIRD, LANES), F32),
            *[jax.ShapeDtypeStruct((3, steps * STEP_ROWS, LANES), BF16) for steps in pieces],
            jax.ShapeDtypeStruct((8, LANES), F32),
        ),
        in_specs=[hbm] * (4 + len(earlier) + len(tables)),
        out_specs=(hbm,) * (2 + len(pieces)),
        scratch_shapes=[
            pltpu.VMEM((2, 3, THIRD, LANES), BF16),
            pltpu.VMEM((2, G, G, LANES), BF16),
            pltpu.VMEM((KPAD * G, LANES), F32),
            pltpu.VMEM((2, 3, THIRD, LANES), F32),
            pltpu.VMEM((3, THIRD, LANES), BF16),
            pltpu.VMEM((G * F_PITCH, LANES), F32),
            pltpu.VMEM((G, G, LANES), BF16),
            pltpu.VMEM((2 * G * Y_PITCH, LANES), F32),
            pltpu.VMEM((4 * Z_ROWS, LANES), F32),
            pltpu.VMEM((KPAD * G, 4 * LANES), BF16),
            pltpu.VMEM((ROWS, LANES), BF16),
            pltpu.VMEM((8, LANES), F32),
            pltpu.VMEM((8, LANES), F32),
            pltpu.VMEM((8, LANES), F32),
            *[pltpu.VMEM(table.shape, BF16) for table in tables],
            pltpu.SemaphoreType.DMA((2,)),
            pltpu.SemaphoreType.DMA((len(tables),)),
            pltpu.SemaphoreType.DMA((6,)),
            pltpu.SemaphoreType.DMA((6 + len(pieces),)),
        ],
        compiler_params=pltpu.CompilerParams(vmem_limit_bytes=63 * MIB),
        cost_estimate=pl.CostEstimate(
            flops=20_000_000_000, bytes_accessed=20_000_000, transcendentals=0
        ),
        interpret=interpret,
        name="pair_terms",
    )(own, own_u, kern, partner, *earlier, *tables)


def piece_kernel(first, size, own, terms, back0, back1, *rest):
    last = first + size == THIRD
    earlier = rest[: len(rest) - 12]
    out, gram_out, own_v, terms_v, back_v, out_v, gram_ref, gram_v, value_ref = rest[-12:-3]
    load_sems, gram_sems, store_sems = rest[-3:]
    rows = size // load_sems.shape[0]
    wide = 6 * rows

    def loads(c):
        start = first + c * rows
        sources = [
            (own, start, own_v), (terms, start, terms_v),
            (back0, start, back_v.at[0]), (back1, c * rows, back_v.at[1]),
        ]
        return [
            copy_rows(src, row, dst, c * rows, rows, load_sems.at[c, i])
            for i, (src, row, dst) in enumerate(sources)
        ]

    chunks = [loads(c) for c in range(load_sems.shape[0])]
    for chunk in chunks:
        for load in chunk:
            load.start()
    gram_loads = []
    if last:
        gram_loads = [
            pltpu.make_async_copy(src, gram_v.at[i], gram_sems.at[i])
            for i, src in enumerate(earlier[:-1])
        ]
        for load in gram_loads:
            load.start()
    gram_ref[...] = jnp.zeros_like(gram_ref)
    for c, chunk in enumerate(chunks):
        for load in chunk:
            load.wait()
        at = pl.ds(c * rows, rows)
        for s in range(3):
            bands = [own_v[i, s, at, :].astype(F32) for i in range(2)]
            for p in range(2):
                exchange = terms_v[p, s, at, :] + back_v[p, s, at, :].astype(F32)
                for i in range(rows // QUADS):
                    row = c * wide + 2 * (i * PLANE + s) + p
                    out_v[pl.ds(row, QUADS, stride=6), :] = exchange[i * QUADS : (i + 1) * QUADS]
                for i in range(2):
                    product = (bands[i] * exchange).reshape(-1, 8, LANES)
                    gram_ref[i, p] += jnp.sum(product, axis=0)
        copy_rows(out_v, c * wide, out, 6 * first + c * wide, wide, store_sems.at[0]).start()

    result = gram_ref
    if last:
        for load in gram_loads:
            load.wait()
        row = lax.broadcasted_iota(jnp.int32, (2, 2), 0)
        column = lax.broadcasted_iota(jnp.int32, (2, 2), 1)
        value = jnp.zeros((2, 2), F32)
        for i in range(2):
            for j in range(2):
                entry = gram_ref[i, j]
                for k in range(len(gram_loads)):
                    entry = entry + gram_v[k, i, j]
                value = jnp.where((row == i) & (column == j), jnp.sum(entry) * F32(1.0 / NGRID), value)
        value_ref[...] = value
        result = value_ref
    report = pltpu.make_async_copy(result, gram_out, store_sems.at[1])
    report.start()
    copy_rows(out_v, 0, out, 6 * first, 6 * size, store_sems.at[0]).wait()
    report.wait()


def add_piece(first, size, own, terms, back0, back1, grams, out, interpret=False):
    hbm = pl.BlockSpec(memory_space=pl.ANY)
    last = first + size == THIRD
    earlier = [] if out is None else [*(grams if last else []), out]
    gram_shape = (2, 2, 8, LANES)
    return pl.pallas_call(
        functools.partial(piece_kernel, first, size),
        out_shape=(
            jax.ShapeDtypeStruct((2 * ROWS, LANES), F32),
            jax.ShapeDtypeStruct((2, 2) if last else gram_shape, F32),
        ),
        in_specs=[hbm] * (4 + len(earlier)),
        out_specs=(hbm, hbm),
        scratch_shapes=[
            pltpu.VMEM((2, 3, size, LANES), BF16),
            pltpu.VMEM((2, 3, size, LANES), F32),
            pltpu.VMEM((2, 3, size, LANES), BF16),
            pltpu.VMEM((6 * size, LANES), F32),
            pltpu.VMEM(gram_shape, F32),
            pltpu.VMEM((len(PIECES), *gram_shape), F32),
            pltpu.VMEM((2, 2), F32),
            pltpu.SemaphoreType.DMA((2 * size // STEP_ROWS, 4)),
            pltpu.SemaphoreType.DMA((len(PIECES),)),
            pltpu.SemaphoreType.DMA((2,)),
        ],
        input_output_aliases={3 + len(earlier): 0} if earlier else {},
        compiler_params=pltpu.CompilerParams(vmem_limit_bytes=52 * MIB),
        cost_estimate=cost(72 * size * LANES),
        interpret=interpret,
        name="add_piece",
    )(own, terms, back0, back1, *earlier)


def from_behind(block, axis, distance):
    size = lax.axis_size(axis)
    return lax.ppermute(block, axis, [((i - distance) % size, i) for i in range(size)])


def after(values, other):
    return lax.optimization_barrier((values, other))[0]


def per_device(orbitals):
    tables = section_tables()
    kern = screening()
    size = lax.axis_size("band")
    share = -2.0 / (NGRID * 2 * size * orbitals.shape[0])
    raw = orbitals.reshape(2, ROWS, LANES).transpose(1, 0, 2).reshape(2 * ROWS, LANES)
    own = [take_band(raw, 0)]
    own.append(take_band(raw, 1, own))
    previous = [from_behind(part, "band", 1) for part in own]
    own_u, thirds = padded_rows(own, tables[-1])
    terms, back0, energy = pair_terms(
        thirds, own_u, previous[0], (), tables, kern, (STEPS,), share
    )
    back0 = from_behind(back0, "band", -1)
    terms, *sent, energy = pair_terms(
        thirds, own_u, previous[1], (terms, energy), tables, kern, PIECES, share
    )
    back1 = [from_behind(piece, "band", -1) for piece in sent]

    steps = []
    if size & (size - 1):
        energy = lax.psum(energy, "band")
    else:
        swap = [(i, i ^ 1) for i in range(size)]
        energy = energy + lax.ppermute(energy, "band", swap)
        steps = [1 << b for b in range(1, size.bit_length() - 1)]
        steps = [b for b in steps if b != 2] + [b for b in steps if b == 2]
        aside = [4 if size > 4 else 2, 8 if size > 8 else 2]
        steps = [[(i, i ^ (b if i % 2 else aside[i // 2 % 2])) for i in range(size)] for b in steps]
    while len(steps) > len(back1) - 1:
        energy = energy + lax.ppermute(energy, "band", steps.pop(0))
    exchange, grams = None, []
    first = 0
    for count, piece in zip(PIECES, back1):
        count *= STEP_ROWS
        got, last = None, piece is back1[-1]
        if last and size & (size - 1) == 0:
            got = lax.ppermute(energy, "band", swap)
        elif steps:
            got = lax.ppermute(energy, "band", steps.pop(0))
        exchange, gram = add_piece(first, count, thirds, terms, back0, piece, grams, exchange)
        if got is not None and last:
            odd = lax.axis_index("band") % 2 == 1
            energy = jnp.where(odd, energy[:1, :1], after(got, gram)[:1, :1])
        elif got is not None:
            energy = energy + after(got, gram)
        grams.append(gram)
        first += count
    exchange = exchange.reshape(ROWS, 2, LANES).transpose(1, 0, 2).reshape(2, NGRID)
    return exchange, gram, energy[0, 0]


def solution(mesh):
    return jax.shard_map(
        per_device,
        mesh=mesh,
        in_specs=(P("band", None),),
        out_specs=(P("band", None), P("band", None), P()),
        check_vma=False,
    )
```

```python
import functools

import jax
import jax.numpy as jnp
import ml_dtypes
import numpy as np
from jax import lax
from jax.experimental import pallas as pl
from jax.experimental.pallas import tpu as pltpu
from jax.sharding import PartitionSpec as P

G = 96
HALF = G // 2 + 1
NGRID = G * G * G
LANES = 128
ROWS = NGRID // LANES
PLANE = G * G // LANES
QUADS = G // 4
KPAD = HALF + 1
Y_ROWS = 104
Y_PITCH = Y_ROWS + 1
Z_PITCH = G + 1
W_PITCH = 2 * G + 1
Z_ROWS = KPAD * Z_PITCH
F_PITCH = PLANE + 1
PLANES = 16
STEP_ROWS = PLANES * QUADS
THIRD = G * QUADS
STEPS = G // PLANES
PIECES = (2, 2, 1, 1)
WAVE_UNIT = 0.05
SCREEN_SQ = 0.0121
MIB = 1024 * 1024
BF16 = jnp.bfloat16
F32 = jnp.float32


def dft_tables():
    n = np.arange(G)
    phases = (n[:, None] * n[None, :]) % G
    angles = phases.astype(np.float32) * np.float32(2.0 * np.pi / G)
    rounded = [f(angles).astype(ml_dtypes.bfloat16).astype(np.float32) for f in (np.cos, np.sin)]
    return rounded[0], rounded[1]


def section_tables():
    c, s = dft_tables()
    h = HALF
    t1 = np.zeros((Y_ROWS, G), np.float32)
    t1[:h] = c[:h]
    t1[h : 2 * h] = -s[:h]
    t2 = np.block([[c, s], [-s, c]])
    t3 = np.zeros((2, LANES, 4, 64), np.float32)
    back = (G - np.arange(h)) % G
    t3[0, :G, 0, :h] = c[:h].T
    t3[1, :G, 0, :h] = s[:h].T
    t3[0, :G, 1, :h] = -s[:h].T
    t3[1, :G, 1, :h] = c[:h].T
    t3[0, :G, 2, :h] = c[back].T
    t3[1, :G, 2, :h] = s[back].T
    t3[0, :G, 3, :h] = s[back].T
    t3[1, :G, 3, :h] = -c[back].T
    t3 = t3.reshape(2 * LANES, 4 * 64)
    order = np.concatenate([np.arange(G // 2), G - 1 - np.arange(G // 2)])
    a1 = np.block([[c[:, order], -s[:, order]], [s[:, order], c[:, order]]])
    rows = np.arange(G).reshape(QUADS, 4).T.reshape(-1)
    a2 = np.block([[c[rows], -s[rows]], [s[rows], c[rows]]])
    weight = np.full((h, 1), 2.0, np.float32)
    weight[0] = weight[h - 1] = 1.0
    a3 = np.zeros((3, 2, 2, 2, 64, 2, LANES), np.float32)
    for third in range(3):
        for lane in range(LANES):
            r, x3 = divmod(third * LANES + lane, G)
            for p in range(2):
                a3[third, r - third, 0, p, :h, p, lane] = weight[:, 0] * c[x3, :h]
                a3[third, r - third, 1, p, :h, p, lane] = -weight[:, 0] * s[x3, :h]
    a3 = a3.reshape(3, 4 * LANES, 2 * LANES)
    sel = np.zeros((2, 2 * LANES, 2 * LANES), np.float32)
    for r in range(4):
        for x in range(G):
            sel[r // 2, r * G + x - (r // 2) * LANES, (r % 2) * LANES + x] = 1.0
    return [t.astype(ml_dtypes.bfloat16) for t in (t1, t2, t3, a1, a2, a3, sel)]


def screening():
    n = np.arange(G)
    m = np.where(n <= G // 2, n, n - G).astype(np.float64)
    sq = m * m
    q2 = WAVE_UNIT * (sq[:HALF, None, None] + sq[None, :, None] + sq[None, None, :HALF])
    safe = np.where(q2 > 0, q2, 1.0)
    kern = 4.0 * np.pi * (1.0 - np.exp(-q2 / (4.0 * SCREEN_SQ))) / safe
    kern = np.where(q2 > 0, kern, np.pi / SCREEN_SQ)
    out = np.zeros((KPAD, G, 2, 64), np.float32)
    out[:HALF, :, :, :HALF] = kern[:, :, None, :]
    return out.reshape(KPAD * G, LANES)


def cost(size):
    return pl.CostEstimate(flops=0, bytes_accessed=size, transcendentals=0)


def dot(a, b):
    return jnp.dot(a, b, preferred_element_type=F32)


def lanes(*parts):
    return jnp.concatenate(parts, axis=1)


def stack(*parts):
    return jnp.concatenate(parts, axis=0)


def split_rows(src, sel_ref, out, first, count):
    rows = [
        [src[pl.ds(3 * (first + i) + s, G, stride=F_PITCH), :].astype(BF16) for s in range(3)]
        for i in range(count)
    ]
    for half in range(2):
        part = dot(stack(*[lanes(r[half], r[half + 1]) for r in rows]), sel_ref[half])
        for i in range(count):
            for e in range(2):
                value = part[i * G : (i + 1) * G, e * LANES : (e + 1) * LANES]
                out[4 * (first + i) + 2 * half + e] = value.astype(BF16)


def widen_planes(src, dst, first):
    @pl.loop(0, src.shape[0] // (2 * PLANE), unroll=8)
    def _(i):
        value = src[pl.ds(pl.multiple_of(i * 2 * PLANE, 16), 2 * PLANE), :].astype(F32)
        dst[pl.ds((first + 2 * i) * F_PITCH, PLANE), :] = value[:PLANE]
        dst[pl.ds((first + 2 * i + 1) * F_PITCH, PLANE), :] = value[PLANE:]


def rows_of(ref, first, count):
    return ref.at[(slice(None),) * (len(ref.shape) - 2) + (pl.ds(first, count), slice(None))]


def copy_rows(src, src_row, dst, dst_row, count, sem):
    return pltpu.make_async_copy(rows_of(src, src_row, count), rows_of(dst, dst_row, count), sem)


def band_kernel(p, raw, *refs):
    out, raw_v, out_v, load_sems, store_sem = refs[-5:]
    chunks = load_sems.shape[0]
    rows = out.shape[0] // chunks
    loads = [
        copy_rows(raw, 2 * c * rows, raw_v, 2 * c * rows, 2 * rows, load_sems.at[c])
        for c in range(chunks)
    ]
    for load in loads:
        load.start()
    shape = (LANES, 2 * LANES)
    row = lax.broadcasted_iota(jnp.int32, shape, 0)
    column = lax.broadcasted_iota(jnp.int32, shape, 1)
    pick = jnp.where(column == 2 * row + p, F32(1.0), F32(0.0)).astype(BF16)
    for c, load in enumerate(loads):
        load.wait()
        for row in range(c * rows, (c + 1) * rows, 2 * LANES):
            blocks = [raw_v[2 * at : 2 * at + 2 * LANES, :] for at in (row, row + LANES)]
            value = dot(pick, lanes(*blocks)).astype(BF16)
            out_v[row : row + LANES, :] = value[:, :LANES]
            out_v[row + LANES : row + 2 * LANES, :] = value[:, LANES:]
        copy_rows(out_v, c * rows, out, c * rows, rows, store_sem).start()
    pltpu.make_async_copy(out_v, out, store_sem).wait()


def take_band(raw, p, earlier=(), interpret=False):
    hbm = pl.BlockSpec(memory_space=pl.ANY)
    return pl.pallas_call(
        functools.partial(band_kernel, p),
        out_shape=jax.ShapeDtypeStruct((ROWS, LANES), BF16),
        in_specs=[hbm] * (1 + len(earlier)),
        out_specs=hbm,
        scratch_shapes=[
            pltpu.VMEM((2 * ROWS, LANES), BF16),
            pltpu.VMEM((ROWS, LANES), BF16),
            pltpu.SemaphoreType.DMA((9,)),
            pltpu.SemaphoreType.DMA,
        ],
        compiler_params=pltpu.CompilerParams(vmem_limit_bytes=63 * MIB),
        cost_estimate=cost(6 * ROWS * LANES),
        interpret=interpret,
        name="take_band",
    )(raw, *earlier)


def rows_kernel(own0, own1, sel, out, thirds, wide):
    for p, own in enumerate((own0, own1)):
        widen_planes(own, wide, 0)

        @pl.loop(0, QUADS // 4, unroll=2)
        def _(q):
            split_rows(wide, sel, out.at[p], 4 * q, 4)

        @pl.loop(0, G // 2, unroll=4)
        def _(i):
            for s in range(3):
                rows = [wide[pl.ds((2 * i + e) * F_PITCH + s, QUADS, stride=3), :] for e in range(2)]
                at = pl.multiple_of(2 * i * QUADS, 16)
                thirds[p, s, pl.ds(at, 2 * QUADS), :] = stack(*rows).astype(BF16)


def padded_rows(own, sel, interpret=False):
    vmem = pl.BlockSpec(memory_space=pltpu.VMEM)
    return pl.pallas_call(
        rows_kernel,
        out_shape=(
            jax.ShapeDtypeStruct((2, G, G, LANES), BF16),
            jax.ShapeDtypeStruct((2, 3, THIRD, LANES), BF16),
        ),
        in_specs=[vmem] * 3,
        out_specs=(vmem, vmem),
        scratch_shapes=[pltpu.VMEM((G * F_PITCH, LANES), F32)],
        compiler_params=pltpu.CompilerParams(vmem_limit_bytes=63 * MIB),
        cost_estimate=cost(16 * NGRID),
        interpret=interpret,
        name="padded_rows",
    )(*own, sel)


def pairs_kernel(pieces, share, own, own_u, kern, par, *refs):
    earlier = []
    if len(pieces) > 1:
        earlier, refs = refs[:2], refs[2:]
    table_refs, own_out = refs[:7], refs[7]
    par_out, energy_out = refs[8 : 8 + len(pieces)], refs[8 + len(pieces)]
    own_v, own_uv, kern_v, own_ov, par_ov, par_f, par_u, yw, z, x34 = refs[9 + len(pieces) : -15]
    par_v, total_ref, energy_v, before_v = refs[-15:-11]
    tables, (par_sems, table_sems, before_sems, sems) = refs[-11:-4], refs[-4:]
    t1, t2, t3, a1, a2, a3, sel = tables
    par_loads = []
    for first in (0, ROWS // 2):
        sem = par_sems.at[len(par_loads)]
        par_loads.append(copy_rows(par, first, par_v, first, ROWS // 2, sem))
    for load in par_loads:
        load.start()
    table_loads = [
        pltpu.make_async_copy(src, dst, table_sems.at[i])
        for i, (src, dst) in enumerate(zip(table_refs, tables))
    ]
    table_loads[6].start()
    table_loads[0].start()
    loads = [
        pltpu.make_async_copy(own_u, own_uv, sems.at[0]),
        pltpu.make_async_copy(kern, kern_v, sems.at[1]),
        pltpu.make_async_copy(own, own_v, sems.at[2]),
    ]
    later = []
    if earlier:
        group = 2 * STEP_ROWS
        later = [
            [
                copy_rows(earlier[0].at[p, s], row, z, (3 * p + s) * THIRD + row, group, before_sems.at[g, 3 * p + s])
                for p in range(2)
                for s in range(3)
            ]
            for g, row in enumerate(range(0, THIRD, group))
        ]
        loads.append(pltpu.make_async_copy(earlier[1], before_v, sems.at[3]))

    for i, load in enumerate(par_loads):
        load.wait()
        for other in ([loads[0]], table_loads[1:5])[i]:
            other.start()
        widen_planes(par_v.at[pl.ds(i * ROWS // 2, ROWS // 2), :], par_f, i * G // 2)
    table_loads[6].wait()

    @pl.loop(0, QUADS // 4, unroll=6)
    def _(q):
        split_rows(par_f, sel, par_u, 4 * q, 4)

    half_y = G * Y_PITCH
    loads[0].wait()
    for load in loads[1:]:
        load.start()
    table_loads[5].start()
    table_loads[0].wait()

    @pl.loop(0, G // 2, unroll=24)
    def _(i):
        density = []
        for e in range(2):
            partner = par_u[2 * i + e].astype(F32)
            for p in range(2):
                density.append((own_uv[p, 2 * i + e].astype(F32) * partner).astype(BF16))
        out = dot(t1[...], lanes(*density))
        for e in range(2):
            for p in range(2):
                at = pl.ds(p * half_y + (2 * i + e) * Y_PITCH, Y_ROWS)
                yw[at, :] = out[:, (2 * e + p) * LANES : (2 * e + p + 1) * LANES]

    table_loads[1].wait()

    @pl.loop(0, KPAD // 2, unroll=25)
    def _(pair):
        def line(k1, part):
            first = part * HALF + k1
            rows = [yw[pl.ds(p * half_y + first, G, stride=Y_PITCH), :].astype(BF16) for p in range(2)]
            return lanes(*rows)

        both = [2 * pair, 2 * pair + 1]
        out = dot(t2[...], lanes(*[stack(line(k1, 0), line(k1, 1)) for k1 in both]))
        for e, k1 in enumerate(both):
            at = pl.ds(pl.multiple_of(k1 * G, 16), G)
            for p in range(2):
                for part in range(2):
                    left = (2 * p + part) * LANES
                    right = (2 * e + p) * LANES
                    value = out[part * G : (part + 1) * G, right : right + LANES]
                    x34[at, left : left + LANES] = value.astype(BF16)

    loads[1].wait()
    table_loads[2].wait()

    many = 5

    @pl.loop(0, KPAD // many, unroll=10)
    def _(m):
        at = pl.ds(pl.multiple_of(m * many * G, 16), many * G)
        factor = kern_v[at, :]
        out = [
            dot(x34[at, 2 * p * LANES : 2 * (p + 1) * LANES], t3[...]).astype(BF16)
            for p in range(2)
        ]
        for part in range(4):
            spectrum = lanes(*[o[:, part * 64 : (part + 1) * 64] for o in out]).astype(F32)
            value = spectrum * factor
            for i in range(many):
                row = part * Z_ROWS + (many * m + i) * Z_PITCH
                z[pl.ds(row, G), :] = value[i * G : (i + 1) * G]

    table_loads[3].wait()

    @pl.loop(0, G // 4, unroll=24)
    def _(four):
        parts = []
        for e in range(4):
            k2 = 4 * four + e
            mirror = Z_PITCH + jnp.where(k2 == 0, 0, G - k2)
            parts.append(
                stack(
                    z[pl.ds(k2, G // 2, stride=Z_PITCH), :].astype(BF16),
                    z[pl.ds(2 * Z_ROWS + mirror, G // 2, stride=Z_PITCH), :].astype(BF16),
                    z[pl.ds(1 * Z_ROWS + k2, G // 2, stride=Z_PITCH), :].astype(BF16),
                    z[pl.ds(3 * Z_ROWS + mirror, G // 2, stride=Z_PITCH), :].astype(BF16),
                )
            )
        out = dot(a1[...], lanes(*parts))
        for e in range(4):
            at = (4 * four + e) * W_PITCH
            yw[pl.ds(at, 2 * G), :] = out[:, e * LANES : (e + 1) * LANES]

    for load in sum(later, []):
        load.start()
    table_loads[4].wait()

    @pl.loop(0, G // 4, unroll=24)
    def _(four):
        parts = []
        for e in range(4):
            x1 = 4 * four + e
            parts.append(
                stack(
                    yw[pl.ds(x1, G, stride=W_PITCH), :].astype(BF16),
                    yw[pl.ds(G + x1, G, stride=W_PITCH), :].astype(BF16),
                )
            )
        out = dot(a2[...], lanes(*parts))
        for r in range(4):
            block = [
                lanes(
                    out[r * QUADS : (r + 1) * QUADS, e * LANES : (e + 1) * LANES],
                    out[G + r * QUADS : G + (r + 1) * QUADS, e * LANES : (e + 1) * LANES],
                )
                for e in range(4)
            ]
            at = pl.multiple_of((r // 2) * G * QUADS + four * 4 * QUADS, 16)
            left = (r % 2) * 2 * LANES
            x34[pl.ds(at, 4 * QUADS), left : left + 2 * LANES] = stack(*block).astype(BF16)

    table_loads[5].wait()
    for load in loads[2:]:
        load.wait()
    total_ref[...] = jnp.zeros_like(total_ref)
    scale = F32(1.0 / NGRID)

    def result(ch):
        at = ch * STEP_ROWS
        rows = pl.ds(at, STEP_ROWS)
        low = x34[rows, :]
        high = x34[pl.ds(THIRD + at, STEP_ROWS), :]
        fields = [low, lanes(low[:, 2 * LANES :], high[:, : 2 * LANES]), high]
        total = jnp.zeros((8, LANES), F32)
        for third in range(3):
            out = dot(fields[third], a3[third]) * scale
            first = ch * PLANES * F_PITCH + third
            partner = stack(
                *[par_f[pl.ds(first + i * F_PITCH, QUADS, stride=3), :] for i in range(PLANES)]
            )
            sent = None
            for p in range(2):
                potential = out[:, p * LANES : (p + 1) * LANES]
                term = potential * partner
                if earlier:
                    term = term + z[pl.ds((3 * p + third) * THIRD + at, STEP_ROWS), :]
                own_ov[p, third, rows, :] = term
                part = potential * own_v[p, third, rows, :].astype(F32)
                sent = part if sent is None else sent + part
            total = total + jnp.sum((sent * partner).reshape(-1, 8, LANES), axis=0)
            par_ov[third, rows, :] = sent.astype(BF16)
        total_ref[...] += total
        copy_rows(own_ov, at, own_out, at, STEP_ROWS, sems.at[4]).start()

    ch = 0
    for i, steps in enumerate(pieces):
        for step in range(steps):
            for load in later[ch // 2] if earlier and ch % 2 == 0 else ():
                load.wait()
            result(ch)
            source, row = ch * STEP_ROWS, step * STEP_ROWS
            copy_rows(par_ov, source, par_out[i], row, STEP_ROWS, sems.at[6 + i]).start()
            ch += 1

    energy = jnp.zeros((1, 1), F32) + jnp.sum(total_ref[...]) * F32(share)
    if earlier:
        energy = energy + before_v[...]
    energy_v[...] = energy
    report = pltpu.make_async_copy(energy_v, energy_out, sems.at[5])
    report.start()
    pltpu.make_async_copy(own_ov, own_out, sems.at[4]).wait()
    first = 0
    for i, steps in enumerate(pieces):
        rows = steps * STEP_ROWS
        copy_rows(par_ov, first, par_out[i], 0, rows, sems.at[6 + i]).wait()
        first += rows
    report.wait()


def pair_terms(own, own_u, partner, earlier, tables, kern, pieces, share, interpret=False):
    hbm = pl.BlockSpec(memory_space=pl.ANY)
    return pl.pallas_call(
        functools.partial(pairs_kernel, pieces, share),
        out_shape=(
            jax.ShapeDtypeStruct((2, 3, THIRD, LANES), F32),
            *[jax.ShapeDtypeStruct((3, steps * STEP_ROWS, LANES), BF16) for steps in pieces],
            jax.ShapeDtypeStruct((1, 1), F32),
        ),
        in_specs=[hbm] * (4 + len(earlier) + len(tables)),
        out_specs=(hbm,) * (2 + len(pieces)),
        scratch_shapes=[
            pltpu.VMEM((2, 3, THIRD, LANES), BF16),
            pltpu.VMEM((2, G, G, LANES), BF16),
            pltpu.VMEM((KPAD * G, LANES), F32),
            pltpu.VMEM((2, 3, THIRD, LANES), F32),
            pltpu.VMEM((3, THIRD, LANES), BF16),
            pltpu.VMEM((G * F_PITCH, LANES), F32),
            pltpu.VMEM((G, G, LANES), BF16),
            pltpu.VMEM((2 * G * Y_PITCH, LANES), F32),
            pltpu.VMEM((4 * Z_ROWS, LANES), F32),
            pltpu.VMEM((KPAD * G, 4 * LANES), BF16),
            pltpu.VMEM((ROWS, LANES), BF16),
            pltpu.VMEM((8, LANES), F32),
            pltpu.VMEM((1, 1), F32),
            pltpu.VMEM((1, 1), F32),
            *[pltpu.VMEM(table.shape, BF16) for table in tables],
            pltpu.SemaphoreType.DMA((2,)),
            pltpu.SemaphoreType.DMA((len(tables),)),
            pltpu.SemaphoreType.DMA((3, 6)),
            pltpu.SemaphoreType.DMA((6 + len(pieces),)),
        ],
        compiler_params=pltpu.CompilerParams(vmem_limit_bytes=63 * MIB),
        cost_estimate=pl.CostEstimate(
            flops=20_000_000_000, bytes_accessed=20_000_000, transcendentals=0
        ),
        interpret=interpret,
        name="pair_terms",
    )(own, own_u, kern, partner, *earlier, *tables)


def piece_kernel(first, size, own, terms, back0, back1, _, *rest):
    last = first + size == THIRD
    earlier = rest[: len(rest) - 12]
    out, gram_out, own_v, terms_v, back_v, out_v, gram_ref, gram_v, value_ref = rest[-12:-3]
    load_sems, gram_sems, store_sems = rest[-3:]
    rows = size // load_sems.shape[0]
    wide = 6 * rows

    def loads(c):
        start = first + c * rows
        sources = [
            (own, start, own_v), (terms, start, terms_v),
            (back0, start, back_v.at[0]), (back1, c * rows, back_v.at[1]),
        ]
        return [
            copy_rows(src, row, dst, c * rows, rows, load_sems.at[c, i])
            for i, (src, row, dst) in enumerate(sources)
        ]

    chunks = [loads(c) for c in range(load_sems.shape[0])]
    for chunk in chunks:
        for load in chunk:
            load.start()
    gram_loads = []
    if last:
        gram_loads = [
            pltpu.make_async_copy(src, gram_v.at[i], gram_sems.at[i])
            for i, src in enumerate(earlier[:-1])
        ]
        for load in gram_loads:
            load.start()
    gram_ref[...] = jnp.zeros_like(gram_ref)
    for c, chunk in enumerate(chunks):
        for load in chunk:
            load.wait()
        at = pl.ds(c * rows, rows)
        for s in range(3):
            bands = [own_v[i, s, at, :].astype(F32) for i in range(2)]
            for p in range(2):
                exchange = terms_v[p, s, at, :] + back_v[p, s, at, :].astype(F32)
                for i in range(rows // QUADS):
                    row = c * wide + 2 * (i * PLANE + s) + p
                    out_v[pl.ds(row, QUADS, stride=6), :] = exchange[i * QUADS : (i + 1) * QUADS]
                for i in range(2):
                    product = (bands[i] * exchange).reshape(-1, 8, LANES)
                    gram_ref[i, p] += jnp.sum(product, axis=0)
        copy_rows(out_v, c * wide, out, 6 * first + c * wide, wide, store_sems.at[0]).start()

    result = gram_ref
    if last:
        for load in gram_loads:
            load.wait()
        row = lax.broadcasted_iota(jnp.int32, (2, 2), 0)
        column = lax.broadcasted_iota(jnp.int32, (2, 2), 1)
        value = jnp.zeros((2, 2), F32)
        for i in range(2):
            for j in range(2):
                entry = gram_ref[i, j]
                for k in range(len(gram_loads)):
                    entry = entry + gram_v[k, i, j]
                value = jnp.where((row == i) & (column == j), jnp.sum(entry) * F32(1.0 / NGRID), value)
        value_ref[...] = value
        result = value_ref
    report = pltpu.make_async_copy(result, gram_out, store_sems.at[1])
    report.start()
    copy_rows(out_v, 0, out, 6 * first, 6 * size, store_sems.at[0]).wait()
    report.wait()


def add_piece(first, size, own, terms, back0, back1, energy, grams, out, interpret=False):
    hbm = pl.BlockSpec(memory_space=pl.ANY)
    last = first + size == THIRD
    earlier = [] if out is None else [*(grams if last else []), out]
    gram_shape = (2, 2, 8, LANES)
    return pl.pallas_call(
        functools.partial(piece_kernel, first, size),
        out_shape=(
            jax.ShapeDtypeStruct((2 * ROWS, LANES), F32),
            jax.ShapeDtypeStruct((2, 2) if last else gram_shape, F32),
        ),
        in_specs=[hbm] * (5 + len(earlier)),
        out_specs=(hbm, hbm),
        scratch_shapes=[
            pltpu.VMEM((2, 3, size, LANES), BF16),
            pltpu.VMEM((2, 3, size, LANES), F32),
            pltpu.VMEM((2, 3, size, LANES), BF16),
            pltpu.VMEM((6 * size, LANES), F32),
            pltpu.VMEM(gram_shape, F32),
            pltpu.VMEM((len(PIECES), *gram_shape), F32),
            pltpu.VMEM((2, 2), F32),
            pltpu.SemaphoreType.DMA((2 * size // STEP_ROWS, 4)),
            pltpu.SemaphoreType.DMA((len(PIECES),)),
            pltpu.SemaphoreType.DMA((2,)),
        ],
        input_output_aliases={4 + len(earlier): 0} if earlier else {},
        compiler_params=pltpu.CompilerParams(vmem_limit_bytes=52 * MIB),
        cost_estimate=cost(72 * size * LANES),
        interpret=interpret,
        name="add_piece",
    )(own, terms, back0, back1, energy, *earlier)


def from_behind(block, axis, distance):
    size = lax.axis_size(axis)
    return lax.ppermute(block, axis, [((i - distance) % size, i) for i in range(size)])


def after(values, other):
    return lax.optimization_barrier((values, other))[0]


def per_device(orbitals):
    tables = section_tables()
    kern = screening()
    size = lax.axis_size("band")
    share = -2.0 / (NGRID * 2 * size * orbitals.shape[0])
    raw = orbitals.reshape(2, ROWS, LANES).transpose(1, 0, 2).reshape(2 * ROWS, LANES)
    own = [take_band(raw, 0)]
    own.append(take_band(raw, 1, own))
    previous = [from_behind(part, "band", 1) for part in own]
    own_u, thirds = padded_rows(own, tables[-1])
    terms, back0, energy = pair_terms(
        thirds, own_u, previous[0], (), tables, kern, (STEPS,), share
    )
    back0 = from_behind(back0, "band", -1)
    terms, *sent, energy = pair_terms(
        thirds, own_u, previous[1], (terms, energy), tables, kern, PIECES, share
    )
    back1 = [from_behind(piece, "band", -1) for piece in sent]

    steps = []
    if size & (size - 1):
        energy = lax.psum(energy, "band")
    else:
        swap = [(i, i ^ 1) for i in range(size)]
        energy = energy + lax.ppermute(energy, "band", swap)
        steps = [1 << b for b in range(1, size.bit_length() - 1)]
        steps = [b for b in steps if b != 2] + [b for b in steps if b == 2]
        aside = [4 if size > 4 else 2, 8 if size > 8 else 2]
        steps = [[(i, i ^ (b if i % 2 else aside[i // 2 % 2])) for i in range(size)] for b in steps]
    while len(steps) > len(back1) - 1:
        energy = energy + lax.ppermute(energy, "band", steps.pop(0))
    exchange, grams = None, []
    first = 0
    for count, piece in zip(PIECES, back1):
        count *= STEP_ROWS
        got, last = None, piece is back1[-1]
        if last and size & (size - 1) == 0:
            got = lax.ppermute(energy, "band", swap)
        elif steps:
            got = lax.ppermute(energy, "band", steps.pop(0))
        exchange, gram = add_piece(
            first, count, thirds, terms, back0, piece, energy, grams, exchange
        )
        if got is not None and last:
            odd = lax.axis_index("band") % 2 == 1
            energy = jnp.where(odd, energy, after(got, gram))
        elif got is not None:
            energy = energy + after(got, gram)
        grams.append(gram)
        first += count
    exchange = exchange.reshape(ROWS, 2, LANES).transpose(1, 0, 2).reshape(2, NGRID)
    return exchange, gram, energy[0, 0]


def solution(mesh):
    return jax.shard_map(
        per_device,
        mesh=mesh,
        in_specs=(P("band", None),),
        out_specs=(P("band", None), P("band", None), P()),
        check_vma=False,
    )
```

```python
import functools

import jax
import jax.numpy as jnp
import ml_dtypes
import numpy as np
from jax import lax
from jax.experimental import pallas as pl
from jax.experimental.pallas import tpu as pltpu
from jax.sharding import PartitionSpec as P

G = 96
HALF = G // 2 + 1
NGRID = G * G * G
LANES = 128
ROWS = NGRID // LANES
PLANE = G * G // LANES
QUADS = G // 4
KPAD = HALF + 1
Y_ROWS = 104
Y_PITCH = Y_ROWS + 1
Z_PITCH = G + 1
W_PITCH = 2 * G + 1
Z_ROWS = KPAD * Z_PITCH
F_PITCH = PLANE + 1
PLANES = 16
STEP_ROWS = PLANES * QUADS
THIRD = G * QUADS
STEPS = G // PLANES
PIECES = (3, 2, 1)
WAVE_UNIT = 0.05
SCREEN_SQ = 0.0121
MIB = 1024 * 1024
BF16 = jnp.bfloat16
F32 = jnp.float32


def dft_tables():
    n = np.arange(G)
    phases = (n[:, None] * n[None, :]) % G
    angles = phases.astype(np.float32) * np.float32(2.0 * np.pi / G)
    rounded = [f(angles).astype(ml_dtypes.bfloat16).astype(np.float32) for f in (np.cos, np.sin)]
    return rounded[0], rounded[1]


def section_tables():
    c, s = dft_tables()
    h = HALF
    t1 = np.zeros((Y_ROWS, G), np.float32)
    t1[:h] = c[:h]
    t1[h : 2 * h] = -s[:h]
    t2 = np.block([[c, s], [-s, c]])
    t3 = np.zeros((2, LANES, 4, 64), np.float32)
    back = (G - np.arange(h)) % G
    t3[0, :G, 0, :h] = c[:h].T
    t3[1, :G, 0, :h] = s[:h].T
    t3[0, :G, 1, :h] = -s[:h].T
    t3[1, :G, 1, :h] = c[:h].T
    t3[0, :G, 2, :h] = c[back].T
    t3[1, :G, 2, :h] = s[back].T
    t3[0, :G, 3, :h] = s[back].T
    t3[1, :G, 3, :h] = -c[back].T
    t3 = t3.reshape(2 * LANES, 4 * 64)
    order = np.concatenate([np.arange(G // 2), G - 1 - np.arange(G // 2)])
    a1 = np.block([[c[:, order], -s[:, order]], [s[:, order], c[:, order]]])
    rows = np.arange(G).reshape(QUADS, 4).T.reshape(-1)
    a2 = np.block([[c[rows], -s[rows]], [s[rows], c[rows]]])
    weight = np.full((h, 1), 2.0, np.float32)
    weight[0] = weight[h - 1] = 1.0
    a3 = np.zeros((3, 2, 2, 2, 64, 2, LANES), np.float32)
    for third in range(3):
        for lane in range(LANES):
            r, x3 = divmod(third * LANES + lane, G)
            for p in range(2):
                a3[third, r - third, 0, p, :h, p, lane] = weight[:, 0] * c[x3, :h]
                a3[third, r - third, 1, p, :h, p, lane] = -weight[:, 0] * s[x3, :h]
    a3 = a3.reshape(3, 4 * LANES, 2 * LANES)
    sel = np.zeros((2, 2 * LANES, 2 * LANES), np.float32)
    for r in range(4):
        for x in range(G):
            sel[r // 2, r * G + x - (r // 2) * LANES, (r % 2) * LANES + x] = 1.0
    return [t.astype(ml_dtypes.bfloat16) for t in (t1, t2, t3, a1, a2, a3, sel)]


def screening():
    n = np.arange(G)
    m = np.where(n <= G // 2, n, n - G).astype(np.float64)
    sq = m * m
    q2 = WAVE_UNIT * (sq[:HALF, None, None] + sq[None, :, None] + sq[None, None, :HALF])
    safe = np.where(q2 > 0, q2, 1.0)
    kern = 4.0 * np.pi * (1.0 - np.exp(-q2 / (4.0 * SCREEN_SQ))) / safe
    kern = np.where(q2 > 0, kern, np.pi / SCREEN_SQ)
    out = np.zeros((KPAD, G, 2, 64), np.float32)
    out[:HALF, :, :, :HALF] = kern[:, :, None, :]
    return out.reshape(KPAD * G, LANES)


def cost(size):
    return pl.CostEstimate(flops=0, bytes_accessed=size, transcendentals=0)


def dot(a, b):
    return jnp.dot(a, b, preferred_element_type=F32)


def lanes(*parts):
    return jnp.concatenate(parts, axis=1)


def stack(*parts):
    return jnp.concatenate(parts, axis=0)


def split_rows(src, sel_ref, out, first, count):
    rows = [
        [src[pl.ds(3 * (first + i) + s, G, stride=F_PITCH), :].astype(BF16) for s in range(3)]
        for i in range(count)
    ]
    for half in range(2):
        part = dot(stack(*[lanes(r[half], r[half + 1]) for r in rows]), sel_ref[half])
        for i in range(count):
            for e in range(2):
                value = part[i * G : (i + 1) * G, e * LANES : (e + 1) * LANES]
                out[4 * (first + i) + 2 * half + e] = value.astype(BF16)


def widen_planes(src, dst, first):
    @pl.loop(0, src.shape[0] // (2 * PLANE), unroll=8)
    def _(i):
        value = src[pl.ds(pl.multiple_of(i * 2 * PLANE, 16), 2 * PLANE), :].astype(F32)
        dst[pl.ds((first + 2 * i) * F_PITCH, PLANE), :] = value[:PLANE]
        dst[pl.ds((first + 2 * i + 1) * F_PITCH, PLANE), :] = value[PLANE:]


def rows_of(ref, first, count):
    return ref.at[(slice(None),) * (len(ref.shape) - 2) + (pl.ds(first, count), slice(None))]


def copy_rows(src, src_row, dst, dst_row, count, sem):
    return pltpu.make_async_copy(rows_of(src, src_row, count), rows_of(dst, dst_row, count), sem)


def band_kernel(p, raw, *refs):
    out, raw_v, out_v, load_sems, store_sem = refs[-5:]
    chunks = load_sems.shape[0]
    rows = out.shape[0] // chunks
    loads = [
        copy_rows(raw, 2 * c * rows, raw_v, 2 * c * rows, 2 * rows, load_sems.at[c])
        for c in range(chunks)
    ]
    for load in loads:
        load.start()
    shape = (LANES, 2 * LANES)
    row = lax.broadcasted_iota(jnp.int32, shape, 0)
    column = lax.broadcasted_iota(jnp.int32, shape, 1)
    pick = jnp.where(column == 2 * row + p, F32(1.0), F32(0.0)).astype(BF16)
    for c, load in enumerate(loads):
        load.wait()
        for row in range(c * rows, (c + 1) * rows, 2 * LANES):
            blocks = [raw_v[2 * at : 2 * at + 2 * LANES, :] for at in (row, row + LANES)]
            value = dot(pick, lanes(*blocks)).astype(BF16)
            out_v[row : row + LANES, :] = value[:, :LANES]
            out_v[row + LANES : row + 2 * LANES, :] = value[:, LANES:]
        copy_rows(out_v, c * rows, out, c * rows, rows, store_sem).start()
    pltpu.make_async_copy(out_v, out, store_sem).wait()


def take_band(raw, p, earlier=(), interpret=False):
    hbm = pl.BlockSpec(memory_space=pl.ANY)
    return pl.pallas_call(
        functools.partial(band_kernel, p),
        out_shape=jax.ShapeDtypeStruct((ROWS, LANES), BF16),
        in_specs=[hbm] * (1 + len(earlier)),
        out_specs=hbm,
        scratch_shapes=[
            pltpu.VMEM((2 * ROWS, LANES), BF16),
            pltpu.VMEM((ROWS, LANES), BF16),
            pltpu.SemaphoreType.DMA((9,)),
            pltpu.SemaphoreType.DMA,
        ],
        compiler_params=pltpu.CompilerParams(vmem_limit_bytes=63 * MIB),
        cost_estimate=cost(6 * ROWS * LANES),
        interpret=interpret,
        name="take_band",
    )(raw, *earlier)


def rows_kernel(own0, own1, sel, out, thirds, wide):
    for p, own in enumerate((own0, own1)):
        widen_planes(own, wide, 0)

        @pl.loop(0, QUADS // 4, unroll=2)
        def _(q):
            split_rows(wide, sel, out.at[p], 4 * q, 4)

        @pl.loop(0, G // 2, unroll=4)
        def _(i):
            for s in range(3):
                rows = [wide[pl.ds((2 * i + e) * F_PITCH + s, QUADS, stride=3), :] for e in range(2)]
                at = pl.multiple_of(2 * i * QUADS, 16)
                thirds[p, s, pl.ds(at, 2 * QUADS), :] = stack(*rows).astype(BF16)


def padded_rows(own, sel, interpret=False):
    vmem = pl.BlockSpec(memory_space=pltpu.VMEM)
    return pl.pallas_call(
        rows_kernel,
        out_shape=(
            jax.ShapeDtypeStruct((2, G, G, LANES), BF16),
            jax.ShapeDtypeStruct((2, 3, THIRD, LANES), BF16),
        ),
        in_specs=[vmem] * 3,
        out_specs=(vmem, vmem),
        scratch_shapes=[pltpu.VMEM((G * F_PITCH, LANES), F32)],
        compiler_params=pltpu.CompilerParams(vmem_limit_bytes=63 * MIB),
        cost_estimate=cost(16 * NGRID),
        interpret=interpret,
        name="padded_rows",
    )(*own, sel)


def pairs_kernel(pieces, share, own, own_u, kern, par, *refs):
    earlier = []
    if len(pieces) > 1:
        earlier, refs = refs[:2], refs[2:]
    table_refs, own_out = refs[:7], refs[7]
    par_out, energy_out = refs[8 : 8 + len(pieces)], refs[8 + len(pieces)]
    own_v, own_uv, kern_v, own_ov, par_ov, par_f, par_u, yw, z, x34 = refs[9 + len(pieces) : -15]
    par_v, total_ref, energy_v, before_v = refs[-15:-11]
    tables, (par_sems, table_sems, before_sems, sems) = refs[-11:-4], refs[-4:]
    t1, t2, t3, a1, a2, a3, sel = tables
    par_loads = []
    for first in (0, ROWS // 2):
        sem = par_sems.at[len(par_loads)]
        par_loads.append(copy_rows(par, first, par_v, first, ROWS // 2, sem))
    for load in par_loads:
        load.start()
    table_loads = [
        pltpu.make_async_copy(src, dst, table_sems.at[i])
        for i, (src, dst) in enumerate(zip(table_refs, tables))
    ]
    table_loads[6].start()
    table_loads[0].start()
    loads = [
        pltpu.make_async_copy(own_u, own_uv, sems.at[0]),
        pltpu.make_async_copy(kern, kern_v, sems.at[1]),
        pltpu.make_async_copy(own, own_v, sems.at[2]),
    ]
    later = []
    if earlier:
        group = 2 * STEP_ROWS
        later = [
            [
                copy_rows(earlier[0].at[p, s], row, z, (3 * p + s) * THIRD + row, group, before_sems.at[g, 3 * p + s])
                for p in range(2)
                for s in range(3)
            ]
            for g, row in enumerate(range(0, THIRD, group))
        ]
        loads.append(pltpu.make_async_copy(earlier[1], before_v, sems.at[3]))

    for i, load in enumerate(par_loads):
        load.wait()
        for other in ([loads[0]], table_loads[1:5])[i]:
            other.start()
        widen_planes(par_v.at[pl.ds(i * ROWS // 2, ROWS // 2), :], par_f, i * G // 2)
    table_loads[6].wait()

    @pl.loop(0, QUADS // 4, unroll=6)
    def _(q):
        split_rows(par_f, sel, par_u, 4 * q, 4)

    half_y = G * Y_PITCH
    loads[0].wait()
    for load in loads[1:]:
        load.start()
    table_loads[5].start()
    table_loads[0].wait()

    @pl.loop(0, G // 2, unroll=24)
    def _(i):
        density = []
        for e in range(2):
            partner = par_u[2 * i + e].astype(F32)
            for p in range(2):
                density.append((own_uv[p, 2 * i + e].astype(F32) * partner).astype(BF16))
        out = dot(t1[...], lanes(*density))
        for e in range(2):
            for p in range(2):
                at = pl.ds(p * half_y + (2 * i + e) * Y_PITCH, Y_ROWS)
                yw[at, :] = out[:, (2 * e + p) * LANES : (2 * e + p + 1) * LANES]

    table_loads[1].wait()

    @pl.loop(0, KPAD // 2, unroll=25)
    def _(pair):
        def line(k1, part):
            first = part * HALF + k1
            rows = [yw[pl.ds(p * half_y + first, G, stride=Y_PITCH), :].astype(BF16) for p in range(2)]
            return lanes(*rows)

        both = [2 * pair, 2 * pair + 1]
        out = dot(t2[...], lanes(*[stack(line(k1, 0), line(k1, 1)) for k1 in both]))
        for e, k1 in enumerate(both):
            at = pl.ds(pl.multiple_of(k1 * G, 16), G)
            for p in range(2):
                for part in range(2):
                    left = (2 * p + part) * LANES
                    right = (2 * e + p) * LANES
                    value = out[part * G : (part + 1) * G, right : right + LANES]
                    x34[at, left : left + LANES] = value.astype(BF16)

    loads[1].wait()
    table_loads[2].wait()

    many = 5

    @pl.loop(0, KPAD // many, unroll=10)
    def _(m):
        at = pl.ds(pl.multiple_of(m * many * G, 16), many * G)
        factor = kern_v[at, :]
        out = [
            dot(x34[at, 2 * p * LANES : 2 * (p + 1) * LANES], t3[...]).astype(BF16)
            for p in range(2)
        ]
        for part in range(4):
            spectrum = lanes(*[o[:, part * 64 : (part + 1) * 64] for o in out]).astype(F32)
            value = spectrum * factor
            for i in range(many):
                row = part * Z_ROWS + (many * m + i) * Z_PITCH
                z[pl.ds(row, G), :] = value[i * G : (i + 1) * G]

    table_loads[3].wait()

    @pl.loop(0, G // 4, unroll=24)
    def _(four):
        parts = []
        for e in range(4):
            k2 = 4 * four + e
            mirror = Z_PITCH + jnp.where(k2 == 0, 0, G - k2)
            parts.append(
                stack(
                    z[pl.ds(k2, G // 2, stride=Z_PITCH), :].astype(BF16),
                    z[pl.ds(2 * Z_ROWS + mirror, G // 2, stride=Z_PITCH), :].astype(BF16),
                    z[pl.ds(1 * Z_ROWS + k2, G // 2, stride=Z_PITCH), :].astype(BF16),
                    z[pl.ds(3 * Z_ROWS + mirror, G // 2, stride=Z_PITCH), :].astype(BF16),
                )
            )
        out = dot(a1[...], lanes(*parts))
        for e in range(4):
            at = (4 * four + e) * W_PITCH
            yw[pl.ds(at, 2 * G), :] = out[:, e * LANES : (e + 1) * LANES]

    for load in sum(later, []):
        load.start()
    table_loads[4].wait()

    @pl.loop(0, G // 4, unroll=24)
    def _(four):
        parts = []
        for e in range(4):
            x1 = 4 * four + e
            parts.append(
                stack(
                    yw[pl.ds(x1, G, stride=W_PITCH), :].astype(BF16),
                    yw[pl.ds(G + x1, G, stride=W_PITCH), :].astype(BF16),
                )
            )
        out = dot(a2[...], lanes(*parts))
        for r in range(4):
            block = [
                lanes(
                    out[r * QUADS : (r + 1) * QUADS, e * LANES : (e + 1) * LANES],
                    out[G + r * QUADS : G + (r + 1) * QUADS, e * LANES : (e + 1) * LANES],
                )
                for e in range(4)
            ]
            at = pl.multiple_of((r // 2) * G * QUADS + four * 4 * QUADS, 16)
            left = (r % 2) * 2 * LANES
            x34[pl.ds(at, 4 * QUADS), left : left + 2 * LANES] = stack(*block).astype(BF16)

    table_loads[5].wait()
    for load in loads[2:]:
        load.wait()
    total_ref[...] = jnp.zeros_like(total_ref)
    scale = F32(1.0 / NGRID)

    def result(ch):
        at = ch * STEP_ROWS
        rows = pl.ds(at, STEP_ROWS)
        low = x34[rows, :]
        high = x34[pl.ds(THIRD + at, STEP_ROWS), :]
        fields = [low, lanes(low[:, 2 * LANES :], high[:, : 2 * LANES]), high]
        total = jnp.zeros((8, LANES), F32)
        for third in range(3):
            out = dot(fields[third], a3[third]) * scale
            first = ch * PLANES * F_PITCH + third
            partner = stack(
                *[par_f[pl.ds(first + i * F_PITCH, QUADS, stride=3), :] for i in range(PLANES)]
            )
            sent = None
            for p in range(2):
                potential = out[:, p * LANES : (p + 1) * LANES]
                term = potential * partner
                if earlier:
                    term = term + z[pl.ds((3 * p + third) * THIRD + at, STEP_ROWS), :]
                own_ov[p, third, rows, :] = term
                part = potential * own_v[p, third, rows, :].astype(F32)
                sent = part if sent is None else sent + part
            total = total + jnp.sum((sent * partner).reshape(-1, 8, LANES), axis=0)
            par_ov[third, rows, :] = sent.astype(BF16)
        total_ref[...] += total
        copy_rows(own_ov, at, own_out, at, STEP_ROWS, sems.at[4]).start()

    ch = 0
    for i, steps in enumerate(pieces):
        for step in range(steps):
            for load in later[ch // 2] if earlier and ch % 2 == 0 else ():
                load.wait()
            result(ch)
            source, row = ch * STEP_ROWS, step * STEP_ROWS
            copy_rows(par_ov, source, par_out[i], row, STEP_ROWS, sems.at[6 + i]).start()
            ch += 1

    energy = jnp.zeros((8, LANES), F32) + jnp.sum(total_ref[...]) * F32(share)
    if earlier:
        energy = energy + before_v[...]
    energy_v[...] = energy
    report = pltpu.make_async_copy(energy_v, energy_out, sems.at[5])
    report.start()
    pltpu.make_async_copy(own_ov, own_out, sems.at[4]).wait()
    first = 0
    for i, steps in enumerate(pieces):
        rows = steps * STEP_ROWS
        copy_rows(par_ov, first, par_out[i], 0, rows, sems.at[6 + i]).wait()
        first += rows
    report.wait()


def pair_terms(own, own_u, partner, earlier, tables, kern, pieces, share, interpret=False):
    hbm = pl.BlockSpec(memory_space=pl.ANY)
    return pl.pallas_call(
        functools.partial(pairs_kernel, pieces, share),
        out_shape=(
            jax.ShapeDtypeStruct((2, 3, THIRD, LANES), F32),
            *[jax.ShapeDtypeStruct((3, steps * STEP_ROWS, LANES), BF16) for steps in pieces],
            jax.ShapeDtypeStruct((8, LANES), F32),
        ),
        in_specs=[hbm] * (4 + len(earlier) + len(tables)),
        out_specs=(hbm,) * (2 + len(pieces)),
        scratch_shapes=[
            pltpu.VMEM((2, 3, THIRD, LANES), BF16),
            pltpu.VMEM((2, G, G, LANES), BF16),
            pltpu.VMEM((KPAD * G, LANES), F32),
            pltpu.VMEM((2, 3, THIRD, LANES), F32),
            pltpu.VMEM((3, THIRD, LANES), BF16),
            pltpu.VMEM((G * F_PITCH, LANES), F32),
            pltpu.VMEM((G, G, LANES), BF16),
            pltpu.VMEM((2 * G * Y_PITCH, LANES), F32),
            pltpu.VMEM((4 * Z_ROWS, LANES), F32),
            pltpu.VMEM((KPAD * G, 4 * LANES), BF16),
            pltpu.VMEM((ROWS, LANES), BF16),
            pltpu.VMEM((8, LANES), F32),
            pltpu.VMEM((8, LANES), F32),
            pltpu.VMEM((8, LANES), F32),
            *[pltpu.VMEM(table.shape, BF16) for table in tables],
            pltpu.SemaphoreType.DMA((2,)),
            pltpu.SemaphoreType.DMA((len(tables),)),
            pltpu.SemaphoreType.DMA((3, 6)),
            pltpu.SemaphoreType.DMA((6 + len(pieces),)),
        ],
        compiler_params=pltpu.CompilerParams(vmem_limit_bytes=63 * MIB),
        cost_estimate=pl.CostEstimate(
            flops=20_000_000_000, bytes_accessed=20_000_000, transcendentals=0
        ),
        interpret=interpret,
        name="pair_terms",
    )(own, own_u, kern, partner, *earlier, *tables)


def piece_kernel(first, size, own, terms, back0, back1, *rest):
    last = first + size == THIRD
    earlier = rest[: len(rest) - 12]
    out, gram_out, own_v, terms_v, back_v, out_v, gram_ref, gram_v, value_ref = rest[-12:-3]
    load_sems, gram_sems, store_sems = rest[-3:]
    rows = size // load_sems.shape[0]
    wide = 6 * rows

    def loads(c):
        start = first + c * rows
        sources = [
            (own, start, own_v), (terms, start, terms_v),
            (back0, start, back_v.at[0]), (back1, c * rows, back_v.at[1]),
        ]
        return [
            copy_rows(src, row, dst, c * rows, rows, load_sems.at[c, i])
            for i, (src, row, dst) in enumerate(sources)
        ]

    chunks = [loads(c) for c in range(load_sems.shape[0])]
    for chunk in chunks:
        for load in chunk:
            load.start()
    gram_loads = []
    if last:
        gram_loads = [
            pltpu.make_async_copy(src, gram_v.at[i], gram_sems.at[i])
            for i, src in enumerate(earlier[1:-1])
        ]
        for load in gram_loads:
            load.start()
    gram_ref[...] = jnp.zeros_like(gram_ref)
    for c, chunk in enumerate(chunks):
        for load in chunk:
            load.wait()
        at = pl.ds(c * rows, rows)
        for s in range(3):
            bands = [own_v[i, s, at, :].astype(F32) for i in range(2)]
            for p in range(2):
                exchange = terms_v[p, s, at, :] + back_v[p, s, at, :].astype(F32)
                for i in range(rows // QUADS):
                    row = c * wide + 2 * (i * PLANE + s) + p
                    out_v[pl.ds(row, QUADS, stride=6), :] = exchange[i * QUADS : (i + 1) * QUADS]
                for i in range(2):
                    product = (bands[i] * exchange).reshape(-1, 8, LANES)
                    gram_ref[i, p] += jnp.sum(product, axis=0)
        copy_rows(out_v, c * wide, out, 6 * first + c * wide, wide, store_sems.at[0]).start()

    result = gram_ref
    if last:
        for load in gram_loads:
            load.wait()
        row = lax.broadcasted_iota(jnp.int32, (2, 2), 0)
        column = lax.broadcasted_iota(jnp.int32, (2, 2), 1)
        value = jnp.zeros((2, 2), F32)
        for i in range(2):
            for j in range(2):
                entry = gram_ref[i, j]
                for k in range(len(gram_loads)):
                    entry = entry + gram_v[k, i, j]
                value = jnp.where((row == i) & (column == j), jnp.sum(entry) * F32(1.0 / NGRID), value)
        value_ref[...] = value
        result = value_ref
    report = pltpu.make_async_copy(result, gram_out, store_sems.at[1])
    report.start()
    copy_rows(out_v, 0, out, 6 * first, 6 * size, store_sems.at[0]).wait()
    report.wait()


def add_piece(first, size, own, terms, back0, back1, energy, grams, out, interpret=False):
    hbm = pl.BlockSpec(memory_space=pl.ANY)
    last = first + size == THIRD
    earlier = [] if out is None else [*([energy, *grams] if last else []), out]
    gram_shape = (2, 2, 8, LANES)
    return pl.pallas_call(
        functools.partial(piece_kernel, first, size),
        out_shape=(
            jax.ShapeDtypeStruct((2 * ROWS, LANES), F32),
            jax.ShapeDtypeStruct((2, 2) if last else gram_shape, F32),
        ),
        in_specs=[hbm] * (4 + len(earlier)),
        out_specs=(hbm, hbm),
        scratch_shapes=[
            pltpu.VMEM((2, 3, size, LANES), BF16),
            pltpu.VMEM((2, 3, size, LANES), F32),
            pltpu.VMEM((2, 3, size, LANES), BF16),
            pltpu.VMEM((6 * size, LANES), F32),
            pltpu.VMEM(gram_shape, F32),
            pltpu.VMEM((len(PIECES), *gram_shape), F32),
            pltpu.VMEM((2, 2), F32),
            pltpu.SemaphoreType.DMA((2 * size // STEP_ROWS, 4)),
            pltpu.SemaphoreType.DMA((len(PIECES),)),
            pltpu.SemaphoreType.DMA((2,)),
        ],
        input_output_aliases={3 + len(earlier): 0} if earlier else {},
        compiler_params=pltpu.CompilerParams(vmem_limit_bytes=52 * MIB),
        cost_estimate=cost(72 * size * LANES),
        interpret=interpret,
        name="add_piece",
    )(own, terms, back0, back1, *earlier)


def from_behind(block, axis, distance):
    size = lax.axis_size(axis)
    return lax.ppermute(block, axis, [((i - distance) % size, i) for i in range(size)])


def after(values, other):
    return lax.optimization_barrier((values, other))[0]


def per_device(orbitals):
    tables = section_tables()
    kern = screening()
    size = lax.axis_size("band")
    share = -2.0 / (NGRID * 2 * size * orbitals.shape[0])
    raw = orbitals.reshape(2, ROWS, LANES).transpose(1, 0, 2).reshape(2 * ROWS, LANES)
    own = [take_band(raw, 0)]
    own.append(take_band(raw, 1, own))
    previous = [from_behind(part, "band", 1) for part in own]
    own_u, thirds = padded_rows(own, tables[-1])
    terms, back0, energy = pair_terms(
        thirds, own_u, previous[0], (), tables, kern, (STEPS,), share
    )
    back0 = from_behind(back0, "band", -1)
    terms, *sent, energy = pair_terms(
        thirds, own_u, previous[1], (terms, energy), tables, kern, PIECES, share
    )
    back1 = [from_behind(piece, "band", -1) for piece in sent]

    steps = []
    if size & (size - 1):
        energy = lax.psum(energy, "band")
    else:
        swap = [(i, i ^ 1) for i in range(size)]
        energy = energy + lax.ppermute(energy, "band", swap)
        steps = [1 << b for b in range(1, size.bit_length() - 1)]
        steps = [b for b in steps if b != 2] + [b for b in steps if b == 2]
        aside = [4 if size > 4 else 2, 8 if size > 8 else 2]
        steps = [[(i, i ^ (b if i % 2 else aside[i // 2 % 2])) for i in range(size)] for b in steps]
    while len(steps) > len(back1) - 1:
        energy = energy + lax.ppermute(energy, "band", steps.pop(0))
    exchange, grams = None, []
    first = 0
    for count, piece in zip(PIECES, back1):
        count *= STEP_ROWS
        got, last = None, piece is back1[-1]
        if last and size & (size - 1) == 0:
            got = lax.ppermute(energy, "band", swap)
            energy = energy[:1, :1]
        elif steps:
            got = lax.ppermute(energy, "band", steps.pop(0))
        exchange, gram = add_piece(
            first, count, thirds, terms, back0, piece, energy, grams, exchange
        )
        if got is not None and last:
            odd = lax.axis_index("band") % 2 == 1
            energy = jnp.where(odd, energy, after(got, gram)[:1, :1])
        elif got is not None:
            energy = energy + after(got, gram)
        grams.append(gram)
        first += count
    exchange = exchange.reshape(ROWS, 2, LANES).transpose(1, 0, 2).reshape(2, NGRID)
    return exchange, gram, energy[0, 0]


def solution(mesh):
    return jax.shard_map(
        per_device,
        mesh=mesh,
        in_specs=(P("band", None),),
        out_specs=(P("band", None), P("band", None), P()),
        check_vma=False,
    )
```

```python
import functools

import jax
import jax.numpy as jnp
import ml_dtypes
import numpy as np
from jax import lax
from jax.experimental import pallas as pl
from jax.experimental.pallas import tpu as pltpu
from jax.sharding import PartitionSpec as P

G = 96
HALF = G // 2 + 1
NGRID = G * G * G
LANES = 128
ROWS = NGRID // LANES
PLANE = G * G // LANES
QUADS = G // 4
KPAD = HALF + 1
Y_ROWS = 104
Y_PITCH = Y_ROWS + 1
Z_PITCH = G + 1
W_PITCH = 2 * G + 1
Z_ROWS = KPAD * Z_PITCH
F_PITCH = PLANE + 1
PLANES = 16
STEP_ROWS = PLANES * QUADS
THIRD = G * QUADS
STEPS = G // PLANES
PIECES = (3, 2, 1)
WAVE_UNIT = 0.05
SCREEN_SQ = 0.0121
MIB = 1024 * 1024
BF16 = jnp.bfloat16
F32 = jnp.float32


def dft_tables():
    n = np.arange(G)
    phases = (n[:, None] * n[None, :]) % G
    angles = phases.astype(np.float32) * np.float32(2.0 * np.pi / G)
    rounded = [f(angles).astype(ml_dtypes.bfloat16).astype(np.float32) for f in (np.cos, np.sin)]
    return rounded[0], rounded[1]


def section_tables():
    c, s = dft_tables()
    h = HALF
    t1 = np.zeros((Y_ROWS, G), np.float32)
    t1[:h] = c[:h]
    t1[h : 2 * h] = -s[:h]
    t2 = np.block([[c, s], [-s, c]])
    t3 = np.zeros((2, LANES, 4, 64), np.float32)
    back = (G - np.arange(h)) % G
    t3[0, :G, 0, :h] = c[:h].T
    t3[1, :G, 0, :h] = s[:h].T
    t3[0, :G, 1, :h] = -s[:h].T
    t3[1, :G, 1, :h] = c[:h].T
    t3[0, :G, 2, :h] = c[back].T
    t3[1, :G, 2, :h] = s[back].T
    t3[0, :G, 3, :h] = s[back].T
    t3[1, :G, 3, :h] = -c[back].T
    t3 = t3.reshape(2 * LANES, 4 * 64)
    order = np.concatenate([np.arange(G // 2), G - 1 - np.arange(G // 2)])
    a1 = np.block([[c[:, order], -s[:, order]], [s[:, order], c[:, order]]])
    rows = np.arange(G).reshape(QUADS, 4).T.reshape(-1)
    a2 = np.block([[c[rows], -s[rows]], [s[rows], c[rows]]])
    weight = np.full((h, 1), 2.0, np.float32)
    weight[0] = weight[h - 1] = 1.0
    a3 = np.zeros((3, 2, 2, 2, 64, 2, LANES), np.float32)
    for third in range(3):
        for lane in range(LANES):
            r, x3 = divmod(third * LANES + lane, G)
            for p in range(2):
                a3[third, r - third, 0, p, :h, p, lane] = weight[:, 0] * c[x3, :h]
                a3[third, r - third, 1, p, :h, p, lane] = -weight[:, 0] * s[x3, :h]
    a3 = a3.reshape(3, 4 * LANES, 2 * LANES)
    sel = np.zeros((2, 2 * LANES, 2 * LANES), np.float32)
    for r in range(4):
        for x in range(G):
            sel[r // 2, r * G + x - (r // 2) * LANES, (r % 2) * LANES + x] = 1.0
    return [t.astype(ml_dtypes.bfloat16) for t in (t1, t2, t3, a1, a2, a3, sel)]


def screening():
    n = np.arange(G)
    m = np.where(n <= G // 2, n, n - G).astype(np.float64)
    sq = m * m
    q2 = WAVE_UNIT * (sq[:HALF, None, None] + sq[None, :, None] + sq[None, None, :HALF])
    safe = np.where(q2 > 0, q2, 1.0)
    kern = 4.0 * np.pi * (1.0 - np.exp(-q2 / (4.0 * SCREEN_SQ))) / safe
    kern = np.where(q2 > 0, kern, np.pi / SCREEN_SQ)
    out = np.zeros((KPAD, G, 2, 64), np.float32)
    out[:HALF, :, :, :HALF] = kern[:, :, None, :]
    return out.reshape(KPAD * G, LANES)


def cost(size):
    return pl.CostEstimate(flops=0, bytes_accessed=size, transcendentals=0)


def dot(a, b):
    return jnp.dot(a, b, preferred_element_type=F32)


def lanes(*parts):
    return jnp.concatenate(parts, axis=1)


def stack(*parts):
    return jnp.concatenate(parts, axis=0)


def split_rows(src, sel_ref, out, first, count):
    rows = [
        [src[pl.ds(3 * (first + i) + s, G, stride=F_PITCH), :].astype(BF16) for s in range(3)]
        for i in range(count)
    ]
    for half in range(2):
        part = dot(stack(*[lanes(r[half], r[half + 1]) for r in rows]), sel_ref[half])
        for i in range(count):
            for e in range(2):
                value = part[i * G : (i + 1) * G, e * LANES : (e + 1) * LANES]
                out[4 * (first + i) + 2 * half + e] = value.astype(BF16)


def widen_planes(src, dst, first):
    @pl.loop(0, src.shape[0] // (2 * PLANE), unroll=8)
    def _(i):
        value = src[pl.ds(pl.multiple_of(i * 2 * PLANE, 16), 2 * PLANE), :].astype(F32)
        dst[pl.ds((first + 2 * i) * F_PITCH, PLANE), :] = value[:PLANE]
        dst[pl.ds((first + 2 * i + 1) * F_PITCH, PLANE), :] = value[PLANE:]


def rows_of(ref, first, count):
    return ref.at[(slice(None),) * (len(ref.shape) - 2) + (pl.ds(first, count), slice(None))]


def copy_rows(src, src_row, dst, dst_row, count, sem):
    return pltpu.make_async_copy(rows_of(src, src_row, count), rows_of(dst, dst_row, count), sem)


def band_kernel(p, raw, *refs):
    out, raw_v, out_v, load_sems, store_sem = refs[-5:]
    chunks = load_sems.shape[0]
    rows = out.shape[0] // chunks
    loads = [
        copy_rows(raw, 2 * c * rows, raw_v, 2 * c * rows, 2 * rows, load_sems.at[c])
        for c in range(chunks)
    ]
    for load in loads:
        load.start()
    shape = (LANES, 2 * LANES)
    row = lax.broadcasted_iota(jnp.int32, shape, 0)
    column = lax.broadcasted_iota(jnp.int32, shape, 1)
    pick = jnp.where(column == 2 * row + p, F32(1.0), F32(0.0)).astype(BF16)
    for c, load in enumerate(loads):
        load.wait()
        for row in range(c * rows, (c + 1) * rows, 2 * LANES):
            blocks = [raw_v[2 * at : 2 * at + 2 * LANES, :] for at in (row, row + LANES)]
            value = dot(pick, lanes(*blocks)).astype(BF16)
            out_v[row : row + LANES, :] = value[:, :LANES]
            out_v[row + LANES : row + 2 * LANES, :] = value[:, LANES:]
        copy_rows(out_v, c * rows, out, c * rows, rows, store_sem).start()
    pltpu.make_async_copy(out_v, out, store_sem).wait()


def take_band(raw, p, earlier=(), interpret=False):
    hbm = pl.BlockSpec(memory_space=pl.ANY)
    return pl.pallas_call(
        functools.partial(band_kernel, p),
        out_shape=jax.ShapeDtypeStruct((ROWS, LANES), BF16),
        in_specs=[hbm] * (1 + len(earlier)),
        out_specs=hbm,
        scratch_shapes=[
            pltpu.VMEM((2 * ROWS, LANES), BF16),
            pltpu.VMEM((ROWS, LANES), BF16),
            pltpu.SemaphoreType.DMA((9,)),
            pltpu.SemaphoreType.DMA,
        ],
        compiler_params=pltpu.CompilerParams(vmem_limit_bytes=63 * MIB),
        cost_estimate=cost(6 * ROWS * LANES),
        interpret=interpret,
        name="take_band",
    )(raw, *earlier)


def rows_kernel(own0, own1, sel, out, thirds, wide):
    for p, own in enumerate((own0, own1)):
        widen_planes(own, wide, 0)

        @pl.loop(0, QUADS // 4, unroll=2)
        def _(q):
            split_rows(wide, sel, out.at[p], 4 * q, 4)

        @pl.loop(0, G // 2, unroll=4)
        def _(i):
            for s in range(3):
                rows = [wide[pl.ds((2 * i + e) * F_PITCH + s, QUADS, stride=3), :] for e in range(2)]
                at = pl.multiple_of(2 * i * QUADS, 16)
                thirds[p, s, pl.ds(at, 2 * QUADS), :] = stack(*rows).astype(BF16)


def padded_rows(own, sel, interpret=False):
    vmem = pl.BlockSpec(memory_space=pltpu.VMEM)
    return pl.pallas_call(
        rows_kernel,
        out_shape=(
            jax.ShapeDtypeStruct((2, G, G, LANES), BF16),
            jax.ShapeDtypeStruct((2, 3, THIRD, LANES), BF16),
        ),
        in_specs=[vmem] * 3,
        out_specs=(vmem, vmem),
        scratch_shapes=[pltpu.VMEM((G * F_PITCH, LANES), F32)],
        compiler_params=pltpu.CompilerParams(vmem_limit_bytes=63 * MIB),
        cost_estimate=cost(16 * NGRID),
        interpret=interpret,
        name="padded_rows",
    )(*own, sel)


def pairs_kernel(pieces, share, own, own_u, kern, par, *refs):
    earlier = []
    if len(pieces) > 1:
        earlier, refs = refs[:2], refs[2:]
    table_refs, own_out = refs[:7], refs[7]
    par_out, energy_out = refs[8 : 8 + len(pieces)], refs[8 + len(pieces)]
    own_v, own_uv, kern_v, own_ov, par_ov, par_f, par_u, yw, z, x34 = refs[9 + len(pieces) : -15]
    par_v, total_ref, energy_v, before_v = refs[-15:-11]
    tables, (par_sems, table_sems, before_sems, sems) = refs[-11:-4], refs[-4:]
    t1, t2, t3, a1, a2, a3, sel = tables
    par_loads = []
    for first in (0, ROWS // 2):
        sem = par_sems.at[len(par_loads)]
        par_loads.append(copy_rows(par, first, par_v, first, ROWS // 2, sem))
    for load in par_loads:
        load.start()
    table_loads = [
        pltpu.make_async_copy(src, dst, table_sems.at[i])
        for i, (src, dst) in enumerate(zip(table_refs, tables))
    ]
    table_loads[6].start()
    table_loads[0].start()
    loads = [
        pltpu.make_async_copy(own_u, own_uv, sems.at[0]),
        pltpu.make_async_copy(kern, kern_v, sems.at[1]),
        pltpu.make_async_copy(own, own_v, sems.at[2]),
    ]
    later = []
    if earlier:
        group = 2 * STEP_ROWS
        later = [
            [
                copy_rows(earlier[0].at[p, s], row, z, (3 * p + s) * THIRD + row, group, before_sems.at[g, 3 * p + s])
                for p in range(2)
                for s in range(3)
            ]
            for g, row in enumerate(range(0, THIRD, group))
        ]
        loads.append(pltpu.make_async_copy(earlier[1], before_v, sems.at[3]))

    for i, load in enumerate(par_loads):
        load.wait()
        for other in ([loads[0]], table_loads[1:5])[i]:
            other.start()
        widen_planes(par_v.at[pl.ds(i * ROWS // 2, ROWS // 2), :], par_f, i * G // 2)
    table_loads[6].wait()

    @pl.loop(0, QUADS // 4, unroll=6)
    def _(q):
        split_rows(par_f, sel, par_u, 4 * q, 4)

    half_y = G * Y_PITCH
    loads[0].wait()
    for load in loads[1:]:
        load.start()
    table_loads[5].start()
    table_loads[0].wait()

    @pl.loop(0, G // 2, unroll=24)
    def _(i):
        density = []
        for e in range(2):
            partner = par_u[2 * i + e].astype(F32)
            for p in range(2):
                density.append((own_uv[p, 2 * i + e].astype(F32) * partner).astype(BF16))
        out = dot(t1[...], lanes(*density))
        for e in range(2):
            for p in range(2):
                at = pl.ds(p * half_y + (2 * i + e) * Y_PITCH, Y_ROWS)
                yw[at, :] = out[:, (2 * e + p) * LANES : (2 * e + p + 1) * LANES]

    table_loads[1].wait()

    @pl.loop(0, KPAD // 2, unroll=25)
    def _(pair):
        def line(k1, part):
            first = part * HALF + k1
            rows = [yw[pl.ds(p * half_y + first, G, stride=Y_PITCH), :].astype(BF16) for p in range(2)]
            return lanes(*rows)

        both = [2 * pair, 2 * pair + 1]
        out = dot(t2[...], lanes(*[stack(line(k1, 0), line(k1, 1)) for k1 in both]))
        for e, k1 in enumerate(both):
            at = pl.ds(pl.multiple_of(k1 * G, 16), G)
            for p in range(2):
                for part in range(2):
                    left = (2 * p + part) * LANES
                    right = (2 * e + p) * LANES
                    value = out[part * G : (part + 1) * G, right : right + LANES]
                    x34[at, left : left + LANES] = value.astype(BF16)

    loads[1].wait()
    table_loads[2].wait()

    many = 5

    @pl.loop(0, KPAD // many, unroll=10)
    def _(m):
        at = pl.ds(pl.multiple_of(m * many * G, 16), many * G)
        factor = kern_v[at, :]
        out = [
            dot(x34[at, 2 * p * LANES : 2 * (p + 1) * LANES], t3[...]).astype(BF16)
            for p in range(2)
        ]
        for part in range(4):
            spectrum = lanes(*[o[:, part * 64 : (part + 1) * 64] for o in out]).astype(F32)
            value = spectrum * factor
            for i in range(many):
                row = part * Z_ROWS + (many * m + i) * Z_PITCH
                z[pl.ds(row, G), :] = value[i * G : (i + 1) * G]

    table_loads[3].wait()

    @pl.loop(0, G // 4, unroll=24)
    def _(four):
        parts = []
        for e in range(4):
            k2 = 4 * four + e
            mirror = Z_PITCH + jnp.where(k2 == 0, 0, G - k2)
            parts.append(
                stack(
                    z[pl.ds(k2, G // 2, stride=Z_PITCH), :].astype(BF16),
                    z[pl.ds(2 * Z_ROWS + mirror, G // 2, stride=Z_PITCH), :].astype(BF16),
                    z[pl.ds(1 * Z_ROWS + k2, G // 2, stride=Z_PITCH), :].astype(BF16),
                    z[pl.ds(3 * Z_ROWS + mirror, G // 2, stride=Z_PITCH), :].astype(BF16),
                )
            )
        out = dot(a1[...], lanes(*parts))
        for e in range(4):
            at = (4 * four + e) * W_PITCH
            yw[pl.ds(at, 2 * G), :] = out[:, e * LANES : (e + 1) * LANES]

    for load in sum(later, []):
        load.start()
    table_loads[4].wait()

    @pl.loop(0, G // 4, unroll=24)
    def _(four):
        parts = []
        for e in range(4):
            x1 = 4 * four + e
            parts.append(
                stack(
                    yw[pl.ds(x1, G, stride=W_PITCH), :].astype(BF16),
                    yw[pl.ds(G + x1, G, stride=W_PITCH), :].astype(BF16),
                )
            )
        out = dot(a2[...], lanes(*parts))
        for r in range(4):
            block = [
                lanes(
                    out[r * QUADS : (r + 1) * QUADS, e * LANES : (e + 1) * LANES],
                    out[G + r * QUADS : G + (r + 1) * QUADS, e * LANES : (e + 1) * LANES],
                )
                for e in range(4)
            ]
            at = pl.multiple_of((r // 2) * G * QUADS + four * 4 * QUADS, 16)
            left = (r % 2) * 2 * LANES
            x34[pl.ds(at, 4 * QUADS), left : left + 2 * LANES] = stack(*block).astype(BF16)

    table_loads[5].wait()
    for load in loads[2:]:
        load.wait()
    total_ref[...] = jnp.zeros_like(total_ref)
    scale = F32(1.0 / NGRID)

    def result(ch):
        at = ch * STEP_ROWS
        rows = pl.ds(at, STEP_ROWS)
        low = x34[rows, :]
        high = x34[pl.ds(THIRD + at, STEP_ROWS), :]
        fields = [low, lanes(low[:, 2 * LANES :], high[:, : 2 * LANES]), high]
        total = jnp.zeros((8, LANES), F32)
        for third in range(3):
            out = dot(fields[third], a3[third]) * scale
            first = ch * PLANES * F_PITCH + third
            partner = stack(
                *[par_f[pl.ds(first + i * F_PITCH, QUADS, stride=3), :] for i in range(PLANES)]
            )
            sent = None
            for p in range(2):
                potential = out[:, p * LANES : (p + 1) * LANES]
                term = potential * partner
                if earlier:
                    term = term + z[pl.ds((3 * p + third) * THIRD + at, STEP_ROWS), :]
                own_ov[p, third, rows, :] = term
                part = potential * own_v[p, third, rows, :].astype(F32)
                sent = part if sent is None else sent + part
            total = total + jnp.sum((sent * partner).reshape(-1, 8, LANES), axis=0)
            par_ov[third, rows, :] = sent.astype(BF16)
        total_ref[...] += total
        copy_rows(own_ov, at, own_out, at, STEP_ROWS, sems.at[4]).start()

    ch = 0
    for i, steps in enumerate(pieces):
        for step in range(steps):
            for load in later[ch // 2] if earlier and ch % 2 == 0 else ():
                load.wait()
            result(ch)
            source, row = ch * STEP_ROWS, step * STEP_ROWS
            copy_rows(par_ov, source, par_out[i], row, STEP_ROWS, sems.at[6 + i]).start()
            ch += 1

    energy = jnp.zeros((8, LANES), F32) + jnp.sum(total_ref[...]) * F32(share)
    if earlier:
        energy = energy + before_v[...]
    energy_v[...] = energy
    report = pltpu.make_async_copy(energy_v, energy_out, sems.at[5])
    report.start()
    pltpu.make_async_copy(own_ov, own_out, sems.at[4]).wait()
    first = 0
    for i, steps in enumerate(pieces):
        rows = steps * STEP_ROWS
        copy_rows(par_ov, first, par_out[i], 0, rows, sems.at[6 + i]).wait()
        first += rows
    report.wait()


def pair_terms(own, own_u, partner, earlier, tables, kern, pieces, share, interpret=False):
    hbm = pl.BlockSpec(memory_space=pl.ANY)
    return pl.pallas_call(
        functools.partial(pairs_kernel, pieces, share),
        out_shape=(
            jax.ShapeDtypeStruct((2, 3, THIRD, LANES), F32),
            *[jax.ShapeDtypeStruct((3, steps * STEP_ROWS, LANES), BF16) for steps in pieces],
            jax.ShapeDtypeStruct((8, LANES), F32),
        ),
        in_specs=[hbm] * (4 + len(earlier) + len(tables)),
        out_specs=(hbm,) * (2 + len(pieces)),
        scratch_shapes=[
            pltpu.VMEM((2, 3, THIRD, LANES), BF16),
            pltpu.VMEM((2, G, G, LANES), BF16),
            pltpu.VMEM((KPAD * G, LANES), F32),
            pltpu.VMEM((2, 3, THIRD, LANES), F32),
            pltpu.VMEM((3, THIRD, LANES), BF16),
            pltpu.VMEM((G * F_PITCH, LANES), F32),
            pltpu.VMEM((G, G, LANES), BF16),
            pltpu.VMEM((2 * G * Y_PITCH, LANES), F32),
            pltpu.VMEM((4 * Z_ROWS, LANES), F32),
            pltpu.VMEM((KPAD * G, 4 * LANES), BF16),
            pltpu.VMEM((ROWS, LANES), BF16),
            pltpu.VMEM((8, LANES), F32),
            pltpu.VMEM((8, LANES), F32),
            pltpu.VMEM((8, LANES), F32),
            *[pltpu.VMEM(table.shape, BF16) for table in tables],
            pltpu.SemaphoreType.DMA((2,)),
            pltpu.SemaphoreType.DMA((len(tables),)),
            pltpu.SemaphoreType.DMA((3, 6)),
            pltpu.SemaphoreType.DMA((6 + len(pieces),)),
        ],
        compiler_params=pltpu.CompilerParams(vmem_limit_bytes=63 * MIB),
        cost_estimate=pl.CostEstimate(
            flops=20_000_000_000, bytes_accessed=20_000_000, transcendentals=0
        ),
        interpret=interpret,
        name="pair_terms",
    )(own, own_u, kern, partner, *earlier, *tables)


def piece_kernel(first, size, own, terms, back0, back1, *rest):
    last = first + size == THIRD
    earlier = rest[: len(rest) - 12]
    out, gram_out, own_v, terms_v, back_v, out_v, gram_ref, gram_v, value_ref = rest[-12:-3]
    load_sems, gram_sems, store_sems = rest[-3:]
    rows = size // load_sems.shape[0]
    wide = 6 * rows

    def loads(c):
        start = first + c * rows
        sources = [
            (own, start, own_v), (terms, start, terms_v),
            (back0, start, back_v.at[0]), (back1, c * rows, back_v.at[1]),
        ]
        return [
            copy_rows(src, row, dst, c * rows, rows, load_sems.at[c, i])
            for i, (src, row, dst) in enumerate(sources)
        ]

    chunks = [loads(c) for c in range(load_sems.shape[0])]
    for chunk in chunks:
        for load in chunk:
            load.start()
    gram_loads = []
    if last:
        gram_loads = [
            pltpu.make_async_copy(src, gram_v.at[i], gram_sems.at[i])
            for i, src in enumerate(earlier[1:-1])
        ]
        for load in gram_loads:
            load.start()
    gram_ref[...] = jnp.zeros_like(gram_ref)
    for c, chunk in enumerate(chunks):
        for load in chunk:
            load.wait()
        at = pl.ds(c * rows, rows)
        for s in range(3):
            bands = [own_v[i, s, at, :].astype(F32) for i in range(2)]
            for p in range(2):
                exchange = terms_v[p, s, at, :] + back_v[p, s, at, :].astype(F32)
                for i in range(rows // QUADS):
                    row = c * wide + 2 * (i * PLANE + s) + p
                    out_v[pl.ds(row, QUADS, stride=6), :] = exchange[i * QUADS : (i + 1) * QUADS]
                for i in range(2):
                    product = (bands[i] * exchange).reshape(-1, 8, LANES)
                    gram_ref[i, p] += jnp.sum(product, axis=0)
        copy_rows(out_v, c * wide, out, 6 * first + c * wide, wide, store_sems.at[0]).start()

    result = gram_ref
    if last:
        for load in gram_loads:
            load.wait()
        row = lax.broadcasted_iota(jnp.int32, (2, 2), 0)
        column = lax.broadcasted_iota(jnp.int32, (2, 2), 1)
        value = jnp.zeros((2, 2), F32)
        for i in range(2):
            for j in range(2):
                entry = gram_ref[i, j]
                for k in range(len(gram_loads)):
                    entry = entry + gram_v[k, i, j]
                value = jnp.where((row == i) & (column == j), jnp.sum(entry) * F32(1.0 / NGRID), value)
        value_ref[...] = value
        result = value_ref
    report = pltpu.make_async_copy(result, gram_out, store_sems.at[1])
    report.start()
    copy_rows(out_v, 0, out, 6 * first, 6 * size, store_sems.at[0]).wait()
    report.wait()


def add_piece(first, size, own, terms, back0, back1, energy, grams, out, interpret=False):
    hbm = pl.BlockSpec(memory_space=pl.ANY)
    last = first + size == THIRD
    earlier = [] if out is None else [*([energy, *grams] if last else []), out]
    gram_shape = (2, 2, 8, LANES)
    return pl.pallas_call(
        functools.partial(piece_kernel, first, size),
        out_shape=(
            jax.ShapeDtypeStruct((2 * ROWS, LANES), F32),
            jax.ShapeDtypeStruct((2, 2) if last else gram_shape, F32),
        ),
        in_specs=[hbm] * (4 + len(earlier)),
        out_specs=(hbm, hbm),
        scratch_shapes=[
            pltpu.VMEM((2, 3, size, LANES), BF16),
            pltpu.VMEM((2, 3, size, LANES), F32),
            pltpu.VMEM((2, 3, size, LANES), BF16),
            pltpu.VMEM((6 * size, LANES), F32),
            pltpu.VMEM(gram_shape, F32),
            pltpu.VMEM((len(PIECES), *gram_shape), F32),
            pltpu.VMEM((2, 2), F32),
            pltpu.SemaphoreType.DMA((2 * size // STEP_ROWS, 4)),
            pltpu.SemaphoreType.DMA((len(PIECES),)),
            pltpu.SemaphoreType.DMA((2,)),
        ],
        input_output_aliases={3 + len(earlier): 0} if earlier else {},
        compiler_params=pltpu.CompilerParams(vmem_limit_bytes=52 * MIB),
        cost_estimate=cost(72 * size * LANES),
        interpret=interpret,
        name="add_piece",
    )(own, terms, back0, back1, *earlier)


def from_behind(block, axis, distance):
    size = lax.axis_size(axis)
    return lax.ppermute(block, axis, [((i - distance) % size, i) for i in range(size)])


def send_among_odd(value, axis, bits):
    size = lax.axis_size(axis)
    aside = [4 if size > 4 else 2, 8 if size > 8 else 2]
    flips = sorted({bits[0], bits[-1], sum(bits)})
    routes = [[(i, i ^ (f if i % 2 else aside[i // 2 % 2])) for i in range(size)] for f in flips]
    return [lax.ppermute(value, axis, route) for route in routes]


def add_up(value, got):
    if len(got) == 1:
        return value + got[0]
    return (value + got[0]) + (got[1] + got[2])


def after(values, other):
    return lax.optimization_barrier((values, other))[0]


def per_device(orbitals):
    tables = section_tables()
    kern = screening()
    size = lax.axis_size("band")
    share = -2.0 / (NGRID * 2 * size * orbitals.shape[0])
    raw = orbitals.reshape(2, ROWS, LANES).transpose(1, 0, 2).reshape(2 * ROWS, LANES)
    own = [take_band(raw, 0)]
    own.append(take_band(raw, 1, own))
    previous = [from_behind(part, "band", 1) for part in own]
    own_u, thirds = padded_rows(own, tables[-1])
    terms, back0, energy = pair_terms(
        thirds, own_u, previous[0], (), tables, kern, (STEPS,), share
    )
    back0 = from_behind(back0, "band", -1)
    terms, *sent, energy = pair_terms(
        thirds, own_u, previous[1], (terms, energy), tables, kern, PIECES, share
    )
    back1 = [from_behind(piece, "band", -1) for piece in sent]

    steps = []
    if size & (size - 1):
        energy = lax.psum(energy, "band")
    else:
        swap = [(i, i ^ 1) for i in range(size)]
        energy = energy + lax.ppermute(energy, "band", swap)
        bits = [1 << b for b in range(2, size.bit_length() - 1)]
        steps = [bits[:1]] + [bits[i : i + 2] for i in range(1, len(bits), 2)]
        steps = [group for group in steps + [[2][: size // 4]] if group]
    while len(steps) > len(back1) - 1:
        energy = add_up(energy, send_among_odd(energy, "band", steps.pop(0)))
    exchange, grams = None, []
    first = 0
    for count, piece in zip(PIECES, back1):
        count *= STEP_ROWS
        got, last = None, piece is back1[-1]
        if last and size & (size - 1) == 0:
            got = lax.ppermute(energy, "band", swap)
            energy = energy[:1, :1]
        elif steps:
            got = send_among_odd(energy, "band", steps.pop(0))
        exchange, gram = add_piece(
            first, count, thirds, terms, back0, piece, energy, grams, exchange
        )
        if got is not None and last:
            odd = lax.axis_index("band") % 2 == 1
            energy = jnp.where(odd, energy, after(got, gram)[:1, :1])
        elif got is not None:
            energy = add_up(energy, after(got, gram))
        grams.append(gram)
        first += count
    exchange = exchange.reshape(ROWS, 2, LANES).transpose(1, 0, 2).reshape(2, NGRID)
    return exchange, gram, energy[0, 0]


def solution(mesh):
    return jax.shard_map(
        per_device,
        mesh=mesh,
        in_specs=(P("band", None),),
        out_specs=(P("band", None), P("band", None), P()),
        check_vma=False,
    )
```

```python
import functools

import jax
import jax.numpy as jnp
import ml_dtypes
import numpy as np
from jax import lax
from jax.experimental import pallas as pl
from jax.experimental.pallas import tpu as pltpu
from jax.sharding import PartitionSpec as P

G = 96
HALF = G // 2 + 1
NGRID = G * G * G
LANES = 128
ROWS = NGRID // LANES
PLANE = G * G // LANES
QUADS = G // 4
KPAD = HALF + 1
Y_ROWS = 104
Y_PITCH = Y_ROWS + 1
Z_PITCH = G + 1
W_PITCH = 2 * G + 1
Z_ROWS = KPAD * Z_PITCH
F_PITCH = PLANE + 1
PLANES = 16
STEP_ROWS = PLANES * QUADS
THIRD = G * QUADS
STEPS = G // PLANES
PIECES = (3, 2, 1)
WAVE_UNIT = 0.05
SCREEN_SQ = 0.0121
MIB = 1024 * 1024
BF16 = jnp.bfloat16
F32 = jnp.float32


def dft_tables():
    n = np.arange(G)
    phases = (n[:, None] * n[None, :]) % G
    angles = phases.astype(np.float32) * np.float32(2.0 * np.pi / G)
    rounded = [f(angles).astype(ml_dtypes.bfloat16).astype(np.float32) for f in (np.cos, np.sin)]
    return rounded[0], rounded[1]


def section_tables():
    c, s = dft_tables()
    h = HALF
    t1 = np.zeros((Y_ROWS, G), np.float32)
    t1[:h] = c[:h]
    t1[h : 2 * h] = -s[:h]
    t2 = np.block([[c, s], [-s, c]])
    t3 = np.zeros((2, LANES, 4, 64), np.float32)
    back = (G - np.arange(h)) % G
    t3[0, :G, 0, :h] = c[:h].T
    t3[1, :G, 0, :h] = s[:h].T
    t3[0, :G, 1, :h] = -s[:h].T
    t3[1, :G, 1, :h] = c[:h].T
    t3[0, :G, 2, :h] = c[back].T
    t3[1, :G, 2, :h] = s[back].T
    t3[0, :G, 3, :h] = s[back].T
    t3[1, :G, 3, :h] = -c[back].T
    t3 = t3.reshape(2 * LANES, 4 * 64)
    order = np.concatenate([np.arange(G // 2), G - 1 - np.arange(G // 2)])
    a1 = np.block([[c[:, order], -s[:, order]], [s[:, order], c[:, order]]])
    rows = np.arange(G).reshape(QUADS, 4).T.reshape(-1)
    a2 = np.block([[c[rows], -s[rows]], [s[rows], c[rows]]])
    weight = np.full((h, 1), 2.0, np.float32)
    weight[0] = weight[h - 1] = 1.0
    a3 = np.zeros((3, 2, 2, 2, 64, 2, LANES), np.float32)
    for third in range(3):
        for lane in range(LANES):
            r, x3 = divmod(third * LANES + lane, G)
            for p in range(2):
                a3[third, r - third, 0, p, :h, p, lane] = weight[:, 0] * c[x3, :h]
                a3[third, r - third, 1, p, :h, p, lane] = -weight[:, 0] * s[x3, :h]
    a3 = a3.reshape(3, 4 * LANES, 2 * LANES)
    sel = np.zeros((2, 2 * LANES, 2 * LANES), np.float32)
    for r in range(4):
        for x in range(G):
            sel[r // 2, r * G + x - (r // 2) * LANES, (r % 2) * LANES + x] = 1.0
    return [t.astype(ml_dtypes.bfloat16) for t in (t1, t2, t3, a1, a2, a3, sel)]


def screening():
    n = np.arange(G)
    m = np.where(n <= G // 2, n, n - G).astype(np.float64)
    sq = m * m
    q2 = WAVE_UNIT * (sq[:HALF, None, None] + sq[None, :, None] + sq[None, None, :HALF])
    safe = np.where(q2 > 0, q2, 1.0)
    kern = 4.0 * np.pi * (1.0 - np.exp(-q2 / (4.0 * SCREEN_SQ))) / safe
    kern = np.where(q2 > 0, kern, np.pi / SCREEN_SQ)
    out = np.zeros((KPAD, G, 2, 64), np.float32)
    out[:HALF, :, :, :HALF] = kern[:, :, None, :]
    return out.reshape(KPAD * G, LANES)


def cost(size):
    return pl.CostEstimate(flops=0, bytes_accessed=size, transcendentals=0)


def dot(a, b):
    return jnp.dot(a, b, preferred_element_type=F32)


def lanes(*parts):
    return jnp.concatenate(parts, axis=1)


def stack(*parts):
    return jnp.concatenate(parts, axis=0)


def split_rows(src, sel_ref, out, first, count):
    rows = [
        [src[pl.ds(3 * (first + i) + s, G, stride=F_PITCH), :].astype(BF16) for s in range(3)]
        for i in range(count)
    ]
    for half in range(2):
        part = dot(stack(*[lanes(r[half], r[half + 1]) for r in rows]), sel_ref[half])
        for i in range(count):
            for e in range(2):
                value = part[i * G : (i + 1) * G, e * LANES : (e + 1) * LANES]
                out[4 * (first + i) + 2 * half + e] = value.astype(BF16)


def widen_planes(src, dst, first):
    @pl.loop(0, src.shape[0] // (2 * PLANE), unroll=8)
    def _(i):
        value = src[pl.ds(pl.multiple_of(i * 2 * PLANE, 16), 2 * PLANE), :].astype(F32)
        dst[pl.ds((first + 2 * i) * F_PITCH, PLANE), :] = value[:PLANE]
        dst[pl.ds((first + 2 * i + 1) * F_PITCH, PLANE), :] = value[PLANE:]


def rows_of(ref, first, count):
    return ref.at[(slice(None),) * (len(ref.shape) - 2) + (pl.ds(first, count), slice(None))]


def copy_rows(src, src_row, dst, dst_row, count, sem):
    return pltpu.make_async_copy(rows_of(src, src_row, count), rows_of(dst, dst_row, count), sem)


def band_kernel(p, raw, *refs):
    out, raw_v, out_v, load_sems, store_sem = refs[-5:]
    chunks = load_sems.shape[0]
    rows = out.shape[0] // chunks
    loads = [
        copy_rows(raw, 2 * c * rows, raw_v, 2 * c * rows, 2 * rows, load_sems.at[c])
        for c in range(chunks)
    ]
    for load in loads:
        load.start()
    shape = (LANES, 2 * LANES)
    row = lax.broadcasted_iota(jnp.int32, shape, 0)
    column = lax.broadcasted_iota(jnp.int32, shape, 1)
    pick = jnp.where(column == 2 * row + p, F32(1.0), F32(0.0)).astype(BF16)
    for c, load in enumerate(loads):
        load.wait()
        for row in range(c * rows, (c + 1) * rows, 2 * LANES):
            blocks = [raw_v[2 * at : 2 * at + 2 * LANES, :] for at in (row, row + LANES)]
            value = dot(pick, lanes(*blocks)).astype(BF16)
            out_v[row : row + LANES, :] = value[:, :LANES]
            out_v[row + LANES : row + 2 * LANES, :] = value[:, LANES:]
        copy_rows(out_v, c * rows, out, c * rows, rows, store_sem).start()
    pltpu.make_async_copy(out_v, out, store_sem).wait()


def take_band(raw, p, earlier=(), interpret=False):
    hbm = pl.BlockSpec(memory_space=pl.ANY)
    return pl.pallas_call(
        functools.partial(band_kernel, p),
        out_shape=jax.ShapeDtypeStruct((ROWS, LANES), BF16),
        in_specs=[hbm] * (1 + len(earlier)),
        out_specs=hbm,
        scratch_shapes=[
            pltpu.VMEM((2 * ROWS, LANES), BF16),
            pltpu.VMEM((ROWS, LANES), BF16),
            pltpu.SemaphoreType.DMA((9,)),
            pltpu.SemaphoreType.DMA,
        ],
        compiler_params=pltpu.CompilerParams(vmem_limit_bytes=63 * MIB),
        cost_estimate=cost(6 * ROWS * LANES),
        interpret=interpret,
        name="take_band",
    )(raw, *earlier)


def rows_kernel(own0, own1, sel, out, thirds, wide):
    for p, own in enumerate((own0, own1)):
        widen_planes(own, wide, 0)

        @pl.loop(0, QUADS // 4, unroll=2)
        def _(q):
            split_rows(wide, sel, out.at[p], 4 * q, 4)

        @pl.loop(0, G // 2, unroll=4)
        def _(i):
            for s in range(3):
                rows = [wide[pl.ds((2 * i + e) * F_PITCH + s, QUADS, stride=3), :] for e in range(2)]
                at = pl.multiple_of(2 * i * QUADS, 16)
                thirds[p, s, pl.ds(at, 2 * QUADS), :] = stack(*rows).astype(BF16)


def padded_rows(own, sel, interpret=False):
    vmem = pl.BlockSpec(memory_space=pltpu.VMEM)
    return pl.pallas_call(
        rows_kernel,
        out_shape=(
            jax.ShapeDtypeStruct((2, G, G, LANES), BF16),
            jax.ShapeDtypeStruct((2, 3, THIRD, LANES), BF16),
        ),
        in_specs=[vmem] * 3,
        out_specs=(vmem, vmem),
        scratch_shapes=[pltpu.VMEM((G * F_PITCH, LANES), F32)],
        compiler_params=pltpu.CompilerParams(vmem_limit_bytes=63 * MIB),
        cost_estimate=cost(16 * NGRID),
        interpret=interpret,
        name="padded_rows",
    )(*own, sel)


def pairs_kernel(pieces, share, own, own_u, kern, par, *refs):
    earlier = []
    if len(pieces) > 1:
        earlier, refs = refs[:2], refs[2:]
    table_refs, own_out = refs[:7], refs[7]
    par_out, energy_out = refs[8 : 8 + len(pieces)], refs[8 + len(pieces)]
    own_v, own_uv, kern_v, own_ov, par_ov, par_f, par_u, yw, z, x34 = refs[9 + len(pieces) : -15]
    par_v, total_ref, energy_v, before_v = refs[-15:-11]
    tables, (par_sems, table_sems, before_sems, sems) = refs[-11:-4], refs[-4:]
    t1, t2, t3, a1, a2, a3, sel = tables
    par_loads = []
    for first in (0, ROWS // 2):
        sem = par_sems.at[len(par_loads)]
        par_loads.append(copy_rows(par, first, par_v, first, ROWS // 2, sem))
    for load in par_loads:
        load.start()
    table_loads = [
        pltpu.make_async_copy(src, dst, table_sems.at[i])
        for i, (src, dst) in enumerate(zip(table_refs, tables))
    ]
    table_loads[6].start()
    table_loads[0].start()
    loads = [
        pltpu.make_async_copy(own_u.at[:, : G // 2], own_uv.at[:, : G // 2], sems.at[0]),
        pltpu.make_async_copy(kern, kern_v, sems.at[1]),
        pltpu.make_async_copy(own, own_v, sems.at[2]),
    ]
    rest_u = pltpu.make_async_copy(
        own_u.at[:, G // 2 :], own_uv.at[:, G // 2 :], sems.at[6 + len(pieces)]
    )
    later = []
    if earlier:
        group = 2 * STEP_ROWS
        later = [
            [
                copy_rows(earlier[0].at[p, s], row, z, (3 * p + s) * THIRD + row, group, before_sems.at[g, 3 * p + s])
                for p in range(2)
                for s in range(3)
            ]
            for g, row in enumerate(range(0, THIRD, group))
        ]
        loads.append(pltpu.make_async_copy(earlier[1], before_v, sems.at[3]))

    for i, load in enumerate(par_loads):
        load.wait()
        for other in ([loads[0]], [rest_u, *table_loads[1:5]])[i]:
            other.start()
        widen_planes(par_v.at[pl.ds(i * ROWS // 2, ROWS // 2), :], par_f, i * G // 2)
    table_loads[6].wait()

    @pl.loop(0, QUADS // 4, unroll=6)
    def _(q):
        split_rows(par_f, sel, par_u, 4 * q, 4)

    half_y = G * Y_PITCH
    for half in range(2):
        if half == 0:
            loads[0].wait()
            table_loads[0].wait()
        else:
            rest_u.wait()
            for load in loads[1:]:
                load.start()
            table_loads[5].start()

        @pl.loop(0, G // 4, unroll=G // 4)
        def _(i):
            b = half * G // 2 + 2 * i
            density = []
            for e in range(2):
                partner = par_u[b + e].astype(F32)
                for p in range(2):
                    density.append((own_uv[p, b + e].astype(F32) * partner).astype(BF16))
            out = dot(t1[...], lanes(*density))
            for e in range(2):
                for p in range(2):
                    at = pl.ds(p * half_y + (b + e) * Y_PITCH, Y_ROWS)
                    yw[at, :] = out[:, (2 * e + p) * LANES : (2 * e + p + 1) * LANES]

    table_loads[1].wait()

    @pl.loop(0, KPAD // 2, unroll=25)
    def _(pair):
        def line(k1, part):
            first = part * HALF + k1
            rows = [yw[pl.ds(p * half_y + first, G, stride=Y_PITCH), :].astype(BF16) for p in range(2)]
            return lanes(*rows)

        both = [2 * pair, 2 * pair + 1]
        out = dot(t2[...], lanes(*[stack(line(k1, 0), line(k1, 1)) for k1 in both]))
        for e, k1 in enumerate(both):
            at = pl.ds(pl.multiple_of(k1 * G, 16), G)
            for p in range(2):
                for part in range(2):
                    left = (2 * p + part) * LANES
                    right = (2 * e + p) * LANES
                    value = out[part * G : (part + 1) * G, right : right + LANES]
                    x34[at, left : left + LANES] = value.astype(BF16)

    loads[1].wait()
    table_loads[2].wait()

    many = 5

    @pl.loop(0, KPAD // many, unroll=10)
    def _(m):
        at = pl.ds(pl.multiple_of(m * many * G, 16), many * G)
        factor = kern_v[at, :]
        out = [
            dot(x34[at, 2 * p * LANES : 2 * (p + 1) * LANES], t3[...]).astype(BF16)
            for p in range(2)
        ]
        for part in range(4):
            spectrum = lanes(*[o[:, part * 64 : (part + 1) * 64] for o in out]).astype(F32)
            value = spectrum * factor
            for i in range(many):
                row = part * Z_ROWS + (many * m + i) * Z_PITCH
                z[pl.ds(row, G), :] = value[i * G : (i + 1) * G]

    table_loads[3].wait()

    @pl.loop(0, G // 4, unroll=24)
    def _(four):
        parts = []
        for e in range(4):
            k2 = 4 * four + e
            mirror = Z_PITCH + jnp.where(k2 == 0, 0, G - k2)
            parts.append(
                stack(
                    z[pl.ds(k2, G // 2, stride=Z_PITCH), :].astype(BF16),
                    z[pl.ds(2 * Z_ROWS + mirror, G // 2, stride=Z_PITCH), :].astype(BF16),
                    z[pl.ds(1 * Z_ROWS + k2, G // 2, stride=Z_PITCH), :].astype(BF16),
                    z[pl.ds(3 * Z_ROWS + mirror, G // 2, stride=Z_PITCH), :].astype(BF16),
                )
            )
        out = dot(a1[...], lanes(*parts))
        for e in range(4):
            at = (4 * four + e) * W_PITCH
            yw[pl.ds(at, 2 * G), :] = out[:, e * LANES : (e + 1) * LANES]

    for load in sum(later, []):
        load.start()
    table_loads[4].wait()

    @pl.loop(0, G // 4, unroll=24)
    def _(four):
        parts = []
        for e in range(4):
            x1 = 4 * four + e
            parts.append(
                stack(
                    yw[pl.ds(x1, G, stride=W_PITCH), :].astype(BF16),
                    yw[pl.ds(G + x1, G, stride=W_PITCH), :].astype(BF16),
                )
            )
        out = dot(a2[...], lanes(*parts))
        for r in range(4):
            block = [
                lanes(
                    out[r * QUADS : (r + 1) * QUADS, e * LANES : (e + 1) * LANES],
                    out[G + r * QUADS : G + (r + 1) * QUADS, e * LANES : (e + 1) * LANES],
                )
                for e in range(4)
            ]
            at = pl.multiple_of((r // 2) * G * QUADS + four * 4 * QUADS, 16)
            left = (r % 2) * 2 * LANES
            x34[pl.ds(at, 4 * QUADS), left : left + 2 * LANES] = stack(*block).astype(BF16)

    table_loads[5].wait()
    for load in loads[2:]:
        load.wait()
    total_ref[...] = jnp.zeros_like(total_ref)
    scale = F32(1.0 / NGRID)

    def result(ch):
        at = ch * STEP_ROWS
        rows = pl.ds(at, STEP_ROWS)
        low = x34[rows, :]
        high = x34[pl.ds(THIRD + at, STEP_ROWS), :]
        fields = [low, lanes(low[:, 2 * LANES :], high[:, : 2 * LANES]), high]
        total = jnp.zeros((8, LANES), F32)
        for third in range(3):
            out = dot(fields[third], a3[third]) * scale
            first = ch * PLANES * F_PITCH + third
            partner = stack(
                *[par_f[pl.ds(first + i * F_PITCH, QUADS, stride=3), :] for i in range(PLANES)]
            )
            sent = None
            for p in range(2):
                potential = out[:, p * LANES : (p + 1) * LANES]
                term = potential * partner
                if earlier:
                    term = term + z[pl.ds((3 * p + third) * THIRD + at, STEP_ROWS), :]
                own_ov[p, third, rows, :] = term
                part = potential * own_v[p, third, rows, :].astype(F32)
                sent = part if sent is None else sent + part
            total = total + jnp.sum((sent * partner).reshape(-1, 8, LANES), axis=0)
            par_ov[third, rows, :] = sent.astype(BF16)
        total_ref[...] += total
        copy_rows(own_ov, at, own_out, at, STEP_ROWS, sems.at[4]).start()

    ch = 0
    for i, steps in enumerate(pieces):
        for step in range(steps):
            for load in later[ch // 2] if earlier and ch % 2 == 0 else ():
                load.wait()
            result(ch)
            source, row = ch * STEP_ROWS, step * STEP_ROWS
            copy_rows(par_ov, source, par_out[i], row, STEP_ROWS, sems.at[6 + i]).start()
            ch += 1

    energy = jnp.zeros((8, LANES), F32) + jnp.sum(total_ref[...]) * F32(share)
    if earlier:
        energy = energy + before_v[...]
    energy_v[...] = energy
    report = pltpu.make_async_copy(energy_v, energy_out, sems.at[5])
    report.start()
    pltpu.make_async_copy(own_ov, own_out, sems.at[4]).wait()
    first = 0
    for i, steps in enumerate(pieces):
        rows = steps * STEP_ROWS
        copy_rows(par_ov, first, par_out[i], 0, rows, sems.at[6 + i]).wait()
        first += rows
    report.wait()


def pair_terms(own, own_u, partner, earlier, tables, kern, pieces, share, interpret=False):
    hbm = pl.BlockSpec(memory_space=pl.ANY)
    return pl.pallas_call(
        functools.partial(pairs_kernel, pieces, share),
        out_shape=(
            jax.ShapeDtypeStruct((2, 3, THIRD, LANES), F32),
            *[jax.ShapeDtypeStruct((3, steps * STEP_ROWS, LANES), BF16) for steps in pieces],
            jax.ShapeDtypeStruct((8, LANES), F32),
        ),
        in_specs=[hbm] * (4 + len(earlier) + len(tables)),
        out_specs=(hbm,) * (2 + len(pieces)),
        scratch_shapes=[
            pltpu.VMEM((2, 3, THIRD, LANES), BF16),
            pltpu.VMEM((2, G, G, LANES), BF16),
            pltpu.VMEM((KPAD * G, LANES), F32),
            pltpu.VMEM((2, 3, THIRD, LANES), F32),
            pltpu.VMEM((3, THIRD, LANES), BF16),
            pltpu.VMEM((G * F_PITCH, LANES), F32),
            pltpu.VMEM((G, G, LANES), BF16),
            pltpu.VMEM((2 * G * Y_PITCH, LANES), F32),
            pltpu.VMEM((4 * Z_ROWS, LANES), F32),
            pltpu.VMEM((KPAD * G, 4 * LANES), BF16),
            pltpu.VMEM((ROWS, LANES), BF16),
            pltpu.VMEM((8, LANES), F32),
            pltpu.VMEM((8, LANES), F32),
            pltpu.VMEM((8, LANES), F32),
            *[pltpu.VMEM(table.shape, BF16) for table in tables],
            pltpu.SemaphoreType.DMA((2,)),
            pltpu.SemaphoreType.DMA((len(tables),)),
            pltpu.SemaphoreType.DMA((3, 6)),
            pltpu.SemaphoreType.DMA((7 + len(pieces),)),
        ],
        compiler_params=pltpu.CompilerParams(vmem_limit_bytes=63 * MIB),
        cost_estimate=pl.CostEstimate(
            flops=20_000_000_000, bytes_accessed=20_000_000, transcendentals=0
        ),
        interpret=interpret,
        name="pair_terms",
    )(own, own_u, kern, partner, *earlier, *tables)


def piece_kernel(first, size, own, terms, back0, back1, *rest):
    last = first + size == THIRD
    earlier = rest[: len(rest) - 12]
    out, gram_out, own_v, terms_v, back_v, out_v, gram_ref, gram_v, value_ref = rest[-12:-3]
    load_sems, gram_sems, store_sems = rest[-3:]
    rows = size // load_sems.shape[0]
    wide = 6 * rows

    def loads(c):
        start = first + c * rows
        sources = [
            (own, start, own_v), (terms, start, terms_v),
            (back0, start, back_v.at[0]), (back1, c * rows, back_v.at[1]),
        ]
        return [
            copy_rows(src, row, dst, c * rows, rows, load_sems.at[c, i])
            for i, (src, row, dst) in enumerate(sources)
        ]

    chunks = [loads(c) for c in range(load_sems.shape[0])]
    for chunk in chunks:
        for load in chunk:
            load.start()
    gram_loads = []
    if last:
        gram_loads = [
            pltpu.make_async_copy(src, gram_v.at[i], gram_sems.at[i])
            for i, src in enumerate(earlier[:-1])
        ]
        for load in gram_loads:
            load.start()
    gram_ref[...] = jnp.zeros_like(gram_ref)
    for c, chunk in enumerate(chunks):
        for load in chunk:
            load.wait()
        at = pl.ds(c * rows, rows)
        for s in range(3):
            bands = [own_v[i, s, at, :].astype(F32) for i in range(2)]
            for p in range(2):
                exchange = terms_v[p, s, at, :] + back_v[p, s, at, :].astype(F32)
                for i in range(rows // QUADS):
                    row = c * wide + 2 * (i * PLANE + s) + p
                    out_v[pl.ds(row, QUADS, stride=6), :] = exchange[i * QUADS : (i + 1) * QUADS]
                for i in range(2):
                    product = (bands[i] * exchange).reshape(-1, 8, LANES)
                    gram_ref[i, p] += jnp.sum(product, axis=0)
        copy_rows(out_v, c * wide, out, 6 * first + c * wide, wide, store_sems.at[0]).start()

    result = gram_ref
    if last:
        for load in gram_loads:
            load.wait()
        row = lax.broadcasted_iota(jnp.int32, (2, 2), 0)
        column = lax.broadcasted_iota(jnp.int32, (2, 2), 1)
        value = jnp.zeros((2, 2), F32)
        for i in range(2):
            for j in range(2):
                entry = gram_ref[i, j]
                for k in range(len(gram_loads)):
                    entry = entry + gram_v[k, i, j]
                value = jnp.where((row == i) & (column == j), jnp.sum(entry) * F32(1.0 / NGRID), value)
        value_ref[...] = value
        result = value_ref
    report = pltpu.make_async_copy(result, gram_out, store_sems.at[1])
    report.start()
    copy_rows(out_v, 0, out, 6 * first, 6 * size, store_sems.at[0]).wait()
    report.wait()


def add_piece(first, size, own, terms, back0, back1, grams, out, interpret=False):
    hbm = pl.BlockSpec(memory_space=pl.ANY)
    last = first + size == THIRD
    earlier = [] if out is None else [*(grams if last else []), out]
    gram_shape = (2, 2, 8, LANES)
    return pl.pallas_call(
        functools.partial(piece_kernel, first, size),
        out_shape=(
            jax.ShapeDtypeStruct((2 * ROWS, LANES), F32),
            jax.ShapeDtypeStruct((2, 2) if last else gram_shape, F32),
        ),
        in_specs=[hbm] * (4 + len(earlier)),
        out_specs=(hbm, hbm),
        scratch_shapes=[
            pltpu.VMEM((2, 3, size, LANES), BF16),
            pltpu.VMEM((2, 3, size, LANES), F32),
            pltpu.VMEM((2, 3, size, LANES), BF16),
            pltpu.VMEM((6 * size, LANES), F32),
            pltpu.VMEM(gram_shape, F32),
            pltpu.VMEM((len(PIECES), *gram_shape), F32),
            pltpu.VMEM((2, 2), F32),
            pltpu.SemaphoreType.DMA((2 * size // STEP_ROWS, 4)),
            pltpu.SemaphoreType.DMA((len(PIECES),)),
            pltpu.SemaphoreType.DMA((2,)),
        ],
        input_output_aliases={3 + len(earlier): 0} if earlier else {},
        compiler_params=pltpu.CompilerParams(vmem_limit_bytes=52 * MIB),
        cost_estimate=cost(72 * size * LANES),
        interpret=interpret,
        name="add_piece",
    )(own, terms, back0, back1, *earlier)


def from_behind(block, axis, distance):
    size = lax.axis_size(axis)
    return lax.ppermute(block, axis, [((i - distance) % size, i) for i in range(size)])


def after(values, other):
    return lax.optimization_barrier((values, other))[0]


def per_device(orbitals):
    tables = section_tables()
    kern = screening()
    size = lax.axis_size("band")
    share = -2.0 / (NGRID * 2 * size * orbitals.shape[0])
    raw = orbitals.reshape(2, ROWS, LANES).transpose(1, 0, 2).reshape(2 * ROWS, LANES)
    own = [take_band(raw, 0)]
    own.append(take_band(raw, 1, own))
    previous = [from_behind(part, "band", 1) for part in own]
    own_u, thirds = padded_rows(own, tables[-1])
    terms, back0, energy = pair_terms(
        thirds, own_u, previous[0], (), tables, kern, (STEPS,), share
    )
    back0 = from_behind(back0, "band", -1)
    terms, *sent, energy = pair_terms(
        thirds, own_u, previous[1], (terms, energy), tables, kern, PIECES, share
    )
    back1 = [from_behind(piece, "band", -1) for piece in sent]

    steps = []
    if size & (size - 1):
        energy = lax.psum(energy, "band")
    else:
        swap = [(i, i ^ 1) for i in range(size)]
        energy = energy + lax.ppermute(energy, "band", swap)
        steps = [1 << b for b in range(1, size.bit_length() - 1)]
        steps = [b for b in steps if b != 2] + [b for b in steps if b == 2]
        aside = [4 if size > 4 else 2, 8 if size > 8 else 2]
        steps = [[(i, i ^ (b if i % 2 else aside[i // 2 % 2])) for i in range(size)] for b in steps]
    while len(steps) > len(back1) - 1:
        energy = energy + lax.ppermute(energy, "band", steps.pop(0))
    exchange, grams = None, []
    first = 0
    for count, piece in zip(PIECES, back1):
        count *= STEP_ROWS
        got, last = None, piece is back1[-1]
        if last and size & (size - 1) == 0:
            got = lax.ppermute(energy, "band", swap)
        elif steps:
            got = lax.ppermute(energy, "band", steps.pop(0))
        exchange, gram = add_piece(first, count, thirds, terms, back0, piece, grams, exchange)
        if got is not None and last:
            odd = lax.axis_index("band") % 2 == 1
            energy = jnp.where(odd, energy[:1, :1], after(got, gram)[:1, :1])
        elif got is not None:
            energy = energy + after(got, gram)
        grams.append(gram)
        first += count
    exchange = exchange.reshape(ROWS, 2, LANES).transpose(1, 0, 2).reshape(2, NGRID)
    return exchange, gram, energy[0, 0]


def solution(mesh):
    return jax.shard_map(
        per_device,
        mesh=mesh,
        in_specs=(P("band", None),),
        out_specs=(P("band", None), P("band", None), P()),
        check_vma=False,
    )
```
